32 devices in a mesh: tm: 2 (over x), space: 4 (over z), clip: 4 (over y, core).
Axes of the slice: x: 2, y: 2, z: 4, core: 2. Of those that a mesh axis runs over, the one named last changes fastest.
Arguments:
- clips_in: bfloat16 [4, 32, 4, 49, 512], P('clip', 'tm', 'space'), may hold values from -6 to 6
- ln1_gain: bfloat16 [2, 512], P(None, ('tm', 'space', 'clip')), may hold values from 0.5 to 1.5
- ln1_bias: bfloat16 [2, 512], P(None, ('tm', 'space', 'clip')), may hold values from -1 to 1
- qkv_weight: bfloat16 [2, 512, 1536], P(None, ('tm', 'space', 'clip')), may hold values from -0.25 to 0.25
- qv_bias: bfloat16 [2, 1024], P(None, ('tm', 'space', 'clip')), may hold values from -1.5 to 1.5
- out_weight: bfloat16 [2, 512, 512], P(None, ('tm', 'space', 'clip')), may hold values from -1 to 1
- out_bias: bfloat16 [2, 512], P(None, ('tm', 'space', 'clip')), may hold values from -1 to 1
- ln2_gain: bfloat16 [2, 512], P(None, ('tm', 'space', 'clip')), may hold values from 0.5 to 1.5
- ln2_bias: bfloat16 [2, 512], P(None, ('tm', 'space', 'clip')), may hold values from -1 to 1
- fc1_weight: bfloat16 [2, 512, 2048], P(None, ('tm', 'space', 'clip')), may hold values from -0.25 to 0.25
- fc1_bias: bfloat16 [2, 2048], P(None, ('tm', 'space', 'clip')), may hold values from -1.5 to 1.5
- fc2_weight: bfloat16 [2, 2048, 512], P(None, ('tm', 'space', 'clip')), may hold values from -0.125 to 0.125
- fc2_bias: bfloat16 [2, 512], P(None, ('tm', 'space', 'clip')), may hold values from -1 to 1
- pos_table: bfloat16 [2, 2535, 16], P(None, None, 'tm'), may hold values from -4 to 4
- out_grad: bfloat16 [4, 32, 4, 49, 512], P('clip', 'tm', 'space'), may hold values from -6 to 6
Outputs:
- clips_out: bfloat16 [4, 32, 4, 49, 512], P('clip', 'tm', 'space')
- in_grad: bfloat16 [4, 32, 4, 49, 512], P('clip', 'tm', 'space')
- ln1_gain_grad: float32 [2, 512], P(None, ('tm', 'space', 'clip'))
- ln1_bias_grad: float32 [2, 512], P(None, ('tm', 'space', 'clip'))
- qkv_weight_grad: float32 [2, 512, 1536], P(None, ('tm', 'space', 'clip'))
- qv_bias_grad: float32 [2, 1024], P(None, ('tm', 'space', 'clip'))
- out_weight_grad: float32 [2, 512, 512], P(None, ('tm', 'space', 'clip'))
- out_bias_grad: float32 [2, 512], P(None, ('tm', 'space', 'clip'))
- ln2_gain_grad: float32 [2, 512], P(None, ('tm', 'space', 'clip'))
- ln2_bias_grad: float32 [2, 512], P(None, ('tm', 'space', 'clip'))
- fc1_weight_grad: float32 [2, 512, 2048], P(None, ('tm', 'space', 'clip'))
- fc1_bias_grad: float32 [2, 2048], P(None, ('tm', 'space', 'clip'))
- fc2_weight_grad: float32 [2, 2048, 512], P(None, ('tm', 'space', 'clip'))
- fc2_bias_grad: float32 [2, 512], P(None, ('tm', 'space', 'clip'))
- pos_table_grad: float32 [2, 2535, 16], P(None, None, 'tm')
The draws below stay inside these ranges and needn't reach their ends.
All inputs are finite; a program needn't handle non-finite values.
Results may differ from the reference program's by a relative error of at most 0.017.
Values may be sent and summed in bfloat16 or wider, within the bound.
No kernel may reach another device: no remote copies, remote signals or barrier semaphores. Data moves between devices by JAX's collectives and lax.ppermute only.
A program may use at most 320 MiB of HBM per device.

```python
import jax
import jax.numpy as jnp
from jax import lax

D = 512
HEADS = 16
MLP = 2048
WIN_T = 8
WIN_HW = 7
FRAMES = 32
LAYERS = 2
CLIPS = 4
RPB = 2535


def shard_levels(own_key, dims, cuts, smallest, high):
    factor_of, own = 1.0, jax.random.fold_in(own_key, 6)
    for axis_at, blocks in cuts:
        steps = jnp.exp(jax.random.uniform(jax.random.fold_in(own, axis_at), (blocks,), jnp.float32, smallest / len(cuts), high / len(cuts)))
        factor_of = factor_of * jnp.repeat(steps, dims[axis_at] // blocks).reshape([-1 if axis == axis_at else 1 for axis in range(len(dims))])
    return factor_of


def noise(own_key, shape, scale, limit, shards=(), kind=jnp.bfloat16):
    values = scale * jax.random.normal(own_key, shape, jnp.float32)
    if shards:
        values = values * shard_levels(own_key, shape, shards, -0.22, 0.18)
    return jnp.clip(values, -limit, limit).astype(kind)


def setup_inputs(seed: int = 0) -> dict:
    arg_keys = jax.random.split(jax.random.key(seed), 16)
    clips_in = noise(arg_keys[0], (CLIPS, FRAMES, 4, WIN_HW * WIN_HW, D), 1.0, 6.0, ((0, 4), (1, 2), (2, 4)))
    ln1_gain = jnp.clip(1.0 + 0.1 * jax.random.normal(arg_keys[1], (LAYERS, D), jnp.float32), 0.5, 1.5).astype(jnp.bfloat16)
    ln1_bias = noise(arg_keys[2], (LAYERS, D), 0.2, 1.0, ((1, 32),))
    qkv_weight = noise(arg_keys[3], (LAYERS, D, 3 * D), D ** -0.5, 0.25, ((1, 32),))
    qv_bias = noise(arg_keys[4], (LAYERS, 2 * D), 0.3, 1.5, ((1, 32),))
    out_weight = noise(arg_keys[5], (LAYERS, D, D), (D // 16) ** -0.5, 1.0, ((1, 32),))
    out_bias = noise(arg_keys[6], (LAYERS, D), 0.2, 1.0, ((1, 32),))
    ln2_gain = jnp.clip(1.0 + 0.1 * jax.random.normal(arg_keys[7], (LAYERS, D), jnp.float32), 0.5, 1.5).astype(jnp.bfloat16)
    ln2_bias = noise(arg_keys[8], (LAYERS, D), 0.2, 1.0, ((1, 32),))
    fc1_weight = noise(arg_keys[9], (LAYERS, D, MLP), D ** -0.5, 0.25, ((1, 32),))
    fc1_bias = noise(arg_keys[10], (LAYERS, MLP), 0.3, 1.5, ((1, 32),))
    fc2_weight = noise(arg_keys[11], (LAYERS, MLP, D), MLP ** -0.5, 0.125, ((1, 32),))
    fc2_bias = noise(arg_keys[12], (LAYERS, D), 0.2, 1.0, ((1, 32),))
    pos_table = noise(arg_keys[13], (LAYERS, RPB, HEADS), 1.0, 4.0, ((2, 2),))
    out_grad = noise(arg_keys[14], (CLIPS, FRAMES, 4, WIN_HW * WIN_HW, D), 1.0, 6.0, ((0, 4), (1, 2), (2, 4)))
    return dict(clips_in=clips_in, ln1_gain=ln1_gain, ln1_bias=ln1_bias, qkv_weight=qkv_weight, qv_bias=qv_bias, out_weight=out_weight, out_bias=out_bias, ln2_gain=ln2_gain, ln2_bias=ln2_bias, fc1_weight=fc1_weight, fc1_bias=fc1_bias, fc2_weight=fc2_weight, fc2_bias=fc2_bias, pos_table=pos_table, out_grad=out_grad)


@jax.custom_vjp
def low(v):
    return lax.optimization_barrier(v.astype(jnp.bfloat16)).astype(jnp.float32)

@jax.custom_vjp
def low_back(v):
    return v

def low_keep(v):
    return (low(v), None)

def low_pass(kept, grad):
    return (grad,)

def back_keep(v):
    return (v, None)

def back_low(kept, grad):
    return (low(grad),)
low.defvjp(low_keep, low_pass)
low_back.defvjp(back_keep, back_low)

def dense(left, right):
    return jnp.einsum('...i,ij->...j', left, right, precision=lax.Precision.HIGHEST)

def norm_rows(values, gain, offset):
    mean_row = lax.optimization_barrier(jnp.mean(values, axis=-1, keepdims=True))
    centered = values - mean_row
    spread = lax.optimization_barrier(jnp.mean(centered * centered, axis=-1, keepdims=True))
    return centered * lax.rsqrt(spread + 1e-05) * gain + offset

def relative_index(win_t, win_hw):
    count = win_t * win_hw * win_hw
    positions = jnp.arange(count, dtype=jnp.int32)
    frame_pos = positions // (win_hw * win_hw)
    row_pos = positions // win_hw % win_hw
    col_pos = positions % win_hw
    span = 2 * win_hw - 1
    frame_off = frame_pos[:, None] - frame_pos[None, :] + win_t - 1
    row_off = row_pos[:, None] - row_pos[None, :] + win_hw - 1
    col_off = col_pos[:, None] - col_pos[None, :] + win_hw - 1
    return (frame_off * span * span + row_off * span + col_off).astype(jnp.int32)

def band_label(coord, extent, window, reach):
    return jnp.where(coord < extent - window, 0, jnp.where(coord < extent - reach, 1, 2)).astype(jnp.int32)

def windows_of(grid):
    frames, side = (grid.shape[0], grid.shape[1])
    parts = grid.reshape(frames // WIN_T, WIN_T, side // WIN_HW, WIN_HW, side // WIN_HW, WIN_HW, grid.shape[-1])
    return parts.transpose(0, 2, 4, 1, 3, 5, 6).reshape(-1, WIN_T * WIN_HW * WIN_HW, grid.shape[-1])

def grid_of(wins, frames, side):
    parts = wins.reshape(frames // WIN_T, side // WIN_HW, side // WIN_HW, WIN_T, WIN_HW, WIN_HW, wins.shape[-1])
    return parts.transpose(0, 3, 1, 4, 2, 5, 6).reshape(frames, side, side, wins.shape[-1])

def clip_layer(grid, params, table, shifted):
    gain_one, bias_one, mix_weight, mix_bias, proj_weight, proj_bias, gain_two, bias_two, wide_weight, wide_bias, narrow_weight, narrow_bias = params
    frames, side, width = (grid.shape[0], grid.shape[1], grid.shape[-1])
    head_size = width // HEADS
    window_tokens = WIN_T * WIN_HW * WIN_HW
    normed = low(norm_rows(grid, gain_one, bias_one))
    if shifted:
        normed = jnp.roll(low_back(normed), (-(WIN_T // 2), -(WIN_HW // 2), -(WIN_HW // 2)), (0, 1, 2))
    mixed = dense(normed, mix_weight)
    queries = low_back(low(mixed[..., :width] + mix_bias[:width]))
    keys = low_back(low(mixed[..., width:2 * width]))
    values = low_back(low(mixed[..., 2 * width:] + mix_bias[width:]))
    query_win = windows_of(queries).reshape(-1, window_tokens, HEADS, head_size)
    key_win = windows_of(keys).reshape(-1, window_tokens, HEADS, head_size)
    value_win = windows_of(values).reshape(-1, window_tokens, HEADS, head_size)
    rel = relative_index(WIN_T, WIN_HW)
    bias = table[rel].transpose(2, 0, 1)
    scores = jnp.einsum('wqhd,wkhd->whqk', query_win, key_win, precision=lax.Precision.HIGHEST) * head_size ** (-0.5) + bias[None]
    if shifted:
        frame_ids = jnp.arange(frames, dtype=jnp.int32)
        line_ids = jnp.arange(side, dtype=jnp.int32)
        label_t = band_label(frame_ids, frames, WIN_T, WIN_T // 2)
        label_r = band_label(line_ids, side, WIN_HW, WIN_HW // 2)
        region = label_t[:, None, None] * 9 + label_r[None, :, None] * 3 + label_r[None, None, :]
        region_win = windows_of(region[..., None])[..., 0]
        same = region_win[:, :, None] == region_win[:, None, :]
        scores = jnp.where(same[:, None], scores, -1000000000.0)
    scores = low_back(scores)
    probs = low(jax.nn.softmax(scores, axis=-1))
    attended_win = jnp.einsum('whqk,wkhd->wqhd', probs, value_win, precision=lax.Precision.HIGHEST)
    attended = low_back(low(grid_of(attended_win.reshape(-1, window_tokens, width), frames, side)))
    if shifted:
        attended = jnp.roll(attended, (WIN_T // 2, WIN_HW // 2, WIN_HW // 2), (0, 1, 2))
    middle = grid + low_back(dense(attended, proj_weight) + proj_bias)
    normed_two = low(norm_rows(middle, gain_two, bias_two))
    hidden_pre = low_back(dense(normed_two, wide_weight) + wide_bias)
    hidden = low(jax.nn.gelu(hidden_pre, approximate=False))
    return middle + low_back(dense(hidden, narrow_weight) + narrow_bias)

def clip_forward(clip_tokens, weights):
    frames, cells, width = (clip_tokens.shape[0], clip_tokens.shape[2], clip_tokens.shape[3])
    grid = clip_tokens.reshape(frames, 2, 2, WIN_HW, WIN_HW, width).transpose(0, 1, 3, 2, 4, 5).reshape(frames, 2 * WIN_HW, 2 * WIN_HW, width)
    for layer in range(LAYERS):
        params = tuple((w[layer] for w in weights[:12]))
        grid = clip_layer(grid, params, weights[12][layer], layer % 2 == 1)
    return grid.reshape(frames, 2, WIN_HW, 2, WIN_HW, width).transpose(0, 1, 3, 2, 4, 5).reshape(frames, 4, cells, width)

def reference(clips_in, ln1_gain, ln1_bias, qkv_weight, qv_bias, out_weight, out_bias, ln2_gain, ln2_bias, fc1_weight, fc1_bias, fc2_weight, fc2_bias, pos_table, out_grad):
    weights = tuple((w.astype(jnp.float32) for w in (ln1_gain, ln1_bias, qkv_weight, qv_bias, out_weight, out_bias, ln2_gain, ln2_bias, fc1_weight, fc1_bias, fc2_weight, fc2_bias, pos_table)))

    def forward(tokens, *params):

        def one_clip(clip_tokens):
            return clip_forward(clip_tokens, params)
        return lax.map(jax.checkpoint(one_clip), tokens)
    result, pull = jax.vjp(forward, clips_in.astype(jnp.float32), *weights)
    grads = pull(out_grad.astype(jnp.float32))
    return (result.astype(jnp.bfloat16), grads[0].astype(jnp.bfloat16), grads[1], grads[2], grads[3], grads[4], grads[5], grads[6], grads[7], grads[8], grads[9], grads[10], grads[11], grads[12], grads[13])
```

```python
import functools
import math

import jax
import jax.numpy as jnp
import numpy as np
from jax import lax
from jax.experimental import pallas as pl
from jax.experimental.pallas import tpu as pltpu
from jax.sharding import PartitionSpec as P

HEADS = 16
WIN_T = 8
WIN_HW = 7
LAYERS = 2


masked_score = -1000000000.0


def partner(value, axis, bit):
    mask = 2**bit
    pairs = [(source, source ^ mask) for source in range(lax.axis_size(axis))]
    return lax.ppermute(value, axis, pairs)


def norm_rows(values, gain, offset):
    mean_row = jnp.mean(values, axis=-1, keepdims=True)
    centered = values - mean_row
    spread = jnp.mean(centered * centered, axis=-1, keepdims=True)
    return centered * lax.rsqrt(spread + 1e-05) * gain + offset


def gelu_exact(values):
    return jax.nn.gelu(values, approximate=False)


def project(left, right):
    return jnp.einsum("...i,ij->...j", left, right, preferred_element_type=jnp.float32)


def project_back(left, right):
    return jnp.einsum("...j,ij->...i", left, right, preferred_element_type=jnp.float32)


def outer_sum(left, right):
    flat_left = left.reshape(-1, left.shape[-1])
    flat_right = right.reshape(-1, right.shape[-1])
    return jnp.einsum("ti,tj->ij", flat_left, flat_right, preferred_element_type=jnp.float32)


def column_sum(values):
    return jnp.sum(values.reshape(-1, values.shape[-1]).astype(jnp.float32), axis=0)


def relative_index(win_t, win_hw):
    count = win_t * win_hw * win_hw
    positions = jnp.arange(count, dtype=jnp.int32)
    frame_pos = positions // (win_hw * win_hw)
    row_pos = positions // win_hw % win_hw
    col_pos = positions % win_hw
    span = 2 * win_hw - 1
    frame_off = frame_pos[:, None] - frame_pos[None, :] + win_t - 1
    row_off = row_pos[:, None] - row_pos[None, :] + win_hw - 1
    col_off = col_pos[:, None] - col_pos[None, :] + win_hw - 1
    return frame_off * span * span + row_off * span + col_off


def band_label(coord, extent, window, reach):
    return jnp.where(coord < extent - window, 0, jnp.where(coord < extent - reach, 1, 2)).astype(
        jnp.int32
    )


def region_match(frames):
    quadrant = lax.axis_index("space")
    row_quad = quadrant // 2
    col_quad = quadrant % 2
    local = jnp.arange(WIN_HW, dtype=jnp.int32)
    label_t = band_label(jnp.arange(frames, dtype=jnp.int32), frames, WIN_T, WIN_T // 2)
    label_r = band_label(row_quad * WIN_HW + local, 2 * WIN_HW, WIN_HW, WIN_HW // 2)
    label_c = band_label(col_quad * WIN_HW + local, 2 * WIN_HW, WIN_HW, WIN_HW // 2)
    region = label_t[:, None, None] * 9 + label_r[None, :, None] * 3 + label_c[None, None, :]
    region = region.reshape(frames // WIN_T, WIN_T * WIN_HW * WIN_HW)
    return region[:, :, None] == region[:, None, :]


def space_roll(field, onward):
    side = field.shape[2]
    reach = side // 2
    sent_rows = field[:, :, :reach] if onward else field[:, :, side - reach :]
    came_rows = partner(sent_rows, "space", 1)
    if onward:
        rows_done = jnp.concatenate([field, came_rows], axis=2)[:, :, reach : reach + side]
    else:
        rows_done = jnp.concatenate([came_rows, field], axis=2)[:, :, :side]
    sent_cols = rows_done[:, :, :, :reach] if onward else rows_done[:, :, :, side - reach :]
    came_cols = partner(sent_cols, "space", 0)
    if onward:
        return jnp.concatenate([rows_done, came_cols], axis=3)[:, :, :, reach : reach + side]
    return jnp.concatenate([came_cols, rows_done], axis=3)[:, :, :, :side]


def gather_layer(shards, layer):
    parts = tuple((w[layer] for w in shards))
    return (
        lax.all_gather(parts[0], ("tm", "space", "clip"), axis=0, tiled=True),
        lax.all_gather(parts[1], ("tm", "space", "clip"), axis=0, tiled=True),
        lax.all_gather(parts[2], ("tm", "space", "clip"), axis=0, tiled=True),
        lax.all_gather(parts[3], ("tm", "space", "clip"), axis=0, tiled=True),
        lax.all_gather(parts[4], ("tm", "space", "clip"), axis=0, tiled=True),
        lax.all_gather(parts[5], ("tm", "space", "clip"), axis=0, tiled=True),
        lax.all_gather(parts[6], ("tm", "space", "clip"), axis=0, tiled=True),
        lax.all_gather(parts[7], ("tm", "space", "clip"), axis=0, tiled=True),
        lax.all_gather(parts[8], ("tm", "space", "clip"), axis=0, tiled=True),
        lax.all_gather(parts[9], ("tm", "space", "clip"), axis=0, tiled=True),
        lax.all_gather(parts[10], ("tm", "space", "clip"), axis=0, tiled=True),
        lax.all_gather(parts[11], ("tm", "space", "clip"), axis=0, tiled=True),
    )


def gather_again(shards, layer):
    parts = tuple((w[layer] for w in shards))
    return (
        lax.all_gather(parts[0], ("tm", "space", "clip"), axis=0, tiled=True),
        lax.all_gather(parts[1], ("tm", "space", "clip"), axis=0, tiled=True),
        lax.all_gather(parts[2], ("tm", "space", "clip"), axis=0, tiled=True),
        lax.all_gather(parts[3], ("tm", "space", "clip"), axis=0, tiled=True),
        lax.all_gather(parts[4], ("tm", "space", "clip"), axis=0, tiled=True),
        lax.all_gather(parts[5], ("tm", "space", "clip"), axis=0, tiled=True),
        lax.all_gather(parts[6], ("tm", "space", "clip"), axis=0, tiled=True),
        lax.all_gather(parts[7], ("tm", "space", "clip"), axis=0, tiled=True),
        lax.all_gather(parts[8], ("tm", "space", "clip"), axis=0, tiled=True),
        lax.all_gather(parts[9], ("tm", "space", "clip"), axis=0, tiled=True),
        lax.all_gather(parts[10], ("tm", "space", "clip"), axis=0, tiled=True),
        lax.all_gather(parts[11], ("tm", "space", "clip"), axis=0, tiled=True),
    )


def table_bias(table):
    rel = relative_index(WIN_T, WIN_HW)
    return table.astype(jnp.float32)[rel].transpose(2, 0, 1)


def window_scores(queries, keys, bias, same, scale):
    scores = (
        jnp.einsum("wqhd,wkhd->whqk", queries, keys, preferred_element_type=jnp.float32) * scale
        + bias[None]
    )
    if same is not None:
        scores = jnp.where(same[:, None], scores, masked_score)
    return scores


def to_windows(field):
    clips, frames, cells, heads_here, head_size = field.shape
    return field.reshape(clips, frames // WIN_T, WIN_T * cells, heads_here, head_size)


def to_frames(field, frames):
    clips = field.shape[0]
    return field.reshape(clips, frames, WIN_HW * WIN_HW, field.shape[3], field.shape[4])


def layer_forward(stream, params, table, shifted):
    (
        gain_one,
        bias_one,
        mix_weight,
        mix_bias,
        proj_weight,
        proj_bias,
        gain_two,
        bias_two,
        wide_weight,
        wide_bias,
        narrow_weight,
        narrow_bias,
    ) = params
    clips, frames_here, side = (stream.shape[0], stream.shape[1], stream.shape[2])
    width = stream.shape[-1]
    head_size = width // HEADS
    scale = head_size ** (-0.5)
    normed = norm_rows(stream, gain_one.astype(jnp.float32), bias_one.astype(jnp.float32)).astype(
        jnp.bfloat16
    )
    if shifted:
        normed = space_roll(normed, True)
    mixed = project(normed, mix_weight)
    mix_bias32 = mix_bias.astype(jnp.float32)
    head_shape = (clips, frames_here, side * side, HEADS, head_size)
    queries = (mixed[..., :width] + mix_bias32[:width]).astype(jnp.bfloat16).reshape(head_shape)
    keys = mixed[..., width : 2 * width].astype(jnp.bfloat16).reshape(head_shape)
    values = (mixed[..., 2 * width :] + mix_bias32[width:]).astype(jnp.bfloat16).reshape(head_shape)
    queries, keys, values = (
        lax.all_to_all(queries, "tm", split_axis=3, concat_axis=1, tiled=True),
        lax.all_to_all(keys, "tm", split_axis=3, concat_axis=1, tiled=True),
        lax.all_to_all(values, "tm", split_axis=3, concat_axis=1, tiled=True),
    )
    frames = queries.shape[1]
    if shifted:
        queries = jnp.roll(queries, -(WIN_T // 2), axis=1)
        keys = jnp.roll(keys, -(WIN_T // 2), axis=1)
        values = jnp.roll(values, -(WIN_T // 2), axis=1)
    queries, keys, values = (to_windows(queries), to_windows(keys), to_windows(values))
    bias = table_bias(table)
    same = region_match(frames) if shifted else None

    def attend_clip(items):
        clip_queries, clip_keys, clip_values = items
        scores = window_scores(clip_queries, clip_keys, bias, same, scale)
        peak = jnp.max(scores, axis=-1, keepdims=True)
        raised = jnp.exp(scores - peak)
        total = jnp.sum(raised, axis=-1, keepdims=True)
        probs = (raised / total).astype(jnp.bfloat16)
        out_win = jnp.einsum(
            "whqk,wkhd->wqhd", probs, clip_values, preferred_element_type=jnp.float32
        ).astype(jnp.bfloat16)
        return (out_win, peak + jnp.log(total))

    attended_heads, log_total = lax.map(attend_clip, (queries, keys, values))
    attended_heads = to_frames(attended_heads, frames)
    if shifted:
        attended_heads = jnp.roll(attended_heads, WIN_T // 2, axis=1)
    attended = lax.all_to_all(attended_heads, "tm", split_axis=1, concat_axis=3, tiled=True)
    attended = attended.reshape(clips, frames_here, side, side, width)
    if shifted:
        attended = space_roll(attended, False)
    middle = stream + project(attended, proj_weight) + proj_bias.astype(jnp.float32)
    normed_two = norm_rows(
        middle, gain_two.astype(jnp.float32), bias_two.astype(jnp.float32)
    ).astype(jnp.bfloat16)
    hidden_pre = project(normed_two, wide_weight) + wide_bias.astype(jnp.float32)
    hidden = gelu_exact(hidden_pre).astype(jnp.bfloat16)
    after = middle + project(hidden, narrow_weight) + narrow_bias.astype(jnp.float32)
    stash = (
        stream,
        normed,
        queries,
        keys,
        values,
        log_total,
        attended,
        middle,
        normed_two,
        hidden_pre,
        hidden,
    )
    return (stash, after)


def layer_backward(grad_after, params, table, stash, shifted):
    (
        gain_one,
        bias_one,
        mix_weight,
        mix_bias,
        proj_weight,
        proj_bias,
        gain_two,
        bias_two,
        wide_weight,
        wide_bias,
        narrow_weight,
        narrow_bias,
    ) = params
    (
        stream,
        normed,
        queries,
        keys,
        values,
        log_total,
        attended,
        middle,
        normed_two,
        hidden_pre,
        hidden,
    ) = stash
    clips, frames_here, side = (stream.shape[0], stream.shape[1], stream.shape[2])
    width = stream.shape[-1]
    head_size = width // HEADS
    scale = head_size ** (-0.5)
    frames = queries.shape[1] * WIN_T
    grad_branch_two = grad_after.astype(jnp.bfloat16)
    narrow_grad = outer_sum(hidden, grad_branch_two)
    narrow_bias_grad = column_sum(grad_branch_two)
    grad_hidden = project_back(grad_branch_two, narrow_weight)
    gelu_pull = jax.vjp(gelu_exact, hidden_pre)[1]
    grad_pre = gelu_pull(grad_hidden)[0].astype(jnp.bfloat16)
    wide_grad = outer_sum(normed_two, grad_pre)
    wide_bias_grad = column_sum(grad_pre)
    grad_normed_two = project_back(grad_pre, wide_weight)
    norm_pull_two = jax.vjp(
        norm_rows, middle, gain_two.astype(jnp.float32), bias_two.astype(jnp.float32)
    )[1]
    grad_mid_part, gain_two_grad, bias_two_grad = norm_pull_two(grad_normed_two)
    grad_middle = grad_after + grad_mid_part
    grad_branch_one = grad_middle.astype(jnp.bfloat16)
    proj_grad = outer_sum(attended, grad_branch_one)
    proj_bias_grad = column_sum(grad_branch_one)
    grad_attended = project_back(grad_branch_one, proj_weight).astype(jnp.bfloat16)
    if shifted:
        grad_attended = space_roll(grad_attended, True)
    grad_attended = grad_attended.reshape(clips, frames_here, side * side, HEADS, head_size)
    grad_attended = lax.all_to_all(grad_attended, "tm", split_axis=3, concat_axis=1, tiled=True)
    if shifted:
        grad_attended = jnp.roll(grad_attended, -(WIN_T // 2), axis=1)
    grad_attended = to_windows(grad_attended)
    bias = table_bias(table)
    same = region_match(frames) if shifted else None

    def attend_back(carry, items):
        clip_queries, clip_keys, clip_values, clip_grad, clip_log = items
        scores = window_scores(clip_queries, clip_keys, bias, same, scale)
        probs = jnp.exp(scores - clip_log)
        grad_probs = jnp.einsum(
            "wqhd,wkhd->whqk", clip_grad, clip_values, preferred_element_type=jnp.float32
        )
        inner = jnp.sum(probs * grad_probs, axis=-1, keepdims=True)
        grad_scores = (probs * (grad_probs - inner)).astype(jnp.bfloat16)
        grad_q = (
            jnp.einsum(
                "whqk,wkhd->wqhd", grad_scores, clip_keys, preferred_element_type=jnp.float32
            )
            * scale
        ).astype(jnp.bfloat16)
        grad_k = (
            jnp.einsum(
                "whqk,wqhd->wkhd", grad_scores, clip_queries, preferred_element_type=jnp.float32
            )
            * scale
        ).astype(jnp.bfloat16)
        grad_v = jnp.einsum(
            "whqk,wqhd->wkhd",
            probs.astype(jnp.bfloat16),
            clip_grad,
            preferred_element_type=jnp.float32,
        ).astype(jnp.bfloat16)
        carry = carry + jnp.sum(grad_scores.astype(jnp.float32), axis=0)
        return (carry, (grad_q, grad_k, grad_v))

    window_tokens = queries.shape[2]
    start_bias = jnp.zeros((queries.shape[3], window_tokens, window_tokens), jnp.float32)
    bias_grad, grads_win = lax.scan(
        attend_back, start_bias, (queries, keys, values, grad_attended, log_total)
    )
    grad_q, grad_k, grad_v = (to_frames(g, frames) for g in grads_win)
    if shifted:
        grad_q = jnp.roll(grad_q, WIN_T // 2, axis=1)
        grad_k = jnp.roll(grad_k, WIN_T // 2, axis=1)
        grad_v = jnp.roll(grad_v, WIN_T // 2, axis=1)
    grad_q, grad_k, grad_v = (
        lax.all_to_all(grad_q, "tm", split_axis=1, concat_axis=3, tiled=True),
        lax.all_to_all(grad_k, "tm", split_axis=1, concat_axis=3, tiled=True),
        lax.all_to_all(grad_v, "tm", split_axis=1, concat_axis=3, tiled=True),
    )
    token_shape = (clips, frames_here, side, side, width)
    grad_q, grad_k, grad_v = (
        grad_q.reshape(token_shape),
        grad_k.reshape(token_shape),
        grad_v.reshape(token_shape),
    )
    grad_mix = jnp.concatenate([grad_q, grad_k, grad_v], axis=-1)
    mix_grad = outer_sum(normed, grad_mix)
    mix_bias_grad = jnp.concatenate([column_sum(grad_q), column_sum(grad_v)])
    grad_normed = project_back(grad_mix, mix_weight)
    if shifted:
        grad_normed = space_roll(grad_normed.astype(jnp.bfloat16), False).astype(jnp.float32)
    norm_pull_one = jax.vjp(
        norm_rows, stream, gain_one.astype(jnp.float32), bias_one.astype(jnp.float32)
    )[1]
    grad_stream_part, gain_one_grad, bias_one_grad = norm_pull_one(grad_normed)
    grad_stream = grad_middle + grad_stream_part
    rel = relative_index(WIN_T, WIN_HW).reshape(-1)
    table_grad = (
        jnp.zeros(table.shape, jnp.float32).at[rel].add(bias_grad.reshape(bias_grad.shape[0], -1).T)
    )
    weight_grads = (
        gain_one_grad,
        bias_one_grad,
        mix_grad,
        mix_bias_grad,
        proj_grad,
        proj_bias_grad,
        gain_two_grad,
        bias_two_grad,
        wide_grad,
        wide_bias_grad,
        narrow_grad,
        narrow_bias_grad,
    )
    return (grad_stream, weight_grads, table_grad)


def per_device(
    clips_in,
    ln1_gain,
    ln1_bias,
    qkv_weight,
    qv_bias,
    out_weight,
    out_bias,
    ln2_gain,
    ln2_bias,
    fc1_weight,
    fc1_bias,
    fc2_weight,
    fc2_bias,
    pos_table,
    out_grad,
):
    clips, frames_here, quads, cells, width = clips_in.shape
    grid_shape = (clips, frames_here, WIN_HW, WIN_HW, width)
    shards = (
        ln1_gain,
        ln1_bias,
        qkv_weight,
        qv_bias,
        out_weight,
        out_bias,
        ln2_gain,
        ln2_bias,
        fc1_weight,
        fc1_bias,
        fc2_weight,
        fc2_bias,
    )
    stream = clips_in.astype(jnp.float32).reshape(grid_shape)
    kept_params = []
    kept_stash = []
    for layer in range(LAYERS):
        params = gather_layer(shards, layer)
        stash, stream = layer_forward(stream, params, pos_table[layer], layer % 2 == 1)
        kept_params.append(params)
        kept_stash.append(stash)
    clips_out = stream.astype(jnp.bfloat16).reshape(clips_in.shape)
    grad_stream = out_grad.astype(jnp.float32).reshape(grid_shape)
    layer_shares = [None] * LAYERS
    table_parts = [None] * LAYERS
    for layer in reversed(range(LAYERS)):
        params = gather_again(shards, layer)
        grad_stream, weight_grads, table_grad = layer_backward(
            grad_stream, params, pos_table[layer], kept_stash[layer], layer % 2 == 1
        )
        layer_shares[layer] = (
            lax.psum_scatter(
                weight_grads[0], ("tm", "space", "clip"), scatter_dimension=0, tiled=True
            ),
            lax.psum_scatter(
                weight_grads[1], ("tm", "space", "clip"), scatter_dimension=0, tiled=True
            ),
            lax.psum_scatter(
                weight_grads[2], ("tm", "space", "clip"), scatter_dimension=0, tiled=True
            ),
            lax.psum_scatter(
                weight_grads[3], ("tm", "space", "clip"), scatter_dimension=0, tiled=True
            ),
            lax.psum_scatter(
                weight_grads[4], ("tm", "space", "clip"), scatter_dimension=0, tiled=True
            ),
            lax.psum_scatter(
                weight_grads[5], ("tm", "space", "clip"), scatter_dimension=0, tiled=True
            ),
            lax.psum_scatter(
                weight_grads[6], ("tm", "space", "clip"), scatter_dimension=0, tiled=True
            ),
            lax.psum_scatter(
                weight_grads[7], ("tm", "space", "clip"), scatter_dimension=0, tiled=True
            ),
            lax.psum_scatter(
                weight_grads[8], ("tm", "space", "clip"), scatter_dimension=0, tiled=True
            ),
            lax.psum_scatter(
                weight_grads[9], ("tm", "space", "clip"), scatter_dimension=0, tiled=True
            ),
            lax.psum_scatter(
                weight_grads[10], ("tm", "space", "clip"), scatter_dimension=0, tiled=True
            ),
            lax.psum_scatter(
                weight_grads[11], ("tm", "space", "clip"), scatter_dimension=0, tiled=True
            ),
        )
        table_parts[layer] = table_grad
    in_grad = grad_stream.astype(jnp.bfloat16).reshape(clips_in.shape)
    table_total = lax.psum(jnp.stack(table_parts), ("space", "clip"))
    stacked = tuple(
        (jnp.stack([layer_shares[n][slot] for n in range(LAYERS)]) for slot in range(12))
    )
    return (
        clips_out,
        in_grad,
        stacked[0],
        stacked[1],
        stacked[2],
        stacked[3],
        stacked[4],
        stacked[5],
        stacked[6],
        stacked[7],
        stacked[8],
        stacked[9],
        stacked[10],
        stacked[11],
        table_total,
    )


F32 = jnp.float32
BF16 = jnp.bfloat16
TOKENS = WIN_T * WIN_HW * WIN_HW
CELLS = WIN_HW * WIN_HW
SPAN = 2 * WIN_HW - 1
STEPS = 2 * WIN_T - 1
LOG2E = math.log2(math.e)
VMEM_BYTES = 56 * 1024 * 1024


def mm(left, right, left_dim=1, right_dim=0):
    dims = (((left_dim,), (right_dim,)), ((), ()))
    return lax.dot_general(left, right, dims, preferred_element_type=F32)


def call(kernel, grid, in_specs, out_specs, out_shape, flops, scratch=()):
    return pl.pallas_call(
        kernel,
        grid=grid,
        in_specs=in_specs,
        out_specs=out_specs,
        out_shape=out_shape,
        scratch_shapes=scratch,
        cost_estimate=pl.CostEstimate(
            flops=int(flops), transcendentals=0, bytes_accessed=8 * 1024 * 1024
        ),
        compiler_params=pltpu.CompilerParams(vmem_limit_bytes=VMEM_BYTES),
    )


def whole_block(shape):
    return pl.BlockSpec(shape, lambda *ids: (0,) * len(shape))


def win_block(width, column=0):
    return pl.BlockSpec((1, TOKENS, width), lambda w: (w, 0, column))


def halo_plan(frames_here):
    half_t, reach = WIN_T // 2, WIN_HW // 2
    frame, row, col = np.meshgrid(
        np.arange(frames_here), np.arange(WIN_HW), np.arange(WIN_HW), indexing="ij"
    )
    frame, row, col = frame.reshape(-1), row.reshape(-1), col.reshape(-1)
    new_t = (frame - half_t) % frames_here
    new_r = (row - reach) % WIN_HW
    new_c = (col - reach) % WIN_HW
    target = new_t * CELLS + new_r * WIN_HW + new_c
    leaves = (frame < half_t) * 4 + (row < reach) * 2 + (col < reach) * 1
    parts = []
    for kind in range(1, 8):
        source = np.nonzero(leaves == kind)[0]
        parts.append((kind, source, target[source]))
    stay = np.nonzero(leaves == 0)[0]
    return parts, (stay, target[stay])


def halo_matrices(frames_here):
    parts, (stay, stay_to) = halo_plan(frames_here)
    count = frames_here * CELLS
    rows = [-(-len(source) // 16) * 16 for _, source, _ in parts]
    starts = np.concatenate([[0], np.cumsum(rows)])
    send = np.zeros((starts[-1], count), np.float32)
    place = np.zeros((count, starts[-1]), np.float32)
    own = np.zeros((count, count), np.float32)
    for (_, source, to), start in zip(parts, starts[:-1]):
        slots = start + np.arange(len(source))
        send[slots, source] = 1
        place[to, slots] = 1
    own[stay_to, stay] = 1
    return send, place, own, rows, starts, [kind for kind, _, _ in parts]


def halo_permute(packed, rows, starts, kinds, onward):
    ring, quads = lax.axis_size("tm"), lax.axis_size("space")
    came = []
    for kind, start, count in zip(kinds, starts, rows):
        piece = packed[start : start + count]
        step = 0 if not kind & 4 else (-1 if onward else 1)
        pairs = []
        for frame_at in range(ring):
            for quad in range(quads):
                to = (frame_at + step) % ring * quads + (quad ^ (kind & 3))
                pairs.append((frame_at * quads + quad, to))
        came.append(lax.ppermute(piece, ("tm", "space"), pairs))
    return came


def pack_kernel(center, send_ref, x_ref, out_ref):
    windows = x_ref.shape[0]
    total = None
    for w in range(windows):
        x = x_ref[w]
        if center:
            x = x - jnp.mean(x, axis=-1, keepdims=True)
        part = mm(send_ref[:, w * TOKENS : (w + 1) * TOKENS], x.astype(BF16))
        total = part if total is None else total + part
    out_ref[...] = total.astype(BF16)


def halo_pack(x, send, center):
    windows, _, width = x.shape
    rows = send.shape[0]
    return call(
        functools.partial(pack_kernel, center),
        (),
        [pl.BlockSpec(memory_space=pltpu.VMEM)] * 2,
        pl.BlockSpec(memory_space=pltpu.VMEM),
        jax.ShapeDtypeStruct((rows, width), BF16),
        2 * rows * windows * TOKENS * width,
    )(jnp.asarray(send, BF16), x)


def unpack_kernel(center, add_mean, starts, own_ref, place_ref, x_ref, base_ref, *refs):
    came_refs, out_ref = refs[:-1], refs[-1]
    windows = x_ref.shape[0]
    total = jnp.zeros((windows * TOKENS, x_ref.shape[-1]), F32)
    for w in range(windows):
        x = x_ref[w].astype(F32)
        if center:
            x = x - jnp.mean(x, axis=-1, keepdims=True)
        high = x.astype(BF16)
        cols = own_ref[:, w * TOKENS : (w + 1) * TOKENS]
        total = total + mm(cols, high)
        if x_ref.dtype == F32:
            total = total + mm(cols, (x - high.astype(F32)).astype(BF16))
    came = jnp.concatenate([r[...] for r in came_refs], axis=0)
    total = total + mm(place_ref[...], came)
    for w in range(windows):
        piece = total[w * TOKENS : (w + 1) * TOKENS]
        if add_mean:
            piece = piece + jnp.mean(base_ref[w], axis=-1, keepdims=True)
        out_ref[w] = piece.astype(out_ref.dtype)


def halo_unpack(x, came, own, place, starts, dtype, center=False, mean_of=None):
    windows, _, width = x.shape
    base = jnp.zeros((windows, 8, 128), F32) if mean_of is None else mean_of
    return call(
        functools.partial(unpack_kernel, center, mean_of is not None, starts),
        (),
        [pl.BlockSpec(memory_space=pltpu.VMEM)] * (4 + len(came)),
        pl.BlockSpec(memory_space=pltpu.VMEM),
        jax.ShapeDtypeStruct((windows, TOKENS, width), dtype),
        4 * (windows * TOKENS) ** 2 * width,
    )(jnp.asarray(own, BF16), jnp.asarray(place, BF16), x, base, *came)


def index_bits():
    bits = []
    for axis in ("tm", "space", "clip"):
        count = lax.axis_size(axis).bit_length() - 1
        bits += [(axis, b) for b in reversed(range(count))]
    return bits


def bit_of(axis, bit):
    return (lax.axis_index(axis) // 2**bit) % 2


def stage_orders():
    bits = index_bits()
    inner = [("clip", 0)] if lax.axis_size("clip") > 1 else []
    tm = [b for b in bits if b[0] == "tm"]
    clip = [b for b in bits if b[0] == "clip" and b not in inner]
    space = [b for b in bits if b[0] == "space"]
    return inner + tm + clip + space, inner + clip + tm + space


def gather_all(shard, order):
    bits = index_bits()
    out = shard.reshape((1,) * len(bits) + shard.shape)
    for axis, bit in reversed(order):
        dim = bits.index((axis, bit))
        other = partner(out, axis, bit)
        out = jnp.where(
            bit_of(axis, bit) == 1,
            jnp.concatenate([other, out], dim),
            jnp.concatenate([out, other], dim),
        )
    return out.reshape((-1,) + shard.shape[1:])


def scatter_all(grad, order):
    bits = index_bits()
    width = grad.shape[-1]
    out = grad.reshape((2,) * len(bits) + (-1, width))
    for axis, bit in order:
        dim = bits.index((axis, bit))
        here = bit_of(axis, bit)
        mine = lax.dynamic_slice_in_dim(out, here, 1, dim)
        sent = lax.dynamic_slice_in_dim(out, 1 - here, 1, dim).astype(BF16)
        out = mine + partner(sent, axis, bit).astype(F32)
    return out.reshape(-1, width)


def table_shift_matrix():
    shift = np.zeros((CELLS, 256, 128), np.float32)
    for row in range(WIN_HW):
        for col in range(WIN_HW):
            offset = (WIN_HW - 1 - row) * SPAN + WIN_HW - 1 - col
            for m in range((WIN_HW - 1) * SPAN + WIN_HW):
                shift[row * WIN_HW + col, m + offset, m] = 1
    return shift


def cell_spread():
    spread = np.zeros((WIN_T * 128, TOKENS), np.float32)
    for frame in range(WIN_T):
        for row in range(WIN_HW):
            for col in range(WIN_HW):
                spread[frame * 128 + row * SPAN + col, frame * CELLS + row * WIN_HW + col] = 1
    return spread


def bias_kernel(slab_ref, spread_ref, out_ref):
    spread = spread_ref[...]
    for key_frame in range(WIN_T):
        first = WIN_T - 1 - key_frame
        slabs = jnp.concatenate([slab_ref[0, first + n] for n in range(WIN_T)], axis=1)
        out_ref[0, key_frame * CELLS : (key_frame + 1) * CELLS, :] = mm(slabs, spread) * LOG2E


def table_to_bias(tables):
    layers, heads, _ = tables.shape
    slabs = tables.reshape(layers * heads, STEPS, SPAN * SPAN)
    slabs = jnp.pad(slabs, ((0, 0), (0, 0), (0, 256 - SPAN * SPAN)))
    shift = jnp.asarray(table_shift_matrix(), BF16)
    shifted = jnp.einsum("hje,kem->hjkm", slabs, shift, preferred_element_type=F32).astype(BF16)
    return call(
        bias_kernel,
        (layers * heads,),
        [
            pl.BlockSpec((1, STEPS, CELLS, 128), lambda h: (h, 0, 0, 0)),
            whole_block((WIN_T * 128, TOKENS)),
        ],
        pl.BlockSpec((1, TOKENS, TOKENS), lambda h: (h, 0, 0)),
        jax.ShapeDtypeStruct((layers * heads, TOKENS, TOKENS), F32),
        2 * layers * heads * TOKENS * WIN_T * 128 * TOKENS,
    )(shifted, jnp.asarray(cell_spread(), BF16))


def bias_grad_to_table(parts):
    shift = jnp.asarray(table_shift_matrix(), F32)
    table = jnp.einsum(
        "hjkm,kem->hje", parts, shift, precision=lax.Precision.HIGH, preferred_element_type=F32
    )
    return table[:, :, : SPAN * SPAN].reshape(parts.shape[0], -1)


def unit_rows(x):
    centered = x - jnp.mean(x, axis=-1, keepdims=True)
    inverse = lax.rsqrt(jnp.mean(centered * centered, axis=-1, keepdims=True) + 1e-05)
    return centered * inverse, inverse


def norm_back(grad, unit, inverse, gain):
    scaled = grad * gain
    return inverse * (
        scaled
        - jnp.mean(scaled, axis=-1, keepdims=True)
        - unit * jnp.mean(scaled * unit, axis=-1, keepdims=True)
    )


def qkv_kernel(x_ref, vec_ref, w_ref, out_ref):
    width = x_ref.shape[-1]
    unit, _ = unit_rows(x_ref[0].astype(F32))
    normed = (unit * vec_ref[0:1] + vec_ref[1:2]).astype(BF16)
    for part in range(3):
        cols = slice(part * width, (part + 1) * width)
        out = mm(normed, w_ref[:, cols])
        if part == 0:
            out = out + vec_ref[2:3]
        if part == 2:
            out = out + vec_ref[3:4]
        out_ref[0, :, cols] = out.astype(BF16)


def run_qkv(x, vec, w_qkv):
    windows, _, width = x.shape
    return call(
        qkv_kernel,
        (windows,),
        [win_block(width), whole_block(vec.shape), whole_block(w_qkv.shape)],
        win_block(3 * width),
        jax.ShapeDtypeStruct((windows, TOKENS, 3 * width), BF16),
        2 * windows * TOKENS * width * 3 * width,
    )(x, vec, w_qkv)


GROUP = 4


def head_masks(head_size):
    lane = lax.broadcasted_iota(jnp.int32, (1, GROUP * head_size), 1)
    return [
        jnp.where((lane >= h * head_size) & (lane < (h + 1) * head_size), 1.0, 0.0).astype(BF16)
        for h in range(GROUP)
    ]


def attend_kernel(shifted, head_size, q_ref, k_ref, v_ref, bias_ref, col_ref, row_ref, out_ref, log_ref):
    q, k = q_ref[0], k_ref[0]
    turned = v_ref[0].astype(F32).T.astype(BF16)
    factor = head_size**-0.5 * LOG2E
    masks = head_masks(head_size)
    outs, logs = [], []
    for h in range(GROUP):
        scores = mm(k * masks[h], q, 1, 1) * factor + bias_ref[h]
        if shifted:
            scores = jnp.where(col_ref[0] == row_ref[0], scores, masked_score)
        peak = jnp.max(scores, axis=0, keepdims=True)
        raised = jnp.exp2(scores - peak)
        total = jnp.sum(raised, axis=0, keepdims=True)
        mixed = mm(turned[h * head_size : (h + 1) * head_size], raised.astype(BF16))
        outs.append(mixed / total)
        logs.append(peak + jnp.log2(total))
    out_ref[0] = jnp.concatenate(outs, axis=0).T.astype(BF16)
    log_ref[0, 0] = jnp.concatenate(logs + logs, axis=0)


def attend_specs(width):
    wide = GROUP * (width // HEADS)
    groups = HEADS // GROUP
    qkv = [
        pl.BlockSpec((1, TOKENS, wide), lambda g, w, p=part: (w, 0, p * groups + g))
        for part in range(3)
    ]
    bias = pl.BlockSpec((GROUP, TOKENS, TOKENS), lambda g, w: (g, 0, 0))
    col = pl.BlockSpec((1, TOKENS, 1), lambda g, w: (w, 0, 0))
    row = pl.BlockSpec((1, 1, TOKENS), lambda g, w: (w, 0, 0))
    flat = pl.BlockSpec((1, TOKENS, wide), lambda g, w: (w, 0, g))
    log = pl.BlockSpec((1, 1, 2 * GROUP, TOKENS), lambda g, w: (w, g, 0, 0))
    return qkv, bias, col, row, flat, log


def run_attend(qkv, bias, labels, shifted):
    windows, _, width3 = qkv.shape
    width = width3 // 3
    groups = HEADS // GROUP
    qkv_specs, bias_spec, col, row, flat, log = attend_specs(width)
    return call(
        functools.partial(attend_kernel, shifted, width // HEADS),
        (groups, windows),
        qkv_specs + [bias_spec, col, row],
        [flat, log],
        [
            jax.ShapeDtypeStruct((windows, TOKENS, width), BF16),
            jax.ShapeDtypeStruct((windows, groups, 2 * GROUP, TOKENS), F32),
        ],
        32 * windows * TOKENS * TOKENS * width,
    )(qkv, qkv, qkv, bias, labels[0], labels[1])


def attend_back_kernel(
    shifted, head_size, q_ref, k_ref, v_ref, g_ref, bias_ref, col_ref, row_ref, log_ref, spread_ref,
    dq_ref, dk_ref, dv_ref, table_ref, sum_ref, slab_ref,
):
    w = pl.program_id(1)
    q, k, v, g = q_ref[0], k_ref[0], v_ref[0], g_ref[0]
    turned = k.astype(F32).T.astype(BF16)
    scale = head_size**-0.5
    factor = scale * LOG2E
    masks = head_masks(head_size)
    grad_q, grad_k, grad_v = [], None, None
    for h in range(GROUP):
        scores = mm(k * masks[h], q, 1, 1) * factor + bias_ref[h]
        if shifted:
            scores = jnp.where(col_ref[0] == row_ref[0], scores, masked_score)
        probs = jnp.exp2(scores - log_ref[0, 0, h : h + 1])
        grad_probs = mm(v * masks[h], g, 1, 1)
        inner = jnp.sum(probs * grad_probs, axis=0, keepdims=True)
        grad_scores = (probs * (grad_probs - inner)).astype(BF16)
        part_v = mm(probs.astype(BF16), g * masks[h])
        part_k = mm(grad_scores, q * masks[h])
        grad_v = part_v if grad_v is None else grad_v + part_v
        grad_k = part_k if grad_k is None else grad_k + part_k
        grad_q.append(mm(turned[h * head_size : (h + 1) * head_size], grad_scores))

        @pl.when(w == 0)
        def _():
            sum_ref[h] = grad_scores.astype(F32)

        @pl.when(w != 0)
        def _():
            sum_ref[h] += grad_scores.astype(F32)

    dq_ref[0] = (jnp.concatenate(grad_q, axis=0) * scale).T.astype(BF16)
    dk_ref[0] = (grad_k * scale).astype(BF16)
    dv_ref[0] = grad_v.astype(BF16)

    @pl.when(w == pl.num_programs(1) - 1)
    def _():
        spread = spread_ref[...]
        for h in range(GROUP):
            slab_ref[...] = jnp.zeros_like(slab_ref)
            for key_frame in range(WIN_T):
                rows = sum_ref[h, key_frame * CELLS : (key_frame + 1) * CELLS, :]
                first = (WIN_T - 1 - key_frame) * 128
                slab_ref[:, first : first + WIN_T * 128] += mm(rows.astype(BF16), spread, 1, 1)
            for step in range(STEPS):
                table_ref[h, step] = slab_ref[:, step * 128 : (step + 1) * 128]


def run_attend_back(qkv, grad, bias, labels, log, shifted):
    windows, _, width3 = qkv.shape
    width = width3 // 3
    groups = HEADS // GROUP
    qkv_specs, bias_spec, col, row, flat, log_spec = attend_specs(width)
    flat_shape = jax.ShapeDtypeStruct((windows, TOKENS, width), BF16)
    return call(
        functools.partial(attend_back_kernel, shifted, width // HEADS),
        (groups, windows),
        qkv_specs + [flat, bias_spec, col, row, log_spec]
        + [pl.BlockSpec((WIN_T * 128, TOKENS), lambda g, w: (0, 0))],
        [flat, flat, flat, pl.BlockSpec((GROUP, STEPS, CELLS, 128), lambda g, w: (g, 0, 0, 0))],
        [flat_shape] * 3 + [jax.ShapeDtypeStruct((HEADS, STEPS, CELLS, 128), F32)],
        80 * windows * TOKENS * TOKENS * width,
        [pltpu.VMEM((GROUP, TOKENS, TOKENS), F32), pltpu.VMEM((CELLS, STEPS * 128), F32)],
    )(qkv, qkv, qkv, grad, bias, labels[0], labels[1], log, jnp.asarray(cell_spread(), BF16))


def branch_kernel(x_ref, att_ref, vec_ref, wo_ref, w1_ref, w2_ref, mid_ref, hid_ref, slope_ref, out_ref):
    chunk = 512
    middle = x_ref[0].astype(F32) + mm(att_ref[0], wo_ref[...]) + vec_ref[4:5]
    mid_ref[0] = middle
    unit, _ = unit_rows(middle)
    normed = (unit * vec_ref[5:6] + vec_ref[6:7]).astype(BF16)
    after = middle + vec_ref[7:8]
    for n in range(w1_ref.shape[1] // chunk):
        cols = slice(n * chunk, (n + 1) * chunk)
        pre = mm(normed, w1_ref[:, cols]) + vec_ref[8 + n : 9 + n]
        below = 0.5 * (1.0 + lax.erf(pre * math.sqrt(0.5)))
        bell = jnp.exp(-0.5 * pre * pre) * (1.0 / math.sqrt(2 * math.pi))
        hidden = (pre * below).astype(BF16)
        hid_ref[0, :, cols] = hidden
        slope_ref[0, :, cols] = (below + pre * bell).astype(BF16)
        after = after + mm(hidden, w2_ref[cols, :])
    out_ref[0] = after.astype(out_ref.dtype)


def run_branch(x, attended, vec, w_mid, w2, out_dtype):
    windows, _, width = x.shape
    wide = w2.shape[0]
    return call(
        branch_kernel,
        (windows,),
        [
            win_block(width),
            win_block(width),
            whole_block(vec.shape),
            pl.BlockSpec((width, width), lambda w: (0, wide // width)),
            pl.BlockSpec((width, wide), lambda w: (0, 0)),
            whole_block(w2.shape),
        ],
        [win_block(width), win_block(wide), win_block(wide), win_block(width)],
        [
            jax.ShapeDtypeStruct((windows, TOKENS, width), F32),
            jax.ShapeDtypeStruct((windows, TOKENS, wide), BF16),
            jax.ShapeDtypeStruct((windows, TOKENS, wide), BF16),
            jax.ShapeDtypeStruct((windows, TOKENS, width), out_dtype),
        ],
        2 * windows * TOKENS * width * (width + 2 * wide),
    )(x, attended, vec, w_mid, w_mid, w2)


def add_rows(ref, rows, value):
    ref[rows, :] += jnp.sum(value.astype(F32), axis=0, keepdims=True)


def branch_back_kernel(
    grad_ref, mid_ref, att_ref, hid_ref, slope_ref, vec_ref, wo_ref, w1_ref, w2_ref,
    gm_ref, ga_ref, d1_ref, d2_ref, vecs_ref,
):
    chunk = 512
    wide = w2_ref.shape[0]

    @pl.when(pl.program_id(0) == 0)
    def _():
        d1_ref[...] = jnp.zeros_like(d1_ref)
        d2_ref[...] = jnp.zeros_like(d2_ref)
        vecs_ref[...] = jnp.zeros_like(vecs_ref)

    grad = grad_ref[0].astype(F32)
    branch = grad.astype(BF16)
    unit, inverse = unit_rows(mid_ref[0])
    normed = (unit * vec_ref[5:6] + vec_ref[6:7]).astype(BF16)
    add_rows(vecs_ref, slice(7, 8), branch)
    back = None
    for n in range(wide // chunk):
        cols = slice(n * chunk, (n + 1) * chunk)
        d2_ref[cols, :] += mm(hid_ref[0, :, cols], branch, 0, 0)
        grad_pre = mm(branch, w2_ref[cols, :], 1, 1) * slope_ref[0, :, cols].astype(F32)
        add_rows(vecs_ref, slice(8 + n, 9 + n), grad_pre.astype(BF16))
        grad_pre = grad_pre.astype(BF16)
        d1_ref[:, cols] += mm(normed, grad_pre, 0, 0)
        part = mm(grad_pre, w1_ref[:, cols], 1, 1)
        back = part if back is None else back + part
    add_rows(vecs_ref, slice(5, 6), back * unit)
    add_rows(vecs_ref, slice(6, 7), back)
    middle_grad = grad + norm_back(back, unit, inverse, vec_ref[5:6])
    gm_ref[0] = middle_grad
    branch = middle_grad.astype(BF16)
    add_rows(vecs_ref, slice(4, 5), branch)
    d1_ref[:, wide:] += mm(att_ref[0], branch, 0, 0)
    ga_ref[0] = mm(branch, wo_ref[...], 1, 1).astype(BF16)


def run_branch_back(grad, middle, attended, hidden, slope, vec, w_mid, w2):
    windows, _, width = middle.shape
    wide = w2.shape[0]
    flat = win_block(width)
    return call(
        branch_back_kernel,
        (windows,),
        [
            flat,
            flat,
            flat,
            win_block(wide),
            win_block(wide),
            whole_block(vec.shape),
            pl.BlockSpec((width, width), lambda w: (0, wide // width)),
            pl.BlockSpec((width, wide), lambda w: (0, 0)),
            whole_block(w2.shape),
        ],
        [flat, flat, whole_block(w_mid.shape), whole_block(w2.shape), whole_block(vec.shape)],
        [
            jax.ShapeDtypeStruct((windows, TOKENS, width), F32),
            jax.ShapeDtypeStruct((windows, TOKENS, width), BF16),
            jax.ShapeDtypeStruct(w_mid.shape, F32),
            jax.ShapeDtypeStruct(w2.shape, F32),
            jax.ShapeDtypeStruct(vec.shape, F32),
        ],
        4 * windows * TOKENS * width * (width + 2 * wide),
    )(grad, middle, attended, hidden, slope, vec, w_mid, w_mid, w2)


def qkv_back_kernel(dq_ref, dk_ref, dv_ref, x_ref, gm_ref, vec_ref, w_ref, out_ref, dw_ref, vecs_ref):
    width = x_ref.shape[-1]

    @pl.when(pl.program_id(0) == 0)
    def _():
        dw_ref[...] = jnp.zeros_like(dw_ref)
        vecs_ref[...] = jnp.zeros_like(vecs_ref)

    unit, inverse = unit_rows(x_ref[0].astype(F32))
    normed = (unit * vec_ref[0:1] + vec_ref[1:2]).astype(BF16)
    back = None
    for part, ref in enumerate((dq_ref, dk_ref, dv_ref)):
        cols = slice(part * width, (part + 1) * width)
        grad = ref[0]
        dw_ref[:, cols] += mm(normed, grad, 0, 0)
        here = mm(grad, w_ref[:, cols], 1, 1)
        back = here if back is None else back + here
        if part == 0:
            add_rows(vecs_ref, slice(2, 3), grad)
        if part == 2:
            add_rows(vecs_ref, slice(3, 4), grad)
    add_rows(vecs_ref, slice(0, 1), back * unit)
    add_rows(vecs_ref, slice(1, 2), back)
    out_ref[0] = (gm_ref[0] + norm_back(back, unit, inverse, vec_ref[0:1])).astype(out_ref.dtype)


def run_qkv_back(grads, x, grad_middle, vec, w_qkv, out_dtype):
    windows, _, width = x.shape
    flat = win_block(width)
    return call(
        qkv_back_kernel,
        (windows,),
        [flat] * 5 + [whole_block(vec.shape), whole_block(w_qkv.shape)],
        [flat, whole_block(w_qkv.shape), whole_block((8, width))],
        [
            jax.ShapeDtypeStruct((windows, TOKENS, width), out_dtype),
            jax.ShapeDtypeStruct(w_qkv.shape, F32),
            jax.ShapeDtypeStruct((8, width), F32),
        ],
        4 * windows * TOKENS * width * 3 * width,
    )(*grads, x, grad_middle, vec, w_qkv)


def vectors_in(shards):
    gain_one, bias_one, mix_bias, proj_bias, gain_two, bias_two, wide_bias, narrow_bias = shards
    own = gain_one.shape[1]
    rows = []
    for v in (gain_one, bias_one, mix_bias, proj_bias, gain_two, bias_two, narrow_bias, wide_bias):
        rows.append(v.reshape(LAYERS, -1, own))
    block = jnp.concatenate(rows, axis=1)
    block = block.transpose(1, 0, 2).reshape(block.shape[1], LAYERS * own)
    return jnp.pad(block, ((0, 16 - block.shape[0]), (0, 128 - block.shape[1])))


def vectors_whole(blocks, own):
    devices = blocks.shape[0] // 16
    parts = blocks.reshape(devices, 16, 128)[:, :, : LAYERS * own]
    parts = parts.reshape(devices, 16, LAYERS, own).transpose(2, 0, 1, 3).astype(F32)

    def joined(first, count):
        return parts[:, :, first : first + count].reshape(LAYERS, -1, devices * own)

    singles = parts.transpose(0, 2, 1, 3).reshape(LAYERS, 16, devices * own)
    return jnp.concatenate(
        [singles[:, 0:2], joined(2, 2), singles[:, 4:8], joined(8, 4), singles[:, 12:16]], axis=1
    )


def vectors_split(rows, devices):
    own = rows.shape[1] // devices

    def shared(first, count):
        return rows[first : first + count].reshape(devices, count, own)

    singles = rows.reshape(16, devices, own).transpose(1, 0, 2)
    block = jnp.concatenate(
        [singles[:, 0:2], shared(2, 2), singles[:, 4:8], shared(8, 4), singles[:, 12:16]], axis=1
    )
    return jnp.pad(block, ((0, 0), (0, 0), (0, 128 - own))).reshape(devices * 16, 128)


def after_that(value, *others):
    return lax.optimization_barrier((value,) + others)[0]


def window_labels(frames_here, windows):
    token = np.arange(TOKENS)
    late_t = token // CELLS >= WIN_T - WIN_T // 2
    late_r = token // WIN_HW % WIN_HW >= WIN_HW - WIN_HW // 2
    late_c = token % WIN_HW >= WIN_HW - WIN_HW // 2
    quadrant = lax.axis_index("space")
    last = (lax.axis_index("tm") == lax.axis_size("tm") - 1).astype(jnp.int32)
    at_end = last * (jnp.arange(windows) == windows - 1).astype(jnp.int32)
    label = (
        4 * at_end[:, None] * jnp.asarray(late_t, jnp.int32)
        + 2 * (quadrant // 2) * jnp.asarray(late_r, jnp.int32)
        + (quadrant % 2) * jnp.asarray(late_c, jnp.int32)
    ).astype(F32)
    return label[:, :, None], label[:, None, :]


def local_windows(
    clips_in,
    ln1_gain,
    ln1_bias,
    qkv_weight,
    qv_bias,
    out_weight,
    out_bias,
    ln2_gain,
    ln2_bias,
    fc1_weight,
    fc1_bias,
    fc2_weight,
    fc2_bias,
    pos_table,
    out_grad,
):
    _, frames_here, _, _, width = clips_in.shape
    windows = frames_here // WIN_T
    own = ln1_gain.shape[1]
    devices = width // own
    one, two = stage_orders()
    half = 3 * width // 2
    flat = (windows, TOKENS, width)

    small = vectors_in(
        (ln1_gain, ln1_bias, qv_bias, out_bias, ln2_gain, ln2_bias, fc1_bias, fc2_bias)
    )
    first = gather_all(jnp.concatenate([qkv_weight[0][:, :half], small], axis=1), one)
    second = gather_all(qkv_weight[0][:, half:], two)
    vec = vectors_whole(first[:, half:], own)
    w_qkv = [jnp.concatenate([first[:, :half], second], axis=1), None]

    tables = pos_table.transpose(0, 2, 1)
    beside = partner(tables, "tm", 0)
    tables = jnp.where(
        lax.axis_index("tm") == 1,
        jnp.concatenate([beside, tables], 1),
        jnp.concatenate([tables, beside], 1),
    )
    bias = table_to_bias(tables).reshape(LAYERS, HEADS, TOKENS, TOKENS)
    labels = window_labels(frames_here, windows)
    send, place, stay, rows, starts, kinds = halo_matrices(frames_here)

    w_mid, w_two = [], []
    gate = (first, second)
    for layer in range(LAYERS):
        if layer > 0:
            shard = after_that(qkv_weight[layer], *gate)
            parts = (gather_all(shard[:, :half], one), gather_all(shard[:, half:], two))
            w_qkv[layer] = jnp.concatenate(parts, axis=1)
            gate = parts
        shard = jnp.concatenate([fc1_weight[layer], out_weight[layer]], axis=1)
        shard, down = lax.optimization_barrier((shard, fc2_weight[layer]) + gate)[:2]
        w_mid.append(gather_all(shard, one))
        w_two.append(gather_all(down, two))
        gate = (w_mid[-1], w_two[-1])

    stream0 = clips_in.reshape(flat)
    qkv0 = run_qkv(stream0, vec[0], w_qkv[0])
    att0, log0 = run_attend(qkv0, bias[0], labels, False)
    mid0, hid0, slope0, stream1 = run_branch(stream0, att0, vec[0], w_mid[0], w_two[0], F32)
    came = halo_permute(halo_pack(stream1, send, True), rows, starts, kinds, True)
    rolled1 = halo_unpack(stream1, came, stay, place, starts, F32, center=True)
    qkv1 = run_qkv(rolled1, vec[1], w_qkv[1])
    att1, log1 = run_attend(qkv1, bias[1], labels, True)
    mid1, hid1, slope1, rolled_out = run_branch(rolled1, att1, vec[1], w_mid[1], w_two[1], F32)
    back = halo_permute(halo_pack(rolled_out, place.T, False), rows, starts, kinds, False)
    clips_out = halo_unpack(rolled_out, back, stay.T, send.T, starts, BF16, mean_of=stream1)

    grad_in = after_that(out_grad, *gate).reshape(flat)
    came = halo_permute(halo_pack(grad_in, send, False), rows, starts, kinds, True)
    grad = halo_unpack(grad_in, came, stay, place, starts, BF16)

    kept = (
        (stream0, qkv0, att0, log0, mid0, hid0, slope0),
        (rolled1, qkv1, att1, log1, mid1, hid1, slope1),
    )
    shares, table_parts = [None] * LAYERS, [None] * LAYERS
    for layer in reversed(range(LAYERS)):
        stream, qkv, att, log, mid, hid, slope = kept[layer]
        grad_mid, grad_att, d_mid, d_two, vecs = run_branch_back(
            grad, mid, att, hid, slope, vec[layer], w_mid[layer], w_two[layer]
        )
        mid_share = scatter_all(d_mid, one)
        two_share = scatter_all(d_two, two)
        *grads, table = run_attend_back(qkv, grad_att, bias[layer], labels, log, layer == 1)
        grad_stream, d_qkv, vecs_one = run_qkv_back(
            grads, stream, grad_mid, vec[layer], w_qkv[layer], F32 if layer else BF16
        )
        vecs = jnp.concatenate([vecs_one[:4], vecs[4:]], axis=0)
        packed = jnp.concatenate([d_qkv[:, :half], vectors_split(vecs, devices)], axis=1)
        left = scatter_all(packed, one)
        right = scatter_all(d_qkv[:, half:], two)
        shares[layer] = (mid_share, two_share, left, right)
        table = bias_grad_to_table(table)
        heads_here = pos_table.shape[2]
        mine = lax.dynamic_slice_in_dim(table, lax.axis_index("tm") * heads_here, heads_here, 0)
        theirs = lax.dynamic_slice_in_dim(
            table, (1 - lax.axis_index("tm")) * heads_here, heads_here, 0
        )
        table = mine + partner(theirs, "tm", 0)
        for axis, bit in one:
            if axis != "tm":
                table = table + partner(table, axis, bit)
        table_parts[layer] = table
        if layer:
            back = halo_permute(halo_pack(grad_stream, place.T, False), rows, starts, kinds, False)
            grad = halo_unpack(grad_stream, back, stay.T, send.T, starts, F32)
    in_grad = grad_stream

    wide = fc1_weight.shape[2]
    mid_share, two_share, left, right = (jnp.stack(s) for s in zip(*shares))
    small = left[:, :, half : half + own]

    def vector(row, count=1):
        return small[:, row : row + count].reshape(LAYERS, count * own)

    return (
        clips_out.reshape(clips_in.shape),
        in_grad.reshape(clips_in.shape),
        vector(0),
        vector(1),
        jnp.concatenate([left[:, :, :half], right], axis=2),
        vector(2, 2),
        mid_share[:, :, wide:],
        vector(4),
        vector(5),
        vector(6),
        mid_share[:, :, :wide],
        vector(8, 4),
        two_share,
        vector(7),
        jnp.stack(table_parts).transpose(0, 2, 1),
    )


def windows_are_local(mesh):
    def decide(clips_in, *rest):
        clips, frames_here = clips_in.shape[:2]
        own = rest[0].shape[1]
        return (
            clips == 1
            and frames_here % WIN_T == 0
            and own == 16
            and mesh.shape["tm"] == 2
            and mesh.shape["space"] == 4
        )

    def program(*args):
        return local_windows(*args) if decide(*args) else per_device(*args)

    return program


def solution(mesh):
    placed = (
        P("clip", "tm", "space", None, None),
        P(None, ("tm", "space", "clip")),
        P(None, ("tm", "space", "clip")),
        P(None, ("tm", "space", "clip"), None),
        P(None, ("tm", "space", "clip")),
        P(None, ("tm", "space", "clip"), None),
        P(None, ("tm", "space", "clip")),
        P(None, ("tm", "space", "clip")),
        P(None, ("tm", "space", "clip")),
        P(None, ("tm", "space", "clip"), None),
        P(None, ("tm", "space", "clip")),
        P(None, ("tm", "space", "clip"), None),
        P(None, ("tm", "space", "clip")),
        P(None, None, "tm"),
        P("clip", "tm", "space", None, None),
    )
    return jax.shard_map(
        windows_are_local(mesh),
        mesh=mesh,
        in_specs=placed,
        out_specs=(
            P("clip", "tm", "space", None, None),
            P("clip", "tm", "space", None, None),
            P(None, ("tm", "space", "clip")),
            P(None, ("tm", "space", "clip")),
            P(None, ("tm", "space", "clip"), None),
            P(None, ("tm", "space", "clip")),
            P(None, ("tm", "space", "clip"), None),
            P(None, ("tm", "space", "clip")),
            P(None, ("tm", "space", "clip")),
            P(None, ("tm", "space", "clip")),
            P(None, ("tm", "space", "clip"), None),
            P(None, ("tm", "space", "clip")),
            P(None, ("tm", "space", "clip"), None),
            P(None, ("tm", "space", "clip")),
            P(None, None, "tm"),
        ),
        check_vma=False,
    )
```

```python
import functools
import math

import jax
import jax.numpy as jnp
import numpy as np
from jax import lax
from jax.experimental import pallas as pl
from jax.experimental.pallas import tpu as pltpu
from jax.sharding import PartitionSpec as P

HEADS = 16
WIN_T = 8
WIN_HW = 7
LAYERS = 2


masked_score = -1000000000.0


def partner(value, axis, bit):
    mask = 2**bit
    pairs = [(source, source ^ mask) for source in range(lax.axis_size(axis))]
    return lax.ppermute(value, axis, pairs)


def norm_rows(values, gain, offset):
    mean_row = jnp.mean(values, axis=-1, keepdims=True)
    centered = values - mean_row
    spread = jnp.mean(centered * centered, axis=-1, keepdims=True)
    return centered * lax.rsqrt(spread + 1e-05) * gain + offset


def gelu_exact(values):
    return jax.nn.gelu(values, approximate=False)


def project(left, right):
    return jnp.einsum("...i,ij->...j", left, right, preferred_element_type=jnp.float32)


def project_back(left, right):
    return jnp.einsum("...j,ij->...i", left, right, preferred_element_type=jnp.float32)


def outer_sum(left, right):
    flat_left = left.reshape(-1, left.shape[-1])
    flat_right = right.reshape(-1, right.shape[-1])
    return jnp.einsum("ti,tj->ij", flat_left, flat_right, preferred_element_type=jnp.float32)


def column_sum(values):
    return jnp.sum(values.reshape(-1, values.shape[-1]).astype(jnp.float32), axis=0)


def relative_index(win_t, win_hw):
    count = win_t * win_hw * win_hw
    positions = jnp.arange(count, dtype=jnp.int32)
    frame_pos = positions // (win_hw * win_hw)
    row_pos = positions // win_hw % win_hw
    col_pos = positions % win_hw
    span = 2 * win_hw - 1
    frame_off = frame_pos[:, None] - frame_pos[None, :] + win_t - 1
    row_off = row_pos[:, None] - row_pos[None, :] + win_hw - 1
    col_off = col_pos[:, None] - col_pos[None, :] + win_hw - 1
    return frame_off * span * span + row_off * span + col_off


def band_label(coord, extent, window, reach):
    return jnp.where(coord < extent - window, 0, jnp.where(coord < extent - reach, 1, 2)).astype(
        jnp.int32
    )


def region_match(frames):
    quadrant = lax.axis_index("space")
    row_quad = quadrant // 2
    col_quad = quadrant % 2
    local = jnp.arange(WIN_HW, dtype=jnp.int32)
    label_t = band_label(jnp.arange(frames, dtype=jnp.int32), frames, WIN_T, WIN_T // 2)
    label_r = band_label(row_quad * WIN_HW + local, 2 * WIN_HW, WIN_HW, WIN_HW // 2)
    label_c = band_label(col_quad * WIN_HW + local, 2 * WIN_HW, WIN_HW, WIN_HW // 2)
    region = label_t[:, None, None] * 9 + label_r[None, :, None] * 3 + label_c[None, None, :]
    region = region.reshape(frames // WIN_T, WIN_T * WIN_HW * WIN_HW)
    return region[:, :, None] == region[:, None, :]


def space_roll(field, onward):
    side = field.shape[2]
    reach = side // 2
    sent_rows = field[:, :, :reach] if onward else field[:, :, side - reach :]
    came_rows = partner(sent_rows, "space", 1)
    if onward:
        rows_done = jnp.concatenate([field, came_rows], axis=2)[:, :, reach : reach + side]
    else:
        rows_done = jnp.concatenate([came_rows, field], axis=2)[:, :, :side]
    sent_cols = rows_done[:, :, :, :reach] if onward else rows_done[:, :, :, side - reach :]
    came_cols = partner(sent_cols, "space", 0)
    if onward:
        return jnp.concatenate([rows_done, came_cols], axis=3)[:, :, :, reach : reach + side]
    return jnp.concatenate([came_cols, rows_done], axis=3)[:, :, :, :side]


def gather_layer(shards, layer):
    parts = tuple((w[layer] for w in shards))
    return (
        lax.all_gather(parts[0], ("tm", "space", "clip"), axis=0, tiled=True),
        lax.all_gather(parts[1], ("tm", "space", "clip"), axis=0, tiled=True),
        lax.all_gather(parts[2], ("tm", "space", "clip"), axis=0, tiled=True),
        lax.all_gather(parts[3], ("tm", "space", "clip"), axis=0, tiled=True),
        lax.all_gather(parts[4], ("tm", "space", "clip"), axis=0, tiled=True),
        lax.all_gather(parts[5], ("tm", "space", "clip"), axis=0, tiled=True),
        lax.all_gather(parts[6], ("tm", "space", "clip"), axis=0, tiled=True),
        lax.all_gather(parts[7], ("tm", "space", "clip"), axis=0, tiled=True),
        lax.all_gather(parts[8], ("tm", "space", "clip"), axis=0, tiled=True),
        lax.all_gather(parts[9], ("tm", "space", "clip"), axis=0, tiled=True),
        lax.all_gather(parts[10], ("tm", "space", "clip"), axis=0, tiled=True),
        lax.all_gather(parts[11], ("tm", "space", "clip"), axis=0, tiled=True),
    )


def gather_again(shards, layer):
    parts = tuple((w[layer] for w in shards))
    return (
        lax.all_gather(parts[0], ("tm", "space", "clip"), axis=0, tiled=True),
        lax.all_gather(parts[1], ("tm", "space", "clip"), axis=0, tiled=True),
        lax.all_gather(parts[2], ("tm", "space", "clip"), axis=0, tiled=True),
        lax.all_gather(parts[3], ("tm", "space", "clip"), axis=0, tiled=True),
        lax.all_gather(parts[4], ("tm", "space", "clip"), axis=0, tiled=True),
        lax.all_gather(parts[5], ("tm", "space", "clip"), axis=0, tiled=True),
        lax.all_gather(parts[6], ("tm", "space", "clip"), axis=0, tiled=True),
        lax.all_gather(parts[7], ("tm", "space", "clip"), axis=0, tiled=True),
        lax.all_gather(parts[8], ("tm", "space", "clip"), axis=0, tiled=True),
        lax.all_gather(parts[9], ("tm", "space", "clip"), axis=0, tiled=True),
        lax.all_gather(parts[10], ("tm", "space", "clip"), axis=0, tiled=True),
        lax.all_gather(parts[11], ("tm", "space", "clip"), axis=0, tiled=True),
    )


def table_bias(table):
    rel = relative_index(WIN_T, WIN_HW)
    return table.astype(jnp.float32)[rel].transpose(2, 0, 1)


def window_scores(queries, keys, bias, same, scale):
    scores = (
        jnp.einsum("wqhd,wkhd->whqk", queries, keys, preferred_element_type=jnp.float32) * scale
        + bias[None]
    )
    if same is not None:
        scores = jnp.where(same[:, None], scores, masked_score)
    return scores


def to_windows(field):
    clips, frames, cells, heads_here, head_size = field.shape
    return field.reshape(clips, frames // WIN_T, WIN_T * cells, heads_here, head_size)


def to_frames(field, frames):
    clips = field.shape[0]
    return field.reshape(clips, frames, WIN_HW * WIN_HW, field.shape[3], field.shape[4])


def layer_forward(stream, params, table, shifted):
    (
        gain_one,
        bias_one,
        mix_weight,
        mix_bias,
        proj_weight,
        proj_bias,
        gain_two,
        bias_two,
        wide_weight,
        wide_bias,
        narrow_weight,
        narrow_bias,
    ) = params
    clips, frames_here, side = (stream.shape[0], stream.shape[1], stream.shape[2])
    width = stream.shape[-1]
    head_size = width // HEADS
    scale = head_size ** (-0.5)
    normed = norm_rows(stream, gain_one.astype(jnp.float32), bias_one.astype(jnp.float32)).astype(
        jnp.bfloat16
    )
    if shifted:
        normed = space_roll(normed, True)
    mixed = project(normed, mix_weight)
    mix_bias32 = mix_bias.astype(jnp.float32)
    head_shape = (clips, frames_here, side * side, HEADS, head_size)
    queries = (mixed[..., :width] + mix_bias32[:width]).astype(jnp.bfloat16).reshape(head_shape)
    keys = mixed[..., width : 2 * width].astype(jnp.bfloat16).reshape(head_shape)
    values = (mixed[..., 2 * width :] + mix_bias32[width:]).astype(jnp.bfloat16).reshape(head_shape)
    queries, keys, values = (
        lax.all_to_all(queries, "tm", split_axis=3, concat_axis=1, tiled=True),
        lax.all_to_all(keys, "tm", split_axis=3, concat_axis=1, tiled=True),
        lax.all_to_all(values, "tm", split_axis=3, concat_axis=1, tiled=True),
    )
    frames = queries.shape[1]
    if shifted:
        queries = jnp.roll(queries, -(WIN_T // 2), axis=1)
        keys = jnp.roll(keys, -(WIN_T // 2), axis=1)
        values = jnp.roll(values, -(WIN_T // 2), axis=1)
    queries, keys, values = (to_windows(queries), to_windows(keys), to_windows(values))
    bias = table_bias(table)
    same = region_match(frames) if shifted else None

    def attend_clip(items):
        clip_queries, clip_keys, clip_values = items
        scores = window_scores(clip_queries, clip_keys, bias, same, scale)
        peak = jnp.max(scores, axis=-1, keepdims=True)
        raised = jnp.exp(scores - peak)
        total = jnp.sum(raised, axis=-1, keepdims=True)
        probs = (raised / total).astype(jnp.bfloat16)
        out_win = jnp.einsum(
            "whqk,wkhd->wqhd", probs, clip_values, preferred_element_type=jnp.float32
        ).astype(jnp.bfloat16)
        return (out_win, peak + jnp.log(total))

    attended_heads, log_total = lax.map(attend_clip, (queries, keys, values))
    attended_heads = to_frames(attended_heads, frames)
    if shifted:
        attended_heads = jnp.roll(attended_heads, WIN_T // 2, axis=1)
    attended = lax.all_to_all(attended_heads, "tm", split_axis=1, concat_axis=3, tiled=True)
    attended = attended.reshape(clips, frames_here, side, side, width)
    if shifted:
        attended = space_roll(attended, False)
    middle = stream + project(attended, proj_weight) + proj_bias.astype(jnp.float32)
    normed_two = norm_rows(
        middle, gain_two.astype(jnp.float32), bias_two.astype(jnp.float32)
    ).astype(jnp.bfloat16)
    hidden_pre = project(normed_two, wide_weight) + wide_bias.astype(jnp.float32)
    hidden = gelu_exact(hidden_pre).astype(jnp.bfloat16)
    after = middle + project(hidden, narrow_weight) + narrow_bias.astype(jnp.float32)
    stash = (
        stream,
        normed,
        queries,
        keys,
        values,
        log_total,
        attended,
        middle,
        normed_two,
        hidden_pre,
        hidden,
    )
    return (stash, after)


def layer_backward(grad_after, params, table, stash, shifted):
    (
        gain_one,
        bias_one,
        mix_weight,
        mix_bias,
        proj_weight,
        proj_bias,
        gain_two,
        bias_two,
        wide_weight,
        wide_bias,
        narrow_weight,
        narrow_bias,
    ) = params
    (
        stream,
        normed,
        queries,
        keys,
        values,
        log_total,
        attended,
        middle,
        normed_two,
        hidden_pre,
        hidden,
    ) = stash
    clips, frames_here, side = (stream.shape[0], stream.shape[1], stream.shape[2])
    width = stream.shape[-1]
    head_size = width // HEADS
    scale = head_size ** (-0.5)
    frames = queries.shape[1] * WIN_T
    grad_branch_two = grad_after.astype(jnp.bfloat16)
    narrow_grad = outer_sum(hidden, grad_branch_two)
    narrow_bias_grad = column_sum(grad_branch_two)
    grad_hidden = project_back(grad_branch_two, narrow_weight)
    gelu_pull = jax.vjp(gelu_exact, hidden_pre)[1]
    grad_pre = gelu_pull(grad_hidden)[0].astype(jnp.bfloat16)
    wide_grad = outer_sum(normed_two, grad_pre)
    wide_bias_grad = column_sum(grad_pre)
    grad_normed_two = project_back(grad_pre, wide_weight)
    norm_pull_two = jax.vjp(
        norm_rows, middle, gain_two.astype(jnp.float32), bias_two.astype(jnp.float32)
    )[1]
    grad_mid_part, gain_two_grad, bias_two_grad = norm_pull_two(grad_normed_two)
    grad_middle = grad_after + grad_mid_part
    grad_branch_one = grad_middle.astype(jnp.bfloat16)
    proj_grad = outer_sum(attended, grad_branch_one)
    proj_bias_grad = column_sum(grad_branch_one)
    grad_attended = project_back(grad_branch_one, proj_weight).astype(jnp.bfloat16)
    if shifted:
        grad_attended = space_roll(grad_attended, True)
    grad_attended = grad_attended.reshape(clips, frames_here, side * side, HEADS, head_size)
    grad_attended = lax.all_to_all(grad_attended, "tm", split_axis=3, concat_axis=1, tiled=True)
    if shifted:
        grad_attended = jnp.roll(grad_attended, -(WIN_T // 2), axis=1)
    grad_attended = to_windows(grad_attended)
    bias = table_bias(table)
    same = region_match(frames) if shifted else None

    def attend_back(carry, items):
        clip_queries, clip_keys, clip_values, clip_grad, clip_log = items
        scores = window_scores(clip_queries, clip_keys, bias, same, scale)
        probs = jnp.exp(scores - clip_log)
        grad_probs = jnp.einsum(
            "wqhd,wkhd->whqk", clip_grad, clip_values, preferred_element_type=jnp.float32
        )
        inner = jnp.sum(probs * grad_probs, axis=-1, keepdims=True)
        grad_scores = (probs * (grad_probs - inner)).astype(jnp.bfloat16)
        grad_q = (
            jnp.einsum(
                "whqk,wkhd->wqhd", grad_scores, clip_keys, preferred_element_type=jnp.float32
            )
            * scale
        ).astype(jnp.bfloat16)
        grad_k = (
            jnp.einsum(
                "whqk,wqhd->wkhd", grad_scores, clip_queries, preferred_element_type=jnp.float32
            )
            * scale
        ).astype(jnp.bfloat16)
        grad_v = jnp.einsum(
            "whqk,wqhd->wkhd",
            probs.astype(jnp.bfloat16),
            clip_grad,
            preferred_element_type=jnp.float32,
        ).astype(jnp.bfloat16)
        carry = carry + jnp.sum(grad_scores.astype(jnp.float32), axis=0)
        return (carry, (grad_q, grad_k, grad_v))

    window_tokens = queries.shape[2]
    start_bias = jnp.zeros((queries.shape[3], window_tokens, window_tokens), jnp.float32)
    bias_grad, grads_win = lax.scan(
        attend_back, start_bias, (queries, keys, values, grad_attended, log_total)
    )
    grad_q, grad_k, grad_v = (to_frames(g, frames) for g in grads_win)
    if shifted:
        grad_q = jnp.roll(grad_q, WIN_T // 2, axis=1)
        grad_k = jnp.roll(grad_k, WIN_T // 2, axis=1)
        grad_v = jnp.roll(grad_v, WIN_T // 2, axis=1)
    grad_q, grad_k, grad_v = (
        lax.all_to_all(grad_q, "tm", split_axis=1, concat_axis=3, tiled=True),
        lax.all_to_all(grad_k, "tm", split_axis=1, concat_axis=3, tiled=True),
        lax.all_to_all(grad_v, "tm", split_axis=1, concat_axis=3, tiled=True),
    )
    token_shape = (clips, frames_here, side, side, width)
    grad_q, grad_k, grad_v = (
        grad_q.reshape(token_shape),
        grad_k.reshape(token_shape),
        grad_v.reshape(token_shape),
    )
    grad_mix = jnp.concatenate([grad_q, grad_k, grad_v], axis=-1)
    mix_grad = outer_sum(normed, grad_mix)
    mix_bias_grad = jnp.concatenate([column_sum(grad_q), column_sum(grad_v)])
    grad_normed = project_back(grad_mix, mix_weight)
    if shifted:
        grad_normed = space_roll(grad_normed.astype(jnp.bfloat16), False).astype(jnp.float32)
    norm_pull_one = jax.vjp(
        norm_rows, stream, gain_one.astype(jnp.float32), bias_one.astype(jnp.float32)
    )[1]
    grad_stream_part, gain_one_grad, bias_one_grad = norm_pull_one(grad_normed)
    grad_stream = grad_middle + grad_stream_part
    rel = relative_index(WIN_T, WIN_HW).reshape(-1)
    table_grad = (
        jnp.zeros(table.shape, jnp.float32).at[rel].add(bias_grad.reshape(bias_grad.shape[0], -1).T)
    )
    weight_grads = (
        gain_one_grad,
        bias_one_grad,
        mix_grad,
        mix_bias_grad,
        proj_grad,
        proj_bias_grad,
        gain_two_grad,
        bias_two_grad,
        wide_grad,
        wide_bias_grad,
        narrow_grad,
        narrow_bias_grad,
    )
    return (grad_stream, weight_grads, table_grad)


def per_device(
    clips_in,
    ln1_gain,
    ln1_bias,
    qkv_weight,
    qv_bias,
    out_weight,
    out_bias,
    ln2_gain,
    ln2_bias,
    fc1_weight,
    fc1_bias,
    fc2_weight,
    fc2_bias,
    pos_table,
    out_grad,
):
    clips, frames_here, quads, cells, width = clips_in.shape
    grid_shape = (clips, frames_here, WIN_HW, WIN_HW, width)
    shards = (
        ln1_gain,
        ln1_bias,
        qkv_weight,
        qv_bias,
        out_weight,
        out_bias,
        ln2_gain,
        ln2_bias,
        fc1_weight,
        fc1_bias,
        fc2_weight,
        fc2_bias,
    )
    stream = clips_in.astype(jnp.float32).reshape(grid_shape)
    kept_params = []
    kept_stash = []
    for layer in range(LAYERS):
        params = gather_layer(shards, layer)
        stash, stream = layer_forward(stream, params, pos_table[layer], layer % 2 == 1)
        kept_params.append(params)
        kept_stash.append(stash)
    clips_out = stream.astype(jnp.bfloat16).reshape(clips_in.shape)
    grad_stream = out_grad.astype(jnp.float32).reshape(grid_shape)
    layer_shares = [None] * LAYERS
    table_parts = [None] * LAYERS
    for layer in reversed(range(LAYERS)):
        params = gather_again(shards, layer)
        grad_stream, weight_grads, table_grad = layer_backward(
            grad_stream, params, pos_table[layer], kept_stash[layer], layer % 2 == 1
        )
        layer_shares[layer] = (
            lax.psum_scatter(
                weight_grads[0], ("tm", "space", "clip"), scatter_dimension=0, tiled=True
            ),
            lax.psum_scatter(
                weight_grads[1], ("tm", "space", "clip"), scatter_dimension=0, tiled=True
            ),
            lax.psum_scatter(
                weight_grads[2], ("tm", "space", "clip"), scatter_dimension=0, tiled=True
            ),
            lax.psum_scatter(
                weight_grads[3], ("tm", "space", "clip"), scatter_dimension=0, tiled=True
            ),
            lax.psum_scatter(
                weight_grads[4], ("tm", "space", "clip"), scatter_dimension=0, tiled=True
            ),
            lax.psum_scatter(
                weight_grads[5], ("tm", "space", "clip"), scatter_dimension=0, tiled=True
            ),
            lax.psum_scatter(
                weight_grads[6], ("tm", "space", "clip"), scatter_dimension=0, tiled=True
            ),
            lax.psum_scatter(
                weight_grads[7], ("tm", "space", "clip"), scatter_dimension=0, tiled=True
            ),
            lax.psum_scatter(
                weight_grads[8], ("tm", "space", "clip"), scatter_dimension=0, tiled=True
            ),
            lax.psum_scatter(
                weight_grads[9], ("tm", "space", "clip"), scatter_dimension=0, tiled=True
            ),
            lax.psum_scatter(
                weight_grads[10], ("tm", "space", "clip"), scatter_dimension=0, tiled=True
            ),
            lax.psum_scatter(
                weight_grads[11], ("tm", "space", "clip"), scatter_dimension=0, tiled=True
            ),
        )
        table_parts[layer] = table_grad
    in_grad = grad_stream.astype(jnp.bfloat16).reshape(clips_in.shape)
    table_total = lax.psum(jnp.stack(table_parts), ("space", "clip"))
    stacked = tuple(
        (jnp.stack([layer_shares[n][slot] for n in range(LAYERS)]) for slot in range(12))
    )
    return (
        clips_out,
        in_grad,
        stacked[0],
        stacked[1],
        stacked[2],
        stacked[3],
        stacked[4],
        stacked[5],
        stacked[6],
        stacked[7],
        stacked[8],
        stacked[9],
        stacked[10],
        stacked[11],
        table_total,
    )


F32 = jnp.float32
BF16 = jnp.bfloat16
TOKENS = WIN_T * WIN_HW * WIN_HW
CELLS = WIN_HW * WIN_HW
SPAN = 2 * WIN_HW - 1
STEPS = 2 * WIN_T - 1
LOG2E = math.log2(math.e)
VMEM_BYTES = 56 * 1024 * 1024


def mm(left, right, left_dim=1, right_dim=0):
    dims = (((left_dim,), (right_dim,)), ((), ()))
    return lax.dot_general(left, right, dims, preferred_element_type=F32)


def call(kernel, grid, in_specs, out_specs, out_shape, flops, scratch=(), after=()):
    inputs, waits = len(in_specs), len(after)

    def body(*refs):
        kernel(*refs[:inputs], *refs[inputs + waits :])

    run = pl.pallas_call(
        body,
        grid=grid,
        in_specs=list(in_specs) + [pl.BlockSpec(memory_space=pl.ANY)] * waits,
        out_specs=out_specs,
        out_shape=out_shape,
        scratch_shapes=scratch,
        cost_estimate=pl.CostEstimate(
            flops=int(flops), transcendentals=0, bytes_accessed=8 * 1024 * 1024
        ),
        compiler_params=pltpu.CompilerParams(vmem_limit_bytes=VMEM_BYTES),
    )
    return lambda *args: run(*args, *after)


def whole_block(shape):
    return pl.BlockSpec(shape, lambda *ids: (0,) * len(shape))


def flag_spec():
    return pl.BlockSpec(memory_space=pltpu.SMEM)


def win_block(width, column=0):
    return pl.BlockSpec((1, TOKENS, width), lambda w: (w, 0, column))


def halo_plan(frames_here):
    half_t, reach = WIN_T // 2, WIN_HW // 2
    frame, row, col = np.meshgrid(
        np.arange(frames_here), np.arange(WIN_HW), np.arange(WIN_HW), indexing="ij"
    )
    frame, row, col = frame.reshape(-1), row.reshape(-1), col.reshape(-1)
    new_t = (frame - half_t) % frames_here
    new_r = (row - reach) % WIN_HW
    new_c = (col - reach) % WIN_HW
    target = new_t * CELLS + new_r * WIN_HW + new_c
    leaves = (frame < half_t) * 4 + (row < reach) * 2 + (col < reach) * 1
    parts = []
    for kind in range(1, 8):
        source = np.nonzero(leaves == kind)[0]
        parts.append((kind, source, target[source]))
    stay = np.nonzero(leaves == 0)[0]
    return parts, (stay, target[stay])


def halo_matrices(frames_here):
    parts, (stay, stay_to) = halo_plan(frames_here)
    count = frames_here * CELLS
    rows = [-(-len(source) // 16) * 16 for _, source, _ in parts]
    starts = np.concatenate([[0], np.cumsum(rows)])
    send = np.zeros((starts[-1], count), np.float32)
    place = np.zeros((count, starts[-1]), np.float32)
    own = np.zeros((count, count), np.float32)
    for (_, source, to), start in zip(parts, starts[:-1]):
        slots = start + np.arange(len(source))
        send[slots, source] = 1
        place[to, slots] = 1
    own[stay_to, stay] = 1
    return send, place, own, rows, starts, [kind for kind, _, _ in parts]


class Flow:
    def __init__(self):
        self.live = []
        self.done = {}

    def start(self, name, task):
        self.live.append((name, task, next(task)))

    def pending(self):
        return [value for _, _, sends in self.live for value, _, _ in sends]

    def step(self, *names):
        live = []
        for name, task, sends in self.live:
            if names and name not in names:
                live.append((name, task, sends))
                continue
            came = [lax.ppermute(value, axis, pairs) for value, axis, pairs in sends]
            try:
                live.append((name, task, task.send(came)))
            except StopIteration as end:
                self.done[name] = end.value
        self.live = live

    def finish(self, name):
        while name not in self.done:
            self.step(name)
        return self.done[name]


def swap_pairs(axis, bit):
    return [(source, source ^ 2**bit) for source in range(lax.axis_size(axis))]


def halo_flow(packed, rows, starts, kinds, onward):
    ring, quads = lax.axis_size("tm"), lax.axis_size("space")
    sends = []
    for kind, start, count in zip(kinds, starts, rows):
        step = 0 if not kind & 4 else (-1 if onward else 1)
        pairs = []
        for frame_at in range(ring):
            for quad in range(quads):
                to = (frame_at + step) % ring * quads + (quad ^ (kind & 3))
                pairs.append((frame_at * quads + quad, to))
        sends.append((packed[start : start + count], ("tm", "space"), pairs))
    return (yield sends)


def pack_kernel(center, send_ref, x_ref, out_ref):
    windows = x_ref.shape[0]
    total = None
    for w in range(windows):
        x = x_ref[w]
        if center:
            x = x - jnp.mean(x, axis=-1, keepdims=True)
        part = mm(send_ref[:, w * TOKENS : (w + 1) * TOKENS], x.astype(BF16))
        total = part if total is None else total + part
    out_ref[...] = total.astype(BF16)


def halo_pack(x, send, center, after=()):
    windows, _, width = x.shape
    rows = send.shape[0]
    return functools.partial(call, after=after)(
        functools.partial(pack_kernel, center),
        (),
        [pl.BlockSpec(memory_space=pltpu.VMEM)] * 2,
        pl.BlockSpec(memory_space=pltpu.VMEM),
        jax.ShapeDtypeStruct((rows, width), BF16),
        2 * rows * windows * TOKENS * width,
    )(jnp.asarray(send, BF16), x)


def unpack_kernel(center, add_mean, starts, own_ref, place_ref, x_ref, base_ref, *refs):
    came_refs, out_ref = refs[:-1], refs[-1]
    windows = x_ref.shape[0]
    total = jnp.zeros((windows * TOKENS, x_ref.shape[-1]), F32)
    for w in range(windows):
        x = x_ref[w].astype(F32)
        if center:
            x = x - jnp.mean(x, axis=-1, keepdims=True)
        high = x.astype(BF16)
        cols = own_ref[:, w * TOKENS : (w + 1) * TOKENS]
        total = total + mm(cols, high)
        if x_ref.dtype == F32:
            total = total + mm(cols, (x - high.astype(F32)).astype(BF16))
    came = jnp.concatenate([r[...] for r in came_refs], axis=0)
    total = total + mm(place_ref[...], came)
    for w in range(windows):
        piece = total[w * TOKENS : (w + 1) * TOKENS]
        if add_mean:
            piece = piece + jnp.mean(base_ref[w], axis=-1, keepdims=True)
        out_ref[w] = piece.astype(out_ref.dtype)


def halo_unpack(x, came, own, place, starts, dtype, center=False, mean_of=None, after=()):
    windows, _, width = x.shape
    base = jnp.zeros((windows, 8, 128), F32) if mean_of is None else mean_of
    return functools.partial(call, after=after)(
        functools.partial(unpack_kernel, center, mean_of is not None, starts),
        (),
        [pl.BlockSpec(memory_space=pltpu.VMEM)] * (4 + len(came)),
        pl.BlockSpec(memory_space=pltpu.VMEM),
        jax.ShapeDtypeStruct((windows, TOKENS, width), dtype),
        4 * (windows * TOKENS) ** 2 * width,
    )(jnp.asarray(own, BF16), jnp.asarray(place, BF16), x, base, *came)


def index_bits():
    bits = []
    for axis in ("tm", "space", "clip"):
        count = lax.axis_size(axis).bit_length() - 1
        bits += [(axis, b) for b in reversed(range(count))]
    return bits


def bit_of(axis, bit):
    return (lax.axis_index(axis) // 2**bit) % 2


def stage_orders():
    bits = index_bits()
    inner = [("clip", 0)] if lax.axis_size("clip") > 1 else []
    tm = [b for b in bits if b[0] == "tm"]
    clip = [b for b in bits if b[0] == "clip" and b not in inner]
    space = [b for b in reversed(bits) if b[0] == "space"]
    return inner + tm + clip + space, inner + clip + tm + space


def gather_flow(shard, order):
    bits = index_bits()
    out = shard.reshape((1,) * len(bits) + shard.shape)
    for axis, bit in reversed(order):
        dim = bits.index((axis, bit))
        (other,) = yield [(out, axis, swap_pairs(axis, bit))]
        out = jnp.where(
            bit_of(axis, bit) == 1,
            jnp.concatenate([other, out], dim),
            jnp.concatenate([out, other], dim),
        )
    return out.reshape((-1,) + shard.shape[1:])


def scatter_flow(own, sent, order):
    bits = index_bits()
    width = own.shape[-1]
    dims = [2] * len(bits)
    for n, (axis, bit) in enumerate(order):
        dim = bits.index((axis, bit))
        if n == 0:
            dims[dim] = 1
            own, sent = (v.reshape(dims + [-1, width]) for v in (own, sent))
        else:
            here = bit_of(axis, bit)
            own = lax.dynamic_slice_in_dim(out, here, 1, dim)
            sent = lax.dynamic_slice_in_dim(out, 1 - here, 1, dim).astype(BF16)
        (came,) = yield [(sent, axis, swap_pairs(axis, bit))]
        out = own + came.astype(F32)
    return out.reshape(-1, width)


def table_flow(tables, heads_here):
    first = lax.axis_index("tm") == 0
    mine = jnp.where(first, tables[0], tables[1])
    (came,) = yield [(jnp.where(first, tables[1], tables[0]), "tm", swap_pairs("tm", 0))]
    table = mine + came
    for axis, bit in index_bits():
        if axis != "tm":
            (came,) = yield [(table, axis, swap_pairs(axis, bit))]
            table = table + came
    return table


WIDE = 768


def column_pick():
    pick = np.zeros((WIN_HW, 256, 128), np.float32)
    for key_col in range(WIN_HW):
        for row in range(SPAN):
            for col in range(WIN_HW):
                entry = row * SPAN + col - key_col + WIN_HW - 1
                pick[key_col, entry, row * WIN_HW + col] = 1
    return pick


def lane_spans(step):
    first, rest = divmod(step * CELLS, 128)
    if rest + CELLS <= 128:
        return [(first, rest, rest + CELLS)]
    return [(first, rest, 128), (first + 1, 0, rest + CELLS - 128)]


def bias_kernel(slab_ref, pick_ref, out_ref, row_ref, wide_ref):
    heads = pl.num_programs(0)

    @pl.when(pl.program_id(0) == 0)
    def _():
        slabs = slab_ref[...]
        for col in range(WIN_HW):
            row_ref[pl.ds(col, slabs.shape[0], stride=8), :] = mm(slabs, pick_ref[col]) * LOG2E

    base = pl.program_id(0) * 128
    lane = lax.broadcasted_iota(jnp.int32, (8, 128), 1)
    for row in range(WIN_HW):
        tiles = [jnp.zeros((8, 128), F32) for _ in range(WIDE // 128)]
        for step in range(STEPS):
            rows = row_ref[pl.ds(pl.multiple_of(base + step * 8, 8), 8), :]
            turn = (step * CELLS - WIN_HW * (WIN_HW - 1 - row)) % 128
            rows = pltpu.roll(rows, turn, 1) if turn else rows
            for tile, low, high in lane_spans(step):
                tiles[tile] = jnp.where((lane >= low) & (lane < high), rows, tiles[tile])
        wide_ref[row * WIN_HW : (row + 1) * WIN_HW, :] = jnp.concatenate(tiles, axis=1)[:WIN_HW]
    wide = wide_ref[:CELLS, :]
    for key_frame in range(WIN_T):
        turned = pltpu.roll(wide, (WIDE - (WIN_T - 1 - key_frame) * CELLS) % WIDE, 1)
        out_ref[0, key_frame * CELLS : (key_frame + 1) * CELLS, :] = turned[:, :TOKENS]


def table_to_bias(tables, after=()):
    heads = tables.shape[0]
    slabs = tables.reshape(heads, STEPS, SPAN * SPAN)
    slabs = jnp.pad(slabs, ((0, 0), (0, 16 - STEPS), (0, 256 - SPAN * SPAN)))
    slabs = slabs.reshape(heads * 16, 256)
    return functools.partial(call, after=after)(
        bias_kernel,
        (heads,),
        [whole_block(slabs.shape), whole_block((WIN_HW, 256, 128))],
        pl.BlockSpec((1, TOKENS, TOKENS), lambda h: (h, 0, 0)),
        jax.ShapeDtypeStruct((heads, TOKENS, TOKENS), F32),
        heads * 500_000_000,
        [pltpu.VMEM((heads * 128, 128), F32), pltpu.VMEM((56, WIDE), F32)],
    )(slabs, jnp.asarray(column_pick(), BF16))


def table_back_kernel(sums_ref, pick_ref, out_ref, row_ref):
    head = pl.program_id(0)
    lane = lax.broadcasted_iota(jnp.int32, (WIN_HW, 128), 1)
    totals = [None] * STEPS
    for row in range(WIN_HW):
        rows = sums_ref[0, row * WIN_HW : (row + 1) * WIN_HW, :]
        start = WIN_HW * (WIN_HW - 1 - row)
        for step in range(STEPS):
            turn = (start - step * CELLS) % 128
            piece = None
            for tile, low, high in lane_spans(step):
                part = rows[:, tile * 128 : (tile + 1) * 128]
                part = jnp.where((lane >= low) & (lane < high), part, 0.0)
                piece = part if piece is None else piece + part
            piece = pltpu.roll(piece, turn, 1) if turn else piece
            totals[step] = piece if totals[step] is None else totals[step] + piece
    blank = jnp.zeros((1, 128), F32)
    for step in range(16):
        rows = jnp.concatenate([totals[step], blank]) if step < STEPS else jnp.zeros((8, 128), F32)
        row_ref[pl.ds(pl.multiple_of(head * 128 + step * 8, 8), 8), :] = rows

    @pl.when(head == pl.num_programs(0) - 1)
    def _():
        total = None
        for col in range(WIN_HW):
            rows = row_ref[pl.ds(col, out_ref.shape[0], stride=8), :]
            high = rows.astype(BF16)
            low = (rows - high.astype(F32)).astype(BF16)
            part = mm(high, pick_ref[col], 1, 1) + mm(low, pick_ref[col], 1, 1)
            total = part if total is None else total + part
        out_ref[...] = total


def sums_to_table(sums, after=()):
    heads = sums.shape[0]
    slabs = functools.partial(call, after=after)(
        table_back_kernel,
        (heads,),
        [pl.BlockSpec((1, CELLS, WIDE), lambda h: (h, 0, 0)), whole_block((WIN_HW, 256, 128))],
        whole_block((heads * 16, 256)),
        jax.ShapeDtypeStruct((heads * 16, 256), F32),
        heads * 300_000_000,
        [pltpu.VMEM((heads * 128, 128), F32)],
    )(sums, jnp.asarray(column_pick(), BF16))
    return slabs.reshape(heads, 16, 256)[:, :STEPS, : SPAN * SPAN].reshape(heads, -1)


def unit_rows(x):
    centered = x - jnp.mean(x, axis=-1, keepdims=True)
    inverse = lax.rsqrt(jnp.mean(centered * centered, axis=-1, keepdims=True) + 1e-05)
    return centered * inverse, inverse


def norm_back(grad, unit, inverse, gain):
    scaled = grad * gain
    return inverse * (
        scaled
        - jnp.mean(scaled, axis=-1, keepdims=True)
        - unit * jnp.mean(scaled * unit, axis=-1, keepdims=True)
    )


def qkv_kernel(x_ref, vec_ref, wq_ref, wk_ref, wv_ref, out_ref):
    width = x_ref.shape[-1]
    unit, _ = unit_rows(x_ref[0].astype(F32))
    normed = (unit * vec_ref[0:1] + vec_ref[1:2]).astype(BF16)
    for part, ref in enumerate((wq_ref, wk_ref, wv_ref)):
        out = mm(normed, ref[...])
        if part == 0:
            out = out + vec_ref[2:3]
        if part == 2:
            out = out + vec_ref[3:4]
        out_ref[0, :, part * width : (part + 1) * width] = out.astype(BF16)


def run_qkv(x, vec, w_qkv, after=()):
    windows, _, width = x.shape
    weight, at = w_qkv
    return functools.partial(call, after=after)(
        qkv_kernel,
        (windows,),
        [win_block(width), whole_block(vec.shape)]
        + [weight_block(width, width, at + n) for n in range(3)],
        win_block(3 * width),
        jax.ShapeDtypeStruct((windows, TOKENS, 3 * width), BF16),
        2 * windows * TOKENS * width * 3 * width,
    )(x, vec, weight, weight, weight)


GROUP = 4


def head_masks(head_size):
    lane = lax.broadcasted_iota(jnp.int32, (1, GROUP * head_size), 1)
    return [
        jnp.where((lane >= h * head_size) & (lane < (h + 1) * head_size), 1.0, 0.0).astype(BF16)
        for h in range(GROUP)
    ]


def region_labels(flag_ref, late_ref, turned_ref, at_end):
    flags = [flag_ref[1 + n].astype(F32) for n in range(3)]
    flags[0] = flags[0] * at_end
    col = sum(flags[n] * late_ref[:, n : n + 1] for n in range(3))
    return col, sum(flags[n] * turned_ref[n : n + 1, :] for n in range(3))


def late_tokens():
    token = np.arange(TOKENS)
    late = np.zeros((TOKENS, 8), np.float32)
    late[:, 0] = 4 * (token // CELLS >= WIN_T - WIN_T // 2)
    late[:, 1] = 2 * (token // WIN_HW % WIN_HW >= WIN_HW - WIN_HW // 2)
    late[:, 2] = token % WIN_HW >= WIN_HW - WIN_HW // 2
    return late


def attend_kernel(
    shifted, head_size, flag_ref, q_ref, k_ref, v_ref, bias_ref, late_ref, turned_ref, out_ref, log_ref
):
    q, k = q_ref[0], k_ref[0]
    if shifted:
        at_end = jnp.where(pl.program_id(1) == pl.num_programs(1) - 1, 1.0, 0.0)
        col, row = region_labels(flag_ref, late_ref, turned_ref, at_end)
    turned = v_ref[0].astype(F32).T.astype(BF16)
    factor = head_size**-0.5 * LOG2E
    masks = head_masks(head_size)
    outs, logs = [], []
    for h in range(GROUP):
        scores = mm(k * masks[h], q, 1, 1) * factor + bias_ref[h]
        if shifted:
            scores = jnp.where(col == row, scores, masked_score)
        peak = jnp.max(scores, axis=0, keepdims=True)
        raised = jnp.exp2(scores - peak)
        total = jnp.sum(raised, axis=0, keepdims=True)
        mixed = mm(turned[h * head_size : (h + 1) * head_size], raised.astype(BF16))
        outs.append(mixed / total)
        logs.append(peak + jnp.log2(total))
    out_ref[0] = jnp.concatenate(outs, axis=0).T.astype(BF16)
    log_ref[0, 0] = jnp.concatenate(logs + logs, axis=0)


def run_attend(qkv, bias, flags, shifted, first, after=()):
    windows, _, width3 = qkv.shape
    width = width3 // 3
    wide = GROUP * (width // HEADS)
    groups, count = HEADS // GROUP, bias.shape[0] // GROUP
    qkv_specs = [
        pl.BlockSpec((1, TOKENS, wide), lambda g, w, p=part: (w, 0, p * groups + first + g))
        for part in range(3)
    ]
    return functools.partial(call, after=after)(
        functools.partial(attend_kernel, shifted, width // HEADS),
        (count, windows),
        [flag_spec()]
        + qkv_specs
        + [
            pl.BlockSpec((GROUP, TOKENS, TOKENS), lambda g, w: (g, 0, 0)),
            whole_block((TOKENS, 8)),
            whole_block((8, TOKENS)),
        ],
        [
            pl.BlockSpec((1, TOKENS, wide), lambda g, w: (w, 0, g)),
            pl.BlockSpec((1, 1, 2 * GROUP, TOKENS), lambda g, w: (w, g, 0, 0)),
        ],
        [
            jax.ShapeDtypeStruct((windows, TOKENS, count * wide), BF16),
            jax.ShapeDtypeStruct((windows, count, 2 * GROUP, TOKENS), F32),
        ],
        64 * windows * TOKENS * TOKENS * count * wide,
    )(flags, qkv, qkv, qkv, bias, late_tokens(), late_tokens().T)


def attend_back_kernel(
    shifted, head_size, flag_ref, q_ref, k_ref, v_ref, g_ref, o_ref, bias_ref, late_ref, turned_ref,
    log_ref, dq_ref, dk_ref, dv_ref, table_ref, sum_ref,
):
    windows = q_ref.shape[0]
    if shifted:
        labels = [
            region_labels(flag_ref, late_ref, turned_ref, float(w == windows - 1))
            for w in range(windows)
        ]
    scale = head_size**-0.5
    factor = scale * LOG2E
    masks = head_masks(head_size)

    @pl.when(pl.program_id(0) == 0)
    def _():
        sum_ref[...] = jnp.zeros_like(sum_ref)

    turned, weighed = [], []
    for w in range(windows):
        turned.append(k_ref[w].astype(F32).T.astype(BF16))
        weighed.append(g_ref[w].astype(F32).T * o_ref[w].astype(F32).T)
    grad_q = [[] for _ in range(windows)]
    grad_k, grad_v = [None] * windows, [None] * windows
    for h in range(GROUP):
        here = slice(h * head_size, (h + 1) * head_size)
        total = None
        for w in range(windows):
            q, k, v, g = q_ref[w], k_ref[w], v_ref[w], g_ref[w]
            inner = jnp.sum(weighed[w][here], axis=0, keepdims=True)
            scores = mm(k * masks[h], q, 1, 1) * factor + bias_ref[h]
            if shifted:
                scores = jnp.where(labels[w][0] == labels[w][1], scores, masked_score)
            probs = jnp.exp2(scores - log_ref[w, 0, h : h + 1])
            grad_probs = mm(v * masks[h], g, 1, 1)
            grad_scores = (probs * (grad_probs - inner)).astype(BF16)
            part_v = mm(probs.astype(BF16), g * masks[h])
            part_k = mm(grad_scores, q * masks[h])
            grad_v[w] = part_v if grad_v[w] is None else grad_v[w] + part_v
            grad_k[w] = part_k if grad_k[w] is None else grad_k[w] + part_k
            grad_q[w].append(mm(turned[w][here], grad_scores))
            wide = grad_scores.astype(F32)
            total = wide if total is None else total + wide
        sum_ref[:, :TOKENS] = total
        sums = None
        for key_frame in range(WIN_T):
            rows = sum_ref[key_frame * CELLS : (key_frame + 1) * CELLS, :]
            step = (WIN_T - 1 - key_frame) * CELLS
            rows = pltpu.roll(rows, step, 1) if step else rows
            sums = rows if sums is None else sums + rows
        table_ref[h] = sums
    for w in range(windows):
        dq_ref[w] = (jnp.concatenate(grad_q[w], axis=0) * scale).T.astype(BF16)
        dk_ref[w] = (grad_k[w] * scale).astype(BF16)
        dv_ref[w] = grad_v[w].astype(BF16)


def run_attend_back(qkv, grad, attended, bias, flags, log, shifted, first, after=()):
    windows, _, width3 = qkv.shape
    width = width3 // 3
    wide = GROUP * (width // HEADS)
    groups, count = HEADS // GROUP, bias.shape[0] // GROUP
    qkv_specs = [
        pl.BlockSpec((windows, TOKENS, wide), lambda g, p=part: (0, 0, p * groups + first + g))
        for part in range(3)
    ]
    flat = pl.BlockSpec((windows, TOKENS, wide), lambda g: (0, 0, g))
    flat_shape = jax.ShapeDtypeStruct((windows, TOKENS, count * wide), BF16)
    return functools.partial(call, after=after)(
        functools.partial(attend_back_kernel, shifted, width // HEADS),
        (count,),
        [flag_spec()]
        + qkv_specs
        + [
            pl.BlockSpec((windows, TOKENS, wide), lambda g: (0, 0, first + g)),
            flat,
            pl.BlockSpec((GROUP, TOKENS, TOKENS), lambda g: (g, 0, 0)),
            whole_block((TOKENS, 8)),
            whole_block((8, TOKENS)),
            pl.BlockSpec((windows, 1, 2 * GROUP, TOKENS), lambda g: (0, g, 0, 0)),
        ],
        [flat, flat, flat, pl.BlockSpec((GROUP, CELLS, WIDE), lambda g: (g, 0, 0))],
        [flat_shape] * 3 + [jax.ShapeDtypeStruct((count * GROUP, CELLS, WIDE), F32)],
        160 * windows * TOKENS * TOKENS * count * wide,
        [pltpu.VMEM((TOKENS, WIDE), F32)],
    )(flags, qkv, qkv, qkv, grad, attended, bias, late_tokens(), late_tokens().T, log)


def normal_below(x):
    bell = jnp.exp2(x * x * (-0.5 * LOG2E)) * (1.0 / math.sqrt(2 * math.pi))
    return 0.5 + 0.5 * lax.erf(x * math.sqrt(0.5)), bell


def spread_down(down_ref, w2_ref):
    _, parts, own, width = w2_ref.shape
    for part in range(parts):
        cols = slice(part * width, (part + 1) * width)
        w2_ref[:, part] = down_ref[:, cols].reshape(-1, own, width)


def chunk_rows(w2_ref, first, chunk):
    _, parts, own, width = w2_ref.shape
    step = chunk // (parts * own)
    return w2_ref[first * step : (first + 1) * step].reshape(chunk, width)


def branch_kernel(count, *refs):
    att_refs = refs[:count]
    x_ref, vec_ref, wo_ref, w1_ref, down_ref, mid_ref, hid_ref, slope_ref, out_ref, w2_ref = refs[count:]

    @pl.when(pl.program_id(0) == 0)
    def _():
        spread_down(down_ref, w2_ref)

    chunk = 512
    attended = jnp.concatenate([ref[0] for ref in att_refs], axis=1)
    middle = x_ref[0].astype(F32) + mm(attended, wo_ref[...]) + vec_ref[4:5]
    mid_ref[0] = middle
    unit, _ = unit_rows(middle)
    normed = (unit * vec_ref[5:6] + vec_ref[6:7]).astype(BF16)
    after = middle + vec_ref[7:8]
    for n in range(w1_ref.shape[1] // chunk):
        cols = slice(n * chunk, (n + 1) * chunk)
        pre = mm(normed, w1_ref[:, cols]) + vec_ref[8 + n : 9 + n]
        below, bell = normal_below(pre)
        hidden = (pre * below).astype(BF16)
        hid_ref[0, :, cols] = hidden
        slope_ref[0, :, cols] = (below + pre * bell).astype(BF16)
        after = after + mm(hidden, chunk_rows(w2_ref, n, chunk))
    out_ref[0] = after.astype(out_ref.dtype)


def weight_block(rows, width, column):
    return pl.BlockSpec((rows, width), lambda *ids: (0, column))


def branch_weights(weights, width, wide):
    (wo, wo_at), (w1, w1_at), (down, down_at) = weights
    specs = [
        weight_block(width, width, wo_at),
        weight_block(width, wide, w1_at),
        weight_block(width, wide, down_at),
    ]
    return (wo, w1, down), specs


def run_branch(x, attended, vec, weights, out_dtype, after=()):
    windows, _, width = x.shape
    wide = 4 * width
    arrays, specs = branch_weights(weights, width, wide)
    return functools.partial(call, after=after)(
        functools.partial(branch_kernel, len(attended)),
        (windows,),
        [win_block(part.shape[-1]) for part in attended]
        + [win_block(width), whole_block(vec.shape)]
        + specs,
        [win_block(width), win_block(wide), win_block(wide), win_block(width)],
        [
            jax.ShapeDtypeStruct((windows, TOKENS, width), F32),
            jax.ShapeDtypeStruct((windows, TOKENS, wide), BF16),
            jax.ShapeDtypeStruct((windows, TOKENS, wide), BF16),
            jax.ShapeDtypeStruct((windows, TOKENS, width), out_dtype),
        ],
        2 * windows * TOKENS * width * (width + 2 * wide),
        [pltpu.VMEM((width // 16, wide // width, 16, width), BF16)],
    )(*attended, x, vec, *arrays)


def add_rows(ref, rows, value):
    ref[rows, :] += jnp.sum(value.astype(F32), axis=0, keepdims=True)


def split_out(sums_ref, core, own_ref, sent_ref):
    own_ref[...] = sums_ref[:, core]
    sent_ref[...] = sums_ref[:, 1 - core].astype(BF16)


def branch_back_kernel(count, split, flag_ref, *refs):
    att_refs = refs[:count]
    grad_ref, mid_ref, hid_ref, slope_ref, vec_ref, wo_ref, w1_ref, down_ref = refs[count : count + 8]
    gm_ref, ga_ref, vecs_ref = refs[count + 8 : count + 11]
    outs, (d1_ref, d2_ref, w2_ref) = refs[count + 11 : -3], refs[-3:]
    chunk = 512
    width, wide = w1_ref.shape

    @pl.when(pl.program_id(0) == 0)
    def _():
        spread_down(down_ref, w2_ref)
        d1_ref[...] = jnp.zeros_like(d1_ref)
        d2_ref[...] = jnp.zeros_like(d2_ref)
        vecs_ref[...] = jnp.zeros_like(vecs_ref)

    grad = grad_ref[0].astype(F32)
    branch = grad.astype(BF16)
    unit, inverse = unit_rows(mid_ref[0])
    normed = (unit * vec_ref[5:6] + vec_ref[6:7]).astype(BF16)
    add_rows(vecs_ref, slice(7, 8), branch)
    back = None
    blocks = chunk // d2_ref.shape[2]
    for n in range(wide // chunk):
        cols = slice(n * chunk, (n + 1) * chunk)
        total = mm(hid_ref[0, :, cols], branch, 0, 0)
        at = slice(n * blocks // 2, (n + 1) * blocks // 2)
        d2_ref[at] += total.reshape((-1,) + d2_ref.shape[1:])
        grad_pre = mm(branch, chunk_rows(w2_ref, n, chunk), 1, 1) * slope_ref[0, :, cols].astype(F32)
        grad_pre = grad_pre.astype(BF16)
        add_rows(vecs_ref, slice(8 + n, 9 + n), grad_pre)
        d1_ref[:, :, :, cols] += mm(normed, grad_pre, 0, 0).reshape(d1_ref.shape[:3] + (chunk,))
        part = mm(grad_pre, w1_ref[:, cols], 1, 1)
        back = part if back is None else back + part
    add_rows(vecs_ref, slice(5, 6), back * unit)
    add_rows(vecs_ref, slice(6, 7), back)
    middle_grad = grad + norm_back(back, unit, inverse, vec_ref[5:6])
    gm_ref[0] = middle_grad
    branch = middle_grad.astype(BF16)
    add_rows(vecs_ref, slice(4, 5), branch)
    attended = jnp.concatenate([ref[0] for ref in att_refs], axis=1)
    total = mm(attended, branch, 0, 0)
    d1_ref[:, :, :, wide:] += total.reshape(d1_ref.shape[:3] + (width,))
    ga_ref[0] = mm(branch, wo_ref[...], 1, 1).astype(BF16)

    @pl.when(pl.program_id(0) == pl.num_programs(0) - 1)
    def _():
        if split:
            split_out(d1_ref, flag_ref[0], *outs[:2])
            split_out(d2_ref, flag_ref[0], *outs[2:])
        else:
            (out_ref,) = outs
            out_ref[:, : wide + width] = d1_ref[...].reshape(width, -1).astype(BF16)
            parts = wide // width
            for part in range(parts):
                first = wide + width + part * width
                piece = d2_ref[:, :, part * 16 : (part + 1) * 16, :].reshape(width, width)
                out_ref[:, first : first + width] = piece.astype(BF16)


def run_branch_back(grad, middle, attended, hidden, slope, vec, weights, flags, split, after=()):
    windows, _, width = middle.shape
    wide = 4 * width
    arrays, specs = branch_weights(weights, width, wide)
    flat = win_block(width)
    pairs = width // 32
    if split:
        shapes = []
        for rows, cols in ((16, wide + width), (64, width)):
            shapes.append(jax.ShapeDtypeStruct((pairs, rows, cols), F32))
            shapes.append(jax.ShapeDtypeStruct((pairs, rows, cols), BF16))
    else:
        shapes = [jax.ShapeDtypeStruct((width, 2 * wide + width), BF16)]
    return functools.partial(call, after=after)(
        functools.partial(branch_back_kernel, len(attended), split),
        (windows,),
        [flag_spec()]
        + [win_block(part.shape[-1]) for part in attended]
        + [flat, flat, win_block(wide), win_block(wide), whole_block(vec.shape)]
        + specs,
        [flat, flat, whole_block(vec.shape)] + [whole_block(s.shape) for s in shapes],
        [
            jax.ShapeDtypeStruct((windows, TOKENS, width), F32),
            jax.ShapeDtypeStruct((windows, TOKENS, width), BF16),
            jax.ShapeDtypeStruct(vec.shape, F32),
        ]
        + shapes,
        4 * windows * TOKENS * width * (width + 2 * wide),
        [
            pltpu.VMEM((pairs, 2, 16, wide + width), F32),
            pltpu.VMEM((pairs, 2, 64, width), F32),
            pltpu.VMEM((pairs * 2, wide // width, 16, width), BF16),
        ],
    )(flags, *attended, grad, middle, hidden, slope, vec, *arrays)


def qkv_back_kernel(count, flag_ref, *refs):
    grads, refs = refs[: 3 * count], refs[3 * count :]
    x_ref, gm_ref, vec_ref, wq_ref, wk_ref, wv_ref, rest_ref, mask_ref, pick_ref, spread_ref = refs[:10]
    out_ref, own_ref, sent_ref, dw_ref, vecs_ref = refs[10:]
    width = x_ref.shape[-1]

    @pl.when(pl.program_id(0) == 0)
    def _():
        dw_ref[...] = jnp.zeros_like(dw_ref)
        vecs_ref[...] = rest_ref[...]

    unit, inverse = unit_rows(x_ref[0].astype(F32))
    normed = (unit * vec_ref[0:1] + vec_ref[1:2]).astype(BF16)
    back = None
    for part, ref in enumerate((wq_ref, wk_ref, wv_ref)):
        grad = jnp.concatenate([g[0] for g in grads[part * count : (part + 1) * count]], axis=1)
        total = mm(normed, grad, 0, 0)
        cols = slice(part * width, (part + 1) * width)
        dw_ref[:, :, :, cols] += total.reshape(dw_ref.shape[:3] + (width,))
        here = mm(grad, ref[...], 1, 1)
        back = here if back is None else back + here
        if part == 0:
            add_rows(vecs_ref, slice(2, 3), grad)
        if part == 2:
            add_rows(vecs_ref, slice(3, 4), grad)
    add_rows(vecs_ref, slice(0, 1), back * unit)
    add_rows(vecs_ref, slice(1, 2), back)
    out_ref[0] = (gm_ref[0] + norm_back(back, unit, inverse, vec_ref[0:1])).astype(out_ref.dtype)

    @pl.when(pl.program_id(0) == pl.num_programs(0) - 1)
    def _():
        rows = vecs_ref[...]
        high = rows.astype(BF16)
        low = (rows - high.astype(F32)).astype(BF16)
        total = None
        for piece in (high, low):
            piece = (mm(pick_ref[...], piece, 0, 0) * mask_ref[...].astype(F32)).astype(BF16)
            piece = mm(piece, spread_ref[0], 1, 1)
            total = piece if total is None else total + piece
        dw_ref[:, :, :, 3 * width :] = total.reshape(dw_ref.shape[:3] + (128,))
        split_out(dw_ref, flag_ref[0], own_ref, sent_ref)


def run_qkv_back(grads, x, grad_middle, vec, w_qkv, rest, flags, out_dtype, after=()):
    windows, _, width = x.shape
    flat = win_block(width)
    weight, at = w_qkv
    extra = [jnp.asarray(a, BF16) for a in vector_slots()]
    shape = (width // 32, 16, 3 * width + 128)
    return functools.partial(call, after=after)(
        functools.partial(qkv_back_kernel, len(grads) // 3),
        (windows,),
        [flag_spec()]
        + [win_block(part.shape[-1]) for part in grads]
        + [flat, flat, whole_block(vec.shape)]
        + [weight_block(width, width, at + n) for n in range(3)]
        + [whole_block(rest.shape)]
        + [whole_block(a.shape) for a in extra],
        [flat, whole_block(shape), whole_block(shape)],
        [
            jax.ShapeDtypeStruct((windows, TOKENS, width), out_dtype),
            jax.ShapeDtypeStruct(shape, F32),
            jax.ShapeDtypeStruct(shape, BF16),
        ],
        4 * windows * TOKENS * width * 3 * width,
        [pltpu.VMEM((shape[0], 2) + shape[1:], F32), pltpu.VMEM(rest.shape, F32)],
    )(flags, *grads, x, grad_middle, vec, weight, weight, weight, rest, *extra)


def pack_shards_kernel(
    gain1_ref, bias1_ref, qkv_ref, qvb_ref, out_ref, outb_ref, gain2_ref, bias2_ref, fc1_ref, fc1b_ref,
    fc2_ref, fc2b_ref, first_ref, mid_ref, down_ref, later_ref, rows_ref,
):
    own, width = out_ref.shape[1:]
    wide = fc1_ref.shape[2]
    rows_ref[...] = jnp.zeros_like(rows_ref)
    row = 0
    lane = lax.broadcasted_iota(jnp.int32, (1, 128), 1)
    for ref in (gain1_ref, bias1_ref, qvb_ref, outb_ref, gain2_ref, bias2_ref, fc2b_ref, fc1b_ref):
        values = ref[...].astype(F32)
        values = jnp.pad(values, ((0, 0), (0, 128 - values.shape[1])))
        for part in range(ref.shape[1] // own):
            line = jnp.zeros((1, 128), F32)
            for layer in range(LAYERS):
                turn = ((layer - part) * own) % 128
                turned = pltpu.roll(values, turn, 1) if turn else values
                here = (lane >= layer * own) & (lane < (layer + 1) * own)
                line = jnp.where(here, turned[layer : layer + 1], line)
            rows_ref[row : row + 1, :] = line
            row += 1
    first_ref[:, : 3 * width] = qkv_ref[0]
    first_ref[:, 3 * width :] = rows_ref[...].astype(BF16)
    mid_ref[:, :wide] = fc1_ref[0]
    mid_ref[:, wide:] = out_ref[0]
    later_ref[:, :wide] = fc1_ref[1]
    later_ref[:, 2 * wide : 2 * wide + 3 * width] = qkv_ref[1]
    later_ref[:, 2 * wide + 3 * width :] = out_ref[1]
    for part in range(wide // width):
        cols = slice(part * width, (part + 1) * width)
        rows = slice(part * own, (part + 1) * own)
        down_ref[:, cols] = fc2_ref[0, rows, :]
        later_ref[:, wide + part * width : wide + (part + 1) * width] = fc2_ref[1, rows, :]


def pack_shards(*shards):
    own, width = shards[4].shape[1:]
    wide = shards[8].shape[2]
    widths = (3 * width + 128, wide + width, wide, 2 * wide + 4 * width)
    return call(
        pack_shards_kernel,
        (1,),
        [whole_block(s.shape) for s in shards],
        [whole_block((own, w)) for w in widths],
        [jax.ShapeDtypeStruct((own, w), BF16) for w in widths],
        1e6,
        [pltpu.VMEM((16, 128), F32)],
    )(*shards)


def vector_slots():
    devices, own = 32, 16
    count = devices * own
    mask = np.zeros((devices * 16, count), np.float32)
    pick = np.zeros((16, devices * 16), np.float32)
    spread = np.zeros((LAYERS, 128, count), np.float32)
    for device in range(devices):
        for first, parts in ((0, 1), (1, 1), (2, 2), (4, 1), (5, 1), (6, 1), (7, 1), (8, 4)):
            for part in range(parts):
                row, start = divmod(device * own * parts + part * own, count)
                slot = device * 16 + first + part
                pick[first + row, slot] = 1
                mask[slot, start : start + own] = 1
    for layer in range(LAYERS):
        for lane in range(count):
            spread[layer, layer * own + lane % own, lane] = 1
    return mask, pick, spread


def vectors_kernel(block_ref, mask_ref, pick_ref, spread_ref, out_ref):
    block = block_ref[...]
    for layer in range(LAYERS):
        lines = mm(block, spread_ref[layer]) * mask_ref[...].astype(F32)
        out_ref[layer] = mm(pick_ref[...], lines.astype(BF16))


def vectors_whole(blocks, after=()):
    count, width = blocks.shape
    extra = [jnp.asarray(a, BF16) for a in vector_slots()]
    return functools.partial(call, after=after)(
        vectors_kernel,
        (1,),
        [pl.BlockSpec((count, 128), lambda n: (0, width // 128 - 1))]
        + [whole_block(a.shape) for a in extra],
        whole_block((LAYERS, 16, count)),
        jax.ShapeDtypeStruct((LAYERS, 16, count), F32),
        1e9,
    )(blocks, *extra)


def place_flags():
    quadrant = lax.axis_index("space")
    last = lax.axis_index("tm") == lax.axis_size("tm") - 1
    flags = [lax.axis_index("clip") % 2, last, quadrant // 2, quadrant % 2]
    return jnp.stack([jnp.asarray(f, jnp.int32) for f in flags])


def local_windows(
    clips_in,
    ln1_gain,
    ln1_bias,
    qkv_weight,
    qv_bias,
    out_weight,
    out_bias,
    ln2_gain,
    ln2_bias,
    fc1_weight,
    fc1_bias,
    fc2_weight,
    fc2_bias,
    pos_table,
    out_grad,
):
    _, frames_here, _, _, width = clips_in.shape
    windows = frames_here // WIN_T
    own = ln1_gain.shape[1]
    heads_here = pos_table.shape[2]
    groups_here = heads_here // GROUP
    one, two = stage_orders()
    flat = (windows, TOKENS, width)
    flags = place_flags()
    send, place, stay, rows, starts, kinds = halo_matrices(frames_here)
    flow = Flow()

    def stepped(run, *args, names=(), **options):
        out = run(*args, after=flow.pending(), **options)
        flow.step(*names)
        return out

    def halo_start(name, packed, onward):
        flow.start(name, halo_flow(packed, rows, starts, kinds, onward))

    def send_table():
        (came,) = yield [(tables, "tm", swap_pairs("tm", 0))]
        first = lax.axis_index("tm") == 0
        return jnp.where(first, tables, came), jnp.where(first, came, tables)

    shards = (
        ln1_gain, ln1_bias, qkv_weight, qv_bias, out_weight, out_bias,
        ln2_gain, ln2_bias, fc1_weight, fc1_bias, fc2_weight, fc2_bias,
    )
    first, mid, down, later = pack_shards(*shards)
    later = lax.all_gather(later, ("tm", "space", "clip"), axis=0, tiled=True)
    tables = pos_table.transpose(0, 2, 1)
    flow.start("tables", send_table())
    flow.start("first", gather_flow(first, one))
    flow.step()
    tables = flow.finish("tables")
    flow.start("mid", gather_flow(mid, one))
    flow.start("down", gather_flow(down, two))
    bias0 = [stepped(table_to_bias, tables[n][0]) for n in range(2)]
    first = flow.finish("first")
    vec = stepped(vectors_whole, first)
    w_qkv = ((first, 0), (later, 8))

    stream0 = clips_in.reshape(flat)
    qkv0 = stepped(run_qkv, stream0, vec[0], w_qkv[0])
    att0, log0 = [None, None], [None, None]
    for n in range(2):
        att0[n], log0[n] = stepped(run_attend, qkv0, bias0[n], flags, False, n * groups_here)
    mid = flow.finish("mid")
    weights = (
        ((mid, 4), (mid, 0), (flow.finish("down"), 0)),
        ((later, 11), (later, 0), (later, 1)),
    )
    mid0, hid0, slope0, stream1 = stepped(run_branch, stream0, att0, vec[0], weights[0], F32)
    halo_start("roll", halo_pack(stream1, send, True), True)
    table1 = jnp.concatenate([tables[0][1], tables[1][1]], axis=0)
    bias1 = [stepped(table_to_bias, table1)]
    rolled1 = halo_unpack(stream1, flow.finish("roll"), stay, place, starts, F32, center=True)
    qkv1 = run_qkv(rolled1, vec[1], w_qkv[1])
    grad_in = out_grad.reshape(flat)
    halo_start("grad", halo_pack(grad_in, send, False, after=[qkv1]), True)
    att1, log1 = stepped(run_attend, qkv1, bias1[0], flags, True, 0)
    mid1, hid1, slope1, rolled_out = run_branch(rolled1, [att1], vec[1], weights[1], F32)
    halo_start("out", halo_pack(rolled_out, place.T, False), False)
    grad = halo_unpack(grad_in, flow.finish("grad"), stay, place, starts, BF16)

    kept = (
        (stream0, qkv0, att0, log0, mid0, hid0, slope0, bias0),
        (rolled1, qkv1, [att1], [log1], mid1, hid1, slope1, bias1),
    )
    rests, tables = [None] * LAYERS, [None] * LAYERS
    for layer in reversed(range(LAYERS)):
        stream, qkv, att, log, mid, hid, slope, bias = kept[layer]
        grad_mid, grad_att, rest, *halves = stepped(
            run_branch_back, grad, mid, att, hid, slope, vec[layer], weights[layer], flags, layer == 0
        )
        if layer == 0:
            flow.start("d_mid", scatter_flow(*halves[:2], one))
            flow.start("d_two", scatter_flow(*halves[2:], two))
        else:
            mid_share1 = lax.psum_scatter(
                halves[0], ("tm", "space", "clip"), scatter_dimension=0, tiled=True
            ).astype(F32)
            clips_out = stepped(
                halo_unpack, rolled_out, flow.finish("out"), stay.T, send.T, starts, BF16,
                mean_of=stream1,
            )
        grads, sums = [], []
        for n in range(len(att)):
            *parts, total = stepped(
                run_attend_back, qkv, grad_att, att[n], bias[n], flags, log[n],
                layer == 1, n * groups_here,
            )
            grads.append(parts)
            sums.append(total)
        grads = [part for group in zip(*grads) for part in group]
        grad_stream, *halves = stepped(
            run_qkv_back, grads, stream, grad_mid, vec[layer], w_qkv[layer], rest, flags,
            F32 if layer else BF16,
        )
        if layer:
            halo_start("back", halo_pack(grad_stream, place.T, False), False)
        flow.start(f"d_qkv{layer}", scatter_flow(*halves, one))
        found = [stepped(sums_to_table, total) for total in sums]
        tables[layer] = jnp.split(found[0], 2) if len(found) == 1 else found
        if layer:
            grad = halo_unpack(grad_stream, flow.finish("back"), stay.T, send.T, starts, F32)
    in_grad = grad_stream
    pairs = [jnp.stack([tables[layer][n] for layer in range(LAYERS)]) for n in range(2)]
    flow.start("table", table_flow(pairs, heads_here))

    while flow.live:
        flow.step()
    wide = fc1_weight.shape[2]
    mixes = jnp.stack([flow.done[f"d_qkv{layer}"] for layer in range(LAYERS)])
    mid_share0, two_share0 = flow.done["d_mid"], flow.done["d_two"]
    two_share1 = jnp.concatenate(
        [mid_share1[:, first : first + width] for first in range(wide + width, wide * 2 + width, width)],
        axis=0,
    )
    small = mixes[:, :, 3 * width : 3 * width + own]

    def vector(row, count=1):
        return small[:, row : row + count].reshape(LAYERS, count * own)

    return (
        clips_out.reshape(clips_in.shape),
        in_grad.reshape(clips_in.shape),
        vector(0),
        vector(1),
        mixes[:, :, : 3 * width],
        vector(2, 2),
        jnp.stack([s[:, wide : wide + width] for s in (mid_share0, mid_share1)]),
        vector(4),
        vector(5),
        vector(6),
        jnp.stack([s[:, :wide] for s in (mid_share0, mid_share1)]),
        vector(8, 4),
        jnp.stack([two_share0, two_share1]),
        vector(7),
        flow.done["table"].transpose(0, 2, 1),
    )


def windows_are_local(mesh):
    def decide(clips_in, *rest):
        clips, frames_here = clips_in.shape[:2]
        own = rest[0].shape[1]
        return (
            clips == 1
            and frames_here % WIN_T == 0
            and own == 16
            and mesh.shape["tm"] == 2
            and mesh.shape["space"] == 4
        )

    def program(*args):
        return local_windows(*args) if decide(*args) else per_device(*args)

    return program


def solution(mesh):
    placed = (
        P("clip", "tm", "space", None, None),
        P(None, ("tm", "space", "clip")),
        P(None, ("tm", "space", "clip")),
        P(None, ("tm", "space", "clip"), None),
        P(None, ("tm", "space", "clip")),
        P(None, ("tm", "space", "clip"), None),
        P(None, ("tm", "space", "clip")),
        P(None, ("tm", "space", "clip")),
        P(None, ("tm", "space", "clip")),
        P(None, ("tm", "space", "clip"), None),
        P(None, ("tm", "space", "clip")),
        P(None, ("tm", "space", "clip"), None),
        P(None, ("tm", "space", "clip")),
        P(None, None, "tm"),
        P("clip", "tm", "space", None, None),
    )
    return jax.shard_map(
        windows_are_local(mesh),
        mesh=mesh,
        in_specs=placed,
        out_specs=(
            P("clip", "tm", "space", None, None),
            P("clip", "tm", "space", None, None),
            P(None, ("tm", "space", "clip")),
            P(None, ("tm", "space", "clip")),
            P(None, ("tm", "space", "clip"), None),
            P(None, ("tm", "space", "clip")),
            P(None, ("tm", "space", "clip"), None),
            P(None, ("tm", "space", "clip")),
            P(None, ("tm", "space", "clip")),
            P(None, ("tm", "space", "clip")),
            P(None, ("tm", "space", "clip"), None),
            P(None, ("tm", "space", "clip")),
            P(None, ("tm", "space", "clip"), None),
            P(None, ("tm", "space", "clip")),
            P(None, None, "tm"),
        ),
        check_vma=False,
    )
```

```python
import functools
import math

import jax
import jax.numpy as jnp
import numpy as np
from jax import lax
from jax.experimental import pallas as pl
from jax.experimental.pallas import tpu as pltpu
from jax.sharding import PartitionSpec as P

HEADS = 16
WIN_T = 8
WIN_HW = 7
LAYERS = 2


masked_score = -1000000000.0
TM, SPACE, CLIP = "tm", "space", "clip"
ALL = (TM, SPACE, CLIP)


def partner(value, axis, bit):
    mask = 2**bit
    pairs = [(source, source ^ mask) for source in range(lax.axis_size(axis))]
    return lax.ppermute(value, axis, pairs)


def norm_rows(values, gain, offset):
    mean_row = jnp.mean(values, axis=-1, keepdims=True)
    centered = values - mean_row
    spread = jnp.mean(centered * centered, axis=-1, keepdims=True)
    return centered * lax.rsqrt(spread + 1e-05) * gain + offset


def gelu_exact(values):
    return jax.nn.gelu(values, approximate=False)


def project(left, right):
    return jnp.einsum("...i,ij->...j", left, right, preferred_element_type=jnp.float32)


def project_back(left, right):
    return jnp.einsum("...j,ij->...i", left, right, preferred_element_type=jnp.float32)


def outer_sum(left, right):
    flat_left = left.reshape(-1, left.shape[-1])
    flat_right = right.reshape(-1, right.shape[-1])
    return jnp.einsum("ti,tj->ij", flat_left, flat_right, preferred_element_type=jnp.float32)


def column_sum(values):
    return jnp.sum(values.reshape(-1, values.shape[-1]).astype(jnp.float32), axis=0)


def relative_index(win_t, win_hw):
    count = win_t * win_hw * win_hw
    positions = jnp.arange(count, dtype=jnp.int32)
    frame_pos = positions // (win_hw * win_hw)
    row_pos = positions // win_hw % win_hw
    col_pos = positions % win_hw
    span = 2 * win_hw - 1
    frame_off = frame_pos[:, None] - frame_pos[None, :] + win_t - 1
    row_off = row_pos[:, None] - row_pos[None, :] + win_hw - 1
    col_off = col_pos[:, None] - col_pos[None, :] + win_hw - 1
    return frame_off * span * span + row_off * span + col_off


def band_label(coord, extent, window, reach):
    return jnp.where(coord < extent - window, 0, jnp.where(coord < extent - reach, 1, 2)).astype(
        jnp.int32
    )


def region_match(frames):
    quadrant = lax.axis_index(SPACE)
    row_quad = quadrant // 2
    col_quad = quadrant % 2
    local = jnp.arange(WIN_HW, dtype=jnp.int32)
    label_t = band_label(jnp.arange(frames, dtype=jnp.int32), frames, WIN_T, WIN_T // 2)
    label_r = band_label(row_quad * WIN_HW + local, 2 * WIN_HW, WIN_HW, WIN_HW // 2)
    label_c = band_label(col_quad * WIN_HW + local, 2 * WIN_HW, WIN_HW, WIN_HW // 2)
    region = label_t[:, None, None] * 9 + label_r[None, :, None] * 3 + label_c[None, None, :]
    region = region.reshape(frames // WIN_T, WIN_T * WIN_HW * WIN_HW)
    return region[:, :, None] == region[:, None, :]


def space_roll(field, onward):
    side = field.shape[2]
    reach = side // 2
    sent_rows = field[:, :, :reach] if onward else field[:, :, side - reach :]
    came_rows = partner(sent_rows, SPACE, 1)
    if onward:
        rows_done = jnp.concatenate([field, came_rows], axis=2)[:, :, reach : reach + side]
    else:
        rows_done = jnp.concatenate([came_rows, field], axis=2)[:, :, :side]
    sent_cols = rows_done[:, :, :, :reach] if onward else rows_done[:, :, :, side - reach :]
    came_cols = partner(sent_cols, SPACE, 0)
    if onward:
        return jnp.concatenate([rows_done, came_cols], axis=3)[:, :, :, reach : reach + side]
    return jnp.concatenate([came_cols, rows_done], axis=3)[:, :, :, :side]


def gather_layer(shards, layer):
    return tuple(lax.all_gather(w[layer], ALL, axis=0, tiled=True) for w in shards)


def table_bias(table):
    rel = relative_index(WIN_T, WIN_HW)
    return table.astype(jnp.float32)[rel].transpose(2, 0, 1)


def window_scores(queries, keys, bias, same, scale):
    scores = (
        jnp.einsum("wqhd,wkhd->whqk", queries, keys, preferred_element_type=jnp.float32) * scale
        + bias[None]
    )
    if same is not None:
        scores = jnp.where(same[:, None], scores, masked_score)
    return scores


def to_windows(field):
    clips, frames, cells, heads_here, head_size = field.shape
    return field.reshape(clips, frames // WIN_T, WIN_T * cells, heads_here, head_size)


def to_frames(field, frames):
    clips = field.shape[0]
    return field.reshape(clips, frames, WIN_HW * WIN_HW, field.shape[3], field.shape[4])


def layer_forward(stream, params, table, shifted):
    (
        gain_one,
        bias_one,
        mix_weight,
        mix_bias,
        proj_weight,
        proj_bias,
        gain_two,
        bias_two,
        wide_weight,
        wide_bias,
        narrow_weight,
        narrow_bias,
    ) = params
    clips, frames_here, side = (stream.shape[0], stream.shape[1], stream.shape[2])
    width = stream.shape[-1]
    head_size = width // HEADS
    scale = head_size ** (-0.5)
    normed = norm_rows(stream, gain_one.astype(jnp.float32), bias_one.astype(jnp.float32)).astype(
        jnp.bfloat16
    )
    if shifted:
        normed = space_roll(normed, True)
    mixed = project(normed, mix_weight)
    mix_bias32 = mix_bias.astype(jnp.float32)
    head_shape = (clips, frames_here, side * side, HEADS, head_size)
    queries = (mixed[..., :width] + mix_bias32[:width]).astype(jnp.bfloat16).reshape(head_shape)
    keys = mixed[..., width : 2 * width].astype(jnp.bfloat16).reshape(head_shape)
    values = (mixed[..., 2 * width :] + mix_bias32[width:]).astype(jnp.bfloat16).reshape(head_shape)
    queries, keys, values = (
        lax.all_to_all(queries, TM, split_axis=3, concat_axis=1, tiled=True),
        lax.all_to_all(keys, TM, split_axis=3, concat_axis=1, tiled=True),
        lax.all_to_all(values, TM, split_axis=3, concat_axis=1, tiled=True),
    )
    frames = queries.shape[1]
    if shifted:
        queries = jnp.roll(queries, -(WIN_T // 2), axis=1)
        keys = jnp.roll(keys, -(WIN_T // 2), axis=1)
        values = jnp.roll(values, -(WIN_T // 2), axis=1)
    queries, keys, values = (to_windows(queries), to_windows(keys), to_windows(values))
    bias = table_bias(table)
    same = region_match(frames) if shifted else None

    def attend_clip(items):
        clip_queries, clip_keys, clip_values = items
        scores = window_scores(clip_queries, clip_keys, bias, same, scale)
        peak = jnp.max(scores, axis=-1, keepdims=True)
        raised = jnp.exp(scores - peak)
        total = jnp.sum(raised, axis=-1, keepdims=True)
        probs = (raised / total).astype(jnp.bfloat16)
        out_win = jnp.einsum(
            "whqk,wkhd->wqhd", probs, clip_values, preferred_element_type=jnp.float32
        ).astype(jnp.bfloat16)
        return (out_win, peak + jnp.log(total))

    attended_heads, log_total = lax.map(attend_clip, (queries, keys, values))
    attended_heads = to_frames(attended_heads, frames)
    if shifted:
        attended_heads = jnp.roll(attended_heads, WIN_T // 2, axis=1)
    attended = lax.all_to_all(attended_heads, TM, split_axis=1, concat_axis=3, tiled=True)
    attended = attended.reshape(clips, frames_here, side, side, width)
    if shifted:
        attended = space_roll(attended, False)
    middle = stream + project(attended, proj_weight) + proj_bias.astype(jnp.float32)
    normed_two = norm_rows(
        middle, gain_two.astype(jnp.float32), bias_two.astype(jnp.float32)
    ).astype(jnp.bfloat16)
    hidden_pre = project(normed_two, wide_weight) + wide_bias.astype(jnp.float32)
    hidden = gelu_exact(hidden_pre).astype(jnp.bfloat16)
    after = middle + project(hidden, narrow_weight) + narrow_bias.astype(jnp.float32)
    stash = (
        stream,
        normed,
        queries,
        keys,
        values,
        log_total,
        attended,
        middle,
        normed_two,
        hidden_pre,
        hidden,
    )
    return (stash, after)


def layer_backward(grad_after, params, table, stash, shifted):
    (
        gain_one,
        bias_one,
        mix_weight,
        mix_bias,
        proj_weight,
        proj_bias,
        gain_two,
        bias_two,
        wide_weight,
        wide_bias,
        narrow_weight,
        narrow_bias,
    ) = params
    (
        stream,
        normed,
        queries,
        keys,
        values,
        log_total,
        attended,
        middle,
        normed_two,
        hidden_pre,
        hidden,
    ) = stash
    clips, frames_here, side = (stream.shape[0], stream.shape[1], stream.shape[2])
    width = stream.shape[-1]
    head_size = width // HEADS
    scale = head_size ** (-0.5)
    frames = queries.shape[1] * WIN_T
    grad_branch_two = grad_after.astype(jnp.bfloat16)
    narrow_grad = outer_sum(hidden, grad_branch_two)
    narrow_bias_grad = column_sum(grad_branch_two)
    grad_hidden = project_back(grad_branch_two, narrow_weight)
    gelu_pull = jax.vjp(gelu_exact, hidden_pre)[1]
    grad_pre = gelu_pull(grad_hidden)[0].astype(jnp.bfloat16)
    wide_grad = outer_sum(normed_two, grad_pre)
    wide_bias_grad = column_sum(grad_pre)
    grad_normed_two = project_back(grad_pre, wide_weight)
    norm_pull_two = jax.vjp(
        norm_rows, middle, gain_two.astype(jnp.float32), bias_two.astype(jnp.float32)
    )[1]
    grad_mid_part, gain_two_grad, bias_two_grad = norm_pull_two(grad_normed_two)
    grad_middle = grad_after + grad_mid_part
    grad_branch_one = grad_middle.astype(jnp.bfloat16)
    proj_grad = outer_sum(attended, grad_branch_one)
    proj_bias_grad = column_sum(grad_branch_one)
    grad_attended = project_back(grad_branch_one, proj_weight).astype(jnp.bfloat16)
    if shifted:
        grad_attended = space_roll(grad_attended, True)
    grad_attended = grad_attended.reshape(clips, frames_here, side * side, HEADS, head_size)
    grad_attended = lax.all_to_all(grad_attended, TM, split_axis=3, concat_axis=1, tiled=True)
    if shifted:
        grad_attended = jnp.roll(grad_attended, -(WIN_T // 2), axis=1)
    grad_attended = to_windows(grad_attended)
    bias = table_bias(table)
    same = region_match(frames) if shifted else None

    def attend_back(carry, items):
        clip_queries, clip_keys, clip_values, clip_grad, clip_log = items
        scores = window_scores(clip_queries, clip_keys, bias, same, scale)
        probs = jnp.exp(scores - clip_log)
        grad_probs = jnp.einsum(
            "wqhd,wkhd->whqk", clip_grad, clip_values, preferred_element_type=jnp.float32
        )
        inner = jnp.sum(probs * grad_probs, axis=-1, keepdims=True)
        grad_scores = (probs * (grad_probs - inner)).astype(jnp.bfloat16)
        grad_q = (
            jnp.einsum(
                "whqk,wkhd->wqhd", grad_scores, clip_keys, preferred_element_type=jnp.float32
            )
            * scale
        ).astype(jnp.bfloat16)
        grad_k = (
            jnp.einsum(
                "whqk,wqhd->wkhd", grad_scores, clip_queries, preferred_element_type=jnp.float32
            )
            * scale
        ).astype(jnp.bfloat16)
        grad_v = jnp.einsum(
            "whqk,wqhd->wkhd",
            probs.astype(jnp.bfloat16),
            clip_grad,
            preferred_element_type=jnp.float32,
        ).astype(jnp.bfloat16)
        carry = carry + jnp.sum(grad_scores.astype(jnp.float32), axis=0)
        return (carry, (grad_q, grad_k, grad_v))

    window_tokens = queries.shape[2]
    start_bias = jnp.zeros((queries.shape[3], window_tokens, window_tokens), jnp.float32)
    bias_grad, grads_win = lax.scan(
        attend_back, start_bias, (queries, keys, values, grad_attended, log_total)
    )
    grad_q, grad_k, grad_v = (to_frames(g, frames) for g in grads_win)
    if shifted:
        grad_q = jnp.roll(grad_q, WIN_T // 2, axis=1)
        grad_k = jnp.roll(grad_k, WIN_T // 2, axis=1)
        grad_v = jnp.roll(grad_v, WIN_T // 2, axis=1)
    grad_q, grad_k, grad_v = (
        lax.all_to_all(grad_q, TM, split_axis=1, concat_axis=3, tiled=True),
        lax.all_to_all(grad_k, TM, split_axis=1, concat_axis=3, tiled=True),
        lax.all_to_all(grad_v, TM, split_axis=1, concat_axis=3, tiled=True),
    )
    token_shape = (clips, frames_here, side, side, width)
    grad_q, grad_k, grad_v = (
        grad_q.reshape(token_shape),
        grad_k.reshape(token_shape),
        grad_v.reshape(token_shape),
    )
    grad_mix = jnp.concatenate([grad_q, grad_k, grad_v], axis=-1)
    mix_grad = outer_sum(normed, grad_mix)
    mix_bias_grad = jnp.concatenate([column_sum(grad_q), column_sum(grad_v)])
    grad_normed = project_back(grad_mix, mix_weight)
    if shifted:
        grad_normed = space_roll(grad_normed.astype(jnp.bfloat16), False).astype(jnp.float32)
    norm_pull_one = jax.vjp(
        norm_rows, stream, gain_one.astype(jnp.float32), bias_one.astype(jnp.float32)
    )[1]
    grad_stream_part, gain_one_grad, bias_one_grad = norm_pull_one(grad_normed)
    grad_stream = grad_middle + grad_stream_part
    rel = relative_index(WIN_T, WIN_HW).reshape(-1)
    table_grad = (
        jnp.zeros(table.shape, jnp.float32).at[rel].add(bias_grad.reshape(bias_grad.shape[0], -1).T)
    )
    weight_grads = (
        gain_one_grad,
        bias_one_grad,
        mix_grad,
        mix_bias_grad,
        proj_grad,
        proj_bias_grad,
        gain_two_grad,
        bias_two_grad,
        wide_grad,
        wide_bias_grad,
        narrow_grad,
        narrow_bias_grad,
    )
    return (grad_stream, weight_grads, table_grad)


def per_device(
    clips_in,
    ln1_gain,
    ln1_bias,
    qkv_weight,
    qv_bias,
    out_weight,
    out_bias,
    ln2_gain,
    ln2_bias,
    fc1_weight,
    fc1_bias,
    fc2_weight,
    fc2_bias,
    pos_table,
    out_grad,
):
    clips, frames_here, quads, cells, width = clips_in.shape
    grid_shape = (clips, frames_here, WIN_HW, WIN_HW, width)
    shards = (
        ln1_gain,
        ln1_bias,
        qkv_weight,
        qv_bias,
        out_weight,
        out_bias,
        ln2_gain,
        ln2_bias,
        fc1_weight,
        fc1_bias,
        fc2_weight,
        fc2_bias,
    )
    stream = clips_in.astype(jnp.float32).reshape(grid_shape)
    kept_params = []
    kept_stash = []
    for layer in range(LAYERS):
        params = gather_layer(shards, layer)
        stash, stream = layer_forward(stream, params, pos_table[layer], layer % 2 == 1)
        kept_params.append(params)
        kept_stash.append(stash)
    clips_out = stream.astype(jnp.bfloat16).reshape(clips_in.shape)
    grad_stream = out_grad.astype(jnp.float32).reshape(grid_shape)
    layer_shares = [None] * LAYERS
    table_parts = [None] * LAYERS
    for layer in reversed(range(LAYERS)):
        params = gather_layer(shards, layer)
        grad_stream, weight_grads, table_grad = layer_backward(
            grad_stream, params, pos_table[layer], kept_stash[layer], layer % 2 == 1
        )
        layer_shares[layer] = tuple(
            lax.psum_scatter(g, ALL, scatter_dimension=0, tiled=True) for g in weight_grads
        )
        table_parts[layer] = table_grad
    in_grad = grad_stream.astype(jnp.bfloat16).reshape(clips_in.shape)
    table_total = lax.psum(jnp.stack(table_parts), (SPACE, CLIP))
    stacked = tuple(
        (jnp.stack([layer_shares[n][slot] for n in range(LAYERS)]) for slot in range(12))
    )
    return (
        clips_out,
        in_grad,
        stacked[0],
        stacked[1],
        stacked[2],
        stacked[3],
        stacked[4],
        stacked[5],
        stacked[6],
        stacked[7],
        stacked[8],
        stacked[9],
        stacked[10],
        stacked[11],
        table_total,
    )


F32 = jnp.float32
BF16 = jnp.bfloat16
TOKENS = WIN_T * WIN_HW * WIN_HW
CELLS = WIN_HW * WIN_HW
SPAN = 2 * WIN_HW - 1
STEPS = 2 * WIN_T - 1
LOG2E = math.log2(math.e)
VMEM_BYTES = 56 * 1024 * 1024


def mm(left, right, left_dim=1, right_dim=0):
    dims = (((left_dim,), (right_dim,)), ((), ()))
    return lax.dot_general(left, right, dims, preferred_element_type=F32)


class Order:
    def __init__(self, waits=()):
        self.waits = list(waits)
        self.token = None


def call(kernel, grid, in_specs, out_specs, out_shape, flops, scratch=(), after=None):
    waits = after.waits if after else []
    inputs = len(in_specs)
    single = not isinstance(out_shape, list)
    out_specs = [out_specs] if single else list(out_specs)
    out_shape = [out_shape] if single else list(out_shape)
    outputs = len(out_shape)
    if after:
        out_specs.append(pl.BlockSpec(memory_space=pltpu.SMEM))
        out_shape.append(jax.ShapeDtypeStruct((1, 1), F32))

    def body(*refs):
        ins, outs = refs[:inputs], refs[inputs + len(waits) :]
        if after:
            outs[outputs][0, 0] = 0.0
        kernel(*ins, *outs[:outputs], *outs[len(out_shape) :])

    run = pl.pallas_call(
        body,
        grid=grid,
        in_specs=list(in_specs) + [pl.BlockSpec(memory_space=pl.ANY)] * len(waits),
        out_specs=out_specs,
        out_shape=out_shape,
        scratch_shapes=scratch,
        cost_estimate=pl.CostEstimate(
            flops=int(flops), transcendentals=0, bytes_accessed=8 * 1024 * 1024
        ),
        compiler_params=pltpu.CompilerParams(vmem_limit_bytes=VMEM_BYTES),
    )

    def result(*args):
        found = run(*args, *waits)
        if after:
            after.token = found[outputs]
        return found[0] if single else found[:outputs]

    return result


def whole_block(shape):
    return pl.BlockSpec(shape, lambda *ids: (0,) * len(shape))


def flag_spec():
    return pl.BlockSpec(memory_space=pltpu.SMEM)


def win_block(width, column=0):
    return pl.BlockSpec((1, TOKENS, width), lambda w: (w, 0, column))


HALF = WIN_T // 2 * CELLS
KINDS = range(1, 8)


class Halo:
    def __init__(self):
        token = np.arange(HALF)
        row, col = token // WIN_HW % WIN_HW, token % WIN_HW
        reach = WIN_HW // 2
        target = token - row * WIN_HW - col
        target = target + (row - reach) % WIN_HW * WIN_HW + (col - reach) % WIN_HW
        leaves = (row < reach) * 2 + (col < reach) * 1
        self.stay = np.zeros((HALF, HALF), np.float32)
        stays = leaves == 0
        self.stay[target[stays], token[stays]] = 1
        self.near, self.near_to = self.ways(leaves, target, (1, 2, 3))
        self.far, self.far_to = self.ways(leaves, target, (0, 1, 2, 3))

    @staticmethod
    def ways(leaves, target, kinds):
        send, place = [], []
        for kind in kinds:
            source = np.nonzero(leaves == kind)[0]
            rows = 64 if kind == 0 else 48
            out, back = np.zeros((rows, HALF), np.float32), np.zeros((HALF, rows), np.float32)
            out[np.arange(len(source)), source] = 1
            back[target[source], np.arange(len(source))] = 1
            send.append(out)
            place.append(back)
        return np.concatenate(send, 0), np.concatenate(place, 1)

    def sends(self, onward):
        return (self.near, self.far) if onward else (self.near_to.T, self.far_to.T)

    def places(self, onward):
        if onward:
            return self.stay, self.near_to, self.far_to
        return self.stay.T, self.near.T, self.far.T


def half_at(half):
    return half // 2, slice(half % 2 * HALF, (half % 2 + 1) * HALF)


class Flow:
    def __init__(self):
        self.live = []
        self.done = {}

    def start(self, name, task):
        self.live.append((name, task, next(task)))

    def pending(self):
        return [value for _, _, sends in self.live for value, _, _ in sends]

    def step(self, token, names=None):
        live = []
        for name, task, sends in self.live:
            if names is not None and name not in names:
                live.append((name, task, sends))
                continue
            came = [lax.ppermute(value, axis, pairs) for value, axis, pairs in sends]
            try:
                live.append((name, task, task.send((came, token))))
            except StopIteration as end:
                self.done[name] = end.value
        self.live = live

    def finish(self, name):
        while name not in self.done:
            self.step(None, (name,))
        return self.done[name]


def swap_pairs(axis, bit):
    return [(source, source ^ 2**bit) for source in range(lax.axis_size(axis))]


def halo_flow(packed, onward):
    ring, quads = lax.axis_size(TM), lax.axis_size(SPACE)
    sends = []
    for kind, piece in zip(KINDS, packed):
        step = 0 if not kind & 4 else (-1 if onward else 1)
        pairs = []
        for frame_at in range(ring):
            for quad in range(quads):
                to = (frame_at + step) % ring * quads + (quad ^ (kind & 3))
                pairs.append((frame_at * quads + quad, to))
        sends.append((piece, (TM, SPACE), pairs))
    came, _ = yield sends
    return came


def pack_kernel(center, onward, near_ref, far_ref, x_ref, *refs):
    out_refs, flat_ref = refs[:-1], refs[-1]
    halves = 2 * x_ref.shape[0]
    for w in range(x_ref.shape[0]):
        x = x_ref[w].astype(F32)
        if center:
            x = x - jnp.mean(x, axis=-1, keepdims=True)
        flat_ref[w] = x
    for n in range(halves - 1):
        w, rows = half_at(n + 1 if onward else n)
        sent = mm(near_ref[...], flat_ref[w, rows].astype(BF16)).astype(BF16)
        for kind in range(3):
            out_refs[kind][n * 48 : (n + 1) * 48] = sent[kind * 48 : (kind + 1) * 48]
    w, rows = half_at(0 if onward else halves - 1)
    sent = mm(far_ref[...], flat_ref[w, rows].astype(BF16)).astype(BF16)
    for kind in range(4):
        first = 0 if kind == 0 else 16 + 48 * kind
        out_refs[3 + kind][...] = sent[first : first + out_refs[3 + kind].shape[0]]


def halo_pack(x, halo, onward, center=False, after=None):
    windows, _, width = x.shape
    near, far = (jnp.asarray(m, BF16) for m in halo.sends(onward))
    rows = [48 * (2 * windows - 1)] * 3 + [64, 48, 48, 48]
    return functools.partial(call, after=after)(
        functools.partial(pack_kernel, center, onward),
        (1,),
        [whole_block(m.shape) for m in (near, far, x)],
        [whole_block((n, width)) for n in rows],
        [jax.ShapeDtypeStruct((n, width), BF16) for n in rows],
        2 * 640 * HALF * width,
        [pltpu.VMEM(x.shape, F32)],
    )(near, far, x)


def unpack_kernel(center, onward, add_mean, stay_ref, near_ref, far_ref, x_ref, *refs):
    base_ref, refs = (refs[0], refs[1:]) if add_mean else (None, refs)
    came_refs, (out_ref, flat_ref, total_ref) = refs[:7], refs[7:]
    windows = x_ref.shape[0]
    halves = 2 * windows
    for w in range(windows):
        x = x_ref[w].astype(F32)
        if center:
            x = x - jnp.mean(x, axis=-1, keepdims=True)
        flat_ref[w] = x
    for n in range(halves - 1):
        w, rows = half_at(n + 1 if onward else n)
        x = flat_ref[w, rows]
        high = x.astype(BF16)
        total = mm(stay_ref[...], high)
        if x_ref.dtype == F32:
            total = total + mm(stay_ref[...], (x - high.astype(F32)).astype(BF16))
        came = jnp.concatenate([ref[n * 48 : (n + 1) * 48] for ref in came_refs[:3]], axis=0)
        w, rows = half_at(n if onward else n + 1)
        total_ref[w, rows] = total + mm(near_ref[...], came)
    came = jnp.concatenate([ref[...] for ref in came_refs[3:]], axis=0)
    w, rows = half_at(halves - 1 if onward else 0)
    total_ref[w, rows] = mm(far_ref[...], came)
    for w in range(windows):
        total = total_ref[w]
        if add_mean:
            total = total + jnp.mean(base_ref[w], axis=-1, keepdims=True)
        out_ref[w] = total.astype(out_ref.dtype)


def halo_unpack(x, came, halo, onward, dtype, center=False, mean_of=None, after=None):
    places = [jnp.asarray(m, BF16) for m in halo.places(onward)]
    operands = places + [x] + ([] if mean_of is None else [mean_of]) + list(came)
    return functools.partial(call, after=after)(
        functools.partial(unpack_kernel, center, onward, mean_of is not None),
        (1,),
        [whole_block(v.shape) for v in operands],
        whole_block(x.shape),
        jax.ShapeDtypeStruct(x.shape, dtype),
        8 * x.size * HALF,
        [pltpu.VMEM(x.shape, F32), pltpu.VMEM(x.shape, F32)],
    )(*operands)


def index_bits():
    bits = []
    for axis in ALL:
        count = lax.axis_size(axis).bit_length() - 1
        bits += [(axis, b) for b in reversed(range(count))]
    return bits


def bit_of(axis, bit):
    return (lax.axis_index(axis) // 2**bit) % 2


def stage_orders():
    bits = index_bits()
    inner = [(CLIP, 0)] if lax.axis_size(CLIP) > 1 else []
    tm = [b for b in bits if b[0] == TM]
    clip = [b for b in bits if b[0] == CLIP and b not in inner]
    space = [b for b in reversed(bits) if b[0] == SPACE]
    return inner + tm + clip + space, inner + clip + tm + space


def gather_flow(shard, order):
    bits = index_bits()
    out = shard.reshape((1,) * len(bits) + shard.shape)
    for axis, bit in reversed(order):
        dim = bits.index((axis, bit))
        (other,), token = yield [(out, axis, swap_pairs(axis, bit))]
        if token is not None:
            other = (other.astype(F32) + token.reshape(())).astype(BF16)
        out = jnp.where(
            bit_of(axis, bit) == 1,
            jnp.concatenate([other, out], dim),
            jnp.concatenate([out, other], dim),
        )
    return out.reshape((-1,) + shard.shape[1:])


def scatter_flow(own, sent, order):
    bits = index_bits()
    width = own.shape[-1]
    dims = [2] * len(bits)
    own, sent = own.reshape(-1, width), sent.reshape(-1, width)
    for n, (axis, bit) in enumerate(order):
        (came,), token = yield [(sent, axis, swap_pairs(axis, bit))]
        dims[bits.index((axis, bit))] = 1
        zero = 0.0 if token is None else token.reshape(())
        if n + 1 == len(order):
            return own + came.astype(F32)
        axis, bit = order[n + 1]
        dim = bits.index((axis, bit))
        here = bit_of(axis, bit)
        own, came = (v.reshape(dims + [-1, width]) for v in (own, came))

        def half(index):
            mine, theirs = (lax.dynamic_slice_in_dim(v, index, 1, dim) for v in (own, came))
            return (mine + theirs.astype(F32) + zero).reshape(-1, width)

        own, sent = half(here), half(1 - here).astype(BF16)


def table_flow(tables, heads_here):
    first = lax.axis_index(TM) == 0
    mine = jnp.where(first, tables[0], tables[1])
    (came,), _ = yield [(jnp.where(first, tables[1], tables[0]), TM, swap_pairs(TM, 0))]
    table = mine + came
    for axis, bit in index_bits():
        if axis != TM:
            (came,), _ = yield [(table, axis, swap_pairs(axis, bit))]
            table = table + came
    return table


WIDE = 768


def column_pick():
    pick = np.zeros((WIN_HW, 256, 128), np.float32)
    for key_col in range(WIN_HW):
        for row in range(SPAN):
            for col in range(WIN_HW):
                entry = row * SPAN + col - key_col + WIN_HW - 1
                pick[key_col, entry, row * WIN_HW + col] = 1
    return pick


def lane_spans(step):
    first, rest = divmod(step * CELLS, 128)
    if rest + CELLS <= 128:
        return [(first, rest, rest + CELLS)]
    return [(first, rest, 128), (first + 1, 0, rest + CELLS - 128)]


def bias_kernel(slab_ref, pick_ref, out_ref, row_ref, wide_ref):
    heads = pl.num_programs(0)

    @pl.when(pl.program_id(0) == 0)
    def _():
        slabs = slab_ref[...]
        for col in range(WIN_HW):
            row_ref[pl.ds(col, slabs.shape[0], stride=8), :] = mm(slabs, pick_ref[col]) * LOG2E

    base = pl.program_id(0) * 128
    lane = lax.broadcasted_iota(jnp.int32, (8, 128), 1)
    for row in range(WIN_HW):
        tiles = [jnp.zeros((8, 128), F32) for _ in range(WIDE // 128)]
        for step in range(STEPS):
            rows = row_ref[pl.ds(pl.multiple_of(base + step * 8, 8), 8), :]
            turn = (step * CELLS - WIN_HW * (WIN_HW - 1 - row)) % 128
            rows = pltpu.roll(rows, turn, 1) if turn else rows
            for tile, low, high in lane_spans(step):
                tiles[tile] = jnp.where((lane >= low) & (lane < high), rows, tiles[tile])
        wide_ref[row * WIN_HW : (row + 1) * WIN_HW, :] = jnp.concatenate(tiles, axis=1)[:WIN_HW]
    wide = wide_ref[:CELLS, :]
    for key_frame in range(WIN_T):
        turned = pltpu.roll(wide, (WIDE - (WIN_T - 1 - key_frame) * CELLS) % WIDE, 1)
        out_ref[0, key_frame * CELLS : (key_frame + 1) * CELLS, :] = turned[:, :TOKENS]


def table_to_bias(tables, after=None):
    heads = tables.shape[0]
    slabs = tables.reshape(heads, STEPS, SPAN * SPAN)
    slabs = jnp.pad(slabs, ((0, 0), (0, 16 - STEPS), (0, 256 - SPAN * SPAN)))
    slabs = slabs.reshape(heads * 16, 256)
    return functools.partial(call, after=after)(
        bias_kernel,
        (heads,),
        [whole_block(slabs.shape), whole_block((WIN_HW, 256, 128))],
        pl.BlockSpec((1, TOKENS, TOKENS), lambda h: (h, 0, 0)),
        jax.ShapeDtypeStruct((heads, TOKENS, TOKENS), F32),
        heads * 500_000_000,
        [pltpu.VMEM((heads * 128, 128), F32), pltpu.VMEM((56, WIDE), F32)],
    )(slabs, jnp.asarray(column_pick(), BF16))


def table_back_kernel(sums_ref, pick_ref, out_ref, row_ref):
    head = pl.program_id(0)
    lane = lax.broadcasted_iota(jnp.int32, (WIN_HW, 128), 1)
    totals = [None] * STEPS
    for row in range(WIN_HW):
        rows = sums_ref[0, row * WIN_HW : (row + 1) * WIN_HW, :]
        start = WIN_HW * (WIN_HW - 1 - row)
        for step in range(STEPS):
            turn = (start - step * CELLS) % 128
            piece = None
            for tile, low, high in lane_spans(step):
                part = rows[:, tile * 128 : (tile + 1) * 128]
                part = jnp.where((lane >= low) & (lane < high), part, 0.0)
                piece = part if piece is None else piece + part
            piece = pltpu.roll(piece, turn, 1) if turn else piece
            totals[step] = piece if totals[step] is None else totals[step] + piece
    blank = jnp.zeros((1, 128), F32)
    for step in range(16):
        rows = jnp.concatenate([totals[step], blank]) if step < STEPS else jnp.zeros((8, 128), F32)
        row_ref[pl.ds(pl.multiple_of(head * 128 + step * 8, 8), 8), :] = rows

    @pl.when(head == pl.num_programs(0) - 1)
    def _():
        total = None
        for col in range(WIN_HW):
            rows = row_ref[pl.ds(col, out_ref.shape[0], stride=8), :]
            high = rows.astype(BF16)
            low = (rows - high.astype(F32)).astype(BF16)
            part = mm(high, pick_ref[col], 1, 1) + mm(low, pick_ref[col], 1, 1)
            total = part if total is None else total + part
        out_ref[...] = total


def sums_to_table(sums, after=None):
    heads = sums.shape[0]
    slabs = functools.partial(call, after=after)(
        table_back_kernel,
        (heads,),
        [pl.BlockSpec((1, CELLS, WIDE), lambda h: (h, 0, 0)), whole_block((WIN_HW, 256, 128))],
        whole_block((heads * 16, 256)),
        jax.ShapeDtypeStruct((heads * 16, 256), F32),
        heads * 300_000_000,
        [pltpu.VMEM((heads * 128, 128), F32)],
    )(sums, jnp.asarray(column_pick(), BF16))
    return slabs.reshape(heads, 16, 256)[:, :STEPS, : SPAN * SPAN].reshape(heads, -1)


def unit_rows(x):
    centered = x - jnp.mean(x, axis=-1, keepdims=True)
    inverse = lax.rsqrt(jnp.mean(centered * centered, axis=-1, keepdims=True) + 1e-05)
    return centered * inverse, inverse


def norm_back(grad, unit, inverse, gain):
    scaled = grad * gain
    return inverse * (
        scaled
        - jnp.mean(scaled, axis=-1, keepdims=True)
        - unit * jnp.mean(scaled * unit, axis=-1, keepdims=True)
    )


def qkv_kernel(x_ref, vec_ref, wq_ref, wk_ref, wv_ref, out_ref):
    width = x_ref.shape[-1]
    unit, _ = unit_rows(x_ref[0].astype(F32))
    normed = (unit * vec_ref[0:1] + vec_ref[1:2]).astype(BF16)
    for part, ref in enumerate((wq_ref, wk_ref, wv_ref)):
        out = mm(normed, ref[...])
        if part == 0:
            out = out + vec_ref[2:3]
        if part == 2:
            out = out + vec_ref[3:4]
        out_ref[0, :, part * width : (part + 1) * width] = out.astype(BF16)


def run_qkv(x, vec, w_qkv, after=None):
    windows, _, width = x.shape
    weight, at = w_qkv
    return functools.partial(call, after=after)(
        qkv_kernel,
        (windows,),
        [win_block(width), whole_block(vec.shape)]
        + [weight_block(width, width, at + n) for n in range(3)],
        win_block(3 * width),
        jax.ShapeDtypeStruct((windows, TOKENS, 3 * width), BF16),
        2 * windows * TOKENS * width * 3 * width,
    )(x, vec, weight, weight, weight)


GROUP = 4


def head_masks(head_size):
    lane = lax.broadcasted_iota(jnp.int32, (1, GROUP * head_size), 1)
    return [
        jnp.where((lane >= h * head_size) & (lane < (h + 1) * head_size), 1.0, 0.0).astype(BF16)
        for h in range(GROUP)
    ]


def region_labels(flag_ref, late_ref, turned_ref, at_end):
    flags = [flag_ref[1 + n].astype(F32) for n in range(3)]
    flags[0] = flags[0] * at_end
    col = sum(flags[n] * late_ref[:, n : n + 1] for n in range(3))
    return col, sum(flags[n] * turned_ref[n : n + 1, :] for n in range(3))


def late_tokens():
    token = np.arange(TOKENS)
    late = np.zeros((TOKENS, 8), np.float32)
    late[:, 0] = 4 * (token // CELLS >= WIN_T - WIN_T // 2)
    late[:, 1] = 2 * (token // WIN_HW % WIN_HW >= WIN_HW - WIN_HW // 2)
    late[:, 2] = token % WIN_HW >= WIN_HW - WIN_HW // 2
    return late


def attend_kernel(
    shifted, head_size, flag_ref, q_ref, k_ref, v_ref, bias_ref, late_ref, turned_ref, out_ref, log_ref
):
    q, k = q_ref[0], k_ref[0]
    if shifted:
        at_end = jnp.where(pl.program_id(1) == pl.num_programs(1) - 1, 1.0, 0.0)
        col, row = region_labels(flag_ref, late_ref, turned_ref, at_end)
    turned = v_ref[0].astype(F32).T.astype(BF16)
    factor = head_size**-0.5 * LOG2E
    masks = head_masks(head_size)
    outs, logs = [], []
    for h in range(GROUP):
        scores = mm(k * masks[h], q, 1, 1) * factor + bias_ref[h]
        if shifted:
            scores = jnp.where(col == row, scores, masked_score)
        peak = jnp.max(scores, axis=0, keepdims=True)
        raised = jnp.exp2(scores - peak)
        total = jnp.sum(raised, axis=0, keepdims=True)
        mixed = mm(turned[h * head_size : (h + 1) * head_size], raised.astype(BF16))
        outs.append(mixed / total)
        logs.append(peak + jnp.log2(total))
    out_ref[0] = jnp.concatenate(outs, axis=0).T.astype(BF16)
    log_ref[0, 0] = jnp.concatenate(logs + logs, axis=0)


def run_attend(qkv, bias, flags, shifted, first, after=None):
    windows, _, width3 = qkv.shape
    width = width3 // 3
    wide = GROUP * (width // HEADS)
    groups, count = HEADS // GROUP, bias.shape[0] // GROUP
    qkv_specs = [
        pl.BlockSpec((1, TOKENS, wide), lambda g, w, p=part: (w, 0, p * groups + first + g))
        for part in range(3)
    ]
    return functools.partial(call, after=after)(
        functools.partial(attend_kernel, shifted, width // HEADS),
        (count, windows),
        [flag_spec()]
        + qkv_specs
        + [
            pl.BlockSpec((GROUP, TOKENS, TOKENS), lambda g, w: (g, 0, 0)),
            whole_block((TOKENS, 8)),
            whole_block((8, TOKENS)),
        ],
        [
            pl.BlockSpec((1, TOKENS, wide), lambda g, w: (w, 0, g)),
            pl.BlockSpec((1, 1, 2 * GROUP, TOKENS), lambda g, w: (w, g, 0, 0)),
        ],
        [
            jax.ShapeDtypeStruct((windows, TOKENS, count * wide), BF16),
            jax.ShapeDtypeStruct((windows, count, 2 * GROUP, TOKENS), F32),
        ],
        64 * windows * TOKENS * TOKENS * count * wide,
    )(flags, qkv, qkv, qkv, bias, late_tokens(), late_tokens().T)


def attend_back_kernel(
    shifted, head_size, flag_ref, q_ref, k_ref, v_ref, g_ref, o_ref, bias_ref, late_ref, turned_ref,
    log_ref, dq_ref, dk_ref, dv_ref, table_ref, sum_ref,
):
    windows = q_ref.shape[0]
    if shifted:
        labels = [
            region_labels(flag_ref, late_ref, turned_ref, float(w == windows - 1))
            for w in range(windows)
        ]
    scale = head_size**-0.5
    factor = scale * LOG2E
    masks = head_masks(head_size)

    @pl.when(pl.program_id(0) == 0)
    def _():
        sum_ref[...] = jnp.zeros_like(sum_ref)

    turned, weighed = [], []
    for w in range(windows):
        turned.append(k_ref[w].astype(F32).T.astype(BF16))
        weighed.append(g_ref[w].astype(F32).T * o_ref[w].astype(F32).T)
    grad_q = [[] for _ in range(windows)]
    grad_k, grad_v = [None] * windows, [None] * windows
    for h in range(GROUP):
        here = slice(h * head_size, (h + 1) * head_size)
        total = None
        for w in range(windows):
            q, k, v, g = q_ref[w], k_ref[w], v_ref[w], g_ref[w]
            inner = jnp.sum(weighed[w][here], axis=0, keepdims=True)
            scores = mm(k * masks[h], q, 1, 1) * factor + bias_ref[h]
            if shifted:
                scores = jnp.where(labels[w][0] == labels[w][1], scores, masked_score)
            probs = jnp.exp2(scores - log_ref[w, 0, h : h + 1])
            grad_probs = mm(v * masks[h], g, 1, 1)
            grad_scores = (probs * (grad_probs - inner)).astype(BF16)
            part_v = mm(probs.astype(BF16), g * masks[h])
            part_k = mm(grad_scores, q * masks[h])
            grad_v[w] = part_v if grad_v[w] is None else grad_v[w] + part_v
            grad_k[w] = part_k if grad_k[w] is None else grad_k[w] + part_k
            grad_q[w].append(mm(turned[w][here], grad_scores))
            wide = grad_scores.astype(F32)
            total = wide if total is None else total + wide
        sum_ref[:, :TOKENS] = total
        sums = None
        for key_frame in range(WIN_T):
            rows = sum_ref[key_frame * CELLS : (key_frame + 1) * CELLS, :]
            step = (WIN_T - 1 - key_frame) * CELLS
            rows = pltpu.roll(rows, step, 1) if step else rows
            sums = rows if sums is None else sums + rows
        table_ref[h] = sums
    for w in range(windows):
        dq_ref[w] = (jnp.concatenate(grad_q[w], axis=0) * scale).T.astype(BF16)
        dk_ref[w] = (grad_k[w] * scale).astype(BF16)
        dv_ref[w] = grad_v[w].astype(BF16)


def run_attend_back(qkv, grad, attended, bias, flags, log, shifted, first, after=None):
    windows, _, width3 = qkv.shape
    width = width3 // 3
    wide = GROUP * (width // HEADS)
    groups, count = HEADS // GROUP, bias.shape[0] // GROUP
    qkv_specs = [
        pl.BlockSpec((windows, TOKENS, wide), lambda g, p=part: (0, 0, p * groups + first + g))
        for part in range(3)
    ]
    flat = pl.BlockSpec((windows, TOKENS, wide), lambda g: (0, 0, g))
    flat_shape = jax.ShapeDtypeStruct((windows, TOKENS, count * wide), BF16)
    return functools.partial(call, after=after)(
        functools.partial(attend_back_kernel, shifted, width // HEADS),
        (count,),
        [flag_spec()]
        + qkv_specs
        + [
            pl.BlockSpec((windows, TOKENS, wide), lambda g: (0, 0, first + g)),
            flat,
            pl.BlockSpec((GROUP, TOKENS, TOKENS), lambda g: (g, 0, 0)),
            whole_block((TOKENS, 8)),
            whole_block((8, TOKENS)),
            pl.BlockSpec((windows, 1, 2 * GROUP, TOKENS), lambda g: (0, g, 0, 0)),
        ],
        [flat, flat, flat, pl.BlockSpec((GROUP, CELLS, WIDE), lambda g: (g, 0, 0))],
        [flat_shape] * 3 + [jax.ShapeDtypeStruct((count * GROUP, CELLS, WIDE), F32)],
        160 * windows * TOKENS * TOKENS * count * wide,
        [pltpu.VMEM((TOKENS, WIDE), F32)],
    )(flags, qkv, qkv, qkv, grad, attended, bias, late_tokens(), late_tokens().T, log)


def normal_below(x):
    bell = jnp.exp2(x * x * (-0.5 * LOG2E)) * (1.0 / math.sqrt(2 * math.pi))
    return 0.5 + 0.5 * lax.erf(x * math.sqrt(0.5)), bell


def spread_down(down_ref, w2_ref):
    _, parts, own, width = w2_ref.shape
    for part in range(parts):
        cols = slice(part * width, (part + 1) * width)
        w2_ref[:, part] = down_ref[:, cols].reshape(-1, own, width)


def chunk_rows(w2_ref, first, chunk):
    _, parts, own, width = w2_ref.shape
    step = chunk // (parts * own)
    return w2_ref[first * step : (first + 1) * step].reshape(chunk, width)


def branch_kernel(count, *refs):
    att_refs = refs[:count]
    x_ref, vec_ref, wo_ref, w1_ref, down_ref, mid_ref, hid_ref, slope_ref, out_ref, w2_ref = refs[count:]

    @pl.when(pl.program_id(0) == 0)
    def _():
        spread_down(down_ref, w2_ref)

    chunk = 512
    attended = jnp.concatenate([ref[0] for ref in att_refs], axis=1)
    middle = x_ref[0].astype(F32) + mm(attended, wo_ref[...]) + vec_ref[4:5]
    mid_ref[0] = middle
    unit, _ = unit_rows(middle)
    normed = (unit * vec_ref[5:6] + vec_ref[6:7]).astype(BF16)
    after = middle + vec_ref[7:8]
    for n in range(w1_ref.shape[1] // chunk):
        cols = slice(n * chunk, (n + 1) * chunk)
        pre = mm(normed, w1_ref[:, cols]) + vec_ref[8 + n : 9 + n]
        below, bell = normal_below(pre)
        hidden = (pre * below).astype(BF16)
        hid_ref[0, :, cols] = hidden
        slope_ref[0, :, cols] = (below + pre * bell).astype(BF16)
        after = after + mm(hidden, chunk_rows(w2_ref, n, chunk))
    out_ref[0] = after.astype(out_ref.dtype)


def weight_block(rows, width, column):
    return pl.BlockSpec((rows, width), lambda *ids: (0, column))


def branch_weights(weights, width, wide):
    (wo, wo_at), (w1, w1_at), (down, down_at) = weights
    specs = [
        weight_block(width, width, wo_at),
        weight_block(width, wide, w1_at),
        weight_block(width, wide, down_at),
    ]
    return (wo, w1, down), specs


def run_branch(x, attended, vec, weights, out_dtype, after=None):
    windows, _, width = x.shape
    wide = 4 * width
    arrays, specs = branch_weights(weights, width, wide)
    return functools.partial(call, after=after)(
        functools.partial(branch_kernel, len(attended)),
        (windows,),
        [win_block(part.shape[-1]) for part in attended]
        + [win_block(width), whole_block(vec.shape)]
        + specs,
        [win_block(width), win_block(wide), win_block(wide), win_block(width)],
        [
            jax.ShapeDtypeStruct((windows, TOKENS, width), F32),
            jax.ShapeDtypeStruct((windows, TOKENS, wide), BF16),
            jax.ShapeDtypeStruct((windows, TOKENS, wide), BF16),
            jax.ShapeDtypeStruct((windows, TOKENS, width), out_dtype),
        ],
        2 * windows * TOKENS * width * (width + 2 * wide),
        [pltpu.VMEM((width // 16, wide // width, 16, width), BF16)],
    )(*attended, x, vec, *arrays)


def add_rows(ref, rows, value):
    ref[rows, :] += jnp.sum(value.astype(F32), axis=0, keepdims=True)


def split_out(sums_ref, core, own_ref, sent_ref):
    own_ref[...] = sums_ref[:, core]
    sent_ref[...] = sums_ref[:, 1 - core].astype(BF16)


def branch_back_kernel(count, split, flag_ref, *refs):
    att_refs = refs[:count]
    grad_ref, mid_ref, hid_ref, slope_ref, vec_ref, wo_ref, w1_ref, down_ref = refs[count : count + 8]
    gm_ref, ga_ref, vecs_ref = refs[count + 8 : count + 11]
    outs, (d1_ref, d2_ref, w2_ref) = refs[count + 11 : -3], refs[-3:]
    chunk = 512
    width, wide = w1_ref.shape

    @pl.when(pl.program_id(0) == 0)
    def _():
        spread_down(down_ref, w2_ref)
        d1_ref[...] = jnp.zeros_like(d1_ref)
        d2_ref[...] = jnp.zeros_like(d2_ref)
        vecs_ref[...] = jnp.zeros_like(vecs_ref)

    grad = grad_ref[0].astype(F32)
    branch = grad.astype(BF16)
    unit, inverse = unit_rows(mid_ref[0])
    normed = (unit * vec_ref[5:6] + vec_ref[6:7]).astype(BF16)
    add_rows(vecs_ref, slice(7, 8), branch)
    back = None
    blocks = chunk // d2_ref.shape[2]
    for n in range(wide // chunk):
        cols = slice(n * chunk, (n + 1) * chunk)
        total = mm(hid_ref[0, :, cols], branch, 0, 0)
        at = slice(n * blocks // 2, (n + 1) * blocks // 2)
        d2_ref[at] += total.reshape((-1,) + d2_ref.shape[1:])
        grad_pre = mm(branch, chunk_rows(w2_ref, n, chunk), 1, 1) * slope_ref[0, :, cols].astype(F32)
        grad_pre = grad_pre.astype(BF16)
        add_rows(vecs_ref, slice(8 + n, 9 + n), grad_pre)
        d1_ref[:, :, :, cols] += mm(normed, grad_pre, 0, 0).reshape(d1_ref.shape[:3] + (chunk,))
        part = mm(grad_pre, w1_ref[:, cols], 1, 1)
        back = part if back is None else back + part
    add_rows(vecs_ref, slice(5, 6), back * unit)
    add_rows(vecs_ref, slice(6, 7), back)
    middle_grad = grad + norm_back(back, unit, inverse, vec_ref[5:6])
    gm_ref[0] = middle_grad
    branch = middle_grad.astype(BF16)
    add_rows(vecs_ref, slice(4, 5), branch)
    attended = jnp.concatenate([ref[0] for ref in att_refs], axis=1)
    total = mm(attended, branch, 0, 0)
    d1_ref[:, :, :, wide:] += total.reshape(d1_ref.shape[:3] + (width,))
    ga_ref[0] = mm(branch, wo_ref[...], 1, 1).astype(BF16)

    @pl.when(pl.program_id(0) == pl.num_programs(0) - 1)
    def _():
        if split:
            split_out(d1_ref, flag_ref[0], *outs[:2])
            split_out(d2_ref, flag_ref[0], *outs[2:])
        else:
            (out_ref,) = outs
            out_ref[:, : wide + width] = d1_ref[...].reshape(width, -1).astype(BF16)
            parts = wide // width
            for part in range(parts):
                first = wide + width + part * width
                piece = d2_ref[:, :, part * 16 : (part + 1) * 16, :].reshape(width, width)
                out_ref[:, first : first + width] = piece.astype(BF16)


def run_branch_back(grad, middle, attended, hidden, slope, vec, weights, flags, split, after=None):
    windows, _, width = middle.shape
    wide = 4 * width
    arrays, specs = branch_weights(weights, width, wide)
    flat = win_block(width)
    pairs = width // 32
    if split:
        shapes = []
        for rows, cols in ((16, wide + width), (64, width)):
            shapes.append(jax.ShapeDtypeStruct((pairs, rows, cols), F32))
            shapes.append(jax.ShapeDtypeStruct((pairs, rows, cols), BF16))
    else:
        shapes = [jax.ShapeDtypeStruct((width, 2 * wide + width), BF16)]
    return functools.partial(call, after=after)(
        functools.partial(branch_back_kernel, len(attended), split),
        (windows,),
        [flag_spec()]
        + [win_block(part.shape[-1]) for part in attended]
        + [flat, flat, win_block(wide), win_block(wide), whole_block(vec.shape)]
        + specs,
        [flat, flat, whole_block(vec.shape)] + [whole_block(s.shape) for s in shapes],
        [
            jax.ShapeDtypeStruct((windows, TOKENS, width), F32),
            jax.ShapeDtypeStruct((windows, TOKENS, width), BF16),
            jax.ShapeDtypeStruct(vec.shape, F32),
        ]
        + shapes,
        4 * windows * TOKENS * width * (width + 2 * wide),
        [
            pltpu.VMEM((pairs, 2, 16, wide + width), F32),
            pltpu.VMEM((pairs, 2, 64, width), F32),
            pltpu.VMEM((pairs * 2, wide // width, 16, width), BF16),
        ],
    )(flags, *attended, grad, middle, hidden, slope, vec, *arrays)


def qkv_back_kernel(count, flag_ref, *refs):
    grads, refs = refs[: 3 * count], refs[3 * count :]
    x_ref, gm_ref, vec_ref, wq_ref, wk_ref, wv_ref, rest_ref, mask_ref, pick_ref, spread_ref = refs[:10]
    out_ref, own_ref, sent_ref, dw_ref, vecs_ref = refs[10:]
    width = x_ref.shape[-1]

    @pl.when(pl.program_id(0) == 0)
    def _():
        dw_ref[...] = jnp.zeros_like(dw_ref)
        vecs_ref[...] = rest_ref[...]

    unit, inverse = unit_rows(x_ref[0].astype(F32))
    normed = (unit * vec_ref[0:1] + vec_ref[1:2]).astype(BF16)
    back = None
    for part, ref in enumerate((wq_ref, wk_ref, wv_ref)):
        grad = jnp.concatenate([g[0] for g in grads[part * count : (part + 1) * count]], axis=1)
        total = mm(normed, grad, 0, 0)
        cols = slice(part * width, (part + 1) * width)
        dw_ref[:, :, :, cols] += total.reshape(dw_ref.shape[:3] + (width,))
        here = mm(grad, ref[...], 1, 1)
        back = here if back is None else back + here
        if part == 0:
            add_rows(vecs_ref, slice(2, 3), grad)
        if part == 2:
            add_rows(vecs_ref, slice(3, 4), grad)
    add_rows(vecs_ref, slice(0, 1), back * unit)
    add_rows(vecs_ref, slice(1, 2), back)
    out_ref[0] = (gm_ref[0] + norm_back(back, unit, inverse, vec_ref[0:1])).astype(out_ref.dtype)

    @pl.when(pl.program_id(0) == pl.num_programs(0) - 1)
    def _():
        rows = vecs_ref[...]
        high = rows.astype(BF16)
        low = (rows - high.astype(F32)).astype(BF16)
        total = None
        for piece in (high, low):
            piece = (mm(pick_ref[...], piece, 0, 0) * mask_ref[...].astype(F32)).astype(BF16)
            piece = mm(piece, spread_ref[0], 1, 1)
            total = piece if total is None else total + piece
        dw_ref[:, :, :, 3 * width :] = total.reshape(dw_ref.shape[:3] + (128,))
        split_out(dw_ref, flag_ref[0], own_ref, sent_ref)


def run_qkv_back(grads, x, grad_middle, vec, w_qkv, rest, flags, out_dtype, after=None):
    windows, _, width = x.shape
    flat = win_block(width)
    weight, at = w_qkv
    extra = [jnp.asarray(a, BF16) for a in vector_slots()]
    shape = (width // 32, 16, 3 * width + 128)
    return functools.partial(call, after=after)(
        functools.partial(qkv_back_kernel, len(grads) // 3),
        (windows,),
        [flag_spec()]
        + [win_block(part.shape[-1]) for part in grads]
        + [flat, flat, whole_block(vec.shape)]
        + [weight_block(width, width, at + n) for n in range(3)]
        + [whole_block(rest.shape)]
        + [whole_block(a.shape) for a in extra],
        [flat, whole_block(shape), whole_block(shape)],
        [
            jax.ShapeDtypeStruct((windows, TOKENS, width), out_dtype),
            jax.ShapeDtypeStruct(shape, F32),
            jax.ShapeDtypeStruct(shape, BF16),
        ],
        4 * windows * TOKENS * width * 3 * width,
        [pltpu.VMEM((shape[0], 2) + shape[1:], F32), pltpu.VMEM(rest.shape, F32)],
    )(flags, *grads, x, grad_middle, vec, weight, weight, weight, rest, *extra)


def pack_first_kernel(qkv_ref, *refs):
    vector_refs, (first_ref, rows_ref) = refs[:-2], refs[-2:]
    own, width3 = qkv_ref.shape[1:]
    rows_ref[...] = jnp.zeros_like(rows_ref)
    row = 0
    lane = lax.broadcasted_iota(jnp.int32, (1, 128), 1)
    for ref in vector_refs:
        values = ref[...].astype(F32)
        values = jnp.pad(values, ((0, 0), (0, 128 - values.shape[1])))
        for part in range(ref.shape[1] // own):
            line = jnp.zeros((1, 128), F32)
            for layer in range(LAYERS):
                turn = ((layer - part) * own) % 128
                turned = pltpu.roll(values, turn, 1) if turn else values
                here = (lane >= layer * own) & (lane < (layer + 1) * own)
                line = jnp.where(here, turned[layer : layer + 1], line)
            rows_ref[row : row + 1, :] = line
            row += 1
    first_ref[:, :width3] = qkv_ref[0]
    first_ref[:, width3:] = rows_ref[...].astype(BF16)


def pack_first(qkv, *vectors, after=None):
    own, width3 = qkv.shape[1:]
    return functools.partial(call, after=after)(
        pack_first_kernel,
        (1,),
        [whole_block((1, own, width3))] + [whole_block(v.shape) for v in vectors],
        whole_block((own, width3 + 128)),
        jax.ShapeDtypeStruct((own, width3 + 128), BF16),
        1e6,
        [pltpu.VMEM((16, 128), F32)],
    )(qkv, *vectors)


def put_down(fc2_ref, layer, out_ref, first):
    own, width = 16, fc2_ref.shape[2]
    for part in range(fc2_ref.shape[1] // own):
        at = first + part * width
        out_ref[:, at : at + width] = fc2_ref[layer, part * own : (part + 1) * own, :]


def pack_mid_kernel(out_ref, fc1_ref, fc2_ref, mid_ref, down_ref):
    wide = fc1_ref.shape[2]
    mid_ref[:, :wide] = fc1_ref[0]
    mid_ref[:, wide:] = out_ref[0]
    put_down(fc2_ref, 0, down_ref, 0)


def pack_later_kernel(qkv_ref, out_ref, fc1_ref, fc2_ref, later_ref):
    width, wide = out_ref.shape[2], fc1_ref.shape[2]
    later_ref[:, :wide] = fc1_ref[1]
    put_down(fc2_ref, 1, later_ref, wide)
    later_ref[:, 2 * wide : 2 * wide + 3 * width] = qkv_ref[1]
    later_ref[:, 2 * wide + 3 * width :] = out_ref[1]


def pack_weights(kernel, widths, *weights, after=None):
    own = weights[0].shape[1]
    return functools.partial(call, after=after)(
        kernel,
        (1,),
        [whole_block(w.shape) for w in weights],
        [whole_block((own, w)) for w in widths],
        [jax.ShapeDtypeStruct((own, w), BF16) for w in widths],
        1e6,
    )(*weights)


def vector_slots():
    devices, own = 32, 16
    count = devices * own
    mask = np.zeros((devices * 16, count), np.float32)
    pick = np.zeros((16, devices * 16), np.float32)
    spread = np.zeros((LAYERS, 128, count), np.float32)
    for device in range(devices):
        for first, parts in ((0, 1), (1, 1), (2, 2), (4, 1), (5, 1), (6, 1), (7, 1), (8, 4)):
            for part in range(parts):
                row, start = divmod(device * own * parts + part * own, count)
                slot = device * 16 + first + part
                pick[first + row, slot] = 1
                mask[slot, start : start + own] = 1
    for layer in range(LAYERS):
        for lane in range(count):
            spread[layer, layer * own + lane % own, lane] = 1
    return mask, pick, spread


def vectors_kernel(block_ref, mask_ref, pick_ref, spread_ref, out_ref):
    block = block_ref[...]
    for layer in range(LAYERS):
        lines = mm(block, spread_ref[layer]) * mask_ref[...].astype(F32)
        out_ref[layer] = mm(pick_ref[...], lines.astype(BF16))


def vectors_whole(blocks, after=None):
    count, width = blocks.shape
    extra = [jnp.asarray(a, BF16) for a in vector_slots()]
    return functools.partial(call, after=after)(
        vectors_kernel,
        (1,),
        [pl.BlockSpec((count, 128), lambda n: (0, width // 128 - 1))]
        + [whole_block(a.shape) for a in extra],
        whole_block((LAYERS, 16, count)),
        jax.ShapeDtypeStruct((LAYERS, 16, count), F32),
        1e9,
    )(blocks, *extra)


def finish_kernel(
    mix0_ref, mix1_ref, mid_ref, two_ref, later_ref, gain1_ref, bias1_ref, qkv_ref, qvb_ref, out_ref,
    outb_ref, gain2_ref, bias2_ref, fc1_ref, fc1b_ref, fc2_ref, fc2b_ref,
):
    width, wide = out_ref.shape[2], fc1_ref.shape[2]
    own = gain1_ref.shape[1]
    lane = lax.broadcasted_iota(jnp.int32, (1, 128), 1)
    for layer, mix_ref in enumerate((mix0_ref, mix1_ref)):
        qkv_ref[layer] = mix_ref[:, : 3 * width]
        row = 0
        for ref in (gain1_ref, bias1_ref, qvb_ref, outb_ref, gain2_ref, bias2_ref, fc2b_ref, fc1b_ref):
            line = jnp.zeros((1, 128), F32)
            for part in range(ref.shape[1] // own):
                piece = mix_ref[row : row + 1, 3 * width : 3 * width + 128]
                piece = pltpu.roll(piece, part * own, 1) if part else piece
                line = jnp.where((lane >= part * own) & (lane < (part + 1) * own), piece, line)
                row += 1
            ref[layer : layer + 1, :] = line[:, : ref.shape[1]]
    fc1_ref[0] = mid_ref[:, :wide]
    out_ref[0] = mid_ref[:, wide:]
    fc2_ref[0] = two_ref[...]
    fc1_ref[1] = later_ref[:, :wide].astype(F32)
    out_ref[1] = later_ref[:, wide : wide + width].astype(F32)
    for part in range(wide // width):
        first = wide + width + part * width
        piece = later_ref[:, first : first + width].astype(F32)
        fc2_ref[1, part * own : (part + 1) * own, :] = piece


def run_finish(mixes, mid, two, later):
    own, width = 16, two.shape[1]
    wide = mid.shape[1] - width
    shapes = [
        (own,), (own,), (own, 3 * width), (2 * own,), (own, width), (own,),
        (own,), (own,), (own, wide), (4 * own,), (4 * own, width), (own,),
    ]
    operands = [*mixes, mid, two, later]
    return call(
        finish_kernel,
        (1,),
        [whole_block(v.shape) for v in operands],
        [whole_block((LAYERS,) + shape) for shape in shapes],
        [jax.ShapeDtypeStruct((LAYERS,) + shape, F32) for shape in shapes],
        1e6,
    )(*operands)


def place_flags():
    quadrant = lax.axis_index(SPACE)
    last = lax.axis_index(TM) == lax.axis_size(TM) - 1
    flags = [lax.axis_index(CLIP) % 2, last, quadrant // 2, quadrant % 2]
    return jnp.stack([jnp.asarray(f, jnp.int32) for f in flags])


FIRST, TABLES, MID, DOWN, ROLL, GRAD, OUT, BACK, D_MID, D_TWO, TABLE, D_QKV = range(12)


def local_windows(
    clips_in,
    ln1_gain,
    ln1_bias,
    qkv_weight,
    qv_bias,
    out_weight,
    out_bias,
    ln2_gain,
    ln2_bias,
    fc1_weight,
    fc1_bias,
    fc2_weight,
    fc2_bias,
    pos_table,
    out_grad,
):
    _, frames_here, _, _, width = clips_in.shape
    windows = frames_here // WIN_T
    own = ln1_gain.shape[1]
    heads_here = pos_table.shape[2]
    groups_here = heads_here // GROUP
    one, two = stage_orders()
    flat = (windows, TOKENS, width)
    flags = place_flags()
    halo = Halo()
    flow = Flow()

    def stepped(run, *args, names=None, waits=(), **options):
        order = Order(flow.pending() + list(waits))
        out = run(*args, after=order, **options)
        flow.step(order.token, names)
        return out

    def halo_start(name, packed, onward):
        flow.start(name, halo_flow(packed, onward))

    def send_table():
        (came,), _ = yield [(tables, TM, swap_pairs(TM, 0))]
        first = lax.axis_index(TM) == 0
        return jnp.where(first, tables, came), jnp.where(first, came, tables)

    wide = fc1_weight.shape[2]
    first = pack_first(
        qkv_weight, ln1_gain, ln1_bias, qv_bias, out_bias, ln2_gain, ln2_bias, fc2_bias, fc1_bias
    )
    flow.start(FIRST, gather_flow(first, one))
    tables = pos_table.transpose(0, 2, 1)
    flow.start(TABLES, send_table())
    mid, down = stepped(
        pack_weights, pack_mid_kernel, (wide + width, wide), out_weight, fc1_weight, fc2_weight
    )
    tables = flow.finish(TABLES)
    flow.start(MID, gather_flow(mid, one))
    flow.start(DOWN, gather_flow(down, two))
    bias0 = [stepped(table_to_bias, tables[n][0]) for n in range(2)]
    (later,) = stepped(
        pack_weights, pack_later_kernel, (2 * wide + 4 * width,),
        qkv_weight, out_weight, fc1_weight, fc2_weight, names=(FIRST,),
    )
    later = lax.all_gather(later, ALL, axis=0, tiled=True)
    first = flow.finish(FIRST)
    vec = stepped(vectors_whole, first)
    w_qkv = ((first, 0), (later, 8))

    stream0 = clips_in.reshape(flat)
    qkv0 = stepped(run_qkv, stream0, vec[0], w_qkv[0], names=())
    att0, log0 = [None, None], [None, None]
    for n in range(2):
        att0[n], log0[n] = stepped(run_attend, qkv0, bias0[n], flags, False, n * groups_here)
    mid = flow.finish(MID)
    weights = (
        ((mid, 4), (mid, 0), (flow.finish(DOWN), 0)),
        ((later, 11), (later, 0), (later, 1)),
    )
    mid0, hid0, slope0, stream1 = stepped(run_branch, stream0, att0, vec[0], weights[0], F32)
    halo_start(ROLL, halo_pack(stream1, halo, True, center=True), True)
    table1 = jnp.concatenate([tables[0][1], tables[1][1]], axis=0)
    bias1 = [stepped(table_to_bias, table1)]
    rolled1 = halo_unpack(
        stream1, flow.finish(ROLL), halo, True, F32, center=True, after=Order(bias1)
    )
    qkv1 = run_qkv(rolled1, vec[1], w_qkv[1])
    grad_in = out_grad.reshape(flat)
    halo_start(GRAD, halo_pack(grad_in, halo, True, after=Order([qkv1])), True)
    att1, log1 = stepped(run_attend, qkv1, bias1[0], flags, True, 0)
    mid1, hid1, slope1, rolled_out = stepped(
        run_branch, rolled1, [att1], vec[1], weights[1], F32, waits=flow.done[GRAD]
    )
    halo_start(OUT, halo_pack(rolled_out, halo, False), False)
    grad = stepped(halo_unpack, grad_in, flow.done[GRAD], halo, True, BF16, names=())

    kept = (
        (stream0, qkv0, att0, log0, mid0, hid0, slope0, bias0),
        (rolled1, qkv1, [att1], [log1], mid1, hid1, slope1, bias1),
    )
    tables = [None] * LAYERS
    for layer in reversed(range(LAYERS)):
        stream, qkv, att, log, mid, hid, slope, bias = kept[layer]
        grad_mid, grad_att, rest, *halves = stepped(
            run_branch_back, grad, mid, att, hid, slope, vec[layer], weights[layer], flags, layer == 0
        )
        if layer == 0:
            flow.start(D_MID, scatter_flow(*halves[:2], one))
            flow.start(D_TWO, scatter_flow(*halves[2:], two))
        else:
            mid_share1 = lax.psum_scatter(halves[0], ALL, scatter_dimension=0, tiled=True)
        grads, sums = [], []
        for n in range(len(att)):
            *parts, total = stepped(
                run_attend_back, qkv, grad_att, att[n], bias[n], flags, log[n],
                layer == 1, n * groups_here, waits=flow.done[OUT] if layer else (),
            )
            grads.append(parts)
            sums.append(total)
        grads = [part for group in zip(*grads) for part in group]
        grad_stream, *halves = stepped(
            run_qkv_back, grads, stream, grad_mid, vec[layer], w_qkv[layer], rest, flags,
            F32 if layer else BF16,
        )
        if layer:
            halo_start(BACK, halo_pack(grad_stream, halo, False), False)
        flow.start(D_QKV + layer, scatter_flow(*halves, one))
        found = [stepped(sums_to_table, total) for total in sums]
        tables[layer] = jnp.split(found[0], 2) if len(found) == 1 else found
        if layer:
            grad = stepped(
                halo_unpack, grad_stream, flow.finish(BACK), halo, False, F32, names=(),
                waits=found,
            )
    in_grad = grad_stream
    pairs = [jnp.stack([tables[layer][n] for layer in range(LAYERS)]) for n in range(2)]
    flow.start(TABLE, table_flow(pairs, heads_here))
    clips_out = stepped(
        halo_unpack, rolled_out, flow.done[OUT], halo, False, BF16, mean_of=stream1
    )
    while flow.live:
        flow.step(None)
    grads = run_finish(
        [flow.done[D_QKV + layer] for layer in range(LAYERS)],
        flow.done[D_MID],
        flow.done[D_TWO],
        mid_share1,
    )
    return (
        clips_out.reshape(clips_in.shape),
        in_grad.reshape(clips_in.shape),
        *grads,
        flow.done[TABLE].transpose(0, 2, 1),
    )


def windows_are_local(mesh):
    def decide(clips_in, *rest):
        clips, frames_here = clips_in.shape[:2]
        own = rest[0].shape[1]
        return (
            clips == 1
            and frames_here % WIN_T == 0
            and own == 16
            and mesh.shape[TM] == 2
            and mesh.shape[SPACE] == 4
        )

    def program(*args):
        return local_windows(*args) if decide(*args) else per_device(*args)

    return program


def solution(mesh):
    placed = (
        P(CLIP, TM, SPACE, None, None),
        P(None, ALL),
        P(None, ALL),
        P(None, ALL, None),
        P(None, ALL),
        P(None, ALL, None),
        P(None, ALL),
        P(None, ALL),
        P(None, ALL),
        P(None, ALL, None),
        P(None, ALL),
        P(None, ALL, None),
        P(None, ALL),
        P(None, None, TM),
        P(CLIP, TM, SPACE, None, None),
    )
    return jax.shard_map(
        windows_are_local(mesh),
        mesh=mesh,
        in_specs=placed,
        out_specs=(
            P(CLIP, TM, SPACE, None, None),
            P(CLIP, TM, SPACE, None, None),
            P(None, ALL),
            P(None, ALL),
            P(None, ALL, None),
            P(None, ALL),
            P(None, ALL, None),
            P(None, ALL),
            P(None, ALL),
            P(None, ALL),
            P(None, ALL, None),
            P(None, ALL),
            P(None, ALL, None),
            P(None, ALL),
            P(None, None, TM),
        ),
        check_vma=False,
    )
```

```python
import functools
import math

import jax
import jax.numpy as jnp
import numpy as np
from jax import lax
from jax.experimental import pallas as pl
from jax.experimental.pallas import tpu as pltpu
from jax.sharding import PartitionSpec as P

HEADS = 16
WIN_T = 8
WIN_HW = 7
LAYERS = 2


masked_score = -1000000000.0
TM, SPACE, CLIP = "tm", "space", "clip"
ALL = (TM, SPACE, CLIP)


def partner(value, axis, bit):
    mask = 2**bit
    pairs = [(source, source ^ mask) for source in range(lax.axis_size(axis))]
    return lax.ppermute(value, axis, pairs)


def norm_rows(values, gain, offset):
    mean_row = jnp.mean(values, axis=-1, keepdims=True)
    centered = values - mean_row
    spread = jnp.mean(centered * centered, axis=-1, keepdims=True)
    return centered * lax.rsqrt(spread + 1e-05) * gain + offset


def gelu_exact(values):
    return jax.nn.gelu(values, approximate=False)


def project(left, right):
    return jnp.einsum("...i,ij->...j", left, right, preferred_element_type=jnp.float32)


def project_back(left, right):
    return jnp.einsum("...j,ij->...i", left, right, preferred_element_type=jnp.float32)


def outer_sum(left, right):
    flat_left = left.reshape(-1, left.shape[-1])
    flat_right = right.reshape(-1, right.shape[-1])
    return jnp.einsum("ti,tj->ij", flat_left, flat_right, preferred_element_type=jnp.float32)


def column_sum(values):
    return jnp.sum(values.reshape(-1, values.shape[-1]).astype(jnp.float32), axis=0)


def relative_index(win_t, win_hw):
    count = win_t * win_hw * win_hw
    positions = jnp.arange(count, dtype=jnp.int32)
    frame_pos = positions // (win_hw * win_hw)
    row_pos = positions // win_hw % win_hw
    col_pos = positions % win_hw
    span = 2 * win_hw - 1
    frame_off = frame_pos[:, None] - frame_pos[None, :] + win_t - 1
    row_off = row_pos[:, None] - row_pos[None, :] + win_hw - 1
    col_off = col_pos[:, None] - col_pos[None, :] + win_hw - 1
    return frame_off * span * span + row_off * span + col_off


def band_label(coord, extent, window, reach):
    return jnp.where(coord < extent - window, 0, jnp.where(coord < extent - reach, 1, 2)).astype(
        jnp.int32
    )


def region_match(frames):
    quadrant = lax.axis_index(SPACE)
    row_quad = quadrant // 2
    col_quad = quadrant % 2
    local = jnp.arange(WIN_HW, dtype=jnp.int32)
    label_t = band_label(jnp.arange(frames, dtype=jnp.int32), frames, WIN_T, WIN_T // 2)
    label_r = band_label(row_quad * WIN_HW + local, 2 * WIN_HW, WIN_HW, WIN_HW // 2)
    label_c = band_label(col_quad * WIN_HW + local, 2 * WIN_HW, WIN_HW, WIN_HW // 2)
    region = label_t[:, None, None] * 9 + label_r[None, :, None] * 3 + label_c[None, None, :]
    region = region.reshape(frames // WIN_T, WIN_T * WIN_HW * WIN_HW)
    return region[:, :, None] == region[:, None, :]


def space_roll(field, onward):
    side = field.shape[2]
    reach = side // 2
    sent_rows = field[:, :, :reach] if onward else field[:, :, side - reach :]
    came_rows = partner(sent_rows, SPACE, 1)
    if onward:
        rows_done = jnp.concatenate([field, came_rows], axis=2)[:, :, reach : reach + side]
    else:
        rows_done = jnp.concatenate([came_rows, field], axis=2)[:, :, :side]
    sent_cols = rows_done[:, :, :, :reach] if onward else rows_done[:, :, :, side - reach :]
    came_cols = partner(sent_cols, SPACE, 0)
    if onward:
        return jnp.concatenate([rows_done, came_cols], axis=3)[:, :, :, reach : reach + side]
    return jnp.concatenate([came_cols, rows_done], axis=3)[:, :, :, :side]


def gather_layer(shards, layer):
    return tuple(lax.all_gather(w[layer], ALL, axis=0, tiled=True) for w in shards)


def table_bias(table):
    rel = relative_index(WIN_T, WIN_HW)
    return table.astype(jnp.float32)[rel].transpose(2, 0, 1)


def window_scores(queries, keys, bias, same, scale):
    scores = (
        jnp.einsum("wqhd,wkhd->whqk", queries, keys, preferred_element_type=jnp.float32) * scale
        + bias[None]
    )
    if same is not None:
        scores = jnp.where(same[:, None], scores, masked_score)
    return scores


def to_windows(field):
    clips, frames, cells, heads_here, head_size = field.shape
    return field.reshape(clips, frames // WIN_T, WIN_T * cells, heads_here, head_size)


def to_frames(field, frames):
    clips = field.shape[0]
    return field.reshape(clips, frames, WIN_HW * WIN_HW, field.shape[3], field.shape[4])


def layer_forward(stream, params, table, shifted):
    (
        gain_one,
        bias_one,
        mix_weight,
        mix_bias,
        proj_weight,
        proj_bias,
        gain_two,
        bias_two,
        wide_weight,
        wide_bias,
        narrow_weight,
        narrow_bias,
    ) = params
    clips, frames_here, side = (stream.shape[0], stream.shape[1], stream.shape[2])
    width = stream.shape[-1]
    head_size = width // HEADS
    scale = head_size ** (-0.5)
    normed = norm_rows(stream, gain_one.astype(jnp.float32), bias_one.astype(jnp.float32)).astype(
        jnp.bfloat16
    )
    if shifted:
        normed = space_roll(normed, True)
    mixed = project(normed, mix_weight)
    mix_bias32 = mix_bias.astype(jnp.float32)
    head_shape = (clips, frames_here, side * side, HEADS, head_size)
    queries = (mixed[..., :width] + mix_bias32[:width]).astype(jnp.bfloat16).reshape(head_shape)
    keys = mixed[..., width : 2 * width].astype(jnp.bfloat16).reshape(head_shape)
    values = (mixed[..., 2 * width :] + mix_bias32[width:]).astype(jnp.bfloat16).reshape(head_shape)
    queries, keys, values = (
        lax.all_to_all(queries, TM, split_axis=3, concat_axis=1, tiled=True),
        lax.all_to_all(keys, TM, split_axis=3, concat_axis=1, tiled=True),
        lax.all_to_all(values, TM, split_axis=3, concat_axis=1, tiled=True),
    )
    frames = queries.shape[1]
    if shifted:
        queries = jnp.roll(queries, -(WIN_T // 2), axis=1)
        keys = jnp.roll(keys, -(WIN_T // 2), axis=1)
        values = jnp.roll(values, -(WIN_T // 2), axis=1)
    queries, keys, values = (to_windows(queries), to_windows(keys), to_windows(values))
    bias = table_bias(table)
    same = region_match(frames) if shifted else None

    def attend_clip(items):
        clip_queries, clip_keys, clip_values = items
        scores = window_scores(clip_queries, clip_keys, bias, same, scale)
        peak = jnp.max(scores, axis=-1, keepdims=True)
        raised = jnp.exp(scores - peak)
        total = jnp.sum(raised, axis=-1, keepdims=True)
        probs = (raised / total).astype(jnp.bfloat16)
        out_win = jnp.einsum(
            "whqk,wkhd->wqhd", probs, clip_values, preferred_element_type=jnp.float32
        ).astype(jnp.bfloat16)
        return (out_win, peak + jnp.log(total))

    attended_heads, log_total = lax.map(attend_clip, (queries, keys, values))
    attended_heads = to_frames(attended_heads, frames)
    if shifted:
        attended_heads = jnp.roll(attended_heads, WIN_T // 2, axis=1)
    attended = lax.all_to_all(attended_heads, TM, split_axis=1, concat_axis=3, tiled=True)
    attended = attended.reshape(clips, frames_here, side, side, width)
    if shifted:
        attended = space_roll(attended, False)
    middle = stream + project(attended, proj_weight) + proj_bias.astype(jnp.float32)
    normed_two = norm_rows(
        middle, gain_two.astype(jnp.float32), bias_two.astype(jnp.float32)
    ).astype(jnp.bfloat16)
    hidden_pre = project(normed_two, wide_weight) + wide_bias.astype(jnp.float32)
    hidden = gelu_exact(hidden_pre).astype(jnp.bfloat16)
    after = middle + project(hidden, narrow_weight) + narrow_bias.astype(jnp.float32)
    stash = (
        stream,
        normed,
        queries,
        keys,
        values,
        log_total,
        attended,
        middle,
        normed_two,
        hidden_pre,
        hidden,
    )
    return (stash, after)


def layer_backward(grad_after, params, table, stash, shifted):
    (
        gain_one,
        bias_one,
        mix_weight,
        mix_bias,
        proj_weight,
        proj_bias,
        gain_two,
        bias_two,
        wide_weight,
        wide_bias,
        narrow_weight,
        narrow_bias,
    ) = params
    (
        stream,
        normed,
        queries,
        keys,
        values,
        log_total,
        attended,
        middle,
        normed_two,
        hidden_pre,
        hidden,
    ) = stash
    clips, frames_here, side = (stream.shape[0], stream.shape[1], stream.shape[2])
    width = stream.shape[-1]
    head_size = width // HEADS
    scale = head_size ** (-0.5)
    frames = queries.shape[1] * WIN_T
    grad_branch_two = grad_after.astype(jnp.bfloat16)
    narrow_grad = outer_sum(hidden, grad_branch_two)
    narrow_bias_grad = column_sum(grad_branch_two)
    grad_hidden = project_back(grad_branch_two, narrow_weight)
    gelu_pull = jax.vjp(gelu_exact, hidden_pre)[1]
    grad_pre = gelu_pull(grad_hidden)[0].astype(jnp.bfloat16)
    wide_grad = outer_sum(normed_two, grad_pre)
    wide_bias_grad = column_sum(grad_pre)
    grad_normed_two = project_back(grad_pre, wide_weight)
    norm_pull_two = jax.vjp(
        norm_rows, middle, gain_two.astype(jnp.float32), bias_two.astype(jnp.float32)
    )[1]
    grad_mid_part, gain_two_grad, bias_two_grad = norm_pull_two(grad_normed_two)
    grad_middle = grad_after + grad_mid_part
    grad_branch_one = grad_middle.astype(jnp.bfloat16)
    proj_grad = outer_sum(attended, grad_branch_one)
    proj_bias_grad = column_sum(grad_branch_one)
    grad_attended = project_back(grad_branch_one, proj_weight).astype(jnp.bfloat16)
    if shifted:
        grad_attended = space_roll(grad_attended, True)
    grad_attended = grad_attended.reshape(clips, frames_here, side * side, HEADS, head_size)
    grad_attended = lax.all_to_all(grad_attended, TM, split_axis=3, concat_axis=1, tiled=True)
    if shifted:
        grad_attended = jnp.roll(grad_attended, -(WIN_T // 2), axis=1)
    grad_attended = to_windows(grad_attended)
    bias = table_bias(table)
    same = region_match(frames) if shifted else None

    def attend_back(carry, items):
        clip_queries, clip_keys, clip_values, clip_grad, clip_log = items
        scores = window_scores(clip_queries, clip_keys, bias, same, scale)
        probs = jnp.exp(scores - clip_log)
        grad_probs = jnp.einsum(
            "wqhd,wkhd->whqk", clip_grad, clip_values, preferred_element_type=jnp.float32
        )
        inner = jnp.sum(probs * grad_probs, axis=-1, keepdims=True)
        grad_scores = (probs * (grad_probs - inner)).astype(jnp.bfloat16)
        grad_q = (
            jnp.einsum(
                "whqk,wkhd->wqhd", grad_scores, clip_keys, preferred_element_type=jnp.float32
            )
            * scale
        ).astype(jnp.bfloat16)
        grad_k = (
            jnp.einsum(
                "whqk,wqhd->wkhd", grad_scores, clip_queries, preferred_element_type=jnp.float32
            )
            * scale
        ).astype(jnp.bfloat16)
        grad_v = jnp.einsum(
            "whqk,wqhd->wkhd",
            probs.astype(jnp.bfloat16),
            clip_grad,
            preferred_element_type=jnp.float32,
        ).astype(jnp.bfloat16)
        carry = carry + jnp.sum(grad_scores.astype(jnp.float32), axis=0)
        return (carry, (grad_q, grad_k, grad_v))

    window_tokens = queries.shape[2]
    start_bias = jnp.zeros((queries.shape[3], window_tokens, window_tokens), jnp.float32)
    bias_grad, grads_win = lax.scan(
        attend_back, start_bias, (queries, keys, values, grad_attended, log_total)
    )
    grad_q, grad_k, grad_v = (to_frames(g, frames) for g in grads_win)
    if shifted:
        grad_q = jnp.roll(grad_q, WIN_T // 2, axis=1)
        grad_k = jnp.roll(grad_k, WIN_T // 2, axis=1)
        grad_v = jnp.roll(grad_v, WIN_T // 2, axis=1)
    grad_q, grad_k, grad_v = (
        lax.all_to_all(grad_q, TM, split_axis=1, concat_axis=3, tiled=True),
        lax.all_to_all(grad_k, TM, split_axis=1, concat_axis=3, tiled=True),
        lax.all_to_all(grad_v, TM, split_axis=1, concat_axis=3, tiled=True),
    )
    token_shape = (clips, frames_here, side, side, width)
    grad_q, grad_k, grad_v = (
        grad_q.reshape(token_shape),
        grad_k.reshape(token_shape),
        grad_v.reshape(token_shape),
    )
    grad_mix = jnp.concatenate([grad_q, grad_k, grad_v], axis=-1)
    mix_grad = outer_sum(normed, grad_mix)
    mix_bias_grad = jnp.concatenate([column_sum(grad_q), column_sum(grad_v)])
    grad_normed = project_back(grad_mix, mix_weight)
    if shifted:
        grad_normed = space_roll(grad_normed.astype(jnp.bfloat16), False).astype(jnp.float32)
    norm_pull_one = jax.vjp(
        norm_rows, stream, gain_one.astype(jnp.float32), bias_one.astype(jnp.float32)
    )[1]
    grad_stream_part, gain_one_grad, bias_one_grad = norm_pull_one(grad_normed)
    grad_stream = grad_middle + grad_stream_part
    rel = relative_index(WIN_T, WIN_HW).reshape(-1)
    table_grad = (
        jnp.zeros(table.shape, jnp.float32).at[rel].add(bias_grad.reshape(bias_grad.shape[0], -1).T)
    )
    weight_grads = (
        gain_one_grad,
        bias_one_grad,
        mix_grad,
        mix_bias_grad,
        proj_grad,
        proj_bias_grad,
        gain_two_grad,
        bias_two_grad,
        wide_grad,
        wide_bias_grad,
        narrow_grad,
        narrow_bias_grad,
    )
    return (grad_stream, weight_grads, table_grad)


def per_device(
    clips_in,
    ln1_gain,
    ln1_bias,
    qkv_weight,
    qv_bias,
    out_weight,
    out_bias,
    ln2_gain,
    ln2_bias,
    fc1_weight,
    fc1_bias,
    fc2_weight,
    fc2_bias,
    pos_table,
    out_grad,
):
    clips, frames_here, quads, cells, width = clips_in.shape
    grid_shape = (clips, frames_here, WIN_HW, WIN_HW, width)
    shards = (
        ln1_gain,
        ln1_bias,
        qkv_weight,
        qv_bias,
        out_weight,
        out_bias,
        ln2_gain,
        ln2_bias,
        fc1_weight,
        fc1_bias,
        fc2_weight,
        fc2_bias,
    )
    stream = clips_in.astype(jnp.float32).reshape(grid_shape)
    kept_params = []
    kept_stash = []
    for layer in range(LAYERS):
        params = gather_layer(shards, layer)
        stash, stream = layer_forward(stream, params, pos_table[layer], layer % 2 == 1)
        kept_params.append(params)
        kept_stash.append(stash)
    clips_out = stream.astype(jnp.bfloat16).reshape(clips_in.shape)
    grad_stream = out_grad.astype(jnp.float32).reshape(grid_shape)
    layer_shares = [None] * LAYERS
    table_parts = [None] * LAYERS
    for layer in reversed(range(LAYERS)):
        params = gather_layer(shards, layer)
        grad_stream, weight_grads, table_grad = layer_backward(
            grad_stream, params, pos_table[layer], kept_stash[layer], layer % 2 == 1
        )
        layer_shares[layer] = tuple(
            lax.psum_scatter(g, ALL, scatter_dimension=0, tiled=True) for g in weight_grads
        )
        table_parts[layer] = table_grad
    in_grad = grad_stream.astype(jnp.bfloat16).reshape(clips_in.shape)
    table_total = lax.psum(jnp.stack(table_parts), (SPACE, CLIP))
    stacked = tuple(
        (jnp.stack([layer_shares[n][slot] for n in range(LAYERS)]) for slot in range(12))
    )
    return (
        clips_out,
        in_grad,
        stacked[0],
        stacked[1],
        stacked[2],
        stacked[3],
        stacked[4],
        stacked[5],
        stacked[6],
        stacked[7],
        stacked[8],
        stacked[9],
        stacked[10],
        stacked[11],
        table_total,
    )


F32 = jnp.float32
BF16 = jnp.bfloat16
TOKENS = WIN_T * WIN_HW * WIN_HW
CELLS = WIN_HW * WIN_HW
SPAN = 2 * WIN_HW - 1
STEPS = 2 * WIN_T - 1
LOG2E = math.log2(math.e)
VMEM_BYTES = 56 * 1024 * 1024


def mm(left, right, left_dim=1, right_dim=0):
    dims = (((left_dim,), (right_dim,)), ((), ()))
    return lax.dot_general(left, right, dims, preferred_element_type=F32)


class Order:
    def __init__(self, waits=()):
        self.waits = list(waits)
        self.token = None


def call(
    kernel, grid, in_specs, out_specs, out_shape, flops, scratch=(), after=None, aliases=None
):
    waits = after.waits if after else []
    inputs = len(in_specs)
    single = not isinstance(out_shape, list)
    out_specs = [out_specs] if single else list(out_specs)
    out_shape = [out_shape] if single else list(out_shape)
    outputs = len(out_shape)
    if after:
        out_specs.append(pl.BlockSpec(memory_space=pltpu.SMEM))
        out_shape.append(jax.ShapeDtypeStruct((1, 1), F32))

    def body(*refs):
        ins, outs = refs[:inputs], refs[inputs + len(waits) :]
        if after:
            outs[outputs][0, 0] = 0.0
        kernel(*ins, *outs[:outputs], *outs[len(out_shape) :])

    run = pl.pallas_call(
        body,
        grid=grid,
        in_specs=list(in_specs) + [pl.BlockSpec(memory_space=pl.ANY)] * len(waits),
        out_specs=out_specs,
        out_shape=out_shape,
        scratch_shapes=scratch,
        input_output_aliases=aliases or {},
        cost_estimate=pl.CostEstimate(
            flops=int(flops), transcendentals=0, bytes_accessed=8 * 1024 * 1024
        ),
        compiler_params=pltpu.CompilerParams(vmem_limit_bytes=VMEM_BYTES),
    )

    def result(*args):
        found = run(*args, *waits)
        if after:
            after.token = found[outputs]
        return found[0] if single else found[:outputs]

    return result


def whole_block(shape):
    return pl.BlockSpec(shape, lambda *ids: (0,) * len(shape))


def flag_spec():
    return pl.BlockSpec(memory_space=pltpu.SMEM)


def win_block(width, column=0):
    return pl.BlockSpec((1, TOKENS, width), lambda w: (w, 0, column))


HALF = WIN_T // 2 * CELLS
KINDS = range(1, 8)


class Halo:
    def __init__(self):
        token = np.arange(HALF)
        row, col = token // WIN_HW % WIN_HW, token % WIN_HW
        reach = WIN_HW // 2
        target = token - row * WIN_HW - col
        target = target + (row - reach) % WIN_HW * WIN_HW + (col - reach) % WIN_HW
        leaves = (row < reach) * 2 + (col < reach) * 1
        self.stay = np.zeros((HALF, HALF), np.float32)
        stays = leaves == 0
        self.stay[target[stays], token[stays]] = 1
        self.near, self.near_to = self.ways(leaves, target, (1, 2, 3))
        self.far, self.far_to = self.ways(leaves, target, (0, 1, 2, 3))

    @staticmethod
    def ways(leaves, target, kinds):
        send, place = [], []
        for kind in kinds:
            source = np.nonzero(leaves == kind)[0]
            rows = 64 if kind == 0 else 48
            out, back = np.zeros((rows, HALF), np.float32), np.zeros((HALF, rows), np.float32)
            out[np.arange(len(source)), source] = 1
            back[target[source], np.arange(len(source))] = 1
            send.append(out)
            place.append(back)
        return np.concatenate(send, 0), np.concatenate(place, 1)

    def sends(self, onward):
        return (self.near, self.far) if onward else (self.near_to.T, self.far_to.T)

    def places(self, onward):
        if onward:
            return self.stay, self.near_to, self.far_to
        return self.stay.T, self.near.T, self.far.T


def half_at(half):
    return half // 2, slice(half % 2 * HALF, (half % 2 + 1) * HALF)


class Flow:
    def __init__(self, flags):
        self.flags = flags
        self.live = []
        self.done = {}

    def start(self, name, task):
        self.live.append((name, task, task.sends() if isinstance(task, Gather) else next(task)))

    def pending(self):
        return [value for _, _, sends in self.live for value, _, _ in sends]

    def step(self, token, names=None):
        live, gathers = [], []
        for name, task, sends in self.live:
            if names is not None and name not in names:
                live.append((name, task, sends))
                continue
            came = [lax.ppermute(value, axis, pairs) for value, axis, pairs in sends]
            if isinstance(task, Gather):
                if len(task.steps) > 1:
                    gathers.append((name, task, came[0]))
                else:
                    self.done[name] = task.last(came[0])
                continue
            try:
                live.append((name, task, task.send((came, token))))
            except StopIteration as end:
                self.done[name] = end.value
        if gathers:
            merge([t for _, t, _ in gathers], [c for _, _, c in gathers], self.flags, token)
        live += [(name, task, task.sends()) for name, task, _ in gathers]
        self.live = live

    def finish(self, name):
        while name not in self.done:
            self.step(None, (name,))
        return self.done[name]


def swap_pairs(axis, bit):
    return [(source, source ^ 2**bit) for source in range(lax.axis_size(axis))]


def halo_flow(packed, onward):
    ring, quads = lax.axis_size(TM), lax.axis_size(SPACE)
    sends = []
    for kind, piece in zip(KINDS, packed):
        step = 0 if not kind & 4 else (-1 if onward else 1)
        pairs = []
        for frame_at in range(ring):
            for quad in range(quads):
                to = (frame_at + step) % ring * quads + (quad ^ (kind & 3))
                pairs.append((frame_at * quads + quad, to))
        sends.append((piece, (TM, SPACE), pairs))
    came, _ = yield sends
    return came


def pack_kernel(center, onward, near_ref, far_ref, x_ref, *refs):
    out_refs, flat_ref = refs[:-1], refs[-1]
    halves = 2 * x_ref.shape[0]
    for w in range(x_ref.shape[0]):
        x = x_ref[w].astype(F32)
        if center:
            x = x - jnp.mean(x, axis=-1, keepdims=True)
        flat_ref[w] = x
    for n in range(halves - 1):
        w, rows = half_at(n + 1 if onward else n)
        sent = mm(near_ref[...], flat_ref[w, rows].astype(BF16)).astype(BF16)
        for kind in range(3):
            out_refs[kind][n * 48 : (n + 1) * 48] = sent[kind * 48 : (kind + 1) * 48]
    w, rows = half_at(0 if onward else halves - 1)
    sent = mm(far_ref[...], flat_ref[w, rows].astype(BF16)).astype(BF16)
    for kind in range(4):
        first = 0 if kind == 0 else 16 + 48 * kind
        out_refs[3 + kind][...] = sent[first : first + out_refs[3 + kind].shape[0]]


def part_rows(windows):
    return [48 * (2 * windows - 1)] * 3 + [64, 48, 48, 48]


def halo_pack(x, halo, onward, center=False, joined=False, after=None):
    windows, _, width = x.shape
    near, far = (jnp.asarray(m, BF16) for m in halo.sends(onward))
    rows = part_rows(windows)

    def kernel(near_ref, far_ref, x_ref, *refs):
        if joined:
            refs = [refs[0].at[pl.ds(sum(rows[:n]), rows[n])] for n in range(7)] + [refs[1]]
        pack_kernel(center, onward, near_ref, far_ref, x_ref, *refs)

    shapes = [(sum(rows), width)] if joined else [(n, width) for n in rows]
    out = functools.partial(call, after=after)(
        kernel,
        (1,),
        [whole_block(m.shape) for m in (near, far, x)],
        [whole_block(shape) for shape in shapes],
        [jax.ShapeDtypeStruct(shape, BF16) for shape in shapes],
        2 * 640 * HALF * width,
        [pltpu.VMEM(x.shape, F32)],
    )(near, far, x)
    return out[0] if joined else out


def halo_gather(packed):
    return lax.all_gather(packed, (TM, SPACE), axis=0, tiled=True)


def halo_senders(onward):
    ring, quads = lax.axis_size(TM), lax.axis_size(SPACE)
    senders = []
    for kind in KINDS:
        step = 0 if not kind & 4 else (1 if onward else -1)
        frame_at = (lax.axis_index(TM) + step + ring) % ring
        senders.append(frame_at * quads + lax.axis_index(SPACE) ^ (kind & 3))
    return jnp.stack([jnp.asarray(n, jnp.int32) for n in senders])


def unpack_kernel(center, onward, add_mean, stay_ref, near_ref, far_ref, x_ref, *refs):
    base_ref, refs = (refs[0], refs[1:]) if add_mean else (None, refs)
    came_refs, (out_ref, flat_ref, total_ref) = refs[:7], refs[7:]
    windows = x_ref.shape[0]
    halves = 2 * windows
    for w in range(windows):
        x = x_ref[w].astype(F32)
        if center:
            x = x - jnp.mean(x, axis=-1, keepdims=True)
        flat_ref[w] = x
    for n in range(halves - 1):
        w, rows = half_at(n + 1 if onward else n)
        x = flat_ref[w, rows]
        high = x.astype(BF16)
        total = mm(stay_ref[...], high)
        if x_ref.dtype == F32:
            total = total + mm(stay_ref[...], (x - high.astype(F32)).astype(BF16))
        came = jnp.concatenate([ref[n * 48 : (n + 1) * 48] for ref in came_refs[:3]], axis=0)
        w, rows = half_at(n if onward else n + 1)
        total_ref[w, rows] = total + mm(near_ref[...], came)
    came = jnp.concatenate([ref[...] for ref in came_refs[3:]], axis=0)
    w, rows = half_at(halves - 1 if onward else 0)
    total_ref[w, rows] = mm(far_ref[...], came)
    for w in range(windows):
        total = total_ref[w]
        if add_mean:
            total = total + jnp.mean(base_ref[w], axis=-1, keepdims=True)
        out_ref[w] = total.astype(out_ref.dtype)


def halo_unpack(x, came, halo, onward, dtype, center=False, mean_of=None, after=None):
    places = [jnp.asarray(m, BF16) for m in halo.places(onward)]
    operands = places + [x] + ([] if mean_of is None else [mean_of])
    joined = not isinstance(came, list)
    senders = [halo_senders(onward)] if joined else []
    operands += [came] if joined else came
    rows = part_rows(x.shape[0])

    def kernel(*refs):
        if joined:
            sender_ref, refs = refs[0], refs[1:]
            count = len(operands)
            parts = []
            for n in range(7):
                first = sender_ref[n] * sum(rows) + sum(rows[:n])
                parts.append(refs[count - 1].at[pl.ds(pl.multiple_of(first, 16), rows[n])])
            refs = refs[: count - 1] + tuple(parts) + refs[count:]
        unpack_kernel(center, onward, mean_of is not None, *refs)

    return functools.partial(call, after=after)(
        kernel,
        (1,),
        [flag_spec()] * joined + [whole_block(v.shape) for v in operands],
        whole_block(x.shape),
        jax.ShapeDtypeStruct(x.shape, dtype),
        8 * x.size * HALF,
        [pltpu.VMEM(x.shape, F32), pltpu.VMEM(x.shape, F32)],
    )(*senders, *operands)


def index_bits():
    bits = []
    for axis in ALL:
        count = lax.axis_size(axis).bit_length() - 1
        bits += [(axis, b) for b in reversed(range(count))]
    return bits


def bit_of(axis, bit):
    return (lax.axis_index(axis) // 2**bit) % 2


def stage_orders():
    bits = index_bits()
    inner = [(CLIP, 0)] if lax.axis_size(CLIP) > 1 else []
    tm = [b for b in bits if b[0] == TM]
    clip = [b for b in bits if b[0] == CLIP and b not in inner]
    space = [b for b in reversed(bits) if b[0] == SPACE]
    return inner + tm + clip + space, inner + clip + tm + space


class Gather:
    def __init__(self, shard, order):
        self.bits, self.steps = index_bits(), list(reversed(order))
        self.dims = [1] * len(self.bits)
        self.rows, self.out = shard.shape[0], shard

    def sends(self):
        axis, bit = self.steps[0]
        return [(self.out, axis, swap_pairs(axis, bit))]

    def split(self):
        dim = self.bits.index(self.steps.pop(0))
        before, after = math.prod(self.dims[:dim]), math.prod(self.dims[dim + 1 :])
        self.dims[dim] = 2
        return before, after * self.rows, 4 + dim

    def last(self, came):
        here = bit_of(*self.steps[0])
        before, after, _ = self.split()
        own, came = (v.reshape(before, 1, after, -1) for v in (self.out, came))
        pair = [jnp.concatenate(p, axis=1) for p in ((own, came), (came, own))]
        return jnp.where(here == 1, pair[1], pair[0]).reshape(-1, own.shape[-1])


def merge_kernel(places, flag_ref, *refs):
    for n, place in enumerate(places):
        own_ref, came_ref, out_ref = refs[2 * n], refs[2 * n + 1], refs[2 * len(places) + n]
        here = flag_ref[place]
        out_ref[:, here] = own_ref[...]
        out_ref[:, 1 - here] = came_ref[...]


def merge(tasks, came, flags, token):
    places, operands, shapes = [], [], []
    for task, piece in zip(tasks, came):
        before, after, place = task.split()
        width = piece.shape[-1]
        places.append(place)
        operands += [v.reshape(before, after, width) for v in (task.out, piece)]
        shapes.append(jax.ShapeDtypeStruct((before, 2, after, width), BF16))
    found = call(
        functools.partial(merge_kernel, places),
        (1,),
        [flag_spec()] + [whole_block(v.shape) for v in operands],
        [whole_block(v.shape) for v in shapes],
        shapes,
        1e6,
        after=None if token is None else Order([token]),
    )(flags, *operands)
    for task, out in zip(tasks, found):
        task.out = out.reshape(-1, out.shape[-1])


def scatter_flow(own, sent, order):
    bits = index_bits()
    width = own.shape[-1]
    dims = [2] * len(bits)
    own, sent = own.reshape(-1, width), sent.reshape(-1, width)
    for n, (axis, bit) in enumerate(order):
        (came,), token = yield [(sent, axis, swap_pairs(axis, bit))]
        dims[bits.index((axis, bit))] = 1
        zero = 0.0 if token is None else token.reshape(())
        if n + 1 == len(order):
            return own + came.astype(F32)
        axis, bit = order[n + 1]
        dim = bits.index((axis, bit))
        here = bit_of(axis, bit)
        own, came = (v.reshape(dims + [-1, width]) for v in (own, came))

        def half(index):
            mine, theirs = (lax.dynamic_slice_in_dim(v, index, 1, dim) for v in (own, came))
            return (mine + theirs.astype(F32) + zero).reshape(-1, width)

        own, sent = half(here), half(1 - here).astype(BF16)


def table_flow(tables, heads_here):
    first = lax.axis_index(TM) == 0
    mine = jnp.where(first, tables[0], tables[1])
    (came,), _ = yield [(jnp.where(first, tables[1], tables[0]), TM, swap_pairs(TM, 0))]
    table = mine + came
    for axis, bit in index_bits():
        if axis != TM:
            (came,), _ = yield [(table, axis, swap_pairs(axis, bit))]
            table = table + came
    return table


WIDE = 768


def column_pick():
    pick = np.zeros((WIN_HW, 256, 128), np.float32)
    for key_col in range(WIN_HW):
        for row in range(SPAN):
            for col in range(WIN_HW):
                entry = row * SPAN + col - key_col + WIN_HW - 1
                pick[key_col, entry, row * WIN_HW + col] = 1
    return pick


def lane_spans(step):
    first, rest = divmod(step * CELLS, 128)
    if rest + CELLS <= 128:
        return [(first, rest, rest + CELLS)]
    return [(first, rest, 128), (first + 1, 0, rest + CELLS - 128)]


def bias_kernel(slab_ref, pick_ref, out_ref, row_ref, wide_ref):
    heads = pl.num_programs(0)

    @pl.when(pl.program_id(0) == 0)
    def _():
        slabs = slab_ref[...]
        for col in range(WIN_HW):
            row_ref[pl.ds(col, slabs.shape[0], stride=8), :] = mm(slabs, pick_ref[col]) * LOG2E

    base = pl.program_id(0) * 128
    lane = lax.broadcasted_iota(jnp.int32, (8, 128), 1)
    for row in range(WIN_HW):
        tiles = [jnp.zeros((8, 128), F32) for _ in range(WIDE // 128)]
        for step in range(STEPS):
            rows = row_ref[pl.ds(pl.multiple_of(base + step * 8, 8), 8), :]
            turn = (step * CELLS - WIN_HW * (WIN_HW - 1 - row)) % 128
            rows = pltpu.roll(rows, turn, 1) if turn else rows
            for tile, low, high in lane_spans(step):
                tiles[tile] = jnp.where((lane >= low) & (lane < high), rows, tiles[tile])
        wide_ref[row * WIN_HW : (row + 1) * WIN_HW, :] = jnp.concatenate(tiles, axis=1)[:WIN_HW]
    wide = wide_ref[:CELLS, :]
    for key_frame in range(WIN_T):
        turned = pltpu.roll(wide, (WIDE - (WIN_T - 1 - key_frame) * CELLS) % WIDE, 1)
        out_ref[0, key_frame * CELLS : (key_frame + 1) * CELLS, :] = turned[:, :TOKENS]


def table_to_bias(tables, rest=None, after=None):
    heads = tables.shape[0]
    slabs = tables.reshape(heads, STEPS, SPAN * SPAN)
    slabs = jnp.pad(slabs, ((0, 0), (0, 16 - STEPS), (0, 256 - SPAN * SPAN)))
    slabs = slabs.reshape(heads * 16, 256)
    held = [] if rest is None else [rest]
    first = 0 if rest is None else heads

    def kernel(slab_ref, pick_ref, *refs):
        bias_kernel(slab_ref, pick_ref, *refs[len(held) :])

    return functools.partial(call, after=after, aliases={2: 0} if held else {})(
        kernel,
        (heads,),
        [whole_block(slabs.shape), whole_block((WIN_HW, 256, 128))]
        + [pl.BlockSpec(memory_space=pl.ANY)] * len(held),
        pl.BlockSpec((1, TOKENS, TOKENS), lambda h: (first + h, 0, 0)),
        jax.ShapeDtypeStruct((2 * heads, TOKENS, TOKENS), F32),
        heads * 500_000_000,
        [pltpu.VMEM((heads * 128, 128), F32), pltpu.VMEM((56, WIDE), F32)],
    )(slabs, jnp.asarray(column_pick(), BF16), *held)


def table_back_kernel(sums_ref, pick_ref, out_ref, row_ref):
    head = pl.program_id(0)
    lane = lax.broadcasted_iota(jnp.int32, (WIN_HW, 128), 1)
    totals = [None] * STEPS
    for row in range(WIN_HW):
        rows = sums_ref[0, row * WIN_HW : (row + 1) * WIN_HW, :]
        start = WIN_HW * (WIN_HW - 1 - row)
        for step in range(STEPS):
            turn = (start - step * CELLS) % 128
            piece = None
            for tile, low, high in lane_spans(step):
                part = rows[:, tile * 128 : (tile + 1) * 128]
                part = jnp.where((lane >= low) & (lane < high), part, 0.0)
                piece = part if piece is None else piece + part
            piece = pltpu.roll(piece, turn, 1) if turn else piece
            totals[step] = piece if totals[step] is None else totals[step] + piece
    blank = jnp.zeros((1, 128), F32)
    for step in range(16):
        rows = jnp.concatenate([totals[step], blank]) if step < STEPS else jnp.zeros((8, 128), F32)
        row_ref[pl.ds(pl.multiple_of(head * 128 + step * 8, 8), 8), :] = rows

    @pl.when(head == pl.num_programs(0) - 1)
    def _():
        total = None
        for col in range(WIN_HW):
            rows = row_ref[pl.ds(col, out_ref.shape[0], stride=8), :]
            high = rows.astype(BF16)
            low = (rows - high.astype(F32)).astype(BF16)
            part = mm(high, pick_ref[col], 1, 1) + mm(low, pick_ref[col], 1, 1)
            total = part if total is None else total + part
        out_ref[...] = total


def sums_to_table(sums, after=None):
    heads = sums.shape[0]
    slabs = functools.partial(call, after=after)(
        table_back_kernel,
        (heads,),
        [pl.BlockSpec((1, CELLS, WIDE), lambda h: (h, 0, 0)), whole_block((WIN_HW, 256, 128))],
        whole_block((heads * 16, 256)),
        jax.ShapeDtypeStruct((heads * 16, 256), F32),
        heads * 300_000_000,
        [pltpu.VMEM((heads * 128, 128), F32)],
    )(sums, jnp.asarray(column_pick(), BF16))
    return slabs.reshape(heads, 16, 256)[:, :STEPS, : SPAN * SPAN].reshape(heads, -1)


def unit_rows(x):
    centered = x - jnp.mean(x, axis=-1, keepdims=True)
    inverse = lax.rsqrt(jnp.mean(centered * centered, axis=-1, keepdims=True) + 1e-05)
    return centered * inverse, inverse


def norm_back(grad, unit, inverse, gain):
    scaled = grad * gain
    return inverse * (
        scaled
        - jnp.mean(scaled, axis=-1, keepdims=True)
        - unit * jnp.mean(scaled * unit, axis=-1, keepdims=True)
    )


def qkv_kernel(x_ref, vec_ref, wq_ref, wk_ref, wv_ref, out_ref):
    width = x_ref.shape[-1]
    unit, _ = unit_rows(x_ref[0].astype(F32))
    normed = (unit * vec_ref[0:1] + vec_ref[1:2]).astype(BF16)
    for part, ref in enumerate((wq_ref, wk_ref, wv_ref)):
        out = mm(normed, ref[...])
        if part == 0:
            out = out + vec_ref[2:3]
        if part == 2:
            out = out + vec_ref[3:4]
        out_ref[0, :, part * width : (part + 1) * width] = out.astype(BF16)


def run_qkv(x, vec, w_qkv, after=None):
    windows, _, width = x.shape
    weight, at = w_qkv
    return functools.partial(call, after=after)(
        qkv_kernel,
        (windows,),
        [win_block(width), whole_block(vec.shape)]
        + [weight_block(width, width, at + n) for n in range(3)],
        win_block(3 * width),
        jax.ShapeDtypeStruct((windows, TOKENS, 3 * width), BF16),
        2 * windows * TOKENS * width * 3 * width,
    )(x, vec, weight, weight, weight)


GROUP = 4


def head_masks(head_size):
    lane = lax.broadcasted_iota(jnp.int32, (1, GROUP * head_size), 1)
    return [
        jnp.where((lane >= h * head_size) & (lane < (h + 1) * head_size), 1.0, 0.0).astype(BF16)
        for h in range(GROUP)
    ]


def region_labels(flag_ref, late_ref, turned_ref, at_end):
    flags = [flag_ref[1 + n].astype(F32) for n in range(3)]
    flags[0] = flags[0] * at_end
    col = sum(flags[n] * late_ref[:, n : n + 1] for n in range(3))
    return col, sum(flags[n] * turned_ref[n : n + 1, :] for n in range(3))


def late_tokens():
    token = np.arange(TOKENS)
    late = np.zeros((TOKENS, 8), np.float32)
    late[:, 0] = 4 * (token // CELLS >= WIN_T - WIN_T // 2)
    late[:, 1] = 2 * (token // WIN_HW % WIN_HW >= WIN_HW - WIN_HW // 2)
    late[:, 2] = token % WIN_HW >= WIN_HW - WIN_HW // 2
    return late


def attend_kernel(
    shifted, head_size, flag_ref, q_ref, k_ref, v_ref, bias_ref, late_ref, turned_ref, out_ref, log_ref
):
    q, k = q_ref[0], k_ref[0]
    if shifted:
        at_end = jnp.where(pl.program_id(1) == pl.num_programs(1) - 1, 1.0, 0.0)
        col, row = region_labels(flag_ref, late_ref, turned_ref, at_end)
    turned = v_ref[0].astype(F32).T.astype(BF16)
    factor = head_size**-0.5 * LOG2E
    masks = head_masks(head_size)
    outs, logs = [], []
    for h in range(GROUP):
        scores = mm(k * masks[h], q, 1, 1) * factor + bias_ref[h]
        if shifted:
            scores = jnp.where(col == row, scores, masked_score)
        peak = jnp.max(scores, axis=0, keepdims=True)
        raised = jnp.exp2(scores - peak)
        total = jnp.sum(raised, axis=0, keepdims=True)
        mixed = mm(turned[h * head_size : (h + 1) * head_size], raised.astype(BF16))
        outs.append(mixed / total)
        logs.append(peak + jnp.log2(total))
    out_ref[0] = jnp.concatenate(outs, axis=0).T.astype(BF16)
    log_ref[0, 0] = jnp.concatenate(logs + logs, axis=0)


def run_attend(qkv, bias, flags, shifted, after=None):
    windows, _, width3 = qkv.shape
    width = width3 // 3
    wide = GROUP * (width // HEADS)
    groups = HEADS // GROUP
    qkv_specs = [
        pl.BlockSpec((1, TOKENS, wide), lambda g, w, p=part: (w, 0, p * groups + g))
        for part in range(3)
    ]
    return functools.partial(call, after=after)(
        functools.partial(attend_kernel, shifted, width // HEADS),
        (groups, windows),
        [flag_spec()]
        + qkv_specs
        + [
            pl.BlockSpec((GROUP, TOKENS, TOKENS), lambda g, w: (g, 0, 0)),
            whole_block((TOKENS, 8)),
            whole_block((8, TOKENS)),
        ],
        [
            pl.BlockSpec((1, TOKENS, wide), lambda g, w: (w, 0, g)),
            pl.BlockSpec((1, 1, 2 * GROUP, TOKENS), lambda g, w: (w, g, 0, 0)),
        ],
        [
            jax.ShapeDtypeStruct((windows, TOKENS, width), BF16),
            jax.ShapeDtypeStruct((windows, groups, 2 * GROUP, TOKENS), F32),
        ],
        64 * windows * TOKENS * TOKENS * width,
    )(flags, qkv, qkv, qkv, bias, late_tokens(), late_tokens().T)


def attend_back_kernel(
    shifted, head_size, flag_ref, q_ref, k_ref, v_ref, g_ref, o_ref, bias_ref, late_ref, turned_ref,
    log_ref, dq_ref, dk_ref, dv_ref, table_ref, sum_ref,
):
    windows = q_ref.shape[0]
    if shifted:
        labels = [
            region_labels(flag_ref, late_ref, turned_ref, float(w == windows - 1))
            for w in range(windows)
        ]
    scale = head_size**-0.5
    factor = scale * LOG2E
    masks = head_masks(head_size)

    @pl.when(pl.program_id(0) == 0)
    def _():
        sum_ref[...] = jnp.zeros_like(sum_ref)

    turned, weighed = [], []
    for w in range(windows):
        turned.append(k_ref[w].astype(F32).T.astype(BF16))
        weighed.append(g_ref[w].astype(F32).T * o_ref[w].astype(F32).T)
    grad_q = [[] for _ in range(windows)]
    grad_k, grad_v = [None] * windows, [None] * windows
    for h in range(GROUP):
        here = slice(h * head_size, (h + 1) * head_size)
        total = None
        for w in range(windows):
            q, k, v, g = q_ref[w], k_ref[w], v_ref[w], g_ref[w]
            inner = jnp.sum(weighed[w][here], axis=0, keepdims=True)
            scores = mm(k * masks[h], q, 1, 1) * factor + bias_ref[h]
            if shifted:
                scores = jnp.where(labels[w][0] == labels[w][1], scores, masked_score)
            probs = jnp.exp2(scores - log_ref[w, 0, h : h + 1])
            grad_probs = mm(v * masks[h], g, 1, 1)
            grad_scores = (probs * (grad_probs - inner)).astype(BF16)
            part_v = mm(probs.astype(BF16), g * masks[h])
            part_k = mm(grad_scores, q * masks[h])
            grad_v[w] = part_v if grad_v[w] is None else grad_v[w] + part_v
            grad_k[w] = part_k if grad_k[w] is None else grad_k[w] + part_k
            grad_q[w].append(mm(turned[w][here], grad_scores))
            wide = grad_scores.astype(F32)
            total = wide if total is None else total + wide
        sum_ref[:, :TOKENS] = total
        sums = None
        for key_frame in range(WIN_T):
            rows = sum_ref[key_frame * CELLS : (key_frame + 1) * CELLS, :]
            step = (WIN_T - 1 - key_frame) * CELLS
            rows = pltpu.roll(rows, step, 1) if step else rows
            sums = rows if sums is None else sums + rows
        table_ref[h] = sums
    for w in range(windows):
        dq_ref[w] = (jnp.concatenate(grad_q[w], axis=0) * scale).T.astype(BF16)
        dk_ref[w] = (grad_k[w] * scale).astype(BF16)
        dv_ref[w] = grad_v[w].astype(BF16)


def run_attend_back(qkv, grad, attended, bias, flags, log, shifted, first, count, after=None):
    windows, _, width3 = qkv.shape
    width = width3 // 3
    wide = GROUP * (width // HEADS)
    groups = HEADS // GROUP
    qkv_specs = [
        pl.BlockSpec((windows, TOKENS, wide), lambda g, p=part: (0, 0, p * groups + first + g))
        for part in range(3)
    ]
    flat = pl.BlockSpec((windows, TOKENS, wide), lambda g: (0, 0, g))
    flat_shape = jax.ShapeDtypeStruct((windows, TOKENS, count * wide), BF16)
    return functools.partial(call, after=after)(
        functools.partial(attend_back_kernel, shifted, width // HEADS),
        (count,),
        [flag_spec()]
        + qkv_specs
        + [
            pl.BlockSpec((windows, TOKENS, wide), lambda g: (0, 0, first + g)),
            pl.BlockSpec((windows, TOKENS, wide), lambda g: (0, 0, first + g)),
            pl.BlockSpec((GROUP, TOKENS, TOKENS), lambda g: (first + g, 0, 0)),
            whole_block((TOKENS, 8)),
            whole_block((8, TOKENS)),
            pl.BlockSpec((windows, 1, 2 * GROUP, TOKENS), lambda g: (0, first + g, 0, 0)),
        ],
        [flat, flat, flat, pl.BlockSpec((GROUP, CELLS, WIDE), lambda g: (g, 0, 0))],
        [flat_shape] * 3 + [jax.ShapeDtypeStruct((count * GROUP, CELLS, WIDE), F32)],
        160 * windows * TOKENS * TOKENS * count * wide,
        [pltpu.VMEM((TOKENS, WIDE), F32)],
    )(flags, qkv, qkv, qkv, grad, attended, bias, late_tokens(), late_tokens().T, log)


def normal_below(x):
    bell = jnp.exp2(x * x * (-0.5 * LOG2E)) * (1.0 / math.sqrt(2 * math.pi))
    return 0.5 + 0.5 * lax.erf(x * math.sqrt(0.5)), bell


def spread_down(down_ref, w2_ref):
    _, parts, own, width = w2_ref.shape
    for part in range(parts):
        cols = slice(part * width, (part + 1) * width)
        w2_ref[:, part] = down_ref[:, cols].reshape(-1, own, width)


def chunk_rows(w2_ref, first, chunk):
    _, parts, own, width = w2_ref.shape
    step = chunk // (parts * own)
    return w2_ref[first * step : (first + 1) * step].reshape(chunk, width)


def branch_kernel(count, *refs):
    att_refs = refs[:count]
    x_ref, vec_ref, wo_ref, w1_ref, down_ref, mid_ref, hid_ref, slope_ref, out_ref, w2_ref = refs[count:]

    @pl.when(pl.program_id(0) == 0)
    def _():
        spread_down(down_ref, w2_ref)

    chunk = 512
    attended = jnp.concatenate([ref[0] for ref in att_refs], axis=1)
    middle = x_ref[0].astype(F32) + mm(attended, wo_ref[...]) + vec_ref[4:5]
    mid_ref[0] = middle
    unit, _ = unit_rows(middle)
    normed = (unit * vec_ref[5:6] + vec_ref[6:7]).astype(BF16)
    after = middle + vec_ref[7:8]
    for n in range(w1_ref.shape[1] // chunk):
        cols = slice(n * chunk, (n + 1) * chunk)
        pre = mm(normed, w1_ref[:, cols]) + vec_ref[8 + n : 9 + n]
        below, bell = normal_below(pre)
        hidden = (pre * below).astype(BF16)
        hid_ref[0, :, cols] = hidden
        slope_ref[0, :, cols] = (below + pre * bell).astype(BF16)
        after = after + mm(hidden, chunk_rows(w2_ref, n, chunk))
    out_ref[0] = after.astype(out_ref.dtype)


def weight_block(rows, width, column):
    return pl.BlockSpec((rows, width), lambda *ids: (0, column))


def branch_weights(weights, width, wide):
    (wo, wo_at), (w1, w1_at), (down, down_at) = weights
    specs = [
        weight_block(width, width, wo_at),
        weight_block(width, wide, w1_at),
        weight_block(width, wide, down_at),
    ]
    return (wo, w1, down), specs


def run_branch(x, attended, vec, weights, out_dtype, after=None):
    windows, _, width = x.shape
    wide = 4 * width
    arrays, specs = branch_weights(weights, width, wide)
    return functools.partial(call, after=after)(
        functools.partial(branch_kernel, len(attended)),
        (windows,),
        [win_block(part.shape[-1]) for part in attended]
        + [win_block(width), whole_block(vec.shape)]
        + specs,
        [win_block(width), win_block(wide), win_block(wide), win_block(width)],
        [
            jax.ShapeDtypeStruct((windows, TOKENS, width), F32),
            jax.ShapeDtypeStruct((windows, TOKENS, wide), BF16),
            jax.ShapeDtypeStruct((windows, TOKENS, wide), BF16),
            jax.ShapeDtypeStruct((windows, TOKENS, width), out_dtype),
        ],
        2 * windows * TOKENS * width * (width + 2 * wide),
        [pltpu.VMEM((width // 16, wide // width, 16, width), BF16)],
    )(*attended, x, vec, *arrays)


def add_rows(ref, rows, value):
    ref[rows, :] += jnp.sum(value.astype(F32), axis=0, keepdims=True)


def split_out(sums_ref, core, own_ref, sent_ref):
    own_ref[...] = sums_ref[:, core]
    sent_ref[...] = sums_ref[:, 1 - core].astype(BF16)


def branch_back_kernel(count, split, flag_ref, *refs):
    att_refs = refs[:count]
    grad_ref, mid_ref, hid_ref, slope_ref, vec_ref, wo_ref, w1_ref, down_ref = refs[count : count + 8]
    gm_ref, ga_ref, vecs_ref = refs[count + 8 : count + 11]
    outs, (d1_ref, d2_ref, w2_ref) = refs[count + 11 : -3], refs[-3:]
    chunk = 512
    width, wide = w1_ref.shape

    @pl.when(pl.program_id(0) == 0)
    def _():
        spread_down(down_ref, w2_ref)
        d1_ref[...] = jnp.zeros_like(d1_ref)
        d2_ref[...] = jnp.zeros_like(d2_ref)
        vecs_ref[...] = jnp.zeros_like(vecs_ref)

    grad = grad_ref[0].astype(F32)
    branch = grad.astype(BF16)
    unit, inverse = unit_rows(mid_ref[0])
    normed = (unit * vec_ref[5:6] + vec_ref[6:7]).astype(BF16)
    add_rows(vecs_ref, slice(7, 8), branch)
    back = None
    blocks = chunk // d2_ref.shape[2]
    for n in range(wide // chunk):
        cols = slice(n * chunk, (n + 1) * chunk)
        total = mm(hid_ref[0, :, cols], branch, 0, 0)
        at = slice(n * blocks // 2, (n + 1) * blocks // 2)
        d2_ref[at] += total.reshape((-1,) + d2_ref.shape[1:])
        grad_pre = mm(branch, chunk_rows(w2_ref, n, chunk), 1, 1) * slope_ref[0, :, cols].astype(F32)
        grad_pre = grad_pre.astype(BF16)
        add_rows(vecs_ref, slice(8 + n, 9 + n), grad_pre)
        d1_ref[:, :, :, cols] += mm(normed, grad_pre, 0, 0).reshape(d1_ref.shape[:3] + (chunk,))
        part = mm(grad_pre, w1_ref[:, cols], 1, 1)
        back = part if back is None else back + part
    add_rows(vecs_ref, slice(5, 6), back * unit)
    add_rows(vecs_ref, slice(6, 7), back)
    middle_grad = grad + norm_back(back, unit, inverse, vec_ref[5:6])
    gm_ref[0] = middle_grad
    branch = middle_grad.astype(BF16)
    add_rows(vecs_ref, slice(4, 5), branch)
    attended = jnp.concatenate([ref[0] for ref in att_refs], axis=1)
    total = mm(attended, branch, 0, 0)
    d1_ref[:, :, :, wide:] += total.reshape(d1_ref.shape[:3] + (width,))
    ga_ref[0] = mm(branch, wo_ref[...], 1, 1).astype(BF16)

    @pl.when(pl.program_id(0) == pl.num_programs(0) - 1)
    def _():
        if split:
            split_out(d1_ref, flag_ref[0], *outs[:2])
            split_out(d2_ref, flag_ref[0], *outs[2:])
        else:
            (out_ref,) = outs
            out_ref[:, : wide + width] = d1_ref[...].reshape(width, -1).astype(BF16)
            parts = wide // width
            for part in range(parts):
                first = wide + width + part * width
                piece = d2_ref[:, :, part * 16 : (part + 1) * 16, :].reshape(width, width)
                out_ref[:, first : first + width] = piece.astype(BF16)


def run_branch_back(grad, middle, attended, hidden, slope, vec, weights, flags, split, after=None):
    windows, _, width = middle.shape
    wide = 4 * width
    arrays, specs = branch_weights(weights, width, wide)
    flat = win_block(width)
    pairs = width // 32
    if split:
        shapes = []
        for rows, cols in ((16, wide + width), (64, width)):
            shapes.append(jax.ShapeDtypeStruct((pairs, rows, cols), F32))
            shapes.append(jax.ShapeDtypeStruct((pairs, rows, cols), BF16))
    else:
        shapes = [jax.ShapeDtypeStruct((width, 2 * wide + width), BF16)]
    return functools.partial(call, after=after)(
        functools.partial(branch_back_kernel, len(attended), split),
        (windows,),
        [flag_spec()]
        + [win_block(part.shape[-1]) for part in attended]
        + [flat, flat, win_block(wide), win_block(wide), whole_block(vec.shape)]
        + specs,
        [flat, flat, whole_block(vec.shape)] + [whole_block(s.shape) for s in shapes],
        [
            jax.ShapeDtypeStruct((windows, TOKENS, width), F32),
            jax.ShapeDtypeStruct((windows, TOKENS, width), BF16),
            jax.ShapeDtypeStruct(vec.shape, F32),
        ]
        + shapes,
        4 * windows * TOKENS * width * (width + 2 * wide),
        [
            pltpu.VMEM((pairs, 2, 16, wide + width), F32),
            pltpu.VMEM((pairs, 2, 64, width), F32),
            pltpu.VMEM((pairs * 2, wide // width, 16, width), BF16),
        ],
    )(flags, *attended, grad, middle, hidden, slope, vec, *arrays)


def qkv_back_kernel(count, flag_ref, *refs):
    grads, refs = refs[: 3 * count], refs[3 * count :]
    x_ref, gm_ref, vec_ref, wq_ref, wk_ref, wv_ref, rest_ref, mask_ref, pick_ref, spread_ref = refs[:10]
    out_ref, own_ref, sent_ref, dw_ref, vecs_ref = refs[10:]
    width = x_ref.shape[-1]

    @pl.when(pl.program_id(0) == 0)
    def _():
        dw_ref[...] = jnp.zeros_like(dw_ref)
        vecs_ref[...] = rest_ref[...]

    unit, inverse = unit_rows(x_ref[0].astype(F32))
    normed = (unit * vec_ref[0:1] + vec_ref[1:2]).astype(BF16)
    back = None
    for part, ref in enumerate((wq_ref, wk_ref, wv_ref)):
        grad = jnp.concatenate([g[0] for g in grads[part * count : (part + 1) * count]], axis=1)
        total = mm(normed, grad, 0, 0)
        cols = slice(part * width, (part + 1) * width)
        dw_ref[:, :, :, cols] += total.reshape(dw_ref.shape[:3] + (width,))
        here = mm(grad, ref[...], 1, 1)
        back = here if back is None else back + here
        if part == 0:
            add_rows(vecs_ref, slice(2, 3), grad)
        if part == 2:
            add_rows(vecs_ref, slice(3, 4), grad)
    add_rows(vecs_ref, slice(0, 1), back * unit)
    add_rows(vecs_ref, slice(1, 2), back)
    out_ref[0] = (gm_ref[0] + norm_back(back, unit, inverse, vec_ref[0:1])).astype(out_ref.dtype)

    @pl.when(pl.program_id(0) == pl.num_programs(0) - 1)
    def _():
        rows = vecs_ref[...]
        high = rows.astype(BF16)
        low = (rows - high.astype(F32)).astype(BF16)
        total = None
        for piece in (high, low):
            piece = (mm(pick_ref[...], piece, 0, 0) * mask_ref[...].astype(F32)).astype(BF16)
            piece = mm(piece, spread_ref[0], 1, 1)
            total = piece if total is None else total + piece
        dw_ref[:, :, :, 3 * width :] = total.reshape(dw_ref.shape[:3] + (128,))
        split_out(dw_ref, flag_ref[0], own_ref, sent_ref)


def run_qkv_back(grads, x, grad_middle, vec, w_qkv, rest, flags, out_dtype, after=None):
    windows, _, width = x.shape
    flat = win_block(width)
    weight, at = w_qkv
    extra = [jnp.asarray(a, BF16) for a in vector_slots()]
    shape = (width // 32, 16, 3 * width + 128)
    return functools.partial(call, after=after)(
        functools.partial(qkv_back_kernel, len(grads) // 3),
        (windows,),
        [flag_spec()]
        + [win_block(part.shape[-1]) for part in grads]
        + [flat, flat, whole_block(vec.shape)]
        + [weight_block(width, width, at + n) for n in range(3)]
        + [whole_block(rest.shape)]
        + [whole_block(a.shape) for a in extra],
        [flat, whole_block(shape), whole_block(shape)],
        [
            jax.ShapeDtypeStruct((windows, TOKENS, width), out_dtype),
            jax.ShapeDtypeStruct(shape, F32),
            jax.ShapeDtypeStruct(shape, BF16),
        ],
        4 * windows * TOKENS * width * 3 * width,
        [pltpu.VMEM((shape[0], 2) + shape[1:], F32), pltpu.VMEM(rest.shape, F32)],
    )(flags, *grads, x, grad_middle, vec, weight, weight, weight, rest, *extra)


def pack_first_kernel(qkv_ref, *refs):
    vector_refs, (first_ref, rows_ref) = refs[:-2], refs[-2:]
    own, width3 = qkv_ref.shape[1:]
    rows_ref[...] = jnp.zeros_like(rows_ref)
    row = 0
    lane = lax.broadcasted_iota(jnp.int32, (1, 128), 1)
    for ref in vector_refs:
        values = ref[...].astype(F32)
        values = jnp.pad(values, ((0, 0), (0, 128 - values.shape[1])))
        for part in range(ref.shape[1] // own):
            line = jnp.zeros((1, 128), F32)
            for layer in range(LAYERS):
                turn = ((layer - part) * own) % 128
                turned = pltpu.roll(values, turn, 1) if turn else values
                here = (lane >= layer * own) & (lane < (layer + 1) * own)
                line = jnp.where(here, turned[layer : layer + 1], line)
            rows_ref[row : row + 1, :] = line
            row += 1
    first_ref[:, :width3] = qkv_ref[0]
    first_ref[:, width3:] = rows_ref[...].astype(BF16)


def pack_first(qkv, *vectors, after=None):
    own, width3 = qkv.shape[1:]
    return functools.partial(call, after=after)(
        pack_first_kernel,
        (1,),
        [whole_block((1, own, width3))] + [whole_block(v.shape) for v in vectors],
        whole_block((own, width3 + 128)),
        jax.ShapeDtypeStruct((own, width3 + 128), BF16),
        1e6,
        [pltpu.VMEM((16, 128), F32)],
    )(qkv, *vectors)


def pack_branch_kernel(layer, out_ref, fc1_ref, fc2_ref, packed_ref):
    own, width, wide = fc1_ref.shape[1], fc2_ref.shape[2], fc1_ref.shape[2]
    packed_ref[:, :wide] = fc1_ref[layer]
    for part in range(wide // width):
        first = wide + part * width
        packed_ref[:, first : first + width] = fc2_ref[layer, part * own : (part + 1) * own, :]
    packed_ref[:, 2 * wide :] = out_ref[layer]


def gather_branch(layer, weights, after=None):
    own, wide = weights[1].shape[1:]
    width = weights[0].shape[2]
    packed = jax.ShapeDtypeStruct((own, 2 * wide + width), BF16)
    shard = functools.partial(call, after=after)(
        functools.partial(pack_branch_kernel, layer),
        (1,),
        [whole_block(w.shape) for w in weights],
        whole_block(packed.shape),
        packed,
        1e6,
    )(*weights)
    whole = lax.all_gather(shard, ALL, axis=0, tiled=True)
    return ((whole, 2 * wide // width), (whole, 0), (whole, 1))


def vector_slots():
    devices, own = 32, 16
    count = devices * own
    mask = np.zeros((devices * 16, count), np.float32)
    pick = np.zeros((16, devices * 16), np.float32)
    spread = np.zeros((LAYERS, 128, count), np.float32)
    for device in range(devices):
        for first, parts in ((0, 1), (1, 1), (2, 2), (4, 1), (5, 1), (6, 1), (7, 1), (8, 4)):
            for part in range(parts):
                row, start = divmod(device * own * parts + part * own, count)
                slot = device * 16 + first + part
                pick[first + row, slot] = 1
                mask[slot, start : start + own] = 1
    for layer in range(LAYERS):
        for lane in range(count):
            spread[layer, layer * own + lane % own, lane] = 1
    return mask, pick, spread


def vectors_kernel(block_ref, mask_ref, pick_ref, spread_ref, out_ref):
    block = block_ref[...]
    for layer in range(LAYERS):
        lines = mm(block, spread_ref[layer]) * mask_ref[...].astype(F32)
        out_ref[layer] = mm(pick_ref[...], lines.astype(BF16))


def vectors_whole(blocks, after=None):
    count, width = blocks.shape
    extra = [jnp.asarray(a, BF16) for a in vector_slots()]
    return functools.partial(call, after=after)(
        vectors_kernel,
        (1,),
        [pl.BlockSpec((count, 128), lambda n: (0, width // 128 - 1))]
        + [whole_block(a.shape) for a in extra],
        whole_block((LAYERS, 16, count)),
        jax.ShapeDtypeStruct((LAYERS, 16, count), F32),
        1e9,
    )(blocks, *extra)


def finish_kernel(
    mix0_ref, mix1_ref, mid_ref, two_ref, later_ref, gain1_ref, bias1_ref, qkv_ref, qvb_ref, out_ref,
    outb_ref, gain2_ref, bias2_ref, fc1_ref, fc1b_ref, fc2_ref, fc2b_ref,
):
    width, wide = out_ref.shape[2], fc1_ref.shape[2]
    own = gain1_ref.shape[1]
    lane = lax.broadcasted_iota(jnp.int32, (1, 128), 1)
    for layer, mix_ref in enumerate((mix0_ref, mix1_ref)):
        qkv_ref[layer] = mix_ref[:, : 3 * width]
        row = 0
        for ref in (gain1_ref, bias1_ref, qvb_ref, outb_ref, gain2_ref, bias2_ref, fc2b_ref, fc1b_ref):
            line = jnp.zeros((1, 128), F32)
            for part in range(ref.shape[1] // own):
                piece = mix_ref[row : row + 1, 3 * width : 3 * width + 128]
                piece = pltpu.roll(piece, part * own, 1) if part else piece
                line = jnp.where((lane >= part * own) & (lane < (part + 1) * own), piece, line)
                row += 1
            ref[layer : layer + 1, :] = line[:, : ref.shape[1]]
    fc1_ref[0] = mid_ref[:, :wide]
    out_ref[0] = mid_ref[:, wide:]
    fc2_ref[0] = two_ref[...]
    fc1_ref[1] = later_ref[:, :wide].astype(F32)
    out_ref[1] = later_ref[:, wide : wide + width].astype(F32)
    for part in range(wide // width):
        first = wide + width + part * width
        piece = later_ref[:, first : first + width].astype(F32)
        fc2_ref[1, part * own : (part + 1) * own, :] = piece


def run_finish(mixes, mid, two, later):
    own, width = 16, two.shape[1]
    wide = mid.shape[1] - width
    shapes = [
        (own,), (own,), (own, 3 * width), (2 * own,), (own, width), (own,),
        (own,), (own,), (own, wide), (4 * own,), (4 * own, width), (own,),
    ]
    operands = [*mixes, mid, two, later]
    return call(
        finish_kernel,
        (1,),
        [whole_block(v.shape) for v in operands],
        [whole_block((LAYERS,) + shape) for shape in shapes],
        [jax.ShapeDtypeStruct((LAYERS,) + shape, F32) for shape in shapes],
        1e6,
    )(*operands)


def place_flags():
    quadrant = lax.axis_index(SPACE)
    last = lax.axis_index(TM) == lax.axis_size(TM) - 1
    flags = [lax.axis_index(CLIP) % 2, last, quadrant // 2, quadrant % 2]
    flags += [bit_of(axis, bit) for axis, bit in index_bits()]
    return jnp.stack([jnp.asarray(f, jnp.int32) for f in flags])


FIRST, TABLES, LATER, ROLL, GRAD, BACK, D_MID, D_TWO, TABLE, D_QKV = range(10)


def local_windows(
    clips_in,
    ln1_gain,
    ln1_bias,
    qkv_weight,
    qv_bias,
    out_weight,
    out_bias,
    ln2_gain,
    ln2_bias,
    fc1_weight,
    fc1_bias,
    fc2_weight,
    fc2_bias,
    pos_table,
    out_grad,
):
    _, frames_here, _, _, width = clips_in.shape
    windows = frames_here // WIN_T
    own = ln1_gain.shape[1]
    heads_here = pos_table.shape[2]
    one, two = stage_orders()
    flat = (windows, TOKENS, width)
    flags = place_flags()
    halo = Halo()
    flow = Flow(flags)

    def stepped(run, *args, names=None, waits=(), **options):
        order = Order(flow.pending() + list(waits))
        out = run(*args, after=order, **options)
        flow.step(order.token, names)
        return out

    def halo_start(name, packed, onward):
        flow.start(name, halo_flow(packed, onward))

    def send_table():
        (came,), _ = yield [(tables, TM, swap_pairs(TM, 0))]
        first = lax.axis_index(TM) == 0
        return jnp.where(first, tables, came), jnp.where(first, came, tables)

    branch = (out_weight, fc1_weight, fc2_weight)
    first = pack_first(
        qkv_weight, ln1_gain, ln1_bias, qv_bias, out_bias, ln2_gain, ln2_bias, fc2_bias, fc1_bias
    )
    flow.start(FIRST, Gather(first, one))
    tables = pos_table.transpose(0, 2, 1)
    flow.start(TABLES, send_table())
    weights0 = stepped(gather_branch, 0, branch)
    tables = flow.finish(TABLES)
    bias0 = stepped(table_to_bias, tables[0][0])
    bias0 = stepped(table_to_bias, tables[1][0], bias0)
    bias1 = stepped(table_to_bias, tables[0][1])
    first = flow.finish(FIRST)
    flow.start(LATER, Gather(qkv_weight[1], one))
    vec = stepped(vectors_whole, first)
    weights1 = gather_branch(1, branch, after=Order([vec]))

    stream0 = clips_in.reshape(flat)
    qkv0 = stepped(run_qkv, stream0, vec[0], (first, 0))
    att0, log0 = stepped(run_attend, qkv0, bias0, flags, False)
    grad_in = out_grad.reshape(flat)
    mid0, hid0, slope0, stream1 = stepped(run_branch, stream0, [att0], vec[0], weights0, F32)
    halo_start(ROLL, halo_pack(stream1, halo, True, center=True), True)
    bias1 = stepped(table_to_bias, tables[1][1], bias1)
    later = flow.finish(LATER)
    rolled1 = halo_unpack(
        stream1, flow.finish(ROLL), halo, True, F32, center=True, after=Order([bias1])
    )
    qkv1 = run_qkv(rolled1, vec[1], (later, 0))
    halo_start(GRAD, halo_pack(grad_in, halo, True, after=Order([qkv1])), True)
    att1, log1 = stepped(run_attend, qkv1, bias1, flags, True)
    mid1, hid1, slope1, rolled_out = stepped(
        run_branch, rolled1, [att1], vec[1], weights1, F32, waits=flow.done[GRAD]
    )
    out_parts = halo_gather(halo_pack(rolled_out, halo, False, joined=True))
    grad = stepped(halo_unpack, grad_in, flow.done[GRAD], halo, True, BF16, names=())

    kept = (
        (stream0, qkv0, att0, log0, mid0, hid0, slope0, bias0, weights0, (first, 0)),
        (rolled1, qkv1, att1, log1, mid1, hid1, slope1, bias1, weights1, (later, 0)),
    )
    tables = [None] * LAYERS
    for layer in reversed(range(LAYERS)):
        stream, qkv, att, log, mid, hid, slope, bias, weights, w_qkv = kept[layer]
        grad_mid, grad_att, rest, *halves = stepped(
            run_branch_back, grad, mid, [att], hid, slope, vec[layer], weights, flags, layer == 0
        )
        if layer == 0:
            flow.start(D_MID, scatter_flow(*halves[:2], one))
            flow.start(D_TWO, scatter_flow(*halves[2:], two))
        else:
            mid_share1 = lax.psum_scatter(halves[0], ALL, scatter_dimension=0, tiled=True)
        grads, sums = [], []
        calls = 1 if layer else 2
        groups = HEADS // GROUP // calls
        for n in range(calls):
            *parts, total = stepped(
                run_attend_back, qkv, grad_att, att, bias, flags, log, layer == 1, n * groups, groups,
            )
            grads.append(parts)
            sums.append(total)
        grads = [part for group in zip(*grads) for part in group]
        if layer == 0:
            tables[0] = [
                stepped(sums_to_table, total, names=names) for total, names in zip(sums, ((), None))
            ]
            pairs = [jnp.stack([tables[layer][n] for layer in range(LAYERS)]) for n in range(2)]
            flow.start(TABLE, table_flow(pairs, heads_here))
        grad_stream, *halves = stepped(
            run_qkv_back, grads, stream, grad_mid, vec[layer], w_qkv, rest, flags,
            F32 if layer else BF16,
        )
        if layer:
            halo_start(BACK, halo_pack(grad_stream, halo, False), False)
        flow.start(D_QKV + layer, scatter_flow(*halves, one))
        if layer:
            found = [stepped(sums_to_table, sums[0])]
            tables[1] = jnp.split(found[0], 2)
            grad = stepped(
                halo_unpack, grad_stream, flow.finish(BACK), halo, False, F32, names=(),
                waits=found,
            )
    in_grad = grad_stream
    clips_out = stepped(
        halo_unpack, rolled_out, out_parts, halo, False, BF16, mean_of=stream1
    )
    while flow.live:
        flow.step(None)
    grads = run_finish(
        [flow.done[D_QKV + layer] for layer in range(LAYERS)],
        flow.done[D_MID],
        flow.done[D_TWO],
        mid_share1,
    )
    return (
        clips_out.reshape(clips_in.shape),
        in_grad.reshape(clips_in.shape),
        *grads,
        flow.done[TABLE].transpose(0, 2, 1),
    )


def windows_are_local(mesh):
    def decide(clips_in, *rest):
        clips, frames_here = clips_in.shape[:2]
        own = rest[0].shape[1]
        return (
            clips == 1
            and frames_here % WIN_T == 0
            and own == 16
            and mesh.shape[TM] == 2
            and mesh.shape[SPACE] == 4
        )

    def program(*args):
        return local_windows(*args) if decide(*args) else per_device(*args)

    return program


def solution(mesh):
    placed = (
        P(CLIP, TM, SPACE, None, None),
        P(None, ALL),
        P(None, ALL),
        P(None, ALL, None),
        P(None, ALL),
        P(None, ALL, None),
        P(None, ALL),
        P(None, ALL),
        P(None, ALL),
        P(None, ALL, None),
        P(None, ALL),
        P(None, ALL, None),
        P(None, ALL),
        P(None, None, TM),
        P(CLIP, TM, SPACE, None, None),
    )
    return jax.shard_map(
        windows_are_local(mesh),
        mesh=mesh,
        in_specs=placed,
        out_specs=(
            P(CLIP, TM, SPACE, None, None),
            P(CLIP, TM, SPACE, None, None),
            P(None, ALL),
            P(None, ALL),
            P(None, ALL, None),
            P(None, ALL),
            P(None, ALL, None),
            P(None, ALL),
            P(None, ALL),
            P(None, ALL),
            P(None, ALL, None),
            P(None, ALL),
            P(None, ALL, None),
            P(None, ALL),
            P(None, None, TM),
        ),
        check_vma=False,
    )
```

```python
import functools
import math

import jax
import jax.numpy as jnp
import numpy as np
from jax import lax
from jax.experimental import pallas as pl
from jax.experimental.pallas import tpu as pltpu
from jax.sharding import PartitionSpec as P

HEADS = 16
WIN_T = 8
WIN_HW = 7
LAYERS = 2


masked_score = -1000000000.0
TM, SPACE, CLIP = "tm", "space", "clip"
ALL = (TM, SPACE, CLIP)


def partner(value, axis, bit):
    mask = 2**bit
    pairs = [(source, source ^ mask) for source in range(lax.axis_size(axis))]
    return lax.ppermute(value, axis, pairs)


def norm_rows(values, gain, offset):
    mean_row = jnp.mean(values, axis=-1, keepdims=True)
    centered = values - mean_row
    spread = jnp.mean(centered * centered, axis=-1, keepdims=True)
    return centered * lax.rsqrt(spread + 1e-05) * gain + offset


def gelu_exact(values):
    return jax.nn.gelu(values, approximate=False)


def project(left, right):
    return jnp.einsum("...i,ij->...j", left, right, preferred_element_type=jnp.float32)


def project_back(left, right):
    return jnp.einsum("...j,ij->...i", left, right, preferred_element_type=jnp.float32)


def outer_sum(left, right):
    flat_left = left.reshape(-1, left.shape[-1])
    flat_right = right.reshape(-1, right.shape[-1])
    return jnp.einsum("ti,tj->ij", flat_left, flat_right, preferred_element_type=jnp.float32)


def column_sum(values):
    return jnp.sum(values.reshape(-1, values.shape[-1]).astype(jnp.float32), axis=0)


def relative_index(win_t, win_hw):
    count = win_t * win_hw * win_hw
    positions = jnp.arange(count, dtype=jnp.int32)
    frame_pos = positions // (win_hw * win_hw)
    row_pos = positions // win_hw % win_hw
    col_pos = positions % win_hw
    span = 2 * win_hw - 1
    frame_off = frame_pos[:, None] - frame_pos[None, :] + win_t - 1
    row_off = row_pos[:, None] - row_pos[None, :] + win_hw - 1
    col_off = col_pos[:, None] - col_pos[None, :] + win_hw - 1
    return frame_off * span * span + row_off * span + col_off


def band_label(coord, extent, window, reach):
    return jnp.where(coord < extent - window, 0, jnp.where(coord < extent - reach, 1, 2)).astype(
        jnp.int32
    )


def region_match(frames):
    quadrant = lax.axis_index(SPACE)
    row_quad = quadrant // 2
    col_quad = quadrant % 2
    local = jnp.arange(WIN_HW, dtype=jnp.int32)
    label_t = band_label(jnp.arange(frames, dtype=jnp.int32), frames, WIN_T, WIN_T // 2)
    label_r = band_label(row_quad * WIN_HW + local, 2 * WIN_HW, WIN_HW, WIN_HW // 2)
    label_c = band_label(col_quad * WIN_HW + local, 2 * WIN_HW, WIN_HW, WIN_HW // 2)
    region = label_t[:, None, None] * 9 + label_r[None, :, None] * 3 + label_c[None, None, :]
    region = region.reshape(frames // WIN_T, WIN_T * WIN_HW * WIN_HW)
    return region[:, :, None] == region[:, None, :]


def space_roll(field, onward):
    side = field.shape[2]
    reach = side // 2
    sent_rows = field[:, :, :reach] if onward else field[:, :, side - reach :]
    came_rows = partner(sent_rows, SPACE, 1)
    if onward:
        rows_done = jnp.concatenate([field, came_rows], axis=2)[:, :, reach : reach + side]
    else:
        rows_done = jnp.concatenate([came_rows, field], axis=2)[:, :, :side]
    sent_cols = rows_done[:, :, :, :reach] if onward else rows_done[:, :, :, side - reach :]
    came_cols = partner(sent_cols, SPACE, 0)
    if onward:
        return jnp.concatenate([rows_done, came_cols], axis=3)[:, :, :, reach : reach + side]
    return jnp.concatenate([came_cols, rows_done], axis=3)[:, :, :, :side]


def gather_layer(shards, layer):
    return tuple(lax.all_gather(w[layer], ALL, axis=0, tiled=True) for w in shards)


def table_bias(table):
    rel = relative_index(WIN_T, WIN_HW)
    return table.astype(jnp.float32)[rel].transpose(2, 0, 1)


def window_scores(queries, keys, bias, same, scale):
    scores = (
        jnp.einsum("wqhd,wkhd->whqk", queries, keys, preferred_element_type=jnp.float32) * scale
        + bias[None]
    )
    if same is not None:
        scores = jnp.where(same[:, None], scores, masked_score)
    return scores


def to_windows(field):
    clips, frames, cells, heads_here, head_size = field.shape
    return field.reshape(clips, frames // WIN_T, WIN_T * cells, heads_here, head_size)


def to_frames(field, frames):
    clips = field.shape[0]
    return field.reshape(clips, frames, WIN_HW * WIN_HW, field.shape[3], field.shape[4])


def layer_forward(stream, params, table, shifted):
    (
        gain_one,
        bias_one,
        mix_weight,
        mix_bias,
        proj_weight,
        proj_bias,
        gain_two,
        bias_two,
        wide_weight,
        wide_bias,
        narrow_weight,
        narrow_bias,
    ) = params
    clips, frames_here, side = (stream.shape[0], stream.shape[1], stream.shape[2])
    width = stream.shape[-1]
    head_size = width // HEADS
    scale = head_size ** (-0.5)
    normed = norm_rows(stream, gain_one.astype(jnp.float32), bias_one.astype(jnp.float32)).astype(
        jnp.bfloat16
    )
    if shifted:
        normed = space_roll(normed, True)
    mixed = project(normed, mix_weight)
    mix_bias32 = mix_bias.astype(jnp.float32)
    head_shape = (clips, frames_here, side * side, HEADS, head_size)
    queries = (mixed[..., :width] + mix_bias32[:width]).astype(jnp.bfloat16).reshape(head_shape)
    keys = mixed[..., width : 2 * width].astype(jnp.bfloat16).reshape(head_shape)
    values = (mixed[..., 2 * width :] + mix_bias32[width:]).astype(jnp.bfloat16).reshape(head_shape)
    queries, keys, values = (
        lax.all_to_all(queries, TM, split_axis=3, concat_axis=1, tiled=True),
        lax.all_to_all(keys, TM, split_axis=3, concat_axis=1, tiled=True),
        lax.all_to_all(values, TM, split_axis=3, concat_axis=1, tiled=True),
    )
    frames = queries.shape[1]
    if shifted:
        queries = jnp.roll(queries, -(WIN_T // 2), axis=1)
        keys = jnp.roll(keys, -(WIN_T // 2), axis=1)
        values = jnp.roll(values, -(WIN_T // 2), axis=1)
    queries, keys, values = (to_windows(queries), to_windows(keys), to_windows(values))
    bias = table_bias(table)
    same = region_match(frames) if shifted else None

    def attend_clip(items):
        clip_queries, clip_keys, clip_values = items
        scores = window_scores(clip_queries, clip_keys, bias, same, scale)
        peak = jnp.max(scores, axis=-1, keepdims=True)
        raised = jnp.exp(scores - peak)
        total = jnp.sum(raised, axis=-1, keepdims=True)
        probs = (raised / total).astype(jnp.bfloat16)
        out_win = jnp.einsum(
            "whqk,wkhd->wqhd", probs, clip_values, preferred_element_type=jnp.float32
        ).astype(jnp.bfloat16)
        return (out_win, peak + jnp.log(total))

    attended_heads, log_total = lax.map(attend_clip, (queries, keys, values))
    attended_heads = to_frames(attended_heads, frames)
    if shifted:
        attended_heads = jnp.roll(attended_heads, WIN_T // 2, axis=1)
    attended = lax.all_to_all(attended_heads, TM, split_axis=1, concat_axis=3, tiled=True)
    attended = attended.reshape(clips, frames_here, side, side, width)
    if shifted:
        attended = space_roll(attended, False)
    middle = stream + project(attended, proj_weight) + proj_bias.astype(jnp.float32)
    normed_two = norm_rows(
        middle, gain_two.astype(jnp.float32), bias_two.astype(jnp.float32)
    ).astype(jnp.bfloat16)
    hidden_pre = project(normed_two, wide_weight) + wide_bias.astype(jnp.float32)
    hidden = gelu_exact(hidden_pre).astype(jnp.bfloat16)
    after = middle + project(hidden, narrow_weight) + narrow_bias.astype(jnp.float32)
    stash = (
        stream,
        normed,
        queries,
        keys,
        values,
        log_total,
        attended,
        middle,
        normed_two,
        hidden_pre,
        hidden,
    )
    return (stash, after)


def layer_backward(grad_after, params, table, stash, shifted):
    (
        gain_one,
        bias_one,
        mix_weight,
        mix_bias,
        proj_weight,
        proj_bias,
        gain_two,
        bias_two,
        wide_weight,
        wide_bias,
        narrow_weight,
        narrow_bias,
    ) = params
    (
        stream,
        normed,
        queries,
        keys,
        values,
        log_total,
        attended,
        middle,
        normed_two,
        hidden_pre,
        hidden,
    ) = stash
    clips, frames_here, side = (stream.shape[0], stream.shape[1], stream.shape[2])
    width = stream.shape[-1]
    head_size = width // HEADS
    scale = head_size ** (-0.5)
    frames = queries.shape[1] * WIN_T
    grad_branch_two = grad_after.astype(jnp.bfloat16)
    narrow_grad = outer_sum(hidden, grad_branch_two)
    narrow_bias_grad = column_sum(grad_branch_two)
    grad_hidden = project_back(grad_branch_two, narrow_weight)
    gelu_pull = jax.vjp(gelu_exact, hidden_pre)[1]
    grad_pre = gelu_pull(grad_hidden)[0].astype(jnp.bfloat16)
    wide_grad = outer_sum(normed_two, grad_pre)
    wide_bias_grad = column_sum(grad_pre)
    grad_normed_two = project_back(grad_pre, wide_weight)
    norm_pull_two = jax.vjp(
        norm_rows, middle, gain_two.astype(jnp.float32), bias_two.astype(jnp.float32)
    )[1]
    grad_mid_part, gain_two_grad, bias_two_grad = norm_pull_two(grad_normed_two)
    grad_middle = grad_after + grad_mid_part
    grad_branch_one = grad_middle.astype(jnp.bfloat16)
    proj_grad = outer_sum(attended, grad_branch_one)
    proj_bias_grad = column_sum(grad_branch_one)
    grad_attended = project_back(grad_branch_one, proj_weight).astype(jnp.bfloat16)
    if shifted:
        grad_attended = space_roll(grad_attended, True)
    grad_attended = grad_attended.reshape(clips, frames_here, side * side, HEADS, head_size)
    grad_attended = lax.all_to_all(grad_attended, TM, split_axis=3, concat_axis=1, tiled=True)
    if shifted:
        grad_attended = jnp.roll(grad_attended, -(WIN_T // 2), axis=1)
    grad_attended = to_windows(grad_attended)
    bias = table_bias(table)
    same = region_match(frames) if shifted else None

    def attend_back(carry, items):
        clip_queries, clip_keys, clip_values, clip_grad, clip_log = items
        scores = window_scores(clip_queries, clip_keys, bias, same, scale)
        probs = jnp.exp(scores - clip_log)
        grad_probs = jnp.einsum(
            "wqhd,wkhd->whqk", clip_grad, clip_values, preferred_element_type=jnp.float32
        )
        inner = jnp.sum(probs * grad_probs, axis=-1, keepdims=True)
        grad_scores = (probs * (grad_probs - inner)).astype(jnp.bfloat16)
        grad_q = (
            jnp.einsum(
                "whqk,wkhd->wqhd", grad_scores, clip_keys, preferred_element_type=jnp.float32
            )
            * scale
        ).astype(jnp.bfloat16)
        grad_k = (
            jnp.einsum(
                "whqk,wqhd->wkhd", grad_scores, clip_queries, preferred_element_type=jnp.float32
            )
            * scale
        ).astype(jnp.bfloat16)
        grad_v = jnp.einsum(
            "whqk,wqhd->wkhd",
            probs.astype(jnp.bfloat16),
            clip_grad,
            preferred_element_type=jnp.float32,
        ).astype(jnp.bfloat16)
        carry = carry + jnp.sum(grad_scores.astype(jnp.float32), axis=0)
        return (carry, (grad_q, grad_k, grad_v))

    window_tokens = queries.shape[2]
    start_bias = jnp.zeros((queries.shape[3], window_tokens, window_tokens), jnp.float32)
    bias_grad, grads_win = lax.scan(
        attend_back, start_bias, (queries, keys, values, grad_attended, log_total)
    )
    grad_q, grad_k, grad_v = (to_frames(g, frames) for g in grads_win)
    if shifted:
        grad_q = jnp.roll(grad_q, WIN_T // 2, axis=1)
        grad_k = jnp.roll(grad_k, WIN_T // 2, axis=1)
        grad_v = jnp.roll(grad_v, WIN_T // 2, axis=1)
    grad_q, grad_k, grad_v = (
        lax.all_to_all(grad_q, TM, split_axis=1, concat_axis=3, tiled=True),
        lax.all_to_all(grad_k, TM, split_axis=1, concat_axis=3, tiled=True),
        lax.all_to_all(grad_v, TM, split_axis=1, concat_axis=3, tiled=True),
    )
    token_shape = (clips, frames_here, side, side, width)
    grad_q, grad_k, grad_v = (
        grad_q.reshape(token_shape),
        grad_k.reshape(token_shape),
        grad_v.reshape(token_shape),
    )
    grad_mix = jnp.concatenate([grad_q, grad_k, grad_v], axis=-1)
    mix_grad = outer_sum(normed, grad_mix)
    mix_bias_grad = jnp.concatenate([column_sum(grad_q), column_sum(grad_v)])
    grad_normed = project_back(grad_mix, mix_weight)
    if shifted:
        grad_normed = space_roll(grad_normed.astype(jnp.bfloat16), False).astype(jnp.float32)
    norm_pull_one = jax.vjp(
        norm_rows, stream, gain_one.astype(jnp.float32), bias_one.astype(jnp.float32)
    )[1]
    grad_stream_part, gain_one_grad, bias_one_grad = norm_pull_one(grad_normed)
    grad_stream = grad_middle + grad_stream_part
    rel = relative_index(WIN_T, WIN_HW).reshape(-1)
    table_grad = (
        jnp.zeros(table.shape, jnp.float32).at[rel].add(bias_grad.reshape(bias_grad.shape[0], -1).T)
    )
    weight_grads = (
        gain_one_grad,
        bias_one_grad,
        mix_grad,
        mix_bias_grad,
        proj_grad,
        proj_bias_grad,
        gain_two_grad,
        bias_two_grad,
        wide_grad,
        wide_bias_grad,
        narrow_grad,
        narrow_bias_grad,
    )
    return (grad_stream, weight_grads, table_grad)


def per_device(
    clips_in,
    ln1_gain,
    ln1_bias,
    qkv_weight,
    qv_bias,
    out_weight,
    out_bias,
    ln2_gain,
    ln2_bias,
    fc1_weight,
    fc1_bias,
    fc2_weight,
    fc2_bias,
    pos_table,
    out_grad,
):
    clips, frames_here, quads, cells, width = clips_in.shape
    grid_shape = (clips, frames_here, WIN_HW, WIN_HW, width)
    shards = (
        ln1_gain,
        ln1_bias,
        qkv_weight,
        qv_bias,
        out_weight,
        out_bias,
        ln2_gain,
        ln2_bias,
        fc1_weight,
        fc1_bias,
        fc2_weight,
        fc2_bias,
    )
    stream = clips_in.astype(jnp.float32).reshape(grid_shape)
    kept_params = []
    kept_stash = []
    for layer in range(LAYERS):
        params = gather_layer(shards, layer)
        stash, stream = layer_forward(stream, params, pos_table[layer], layer % 2 == 1)
        kept_params.append(params)
        kept_stash.append(stash)
    clips_out = stream.astype(jnp.bfloat16).reshape(clips_in.shape)
    grad_stream = out_grad.astype(jnp.float32).reshape(grid_shape)
    layer_shares = [None] * LAYERS
    table_parts = [None] * LAYERS
    for layer in reversed(range(LAYERS)):
        params = gather_layer(shards, layer)
        grad_stream, weight_grads, table_grad = layer_backward(
            grad_stream, params, pos_table[layer], kept_stash[layer], layer % 2 == 1
        )
        layer_shares[layer] = tuple(
            lax.psum_scatter(g, ALL, scatter_dimension=0, tiled=True) for g in weight_grads
        )
        table_parts[layer] = table_grad
    in_grad = grad_stream.astype(jnp.bfloat16).reshape(clips_in.shape)
    table_total = lax.psum(jnp.stack(table_parts), (SPACE, CLIP))
    stacked = tuple(
        (jnp.stack([layer_shares[n][slot] for n in range(LAYERS)]) for slot in range(12))
    )
    return (
        clips_out,
        in_grad,
        stacked[0],
        stacked[1],
        stacked[2],
        stacked[3],
        stacked[4],
        stacked[5],
        stacked[6],
        stacked[7],
        stacked[8],
        stacked[9],
        stacked[10],
        stacked[11],
        table_total,
    )


F32 = jnp.float32
BF16 = jnp.bfloat16
TOKENS = WIN_T * WIN_HW * WIN_HW
CELLS = WIN_HW * WIN_HW
SPAN = 2 * WIN_HW - 1
STEPS = 2 * WIN_T - 1
LOG2E = math.log2(math.e)
VMEM_BYTES = 56 * 1024 * 1024


def mm(left, right, left_dim=1, right_dim=0):
    dims = (((left_dim,), (right_dim,)), ((), ()))
    return lax.dot_general(left, right, dims, preferred_element_type=F32)


class Order:
    def __init__(self, waits=()):
        self.waits = list(waits)
        self.token = None


def call(
    kernel, grid, in_specs, out_specs, out_shape, flops, scratch=(), after=None, aliases=None
):
    waits = after.waits if after else []
    inputs = len(in_specs)
    single = not isinstance(out_shape, list)
    out_specs = [out_specs] if single else list(out_specs)
    out_shape = [out_shape] if single else list(out_shape)
    outputs = len(out_shape)
    if after:
        out_specs.append(pl.BlockSpec(memory_space=pltpu.SMEM))
        out_shape.append(jax.ShapeDtypeStruct((1, 1), F32))

    def body(*refs):
        ins, outs = refs[:inputs], refs[inputs + len(waits) :]
        if after:
            outs[outputs][0, 0] = 0.0
        kernel(*ins, *outs[:outputs], *outs[len(out_shape) :])

    run = pl.pallas_call(
        body,
        grid=grid,
        in_specs=list(in_specs) + [pl.BlockSpec(memory_space=pl.ANY)] * len(waits),
        out_specs=out_specs,
        out_shape=out_shape,
        scratch_shapes=scratch,
        input_output_aliases=aliases or {},
        cost_estimate=pl.CostEstimate(
            flops=int(flops), transcendentals=0, bytes_accessed=8 * 1024 * 1024
        ),
        compiler_params=pltpu.CompilerParams(vmem_limit_bytes=VMEM_BYTES),
    )

    def result(*args):
        found = run(*args, *waits)
        if after:
            after.token = found[outputs]
        return found[0] if single else found[:outputs]

    return result


def whole_block(shape):
    return pl.BlockSpec(shape, lambda *ids: (0,) * len(shape))


def flag_spec():
    return pl.BlockSpec(memory_space=pltpu.SMEM)


def win_block(width, column=0):
    return pl.BlockSpec((1, TOKENS, width), lambda w: (w, 0, column))


HALF = WIN_T // 2 * CELLS
KINDS = range(1, 8)


class Halo:
    def __init__(self):
        token = np.arange(HALF)
        row, col = token // WIN_HW % WIN_HW, token % WIN_HW
        reach = WIN_HW // 2
        target = token - row * WIN_HW - col
        target = target + (row - reach) % WIN_HW * WIN_HW + (col - reach) % WIN_HW
        leaves = (row < reach) * 2 + (col < reach) * 1
        self.stay = np.zeros((HALF, HALF), np.float32)
        stays = leaves == 0
        self.stay[target[stays], token[stays]] = 1
        self.near, self.near_to = self.ways(leaves, target, (1, 2, 3))
        self.far, self.far_to = self.ways(leaves, target, (0, 1, 2, 3))

    @staticmethod
    def ways(leaves, target, kinds):
        send, place = [], []
        for kind in kinds:
            source = np.nonzero(leaves == kind)[0]
            rows = 64 if kind == 0 else 48
            out, back = np.zeros((rows, HALF), np.float32), np.zeros((HALF, rows), np.float32)
            out[np.arange(len(source)), source] = 1
            back[target[source], np.arange(len(source))] = 1
            send.append(out)
            place.append(back)
        return np.concatenate(send, 0), np.concatenate(place, 1)

    def sends(self, onward):
        return (self.near, self.far) if onward else (self.near_to.T, self.far_to.T)

    def places(self, onward):
        if onward:
            return self.stay, self.near_to, self.far_to
        return self.stay.T, self.near.T, self.far.T


def half_at(half):
    return half // 2, slice(half % 2 * HALF, (half % 2 + 1) * HALF)


class Flow:
    def __init__(self):
        self.live = []
        self.done = {}

    def start(self, name, task):
        self.live.append((name, task, task.sends() if isinstance(task, Gather) else next(task)))

    def pending(self):
        return [value for _, _, sends in self.live for value, _, _ in sends]

    def step(self, token, names=None):
        live = []
        for name, task, sends in self.live:
            if names is not None and name not in names:
                live.append((name, task, sends))
                continue
            came = [lax.ppermute(value, axis, pairs) for value, axis, pairs in sends]
            if isinstance(task, Gather):
                task.step(came[0], token if len(task.steps) > 1 else None)
                if task.steps:
                    live.append((name, task, task.sends()))
                else:
                    self.done[name] = task.out
                continue
            try:
                live.append((name, task, task.send((came, token))))
            except StopIteration as end:
                self.done[name] = end.value
        self.live = live

    def finish(self, name):
        while name not in self.done:
            self.step(None, (name,))
        return self.done[name]


def swap_pairs(axis, bit):
    return [(source, source ^ 2**bit) for source in range(lax.axis_size(axis))]


def halo_flow(packed, onward):
    ring, quads = lax.axis_size(TM), lax.axis_size(SPACE)
    sends = []
    for kind, piece in zip(KINDS, packed):
        step = 0 if not kind & 4 else (-1 if onward else 1)
        pairs = []
        for frame_at in range(ring):
            for quad in range(quads):
                to = (frame_at + step) % ring * quads + (quad ^ (kind & 3))
                pairs.append((frame_at * quads + quad, to))
        sends.append((piece, (TM, SPACE), pairs))
    came, _ = yield sends
    return came


def pack_kernel(center, onward, near_ref, far_ref, x_ref, *refs):
    out_refs, flat_ref = refs[:-1], refs[-1]
    halves = 2 * x_ref.shape[0]
    for w in range(x_ref.shape[0]):
        x = x_ref[w].astype(F32)
        if center:
            x = x - jnp.mean(x, axis=-1, keepdims=True)
        flat_ref[w] = x
    for n in range(halves - 1):
        w, rows = half_at(n + 1 if onward else n)
        sent = mm(near_ref[...], flat_ref[w, rows].astype(BF16)).astype(BF16)
        for kind in range(3):
            out_refs[kind][n * 48 : (n + 1) * 48] = sent[kind * 48 : (kind + 1) * 48]
    w, rows = half_at(0 if onward else halves - 1)
    sent = mm(far_ref[...], flat_ref[w, rows].astype(BF16)).astype(BF16)
    for kind in range(4):
        first = 0 if kind == 0 else 16 + 48 * kind
        out_refs[3 + kind][...] = sent[first : first + out_refs[3 + kind].shape[0]]


def part_rows(windows):
    return [48 * (2 * windows - 1)] * 3 + [64, 48, 48, 48]


def halo_pack(x, halo, onward, center=False, joined=False, after=None):
    windows, _, width = x.shape
    near, far = (jnp.asarray(m, BF16) for m in halo.sends(onward))
    rows = part_rows(windows)

    def kernel(near_ref, far_ref, x_ref, *refs):
        if joined:
            refs = [refs[0].at[pl.ds(sum(rows[:n]), rows[n])] for n in range(7)] + [refs[1]]
        pack_kernel(center, onward, near_ref, far_ref, x_ref, *refs)

    shapes = [(sum(rows), width)] if joined else [(n, width) for n in rows]
    out = functools.partial(call, after=after)(
        kernel,
        (1,),
        [whole_block(m.shape) for m in (near, far, x)],
        [whole_block(shape) for shape in shapes],
        [jax.ShapeDtypeStruct(shape, BF16) for shape in shapes],
        2 * 640 * HALF * width,
        [pltpu.VMEM(x.shape, F32)],
    )(near, far, x)
    return out[0] if joined else out


def halo_gather(packed):
    return lax.all_gather(packed, (TM, SPACE), axis=0, tiled=True)


def halo_senders(onward):
    ring, quads = lax.axis_size(TM), lax.axis_size(SPACE)
    senders = []
    for kind in KINDS:
        step = 0 if not kind & 4 else (1 if onward else -1)
        frame_at = (lax.axis_index(TM) + step + ring) % ring
        senders.append(frame_at * quads + lax.axis_index(SPACE) ^ (kind & 3))
    return jnp.stack([jnp.asarray(n, jnp.int32) for n in senders])


def unpack_kernel(center, onward, add_mean, stay_ref, near_ref, far_ref, x_ref, *refs):
    base_ref, refs = (refs[0], refs[1:]) if add_mean else (None, refs)
    came_refs, (out_ref, flat_ref, total_ref) = refs[:7], refs[7:]
    windows = x_ref.shape[0]
    halves = 2 * windows
    for w in range(windows):
        x = x_ref[w].astype(F32)
        if center:
            x = x - jnp.mean(x, axis=-1, keepdims=True)
        flat_ref[w] = x
    for n in range(halves - 1):
        w, rows = half_at(n + 1 if onward else n)
        x = flat_ref[w, rows]
        high = x.astype(BF16)
        total = mm(stay_ref[...], high)
        if x_ref.dtype == F32:
            total = total + mm(stay_ref[...], (x - high.astype(F32)).astype(BF16))
        came = jnp.concatenate([ref[n * 48 : (n + 1) * 48] for ref in came_refs[:3]], axis=0)
        w, rows = half_at(n if onward else n + 1)
        total_ref[w, rows] = total + mm(near_ref[...], came)
    came = jnp.concatenate([ref[...] for ref in came_refs[3:]], axis=0)
    w, rows = half_at(halves - 1 if onward else 0)
    total_ref[w, rows] = mm(far_ref[...], came)
    for w in range(windows):
        total = total_ref[w]
        if add_mean:
            total = total + jnp.mean(base_ref[w], axis=-1, keepdims=True)
        out_ref[w] = total.astype(out_ref.dtype)


def halo_unpack(x, came, halo, onward, dtype, center=False, mean_of=None, after=None):
    places = [jnp.asarray(m, BF16) for m in halo.places(onward)]
    operands = places + [x] + ([] if mean_of is None else [mean_of])
    joined = not isinstance(came, list)
    senders = [halo_senders(onward)] if joined else []
    operands += [came] if joined else came
    rows = part_rows(x.shape[0])

    def kernel(*refs):
        if joined:
            sender_ref, refs = refs[0], refs[1:]
            count = len(operands)
            parts = []
            for n in range(7):
                first = sender_ref[n] * sum(rows) + sum(rows[:n])
                parts.append(refs[count - 1].at[pl.ds(pl.multiple_of(first, 16), rows[n])])
            refs = refs[: count - 1] + tuple(parts) + refs[count:]
        unpack_kernel(center, onward, mean_of is not None, *refs)

    return functools.partial(call, after=after)(
        kernel,
        (1,),
        [flag_spec()] * joined + [whole_block(v.shape) for v in operands],
        whole_block(x.shape),
        jax.ShapeDtypeStruct(x.shape, dtype),
        8 * x.size * HALF,
        [pltpu.VMEM(x.shape, F32), pltpu.VMEM(x.shape, F32)],
    )(*senders, *operands)


def index_bits():
    bits = []
    for axis in ALL:
        count = lax.axis_size(axis).bit_length() - 1
        bits += [(axis, b) for b in reversed(range(count))]
    return bits


def bit_of(axis, bit):
    return (lax.axis_index(axis) // 2**bit) % 2


def stage_orders():
    bits = index_bits()
    inner = [(CLIP, 0)] if lax.axis_size(CLIP) > 1 else []
    tm = [b for b in bits if b[0] == TM]
    clip = [b for b in bits if b[0] == CLIP and b not in inner]
    space = [b for b in reversed(bits) if b[0] == SPACE]
    return inner + tm + clip + space, inner + clip + tm + space


class Gather:
    def __init__(self, shard, order):
        self.bits, self.steps = index_bits(), list(reversed(order))
        self.dims = [1] * len(self.bits)
        self.rows, self.out = shard.shape[0], shard

    def sends(self):
        axis, bit = self.steps[0]
        return [(self.out, axis, swap_pairs(axis, bit))]

    def step(self, came, token):
        axis, bit = self.steps.pop(0)
        dim = self.bits.index((axis, bit))
        before, after = math.prod(self.dims[:dim]), math.prod(self.dims[dim + 1 :])
        self.dims[dim] = 2
        here = bit_of(axis, bit).astype(F32) + (0.0 if token is None else token.reshape(()))
        own, came = (v.reshape(before, 1, after * self.rows, -1) for v in (self.out, came))
        low, high = jnp.where(here > 0.5, came, own), jnp.where(here > 0.5, own, came)
        self.out = jnp.concatenate([low, high], axis=1).reshape(-1, own.shape[-1])


def scatter_flow(own, sent, order):
    bits = index_bits()
    width = own.shape[-1]
    dims = [2] * len(bits)
    own, sent = own.reshape(-1, width), sent.reshape(-1, width)
    for n, (axis, bit) in enumerate(order):
        (came,), token = yield [(sent, axis, swap_pairs(axis, bit))]
        dims[bits.index((axis, bit))] = 1
        zero = 0.0 if token is None else token.reshape(())
        if n + 1 == len(order):
            return own + came.astype(F32)
        axis, bit = order[n + 1]
        dim = bits.index((axis, bit))
        here = bit_of(axis, bit)
        own, came = (v.reshape(dims + [-1, width]) for v in (own, came))

        def half(index):
            mine, theirs = (lax.dynamic_slice_in_dim(v, index, 1, dim) for v in (own, came))
            return (mine + theirs.astype(F32) + zero).reshape(-1, width)

        own, sent = half(here), half(1 - here).astype(BF16)


def table_flow(tables, heads_here):
    first = lax.axis_index(TM) == 0
    mine = jnp.where(first, tables[0], tables[1])
    (came,), _ = yield [(jnp.where(first, tables[1], tables[0]), TM, swap_pairs(TM, 0))]
    table = mine + came
    for axis, bit in index_bits():
        if axis != TM:
            (came,), _ = yield [(table, axis, swap_pairs(axis, bit))]
            table = table + came
    return table


WIDE = 768


def column_pick():
    pick = np.zeros((WIN_HW, 256, 128), np.float32)
    for key_col in range(WIN_HW):
        for row in range(SPAN):
            for col in range(WIN_HW):
                entry = row * SPAN + col - key_col + WIN_HW - 1
                pick[key_col, entry, row * WIN_HW + col] = 1
    return pick


def lane_spans(step):
    first, rest = divmod(step * CELLS, 128)
    if rest + CELLS <= 128:
        return [(first, rest, rest + CELLS)]
    return [(first, rest, 128), (first + 1, 0, rest + CELLS - 128)]


def bias_kernel(slab_ref, pick_ref, out_ref, row_ref, wide_ref):
    heads = pl.num_programs(0)

    @pl.when(pl.program_id(0) == 0)
    def _():
        slabs = slab_ref[...]
        for col in range(WIN_HW):
            row_ref[pl.ds(col, slabs.shape[0], stride=8), :] = mm(slabs, pick_ref[col]) * LOG2E

    base = pl.program_id(0) * 128
    lane = lax.broadcasted_iota(jnp.int32, (8, 128), 1)
    for row in range(WIN_HW):
        tiles = [jnp.zeros((8, 128), F32) for _ in range(WIDE // 128)]
        for step in range(STEPS):
            rows = row_ref[pl.ds(pl.multiple_of(base + step * 8, 8), 8), :]
            turn = (step * CELLS - WIN_HW * (WIN_HW - 1 - row)) % 128
            rows = pltpu.roll(rows, turn, 1) if turn else rows
            for tile, low, high in lane_spans(step):
                tiles[tile] = jnp.where((lane >= low) & (lane < high), rows, tiles[tile])
        wide_ref[row * WIN_HW : (row + 1) * WIN_HW, :] = jnp.concatenate(tiles, axis=1)[:WIN_HW]
    wide = wide_ref[:CELLS, :]
    for key_frame in range(WIN_T):
        turned = pltpu.roll(wide, (WIDE - (WIN_T - 1 - key_frame) * CELLS) % WIDE, 1)
        out_ref[0, key_frame * CELLS : (key_frame + 1) * CELLS, :] = turned[:, :TOKENS]


def table_to_bias(tables, rest=None, after=None):
    heads = tables.shape[0]
    slabs = tables.reshape(heads, STEPS, SPAN * SPAN)
    slabs = jnp.pad(slabs, ((0, 0), (0, 16 - STEPS), (0, 256 - SPAN * SPAN)))
    slabs = slabs.reshape(heads * 16, 256)
    held = [] if rest is None else [rest]
    first = 0 if rest is None else heads

    def kernel(slab_ref, pick_ref, *refs):
        bias_kernel(slab_ref, pick_ref, *refs[len(held) :])

    return functools.partial(call, after=after, aliases={2: 0} if held else {})(
        kernel,
        (heads,),
        [whole_block(slabs.shape), whole_block((WIN_HW, 256, 128))]
        + [pl.BlockSpec(memory_space=pl.ANY)] * len(held),
        pl.BlockSpec((1, TOKENS, TOKENS), lambda h: (first + h, 0, 0)),
        jax.ShapeDtypeStruct((2 * heads, TOKENS, TOKENS), F32),
        heads * 500_000_000,
        [pltpu.VMEM((heads * 128, 128), F32), pltpu.VMEM((56, WIDE), F32)],
    )(slabs, jnp.asarray(column_pick(), BF16), *held)


def table_back_kernel(sums_ref, pick_ref, out_ref, row_ref):
    head = pl.program_id(0)
    lane = lax.broadcasted_iota(jnp.int32, (WIN_HW, 128), 1)
    totals = [None] * STEPS
    for row in range(WIN_HW):
        rows = sums_ref[0, row * WIN_HW : (row + 1) * WIN_HW, :]
        start = WIN_HW * (WIN_HW - 1 - row)
        for step in range(STEPS):
            turn = (start - step * CELLS) % 128
            piece = None
            for tile, low, high in lane_spans(step):
                part = rows[:, tile * 128 : (tile + 1) * 128]
                part = jnp.where((lane >= low) & (lane < high), part, 0.0)
                piece = part if piece is None else piece + part
            piece = pltpu.roll(piece, turn, 1) if turn else piece
            totals[step] = piece if totals[step] is None else totals[step] + piece
    blank = jnp.zeros((1, 128), F32)
    for step in range(16):
        rows = jnp.concatenate([totals[step], blank]) if step < STEPS else jnp.zeros((8, 128), F32)
        row_ref[pl.ds(pl.multiple_of(head * 128 + step * 8, 8), 8), :] = rows

    @pl.when(head == pl.num_programs(0) - 1)
    def _():
        total = None
        for col in range(WIN_HW):
            rows = row_ref[pl.ds(col, out_ref.shape[0], stride=8), :]
            high = rows.astype(BF16)
            low = (rows - high.astype(F32)).astype(BF16)
            part = mm(high, pick_ref[col], 1, 1) + mm(low, pick_ref[col], 1, 1)
            total = part if total is None else total + part
        out_ref[...] = total


def sums_to_table(sums, first=0, heads=None, after=None):
    heads = heads or sums.shape[0]
    slabs = functools.partial(call, after=after)(
        table_back_kernel,
        (heads,),
        [
            pl.BlockSpec((1, CELLS, WIDE), lambda h: (first + h, 0, 0)),
            whole_block((WIN_HW, 256, 128)),
        ],
        whole_block((heads * 16, 256)),
        jax.ShapeDtypeStruct((heads * 16, 256), F32),
        heads * 300_000_000,
        [pltpu.VMEM((heads * 128, 128), F32)],
    )(sums, jnp.asarray(column_pick(), BF16))
    return slabs.reshape(heads, 16, 256)[:, :STEPS, : SPAN * SPAN].reshape(heads, -1)


def unit_rows(x):
    centered = x - jnp.mean(x, axis=-1, keepdims=True)
    inverse = lax.rsqrt(jnp.mean(centered * centered, axis=-1, keepdims=True) + 1e-05)
    return centered * inverse, inverse


def norm_back(grad, unit, inverse, gain):
    scaled = grad * gain
    return inverse * (
        scaled
        - jnp.mean(scaled, axis=-1, keepdims=True)
        - unit * jnp.mean(scaled * unit, axis=-1, keepdims=True)
    )


def qkv_kernel(x_ref, vec_ref, wq_ref, wk_ref, wv_ref, out_ref):
    width = x_ref.shape[-1]
    unit, _ = unit_rows(x_ref[0].astype(F32))
    normed = (unit * vec_ref[0:1] + vec_ref[1:2]).astype(BF16)
    for part, ref in enumerate((wq_ref, wk_ref, wv_ref)):
        out = mm(normed, ref[...])
        if part == 0:
            out = out + vec_ref[2:3]
        if part == 2:
            out = out + vec_ref[3:4]
        out_ref[0, :, part * width : (part + 1) * width] = out.astype(BF16)


def run_qkv(x, vec, w_qkv, after=None):
    windows, _, width = x.shape
    weight, at = w_qkv
    return functools.partial(call, after=after)(
        qkv_kernel,
        (windows,),
        [win_block(width), whole_block(vec.shape)]
        + [weight_block(width, width, at + n) for n in range(3)],
        win_block(3 * width),
        jax.ShapeDtypeStruct((windows, TOKENS, 3 * width), BF16),
        2 * windows * TOKENS * width * 3 * width,
    )(x, vec, weight, weight, weight)


GROUP = 4


def head_masks(head_size):
    lane = lax.broadcasted_iota(jnp.int32, (1, GROUP * head_size), 1)
    return [
        jnp.where((lane >= h * head_size) & (lane < (h + 1) * head_size), 1.0, 0.0).astype(BF16)
        for h in range(GROUP)
    ]


def region_labels(flag_ref, late_ref, turned_ref, at_end):
    flags = [flag_ref[1 + n].astype(F32) for n in range(3)]
    flags[0] = flags[0] * at_end
    col = sum(flags[n] * late_ref[:, n : n + 1] for n in range(3))
    return col, sum(flags[n] * turned_ref[n : n + 1, :] for n in range(3))


def late_tokens():
    token = np.arange(TOKENS)
    late = np.zeros((TOKENS, 8), np.float32)
    late[:, 0] = 4 * (token // CELLS >= WIN_T - WIN_T // 2)
    late[:, 1] = 2 * (token // WIN_HW % WIN_HW >= WIN_HW - WIN_HW // 2)
    late[:, 2] = token % WIN_HW >= WIN_HW - WIN_HW // 2
    return late


def attend_kernel(
    shifted, head_size, flag_ref, q_ref, k_ref, v_ref, bias_ref, late_ref, turned_ref, out_ref, log_ref
):
    q, k = q_ref[0], k_ref[0]
    if shifted:
        at_end = jnp.where(pl.program_id(1) == pl.num_programs(1) - 1, 1.0, 0.0)
        col, row = region_labels(flag_ref, late_ref, turned_ref, at_end)
    turned = v_ref[0].astype(F32).T.astype(BF16)
    factor = head_size**-0.5 * LOG2E
    masks = head_masks(head_size)
    outs, logs = [], []
    for h in range(GROUP):
        scores = mm(k * masks[h], q, 1, 1) * factor + bias_ref[h]
        if shifted:
            scores = jnp.where(col == row, scores, masked_score)
        peak = jnp.max(scores, axis=0, keepdims=True)
        raised = jnp.exp2(scores - peak)
        total = jnp.sum(raised, axis=0, keepdims=True)
        mixed = mm(turned[h * head_size : (h + 1) * head_size], raised.astype(BF16))
        outs.append(mixed / total)
        logs.append(peak + jnp.log2(total))
    out_ref[0] = jnp.concatenate(outs, axis=0).T.astype(BF16)
    log_ref[0, 0] = jnp.concatenate(logs + logs, axis=0)


def run_attend(qkv, bias, flags, shifted, after=None):
    windows, _, width3 = qkv.shape
    width = width3 // 3
    wide = GROUP * (width // HEADS)
    groups = HEADS // GROUP
    qkv_specs = [
        pl.BlockSpec((1, TOKENS, wide), lambda g, w, p=part: (w, 0, p * groups + g))
        for part in range(3)
    ]
    return functools.partial(call, after=after)(
        functools.partial(attend_kernel, shifted, width // HEADS),
        (groups, windows),
        [flag_spec()]
        + qkv_specs
        + [
            pl.BlockSpec((GROUP, TOKENS, TOKENS), lambda g, w: (g, 0, 0)),
            whole_block((TOKENS, 8)),
            whole_block((8, TOKENS)),
        ],
        [
            pl.BlockSpec((1, TOKENS, wide), lambda g, w: (w, 0, g)),
            pl.BlockSpec((1, 1, 2 * GROUP, TOKENS), lambda g, w: (w, g, 0, 0)),
        ],
        [
            jax.ShapeDtypeStruct((windows, TOKENS, width), BF16),
            jax.ShapeDtypeStruct((windows, groups, 2 * GROUP, TOKENS), F32),
        ],
        64 * windows * TOKENS * TOKENS * width,
    )(flags, qkv, qkv, qkv, bias, late_tokens(), late_tokens().T)


def attend_back_kernel(
    shifted, head_size, flag_ref, q_ref, k_ref, v_ref, g_ref, o_ref, bias_ref, late_ref, turned_ref,
    log_ref, dq_ref, dk_ref, dv_ref, table_ref, sum_ref,
):
    windows = q_ref.shape[0]
    if shifted:
        labels = [
            region_labels(flag_ref, late_ref, turned_ref, float(w == windows - 1))
            for w in range(windows)
        ]
    scale = head_size**-0.5
    factor = scale * LOG2E
    masks = head_masks(head_size)

    @pl.when(pl.program_id(0) == 0)
    def _():
        sum_ref[...] = jnp.zeros_like(sum_ref)

    turned, weighed = [], []
    for w in range(windows):
        turned.append(k_ref[w].astype(F32).T.astype(BF16))
        weighed.append(g_ref[w].astype(F32).T * o_ref[w].astype(F32).T)
    grad_q = [[] for _ in range(windows)]
    grad_k, grad_v = [None] * windows, [None] * windows
    for h in range(GROUP):
        here = slice(h * head_size, (h + 1) * head_size)
        total = None
        for w in range(windows):
            q, k, v, g = q_ref[w], k_ref[w], v_ref[w], g_ref[w]
            inner = jnp.sum(weighed[w][here], axis=0, keepdims=True)
            scores = mm(k * masks[h], q, 1, 1) * factor + bias_ref[h]
            if shifted:
                scores = jnp.where(labels[w][0] == labels[w][1], scores, masked_score)
            probs = jnp.exp2(scores - log_ref[w, 0, h : h + 1])
            grad_probs = mm(v * masks[h], g, 1, 1)
            grad_scores = (probs * (grad_probs - inner)).astype(BF16)
            part_v = mm(probs.astype(BF16), g * masks[h])
            part_k = mm(grad_scores, q * masks[h])
            grad_v[w] = part_v if grad_v[w] is None else grad_v[w] + part_v
            grad_k[w] = part_k if grad_k[w] is None else grad_k[w] + part_k
            grad_q[w].append(mm(turned[w][here], grad_scores))
            wide = grad_scores.astype(F32)
            total = wide if total is None else total + wide
        sum_ref[:, :TOKENS] = total
        sums = None
        for key_frame in range(WIN_T):
            rows = sum_ref[key_frame * CELLS : (key_frame + 1) * CELLS, :]
            step = (WIN_T - 1 - key_frame) * CELLS
            rows = pltpu.roll(rows, step, 1) if step else rows
            sums = rows if sums is None else sums + rows
        table_ref[h] = sums
    for w in range(windows):
        dq_ref[w] = (jnp.concatenate(grad_q[w], axis=0) * scale).T.astype(BF16)
        dk_ref[w] = (grad_k[w] * scale).astype(BF16)
        dv_ref[w] = grad_v[w].astype(BF16)


def run_attend_back(qkv, grad, attended, bias, flags, log, shifted, first, count, after=None):
    windows, _, width3 = qkv.shape
    width = width3 // 3
    wide = GROUP * (width // HEADS)
    groups = HEADS // GROUP
    qkv_specs = [
        pl.BlockSpec((windows, TOKENS, wide), lambda g, p=part: (0, 0, p * groups + first + g))
        for part in range(3)
    ]
    flat = pl.BlockSpec((windows, TOKENS, wide), lambda g: (0, 0, g))
    flat_shape = jax.ShapeDtypeStruct((windows, TOKENS, count * wide), BF16)
    return functools.partial(call, after=after)(
        functools.partial(attend_back_kernel, shifted, width // HEADS),
        (count,),
        [flag_spec()]
        + qkv_specs
        + [
            pl.BlockSpec((windows, TOKENS, wide), lambda g: (0, 0, first + g)),
            pl.BlockSpec((windows, TOKENS, wide), lambda g: (0, 0, first + g)),
            pl.BlockSpec((GROUP, TOKENS, TOKENS), lambda g: (first + g, 0, 0)),
            whole_block((TOKENS, 8)),
            whole_block((8, TOKENS)),
            pl.BlockSpec((windows, 1, 2 * GROUP, TOKENS), lambda g: (0, first + g, 0, 0)),
        ],
        [flat, flat, flat, pl.BlockSpec((GROUP, CELLS, WIDE), lambda g: (g, 0, 0))],
        [flat_shape] * 3 + [jax.ShapeDtypeStruct((count * GROUP, CELLS, WIDE), F32)],
        160 * windows * TOKENS * TOKENS * count * wide,
        [pltpu.VMEM((TOKENS, WIDE), F32)],
    )(flags, qkv, qkv, qkv, grad, attended, bias, late_tokens(), late_tokens().T, log)


def normal_below(x):
    bell = jnp.exp2(x * x * (-0.5 * LOG2E)) * (1.0 / math.sqrt(2 * math.pi))
    return 0.5 + 0.5 * lax.erf(x * math.sqrt(0.5)), bell


def spread_down(down_ref, w2_ref):
    _, parts, own, width = w2_ref.shape
    for part in range(parts):
        cols = slice(part * width, (part + 1) * width)
        w2_ref[:, part] = down_ref[:, cols].reshape(-1, own, width)


def chunk_rows(w2_ref, first, chunk):
    _, parts, own, width = w2_ref.shape
    step = chunk // (parts * own)
    return w2_ref[first * step : (first + 1) * step].reshape(chunk, width)


def branch_kernel(count, *refs):
    att_refs = refs[:count]
    x_ref, vec_ref, wo_ref, w1_ref, down_ref, mid_ref, hid_ref, slope_ref, out_ref, w2_ref = refs[count:]

    @pl.when(pl.program_id(0) == 0)
    def _():
        spread_down(down_ref, w2_ref)

    chunk = 512
    attended = jnp.concatenate([ref[0] for ref in att_refs], axis=1)
    middle = x_ref[0].astype(F32) + mm(attended, wo_ref[...]) + vec_ref[4:5]
    mid_ref[0] = middle
    unit, _ = unit_rows(middle)
    normed = (unit * vec_ref[5:6] + vec_ref[6:7]).astype(BF16)
    after = middle + vec_ref[7:8]
    for n in range(w1_ref.shape[1] // chunk):
        cols = slice(n * chunk, (n + 1) * chunk)
        pre = mm(normed, w1_ref[:, cols]) + vec_ref[8 + n : 9 + n]
        below, bell = normal_below(pre)
        hidden = (pre * below).astype(BF16)
        hid_ref[0, :, cols] = hidden
        slope_ref[0, :, cols] = (below + pre * bell).astype(BF16)
        after = after + mm(hidden, chunk_rows(w2_ref, n, chunk))
    out_ref[0] = after.astype(out_ref.dtype)


def weight_block(rows, width, column):
    return pl.BlockSpec((rows, width), lambda *ids: (0, column))


def branch_weights(weights, width, wide):
    (wo, wo_at), (w1, w1_at), (down, down_at) = weights
    specs = [
        weight_block(width, width, wo_at),
        weight_block(width, wide, w1_at),
        weight_block(width, wide, down_at),
    ]
    return (wo, w1, down), specs


def run_branch(x, attended, vec, weights, out_dtype, after=None):
    windows, _, width = x.shape
    wide = 4 * width
    arrays, specs = branch_weights(weights, width, wide)
    return functools.partial(call, after=after)(
        functools.partial(branch_kernel, len(attended)),
        (windows,),
        [win_block(part.shape[-1]) for part in attended]
        + [win_block(width), whole_block(vec.shape)]
        + specs,
        [win_block(width), win_block(wide), win_block(wide), win_block(width)],
        [
            jax.ShapeDtypeStruct((windows, TOKENS, width), F32),
            jax.ShapeDtypeStruct((windows, TOKENS, wide), BF16),
            jax.ShapeDtypeStruct((windows, TOKENS, wide), BF16),
            jax.ShapeDtypeStruct((windows, TOKENS, width), out_dtype),
        ],
        2 * windows * TOKENS * width * (width + 2 * wide),
        [pltpu.VMEM((width // 16, wide // width, 16, width), BF16)],
    )(*attended, x, vec, *arrays)


def add_rows(ref, rows, value):
    ref[rows, :] += jnp.sum(value.astype(F32), axis=0, keepdims=True)


def split_out(sums_ref, core, own_ref, sent_ref):
    own_ref[...] = sums_ref[:, core]
    sent_ref[...] = sums_ref[:, 1 - core].astype(BF16)


def branch_back_kernel(count, split, flag_ref, *refs):
    att_refs = refs[:count]
    grad_ref, mid_ref, hid_ref, slope_ref, vec_ref, wo_ref, w1_ref, down_ref = refs[count : count + 8]
    gm_ref, ga_ref, vecs_ref = refs[count + 8 : count + 11]
    outs, (d1_ref, d2_ref, w2_ref) = refs[count + 11 : -3], refs[-3:]
    chunk = 512
    width, wide = w1_ref.shape

    @pl.when(pl.program_id(0) == 0)
    def _():
        spread_down(down_ref, w2_ref)
        d1_ref[...] = jnp.zeros_like(d1_ref)
        d2_ref[...] = jnp.zeros_like(d2_ref)
        vecs_ref[...] = jnp.zeros_like(vecs_ref)

    grad = grad_ref[0].astype(F32)
    branch = grad.astype(BF16)
    unit, inverse = unit_rows(mid_ref[0])
    normed = (unit * vec_ref[5:6] + vec_ref[6:7]).astype(BF16)
    add_rows(vecs_ref, slice(7, 8), branch)
    back = None
    blocks = chunk // d2_ref.shape[2]
    for n in range(wide // chunk):
        cols = slice(n * chunk, (n + 1) * chunk)
        total = mm(hid_ref[0, :, cols], branch, 0, 0)
        at = slice(n * blocks // 2, (n + 1) * blocks // 2)
        d2_ref[at] += total.reshape((-1,) + d2_ref.shape[1:])
        grad_pre = mm(branch, chunk_rows(w2_ref, n, chunk), 1, 1) * slope_ref[0, :, cols].astype(F32)
        grad_pre = grad_pre.astype(BF16)
        add_rows(vecs_ref, slice(8 + n, 9 + n), grad_pre)
        d1_ref[:, :, :, cols] += mm(normed, grad_pre, 0, 0).reshape(d1_ref.shape[:3] + (chunk,))
        part = mm(grad_pre, w1_ref[:, cols], 1, 1)
        back = part if back is None else back + part
    add_rows(vecs_ref, slice(5, 6), back * unit)
    add_rows(vecs_ref, slice(6, 7), back)
    middle_grad = grad + norm_back(back, unit, inverse, vec_ref[5:6])
    gm_ref[0] = middle_grad
    branch = middle_grad.astype(BF16)
    add_rows(vecs_ref, slice(4, 5), branch)
    attended = jnp.concatenate([ref[0] for ref in att_refs], axis=1)
    total = mm(attended, branch, 0, 0)
    d1_ref[:, :, :, wide:] += total.reshape(d1_ref.shape[:3] + (width,))
    ga_ref[0] = mm(branch, wo_ref[...], 1, 1).astype(BF16)

    @pl.when(pl.program_id(0) == pl.num_programs(0) - 1)
    def _():
        if split:
            split_out(d1_ref, flag_ref[0], *outs[:2])
            split_out(d2_ref, flag_ref[0], *outs[2:])
        else:
            (out_ref,) = outs
            out_ref[:, : wide + width] = d1_ref[...].reshape(width, -1).astype(BF16)
            parts = wide // width
            for part in range(parts):
                first = wide + width + part * width
                piece = d2_ref[:, :, part * 16 : (part + 1) * 16, :].reshape(width, width)
                out_ref[:, first : first + width] = piece.astype(BF16)


def run_branch_back(grad, middle, attended, hidden, slope, vec, weights, flags, split, after=None):
    windows, _, width = middle.shape
    wide = 4 * width
    arrays, specs = branch_weights(weights, width, wide)
    flat = win_block(width)
    pairs = width // 32
    if split:
        shapes = []
        for rows, cols in ((16, wide + width), (64, width)):
            shapes.append(jax.ShapeDtypeStruct((pairs, rows, cols), F32))
            shapes.append(jax.ShapeDtypeStruct((pairs, rows, cols), BF16))
    else:
        shapes = [jax.ShapeDtypeStruct((width, 2 * wide + width), BF16)]
    return functools.partial(call, after=after)(
        functools.partial(branch_back_kernel, len(attended), split),
        (windows,),
        [flag_spec()]
        + [win_block(part.shape[-1]) for part in attended]
        + [flat, flat, win_block(wide), win_block(wide), whole_block(vec.shape)]
        + specs,
        [flat, flat, whole_block(vec.shape)] + [whole_block(s.shape) for s in shapes],
        [
            jax.ShapeDtypeStruct((windows, TOKENS, width), F32),
            jax.ShapeDtypeStruct((windows, TOKENS, width), BF16),
            jax.ShapeDtypeStruct(vec.shape, F32),
        ]
        + shapes,
        4 * windows * TOKENS * width * (width + 2 * wide),
        [
            pltpu.VMEM((pairs, 2, 16, wide + width), F32),
            pltpu.VMEM((pairs, 2, 64, width), F32),
            pltpu.VMEM((pairs * 2, wide // width, 16, width), BF16),
        ],
    )(flags, *attended, grad, middle, hidden, slope, vec, *arrays)


def qkv_back_kernel(count, flag_ref, *refs):
    grads, refs = refs[: 3 * count], refs[3 * count :]
    x_ref, gm_ref, vec_ref, wq_ref, wk_ref, wv_ref, rest_ref, mask_ref, pick_ref, spread_ref = refs[:10]
    out_ref, own_ref, sent_ref, dw_ref, vecs_ref = refs[10:]
    width = x_ref.shape[-1]

    @pl.when(pl.program_id(0) == 0)
    def _():
        dw_ref[...] = jnp.zeros_like(dw_ref)
        vecs_ref[...] = rest_ref[...]

    unit, inverse = unit_rows(x_ref[0].astype(F32))
    normed = (unit * vec_ref[0:1] + vec_ref[1:2]).astype(BF16)
    back = None
    for part, ref in enumerate((wq_ref, wk_ref, wv_ref)):
        grad = jnp.concatenate([g[0] for g in grads[part * count : (part + 1) * count]], axis=1)
        total = mm(normed, grad, 0, 0)
        cols = slice(part * width, (part + 1) * width)
        dw_ref[:, :, :, cols] += total.reshape(dw_ref.shape[:3] + (width,))
        here = mm(grad, ref[...], 1, 1)
        back = here if back is None else back + here
        if part == 0:
            add_rows(vecs_ref, slice(2, 3), grad)
        if part == 2:
            add_rows(vecs_ref, slice(3, 4), grad)
    add_rows(vecs_ref, slice(0, 1), back * unit)
    add_rows(vecs_ref, slice(1, 2), back)
    out_ref[0] = (gm_ref[0] + norm_back(back, unit, inverse, vec_ref[0:1])).astype(out_ref.dtype)

    @pl.when(pl.program_id(0) == pl.num_programs(0) - 1)
    def _():
        rows = vecs_ref[...]
        high = rows.astype(BF16)
        low = (rows - high.astype(F32)).astype(BF16)
        total = None
        for piece in (high, low):
            piece = (mm(pick_ref[...], piece, 0, 0) * mask_ref[...].astype(F32)).astype(BF16)
            piece = mm(piece, spread_ref[0], 1, 1)
            total = piece if total is None else total + piece
        dw_ref[:, :, :, 3 * width :] = total.reshape(dw_ref.shape[:3] + (128,))
        split_out(dw_ref, flag_ref[0], own_ref, sent_ref)


def run_qkv_back(grads, x, grad_middle, vec, w_qkv, rest, flags, out_dtype, after=None):
    windows, _, width = x.shape
    flat = win_block(width)
    weight, at = w_qkv
    extra = [jnp.asarray(a, BF16) for a in vector_slots()]
    shape = (width // 32, 16, 3 * width + 128)
    return functools.partial(call, after=after)(
        functools.partial(qkv_back_kernel, len(grads) // 3),
        (windows,),
        [flag_spec()]
        + [win_block(part.shape[-1]) for part in grads]
        + [flat, flat, whole_block(vec.shape)]
        + [weight_block(width, width, at + n) for n in range(3)]
        + [whole_block(rest.shape)]
        + [whole_block(a.shape) for a in extra],
        [flat, whole_block(shape), whole_block(shape)],
        [
            jax.ShapeDtypeStruct((windows, TOKENS, width), out_dtype),
            jax.ShapeDtypeStruct(shape, F32),
            jax.ShapeDtypeStruct(shape, BF16),
        ],
        4 * windows * TOKENS * width * 3 * width,
        [pltpu.VMEM((shape[0], 2) + shape[1:], F32), pltpu.VMEM(rest.shape, F32)],
    )(flags, *grads, x, grad_middle, vec, weight, weight, weight, rest, *extra)


def pack_first_kernel(qkv_ref, *refs):
    vector_refs, (first_ref, rows_ref) = refs[:-2], refs[-2:]
    own, width3 = qkv_ref.shape[1:]
    rows_ref[...] = jnp.zeros_like(rows_ref)
    row = 0
    lane = lax.broadcasted_iota(jnp.int32, (1, 128), 1)
    for ref in vector_refs:
        values = ref[...].astype(F32)
        values = jnp.pad(values, ((0, 0), (0, 128 - values.shape[1])))
        for part in range(ref.shape[1] // own):
            line = jnp.zeros((1, 128), F32)
            for layer in range(LAYERS):
                turn = ((layer - part) * own) % 128
                turned = pltpu.roll(values, turn, 1) if turn else values
                here = (lane >= layer * own) & (lane < (layer + 1) * own)
                line = jnp.where(here, turned[layer : layer + 1], line)
            rows_ref[row : row + 1, :] = line
            row += 1
    first_ref[:, :width3] = qkv_ref[0]
    first_ref[:, width3:] = rows_ref[...].astype(BF16)


def pack_first(qkv, *vectors, after=None):
    own, width3 = qkv.shape[1:]
    return functools.partial(call, after=after)(
        pack_first_kernel,
        (1,),
        [whole_block((1, own, width3))] + [whole_block(v.shape) for v in vectors],
        whole_block((own, width3 + 128)),
        jax.ShapeDtypeStruct((own, width3 + 128), BF16),
        1e6,
        [pltpu.VMEM((16, 128), F32)],
    )(qkv, *vectors)


def pack_branch_kernel(out_ref, fc1_ref, fc2_ref, packed_ref):
    own, width, wide = fc1_ref.shape[1], fc2_ref.shape[2], fc1_ref.shape[2]
    for layer in range(LAYERS):
        first = 2 * wide * layer
        packed_ref[:, first : first + wide] = fc1_ref[layer]
        for part in range(wide // width):
            at = first + wide + part * width
            packed_ref[:, at : at + width] = fc2_ref[layer, part * own : (part + 1) * own, :]
        at = 2 * wide * LAYERS + layer * width
        packed_ref[:, at : at + width] = out_ref[layer]


def gather_branch(weights, after=None):
    own, wide = weights[1].shape[1:]
    width = weights[0].shape[2]
    packed = jax.ShapeDtypeStruct((own, LAYERS * (2 * wide + width)), BF16)
    shard = functools.partial(call, after=after)(
        pack_branch_kernel,
        (1,),
        [whole_block(w.shape) for w in weights],
        whole_block(packed.shape),
        packed,
        1e6,
    )(*weights)
    whole = lax.all_gather(shard, ALL, axis=0, tiled=True)
    outs = 2 * wide * LAYERS // width
    return [((whole, outs + n), (whole, 2 * n), (whole, 2 * n + 1)) for n in range(LAYERS)]


def vector_slots():
    devices, own = 32, 16
    count = devices * own
    mask = np.zeros((devices * 16, count), np.float32)
    pick = np.zeros((16, devices * 16), np.float32)
    spread = np.zeros((LAYERS, 128, count), np.float32)
    for device in range(devices):
        for first, parts in ((0, 1), (1, 1), (2, 2), (4, 1), (5, 1), (6, 1), (7, 1), (8, 4)):
            for part in range(parts):
                row, start = divmod(device * own * parts + part * own, count)
                slot = device * 16 + first + part
                pick[first + row, slot] = 1
                mask[slot, start : start + own] = 1
    for layer in range(LAYERS):
        for lane in range(count):
            spread[layer, layer * own + lane % own, lane] = 1
    return mask, pick, spread


def vectors_kernel(block_ref, mask_ref, pick_ref, spread_ref, out_ref):
    block = block_ref[...]
    for layer in range(LAYERS):
        lines = mm(block, spread_ref[layer]) * mask_ref[...].astype(F32)
        out_ref[layer] = mm(pick_ref[...], lines.astype(BF16))


def vectors_whole(blocks, after=None):
    count, width = blocks.shape
    extra = [jnp.asarray(a, BF16) for a in vector_slots()]
    return functools.partial(call, after=after)(
        vectors_kernel,
        (1,),
        [pl.BlockSpec((count, 128), lambda n: (0, width // 128 - 1))]
        + [whole_block(a.shape) for a in extra],
        whole_block((LAYERS, 16, count)),
        jax.ShapeDtypeStruct((LAYERS, 16, count), F32),
        1e9,
    )(blocks, *extra)


def finish_kernel(
    mix0_ref, mix1_ref, mid_ref, two_ref, later_ref, gain1_ref, bias1_ref, qkv_ref, qvb_ref, out_ref,
    outb_ref, gain2_ref, bias2_ref, fc1_ref, fc1b_ref, fc2_ref, fc2b_ref,
):
    width, wide = out_ref.shape[2], fc1_ref.shape[2]
    own = gain1_ref.shape[1]
    lane = lax.broadcasted_iota(jnp.int32, (1, 128), 1)
    for layer, mix_ref in enumerate((mix0_ref, mix1_ref)):
        qkv_ref[layer] = mix_ref[:, : 3 * width]
        row = 0
        for ref in (gain1_ref, bias1_ref, qvb_ref, outb_ref, gain2_ref, bias2_ref, fc2b_ref, fc1b_ref):
            line = jnp.zeros((1, 128), F32)
            for part in range(ref.shape[1] // own):
                piece = mix_ref[row : row + 1, 3 * width : 3 * width + 128]
                piece = pltpu.roll(piece, part * own, 1) if part else piece
                line = jnp.where((lane >= part * own) & (lane < (part + 1) * own), piece, line)
                row += 1
            ref[layer : layer + 1, :] = line[:, : ref.shape[1]]
    fc1_ref[0] = mid_ref[:, :wide]
    out_ref[0] = mid_ref[:, wide:]
    fc2_ref[0] = two_ref[...]
    fc1_ref[1] = later_ref[:, :wide].astype(F32)
    out_ref[1] = later_ref[:, wide : wide + width].astype(F32)
    for part in range(wide // width):
        first = wide + width + part * width
        piece = later_ref[:, first : first + width].astype(F32)
        fc2_ref[1, part * own : (part + 1) * own, :] = piece


def run_finish(mixes, mid, two, later):
    own, width = 16, two.shape[1]
    wide = mid.shape[1] - width
    shapes = [
        (own,), (own,), (own, 3 * width), (2 * own,), (own, width), (own,),
        (own,), (own,), (own, wide), (4 * own,), (4 * own, width), (own,),
    ]
    operands = [*mixes, mid, two, later]
    return call(
        finish_kernel,
        (1,),
        [whole_block(v.shape) for v in operands],
        [whole_block((LAYERS,) + shape) for shape in shapes],
        [jax.ShapeDtypeStruct((LAYERS,) + shape, F32) for shape in shapes],
        1e6,
    )(*operands)


def place_flags():
    quadrant = lax.axis_index(SPACE)
    last = lax.axis_index(TM) == lax.axis_size(TM) - 1
    flags = [lax.axis_index(CLIP) % 2, last, quadrant // 2, quadrant % 2]
    return jnp.stack([jnp.asarray(f, jnp.int32) for f in flags])


FIRST, TABLES, LATER, ROLL, GRAD, BACK, D_MID, D_TWO, TABLE, D_QKV = range(10)


def local_windows(
    clips_in,
    ln1_gain,
    ln1_bias,
    qkv_weight,
    qv_bias,
    out_weight,
    out_bias,
    ln2_gain,
    ln2_bias,
    fc1_weight,
    fc1_bias,
    fc2_weight,
    fc2_bias,
    pos_table,
    out_grad,
):
    _, frames_here, _, _, width = clips_in.shape
    windows = frames_here // WIN_T
    own = ln1_gain.shape[1]
    heads_here = pos_table.shape[2]
    one, two = stage_orders()
    flat = (windows, TOKENS, width)
    flags = place_flags()
    halo = Halo()
    flow = Flow()

    def stepped(run, *args, names=None, waits=(), **options):
        order = Order(flow.pending() + list(waits))
        out = run(*args, after=order, **options)
        flow.step(order.token, names)
        return out

    def halo_start(name, packed, onward):
        flow.start(name, halo_flow(packed, onward))

    def send_table():
        (came,), _ = yield [(tables, TM, swap_pairs(TM, 0))]
        first = lax.axis_index(TM) == 0
        return jnp.where(first, tables, came), jnp.where(first, came, tables)

    branch = (out_weight, fc1_weight, fc2_weight)
    first = pack_first(
        qkv_weight, ln1_gain, ln1_bias, qv_bias, out_bias, ln2_gain, ln2_bias, fc2_bias, fc1_bias
    )
    flow.start(FIRST, Gather(first, one))
    tables = pos_table.transpose(0, 2, 1)
    flow.start(TABLES, send_table())
    weights0, weights1 = stepped(gather_branch, branch)
    tables = flow.finish(TABLES)
    bias0 = stepped(table_to_bias, tables[0][0])
    bias0 = stepped(table_to_bias, tables[1][0], bias0)
    bias1 = stepped(table_to_bias, tables[0][1])
    first = flow.finish(FIRST)
    flow.start(LATER, Gather(qkv_weight[1], one))
    vec = stepped(vectors_whole, first)

    stream0 = clips_in.reshape(flat)
    qkv0 = stepped(run_qkv, stream0, vec[0], (first, 0))
    att0, log0 = stepped(run_attend, qkv0, bias0, flags, False)
    grad_in = out_grad.reshape(flat)
    mid0, hid0, slope0, stream1 = stepped(run_branch, stream0, [att0], vec[0], weights0, F32)
    halo_start(ROLL, halo_pack(stream1, halo, True, center=True), True)
    bias1 = stepped(table_to_bias, tables[1][1], bias1)
    later = flow.finish(LATER)
    rolled1 = halo_unpack(
        stream1, flow.finish(ROLL), halo, True, F32, center=True, after=Order([bias1])
    )
    qkv1 = run_qkv(rolled1, vec[1], (later, 0))
    halo_start(GRAD, halo_pack(grad_in, halo, True, after=Order([qkv1])), True)
    att1, log1 = stepped(run_attend, qkv1, bias1, flags, True)
    mid1, hid1, slope1, rolled_out = stepped(
        run_branch, rolled1, [att1], vec[1], weights1, F32, waits=flow.done[GRAD]
    )
    out_packed = halo_pack(rolled_out, halo, False, joined=True)
    out_parts = halo_gather(out_packed)
    grad = stepped(halo_unpack, grad_in, flow.done[GRAD], halo, True, BF16, names=())

    kept = (
        (stream0, qkv0, att0, log0, mid0, hid0, slope0, bias0, weights0, (first, 0)),
        (rolled1, qkv1, att1, log1, mid1, hid1, slope1, bias1, weights1, (later, 0)),
    )
    tables = [None] * LAYERS
    for layer in reversed(range(LAYERS)):
        stream, qkv, att, log, mid, hid, slope, bias, weights, w_qkv = kept[layer]
        grad_mid, grad_att, rest, *halves = stepped(
            run_branch_back, grad, mid, [att], hid, slope, vec[layer], weights, flags, layer == 0,
            waits=[out_packed if layer else out_parts],
        )
        if layer == 0:
            flow.start(D_MID, scatter_flow(*halves[:2], one))
            flow.start(D_TWO, scatter_flow(*halves[2:], two))
        else:
            mid_share1 = lax.psum_scatter(halves[0], ALL, scatter_dimension=0, tiled=True)
        grads, sums = [], []
        calls = 1 if layer else 2
        groups = HEADS // GROUP // calls
        for n in range(calls):
            *parts, total = stepped(
                run_attend_back, qkv, grad_att, att, bias, flags, log, layer == 1, n * groups, groups,
            )
            grads.append(parts)
            sums.append(total)
        grads = [part for group in zip(*grads) for part in group]
        if layer == 0:
            tables[0] = [
                stepped(sums_to_table, total, names=names) for total, names in zip(sums, ((), None))
            ]
            pairs = [jnp.stack([tables[layer][n] for layer in range(LAYERS)]) for n in range(2)]
            flow.start(TABLE, table_flow(pairs, heads_here))
        grad_stream, *halves = stepped(
            run_qkv_back, grads, stream, grad_mid, vec[layer], w_qkv, rest, flags,
            F32 if layer else BF16,
        )
        if layer:
            halo_start(BACK, halo_pack(grad_stream, halo, False), False)
        flow.start(D_QKV + layer, scatter_flow(*halves, one))
        if layer:
            found = [
                stepped(sums_to_table, sums[0], n * heads_here, heads_here, names=names)
                for n, names in enumerate(((), None))
            ]
            tables[1] = found
            grad = stepped(
                halo_unpack, grad_stream, flow.finish(BACK), halo, False, F32, names=(),
                waits=found,
            )
    in_grad = grad_stream
    clips_out = stepped(
        halo_unpack, rolled_out, out_parts, halo, False, BF16, mean_of=stream1
    )
    while flow.live:
        flow.step(None)
    grads = run_finish(
        [flow.done[D_QKV + layer] for layer in range(LAYERS)],
        flow.done[D_MID],
        flow.done[D_TWO],
        mid_share1,
    )
    return (
        clips_out.reshape(clips_in.shape),
        in_grad.reshape(clips_in.shape),
        *grads,
        flow.done[TABLE].transpose(0, 2, 1),
    )


def windows_are_local(mesh):
    def decide(clips_in, *rest):
        clips, frames_here = clips_in.shape[:2]
        own = rest[0].shape[1]
        return (
            clips == 1
            and frames_here % WIN_T == 0
            and own == 16
            and mesh.shape[TM] == 2
            and mesh.shape[SPACE] == 4
        )

    def program(*args):
        return local_windows(*args) if decide(*args) else per_device(*args)

    return program


def solution(mesh):
    placed = (
        P(CLIP, TM, SPACE, None, None),
        P(None, ALL),
        P(None, ALL),
        P(None, ALL, None),
        P(None, ALL),
        P(None, ALL, None),
        P(None, ALL),
        P(None, ALL),
        P(None, ALL),
        P(None, ALL, None),
        P(None, ALL),
        P(None, ALL, None),
        P(None, ALL),
        P(None, None, TM),
        P(CLIP, TM, SPACE, None, None),
    )
    return jax.shard_map(
        windows_are_local(mesh),
        mesh=mesh,
        in_specs=placed,
        out_specs=(
            P(CLIP, TM, SPACE, None, None),
            P(CLIP, TM, SPACE, None, None),
            P(None, ALL),
            P(None, ALL),
            P(None, ALL, None),
            P(None, ALL),
            P(None, ALL, None),
            P(None, ALL),
            P(None, ALL),
            P(None, ALL),
            P(None, ALL, None),
            P(None, ALL),
            P(None, ALL, None),
            P(None, ALL),
            P(None, None, TM),
        ),
        check_vma=False,
    )
```

```python
import functools
import math

import jax
import jax.numpy as jnp
import numpy as np
from jax import lax
from jax.experimental import pallas as pl
from jax.experimental.pallas import tpu as pltpu
from jax.sharding import PartitionSpec as P

HEADS = 16
WIN_T = 8
WIN_HW = 7
LAYERS = 2


masked_score = -1000000000.0
TM, SPACE, CLIP = "tm", "space", "clip"
ALL = (TM, SPACE, CLIP)


def partner(value, axis, bit):
    mask = 2**bit
    pairs = [(source, source ^ mask) for source in range(lax.axis_size(axis))]
    return lax.ppermute(value, axis, pairs)


def norm_rows(values, gain, offset):
    mean_row = jnp.mean(values, axis=-1, keepdims=True)
    centered = values - mean_row
    spread = jnp.mean(centered * centered, axis=-1, keepdims=True)
    return centered * lax.rsqrt(spread + 1e-05) * gain + offset


def gelu_exact(values):
    return jax.nn.gelu(values, approximate=False)


def project(left, right):
    return jnp.einsum("...i,ij->...j", left, right, preferred_element_type=jnp.float32)


def project_back(left, right):
    return jnp.einsum("...j,ij->...i", left, right, preferred_element_type=jnp.float32)


def outer_sum(left, right):
    flat_left = left.reshape(-1, left.shape[-1])
    flat_right = right.reshape(-1, right.shape[-1])
    return jnp.einsum("ti,tj->ij", flat_left, flat_right, preferred_element_type=jnp.float32)


def column_sum(values):
    return jnp.sum(values.reshape(-1, values.shape[-1]).astype(jnp.float32), axis=0)


def relative_index(win_t, win_hw):
    count = win_t * win_hw * win_hw
    positions = jnp.arange(count, dtype=jnp.int32)
    frame_pos = positions // (win_hw * win_hw)
    row_pos = positions // win_hw % win_hw
    col_pos = positions % win_hw
    span = 2 * win_hw - 1
    frame_off = frame_pos[:, None] - frame_pos[None, :] + win_t - 1
    row_off = row_pos[:, None] - row_pos[None, :] + win_hw - 1
    col_off = col_pos[:, None] - col_pos[None, :] + win_hw - 1
    return frame_off * span * span + row_off * span + col_off


def band_label(coord, extent, window, reach):
    return jnp.where(coord < extent - window, 0, jnp.where(coord < extent - reach, 1, 2)).astype(
        jnp.int32
    )


def region_match(frames):
    quadrant = lax.axis_index(SPACE)
    row_quad = quadrant // 2
    col_quad = quadrant % 2
    local = jnp.arange(WIN_HW, dtype=jnp.int32)
    label_t = band_label(jnp.arange(frames, dtype=jnp.int32), frames, WIN_T, WIN_T // 2)
    label_r = band_label(row_quad * WIN_HW + local, 2 * WIN_HW, WIN_HW, WIN_HW // 2)
    label_c = band_label(col_quad * WIN_HW + local, 2 * WIN_HW, WIN_HW, WIN_HW // 2)
    region = label_t[:, None, None] * 9 + label_r[None, :, None] * 3 + label_c[None, None, :]
    region = region.reshape(frames // WIN_T, WIN_T * WIN_HW * WIN_HW)
    return region[:, :, None] == region[:, None, :]


def space_roll(field, onward):
    side = field.shape[2]
    reach = side // 2
    sent_rows = field[:, :, :reach] if onward else field[:, :, side - reach :]
    came_rows = partner(sent_rows, SPACE, 1)
    if onward:
        rows_done = jnp.concatenate([field, came_rows], axis=2)[:, :, reach : reach + side]
    else:
        rows_done = jnp.concatenate([came_rows, field], axis=2)[:, :, :side]
    sent_cols = rows_done[:, :, :, :reach] if onward else rows_done[:, :, :, side - reach :]
    came_cols = partner(sent_cols, SPACE, 0)
    if onward:
        return jnp.concatenate([rows_done, came_cols], axis=3)[:, :, :, reach : reach + side]
    return jnp.concatenate([came_cols, rows_done], axis=3)[:, :, :, :side]


def gather_layer(shards, layer):
    return tuple(lax.all_gather(w[layer], ALL, axis=0, tiled=True) for w in shards)


def table_bias(table):
    rel = relative_index(WIN_T, WIN_HW)
    return table.astype(jnp.float32)[rel].transpose(2, 0, 1)


def window_scores(queries, keys, bias, same, scale):
    scores = (
        jnp.einsum("wqhd,wkhd->whqk", queries, keys, preferred_element_type=jnp.float32) * scale
        + bias[None]
    )
    if same is not None:
        scores = jnp.where(same[:, None], scores, masked_score)
    return scores


def to_windows(field):
    clips, frames, cells, heads_here, head_size = field.shape
    return field.reshape(clips, frames // WIN_T, WIN_T * cells, heads_here, head_size)


def to_frames(field, frames):
    clips = field.shape[0]
    return field.reshape(clips, frames, WIN_HW * WIN_HW, field.shape[3], field.shape[4])


def layer_forward(stream, params, table, shifted):
    (
        gain_one,
        bias_one,
        mix_weight,
        mix_bias,
        proj_weight,
        proj_bias,
        gain_two,
        bias_two,
        wide_weight,
        wide_bias,
        narrow_weight,
        narrow_bias,
    ) = params
    clips, frames_here, side = (stream.shape[0], stream.shape[1], stream.shape[2])
    width = stream.shape[-1]
    head_size = width // HEADS
    scale = head_size ** (-0.5)
    normed = norm_rows(stream, gain_one.astype(jnp.float32), bias_one.astype(jnp.float32)).astype(
        jnp.bfloat16
    )
    if shifted:
        normed = space_roll(normed, True)
    mixed = project(normed, mix_weight)
    mix_bias32 = mix_bias.astype(jnp.float32)
    head_shape = (clips, frames_here, side * side, HEADS, head_size)
    queries = (mixed[..., :width] + mix_bias32[:width]).astype(jnp.bfloat16).reshape(head_shape)
    keys = mixed[..., width : 2 * width].astype(jnp.bfloat16).reshape(head_shape)
    values = (mixed[..., 2 * width :] + mix_bias32[width:]).astype(jnp.bfloat16).reshape(head_shape)
    queries, keys, values = (
        lax.all_to_all(queries, TM, split_axis=3, concat_axis=1, tiled=True),
        lax.all_to_all(keys, TM, split_axis=3, concat_axis=1, tiled=True),
        lax.all_to_all(values, TM, split_axis=3, concat_axis=1, tiled=True),
    )
    frames = queries.shape[1]
    if shifted:
        queries = jnp.roll(queries, -(WIN_T // 2), axis=1)
        keys = jnp.roll(keys, -(WIN_T // 2), axis=1)
        values = jnp.roll(values, -(WIN_T // 2), axis=1)
    queries, keys, values = (to_windows(queries), to_windows(keys), to_windows(values))
    bias = table_bias(table)
    same = region_match(frames) if shifted else None

    def attend_clip(items):
        clip_queries, clip_keys, clip_values = items
        scores = window_scores(clip_queries, clip_keys, bias, same, scale)
        peak = jnp.max(scores, axis=-1, keepdims=True)
        raised = jnp.exp(scores - peak)
        total = jnp.sum(raised, axis=-1, keepdims=True)
        probs = (raised / total).astype(jnp.bfloat16)
        out_win = jnp.einsum(
            "whqk,wkhd->wqhd", probs, clip_values, preferred_element_type=jnp.float32
        ).astype(jnp.bfloat16)
        return (out_win, peak + jnp.log(total))

    attended_heads, log_total = lax.map(attend_clip, (queries, keys, values))
    attended_heads = to_frames(attended_heads, frames)
    if shifted:
        attended_heads = jnp.roll(attended_heads, WIN_T // 2, axis=1)
    attended = lax.all_to_all(attended_heads, TM, split_axis=1, concat_axis=3, tiled=True)
    attended = attended.reshape(clips, frames_here, side, side, width)
    if shifted:
        attended = space_roll(attended, False)
    middle = stream + project(attended, proj_weight) + proj_bias.astype(jnp.float32)
    normed_two = norm_rows(
        middle, gain_two.astype(jnp.float32), bias_two.astype(jnp.float32)
    ).astype(jnp.bfloat16)
    hidden_pre = project(normed_two, wide_weight) + wide_bias.astype(jnp.float32)
    hidden = gelu_exact(hidden_pre).astype(jnp.bfloat16)
    after = middle + project(hidden, narrow_weight) + narrow_bias.astype(jnp.float32)
    stash = (
        stream,
        normed,
        queries,
        keys,
        values,
        log_total,
        attended,
        middle,
        normed_two,
        hidden_pre,
        hidden,
    )
    return (stash, after)


def layer_backward(grad_after, params, table, stash, shifted):
    (
        gain_one,
        bias_one,
        mix_weight,
        mix_bias,
        proj_weight,
        proj_bias,
        gain_two,
        bias_two,
        wide_weight,
        wide_bias,
        narrow_weight,
        narrow_bias,
    ) = params
    (
        stream,
        normed,
        queries,
        keys,
        values,
        log_total,
        attended,
        middle,
        normed_two,
        hidden_pre,
        hidden,
    ) = stash
    clips, frames_here, side = (stream.shape[0], stream.shape[1], stream.shape[2])
    width = stream.shape[-1]
    head_size = width // HEADS
    scale = head_size ** (-0.5)
    frames = queries.shape[1] * WIN_T
    grad_branch_two = grad_after.astype(jnp.bfloat16)
    narrow_grad = outer_sum(hidden, grad_branch_two)
    narrow_bias_grad = column_sum(grad_branch_two)
    grad_hidden = project_back(grad_branch_two, narrow_weight)
    gelu_pull = jax.vjp(gelu_exact, hidden_pre)[1]
    grad_pre = gelu_pull(grad_hidden)[0].astype(jnp.bfloat16)
    wide_grad = outer_sum(normed_two, grad_pre)
    wide_bias_grad = column_sum(grad_pre)
    grad_normed_two = project_back(grad_pre, wide_weight)
    norm_pull_two = jax.vjp(
        norm_rows, middle, gain_two.astype(jnp.float32), bias_two.astype(jnp.float32)
    )[1]
    grad_mid_part, gain_two_grad, bias_two_grad = norm_pull_two(grad_normed_two)
    grad_middle = grad_after + grad_mid_part
    grad_branch_one = grad_middle.astype(jnp.bfloat16)
    proj_grad = outer_sum(attended, grad_branch_one)
    proj_bias_grad = column_sum(grad_branch_one)
    grad_attended = project_back(grad_branch_one, proj_weight).astype(jnp.bfloat16)
    if shifted:
        grad_attended = space_roll(grad_attended, True)
    grad_attended = grad_attended.reshape(clips, frames_here, side * side, HEADS, head_size)
    grad_attended = lax.all_to_all(grad_attended, TM, split_axis=3, concat_axis=1, tiled=True)
    if shifted:
        grad_attended = jnp.roll(grad_attended, -(WIN_T // 2), axis=1)
    grad_attended = to_windows(grad_attended)
    bias = table_bias(table)
    same = region_match(frames) if shifted else None

    def attend_back(carry, items):
        clip_queries, clip_keys, clip_values, clip_grad, clip_log = items
        scores = window_scores(clip_queries, clip_keys, bias, same, scale)
        probs = jnp.exp(scores - clip_log)
        grad_probs = jnp.einsum(
            "wqhd,wkhd->whqk", clip_grad, clip_values, preferred_element_type=jnp.float32
        )
        inner = jnp.sum(probs * grad_probs, axis=-1, keepdims=True)
        grad_scores = (probs * (grad_probs - inner)).astype(jnp.bfloat16)
        grad_q = (
            jnp.einsum(
                "whqk,wkhd->wqhd", grad_scores, clip_keys, preferred_element_type=jnp.float32
            )
            * scale
        ).astype(jnp.bfloat16)
        grad_k = (
            jnp.einsum(
                "whqk,wqhd->wkhd", grad_scores, clip_queries, preferred_element_type=jnp.float32
            )
            * scale
        ).astype(jnp.bfloat16)
        grad_v = jnp.einsum(
            "whqk,wqhd->wkhd",
            probs.astype(jnp.bfloat16),
            clip_grad,
            preferred_element_type=jnp.float32,
        ).astype(jnp.bfloat16)
        carry = carry + jnp.sum(grad_scores.astype(jnp.float32), axis=0)
        return (carry, (grad_q, grad_k, grad_v))

    window_tokens = queries.shape[2]
    start_bias = jnp.zeros((queries.shape[3], window_tokens, window_tokens), jnp.float32)
    bias_grad, grads_win = lax.scan(
        attend_back, start_bias, (queries, keys, values, grad_attended, log_total)
    )
    grad_q, grad_k, grad_v = (to_frames(g, frames) for g in grads_win)
    if shifted:
        grad_q = jnp.roll(grad_q, WIN_T // 2, axis=1)
        grad_k = jnp.roll(grad_k, WIN_T // 2, axis=1)
        grad_v = jnp.roll(grad_v, WIN_T // 2, axis=1)
    grad_q, grad_k, grad_v = (
        lax.all_to_all(grad_q, TM, split_axis=1, concat_axis=3, tiled=True),
        lax.all_to_all(grad_k, TM, split_axis=1, concat_axis=3, tiled=True),
        lax.all_to_all(grad_v, TM, split_axis=1, concat_axis=3, tiled=True),
    )
    token_shape = (clips, frames_here, side, side, width)
    grad_q, grad_k, grad_v = (
        grad_q.reshape(token_shape),
        grad_k.reshape(token_shape),
        grad_v.reshape(token_shape),
    )
    grad_mix = jnp.concatenate([grad_q, grad_k, grad_v], axis=-1)
    mix_grad = outer_sum(normed, grad_mix)
    mix_bias_grad = jnp.concatenate([column_sum(grad_q), column_sum(grad_v)])
    grad_normed = project_back(grad_mix, mix_weight)
    if shifted:
        grad_normed = space_roll(grad_normed.astype(jnp.bfloat16), False).astype(jnp.float32)
    norm_pull_one = jax.vjp(
        norm_rows, stream, gain_one.astype(jnp.float32), bias_one.astype(jnp.float32)
    )[1]
    grad_stream_part, gain_one_grad, bias_one_grad = norm_pull_one(grad_normed)
    grad_stream = grad_middle + grad_stream_part
    rel = relative_index(WIN_T, WIN_HW).reshape(-1)
    table_grad = (
        jnp.zeros(table.shape, jnp.float32).at[rel].add(bias_grad.reshape(bias_grad.shape[0], -1).T)
    )
    weight_grads = (
        gain_one_grad,
        bias_one_grad,
        mix_grad,
        mix_bias_grad,
        proj_grad,
        proj_bias_grad,
        gain_two_grad,
        bias_two_grad,
        wide_grad,
        wide_bias_grad,
        narrow_grad,
        narrow_bias_grad,
    )
    return (grad_stream, weight_grads, table_grad)


def per_device(
    clips_in,
    ln1_gain,
    ln1_bias,
    qkv_weight,
    qv_bias,
    out_weight,
    out_bias,
    ln2_gain,
    ln2_bias,
    fc1_weight,
    fc1_bias,
    fc2_weight,
    fc2_bias,
    pos_table,
    out_grad,
):
    clips, frames_here, quads, cells, width = clips_in.shape
    grid_shape = (clips, frames_here, WIN_HW, WIN_HW, width)
    shards = (
        ln1_gain,
        ln1_bias,
        qkv_weight,
        qv_bias,
        out_weight,
        out_bias,
        ln2_gain,
        ln2_bias,
        fc1_weight,
        fc1_bias,
        fc2_weight,
        fc2_bias,
    )
    stream = clips_in.astype(jnp.float32).reshape(grid_shape)
    kept_params = []
    kept_stash = []
    for layer in range(LAYERS):
        params = gather_layer(shards, layer)
        stash, stream = layer_forward(stream, params, pos_table[layer], layer % 2 == 1)
        kept_params.append(params)
        kept_stash.append(stash)
    clips_out = stream.astype(jnp.bfloat16).reshape(clips_in.shape)
    grad_stream = out_grad.astype(jnp.float32).reshape(grid_shape)
    layer_shares = [None] * LAYERS
    table_parts = [None] * LAYERS
    for layer in reversed(range(LAYERS)):
        params = gather_layer(shards, layer)
        grad_stream, weight_grads, table_grad = layer_backward(
            grad_stream, params, pos_table[layer], kept_stash[layer], layer % 2 == 1
        )
        layer_shares[layer] = tuple(
            lax.psum_scatter(g, ALL, scatter_dimension=0, tiled=True) for g in weight_grads
        )
        table_parts[layer] = table_grad
    in_grad = grad_stream.astype(jnp.bfloat16).reshape(clips_in.shape)
    table_total = lax.psum(jnp.stack(table_parts), (SPACE, CLIP))
    stacked = tuple(
        (jnp.stack([layer_shares[n][slot] for n in range(LAYERS)]) for slot in range(12))
    )
    return (
        clips_out,
        in_grad,
        stacked[0],
        stacked[1],
        stacked[2],
        stacked[3],
        stacked[4],
        stacked[5],
        stacked[6],
        stacked[7],
        stacked[8],
        stacked[9],
        stacked[10],
        stacked[11],
        table_total,
    )


F32 = jnp.float32
BF16 = jnp.bfloat16
TOKENS = WIN_T * WIN_HW * WIN_HW
CELLS = WIN_HW * WIN_HW
SPAN = 2 * WIN_HW - 1
STEPS = 2 * WIN_T - 1
LOG2E = math.log2(math.e)
VMEM_BYTES = 56 * 1024 * 1024


def mm(left, right, left_dim=1, right_dim=0):
    dims = (((left_dim,), (right_dim,)), ((), ()))
    return lax.dot_general(left, right, dims, preferred_element_type=F32)


class Order:
    def __init__(self, waits=()):
        self.waits = list(waits)
        self.token = None


def call(
    kernel, grid, in_specs, out_specs, out_shape, flops, scratch=(), after=None, aliases=None
):
    waits = after.waits if after else []
    inputs = len(in_specs)
    single = not isinstance(out_shape, list)
    out_specs = [out_specs] if single else list(out_specs)
    out_shape = [out_shape] if single else list(out_shape)
    outputs = len(out_shape)
    if after:
        out_specs.append(pl.BlockSpec(memory_space=pltpu.SMEM))
        out_shape.append(jax.ShapeDtypeStruct((1, 1), F32))

    def body(*refs):
        ins, outs = refs[:inputs], refs[inputs + len(waits) :]
        if after:
            outs[outputs][0, 0] = 0.0
        kernel(*ins, *outs[:outputs], *outs[len(out_shape) :])

    run = pl.pallas_call(
        body,
        grid=grid,
        in_specs=list(in_specs) + [pl.BlockSpec(memory_space=pl.ANY)] * len(waits),
        out_specs=out_specs,
        out_shape=out_shape,
        scratch_shapes=scratch,
        input_output_aliases=aliases or {},
        cost_estimate=pl.CostEstimate(
            flops=int(flops), transcendentals=0, bytes_accessed=8 * 1024 * 1024
        ),
        compiler_params=pltpu.CompilerParams(vmem_limit_bytes=VMEM_BYTES),
    )

    def result(*args):
        found = run(*args, *waits)
        if after:
            after.token = found[outputs]
        return found[0] if single else found[:outputs]

    return result


def whole_block(shape):
    return pl.BlockSpec(shape, lambda *ids: (0,) * len(shape))


def flag_spec():
    return pl.BlockSpec(memory_space=pltpu.SMEM)


def win_block(width, column=0):
    return pl.BlockSpec((1, TOKENS, width), lambda w: (w, 0, column))


HALF = WIN_T // 2 * CELLS
KINDS = range(1, 8)


class Halo:
    def __init__(self):
        token = np.arange(HALF)
        row, col = token // WIN_HW % WIN_HW, token % WIN_HW
        reach = WIN_HW // 2
        target = token - row * WIN_HW - col
        target = target + (row - reach) % WIN_HW * WIN_HW + (col - reach) % WIN_HW
        leaves = (row < reach) * 2 + (col < reach) * 1
        self.stay = np.zeros((HALF, HALF), np.float32)
        stays = leaves == 0
        self.stay[target[stays], token[stays]] = 1
        self.near, self.near_to = self.ways(leaves, target, (1, 2, 3))
        self.far, self.far_to = self.ways(leaves, target, (0, 1, 2, 3))

    @staticmethod
    def ways(leaves, target, kinds):
        send, place = [], []
        for kind in kinds:
            source = np.nonzero(leaves == kind)[0]
            rows = 64 if kind == 0 else 48
            out, back = np.zeros((rows, HALF), np.float32), np.zeros((HALF, rows), np.float32)
            out[np.arange(len(source)), source] = 1
            back[target[source], np.arange(len(source))] = 1
            send.append(out)
            place.append(back)
        return np.concatenate(send, 0), np.concatenate(place, 1)

    def sends(self, onward):
        return (self.near, self.far) if onward else (self.near_to.T, self.far_to.T)

    def places(self, onward):
        if onward:
            return self.stay, self.near_to, self.far_to
        return self.stay.T, self.near.T, self.far.T


def half_at(half):
    return half // 2, slice(half % 2 * HALF, (half % 2 + 1) * HALF)


class Flow:
    def __init__(self):
        self.live = []
        self.done = {}

    def start(self, name, task):
        self.live.append((name, task, task.sends() if isinstance(task, Gather) else next(task)))

    def pending(self):
        return [value for _, _, sends in self.live for value, _, _ in sends]

    def step(self, token, names=None):
        live = []
        for name, task, sends in self.live:
            if names is not None and name not in names:
                live.append((name, task, sends))
                continue
            came = [lax.ppermute(value, axis, pairs) for value, axis, pairs in sends]
            if isinstance(task, Gather):
                task.step(came[0], token if len(task.steps) > 1 else None)
                if task.steps:
                    live.append((name, task, task.sends()))
                else:
                    self.done[name] = task.out
                continue
            try:
                live.append((name, task, task.send((came, token))))
            except StopIteration as end:
                self.done[name] = end.value
        self.live = live

    def finish(self, name):
        while name not in self.done:
            self.step(None, (name,))
        return self.done[name]


def swap_pairs(axis, bit):
    return [(source, source ^ 2**bit) for source in range(lax.axis_size(axis))]


def halo_flow(packed, onward):
    ring, quads = lax.axis_size(TM), lax.axis_size(SPACE)
    sends = []
    for kind, piece in zip(KINDS, packed):
        step = 0 if not kind & 4 else (-1 if onward else 1)
        pairs = []
        for frame_at in range(ring):
            for quad in range(quads):
                to = (frame_at + step) % ring * quads + (quad ^ (kind & 3))
                pairs.append((frame_at * quads + quad, to))
        sends.append((piece, (TM, SPACE), pairs))
    came, _ = yield sends
    return came


def pack_kernel(center, onward, near_ref, far_ref, x_ref, *refs):
    out_refs, flat_ref = refs[:-1], refs[-1]
    halves = 2 * x_ref.shape[0]
    for w in range(x_ref.shape[0]):
        x = x_ref[w].astype(F32)
        if center:
            x = x - jnp.mean(x, axis=-1, keepdims=True)
        flat_ref[w] = x
    for n in range(halves - 1):
        w, rows = half_at(n + 1 if onward else n)
        sent = mm(near_ref[...], flat_ref[w, rows].astype(BF16)).astype(BF16)
        for kind in range(3):
            out_refs[kind][n * 48 : (n + 1) * 48] = sent[kind * 48 : (kind + 1) * 48]
    w, rows = half_at(0 if onward else halves - 1)
    sent = mm(far_ref[...], flat_ref[w, rows].astype(BF16)).astype(BF16)
    for kind in range(4):
        first = 0 if kind == 0 else 16 + 48 * kind
        out_refs[3 + kind][...] = sent[first : first + out_refs[3 + kind].shape[0]]


def part_rows(windows):
    return [48 * (2 * windows - 1)] * 3 + [64, 48, 48, 48]


def halo_pack(x, halo, onward, center=False, joined=False, after=None):
    windows, _, width = x.shape
    near, far = (jnp.asarray(m, BF16) for m in halo.sends(onward))
    rows = part_rows(windows)

    def kernel(near_ref, far_ref, x_ref, *refs):
        if joined:
            refs = [refs[0].at[pl.ds(sum(rows[:n]), rows[n])] for n in range(7)] + [refs[1]]
        pack_kernel(center, onward, near_ref, far_ref, x_ref, *refs)

    shapes = [(sum(rows), width)] if joined else [(n, width) for n in rows]
    out = functools.partial(call, after=after)(
        kernel,
        (1,),
        [whole_block(m.shape) for m in (near, far, x)],
        [whole_block(shape) for shape in shapes],
        [jax.ShapeDtypeStruct(shape, BF16) for shape in shapes],
        2 * 640 * HALF * width,
        [pltpu.VMEM(x.shape, F32)],
    )(near, far, x)
    return out[0] if joined else out


def halo_gather(packed):
    return lax.all_gather(packed, (TM, SPACE), axis=0, tiled=True)


def halo_senders(onward):
    ring, quads = lax.axis_size(TM), lax.axis_size(SPACE)
    senders = []
    for kind in KINDS:
        step = 0 if not kind & 4 else (1 if onward else -1)
        frame_at = (lax.axis_index(TM) + step + ring) % ring
        senders.append(frame_at * quads + lax.axis_index(SPACE) ^ (kind & 3))
    return jnp.stack([jnp.asarray(n, jnp.int32) for n in senders])


def unpack_kernel(center, onward, add_mean, stay_ref, near_ref, far_ref, x_ref, *refs):
    base_ref, refs = (refs[0], refs[1:]) if add_mean else (None, refs)
    came_refs, (out_ref, flat_ref, total_ref) = refs[:7], refs[7:]
    windows = x_ref.shape[0]
    halves = 2 * windows
    for w in range(windows):
        x = x_ref[w].astype(F32)
        if center:
            x = x - jnp.mean(x, axis=-1, keepdims=True)
        flat_ref[w] = x
    for n in range(halves - 1):
        w, rows = half_at(n + 1 if onward else n)
        x = flat_ref[w, rows]
        high = x.astype(BF16)
        total = mm(stay_ref[...], high)
        if x_ref.dtype == F32:
            total = total + mm(stay_ref[...], (x - high.astype(F32)).astype(BF16))
        came = jnp.concatenate([ref[n * 48 : (n + 1) * 48] for ref in came_refs[:3]], axis=0)
        w, rows = half_at(n if onward else n + 1)
        total_ref[w, rows] = total + mm(near_ref[...], came)
    came = jnp.concatenate([ref[...] for ref in came_refs[3:]], axis=0)
    w, rows = half_at(halves - 1 if onward else 0)
    total_ref[w, rows] = mm(far_ref[...], came)
    for w in range(windows):
        total = total_ref[w]
        if add_mean:
            total = total + jnp.mean(base_ref[w], axis=-1, keepdims=True)
        out_ref[w] = total.astype(out_ref.dtype)


def halo_unpack(x, came, halo, onward, dtype, center=False, mean_of=None, after=None):
    places = [jnp.asarray(m, BF16) for m in halo.places(onward)]
    operands = places + [x] + ([] if mean_of is None else [mean_of])
    joined = not isinstance(came, list)
    senders = [halo_senders(onward)] if joined else []
    operands += [came] if joined else came
    rows = part_rows(x.shape[0])

    def kernel(*refs):
        if joined:
            sender_ref, refs = refs[0], refs[1:]
            count = len(operands)
            parts = []
            for n in range(7):
                first = sender_ref[n] * sum(rows) + sum(rows[:n])
                parts.append(refs[count - 1].at[pl.ds(pl.multiple_of(first, 16), rows[n])])
            refs = refs[: count - 1] + tuple(parts) + refs[count:]
        unpack_kernel(center, onward, mean_of is not None, *refs)

    return functools.partial(call, after=after)(
        kernel,
        (1,),
        [flag_spec()] * joined + [whole_block(v.shape) for v in operands],
        whole_block(x.shape),
        jax.ShapeDtypeStruct(x.shape, dtype),
        8 * x.size * HALF,
        [pltpu.VMEM(x.shape, F32), pltpu.VMEM(x.shape, F32)],
    )(*senders, *operands)


def index_bits():
    bits = []
    for axis in ALL:
        count = lax.axis_size(axis).bit_length() - 1
        bits += [(axis, b) for b in reversed(range(count))]
    return bits


def bit_of(axis, bit):
    return (lax.axis_index(axis) // 2**bit) % 2


def stage_orders():
    bits = index_bits()
    inner = [(CLIP, 0)] if lax.axis_size(CLIP) > 1 else []
    tm = [b for b in bits if b[0] == TM]
    clip = [b for b in bits if b[0] == CLIP and b not in inner]
    space = [b for b in reversed(bits) if b[0] == SPACE]
    return inner + tm + clip + space, inner + clip + tm + space


class Gather:
    def __init__(self, shard, order):
        self.bits, self.steps = index_bits(), list(reversed(order))
        self.dims = [1] * len(self.bits)
        self.rows, self.out = shard.shape[0], shard

    def sends(self):
        axis, bit = self.steps[0]
        return [(self.out, axis, swap_pairs(axis, bit))]

    def step(self, came, token):
        axis, bit = self.steps.pop(0)
        dim = self.bits.index((axis, bit))
        before, after = math.prod(self.dims[:dim]), math.prod(self.dims[dim + 1 :])
        self.dims[dim] = 2
        here = bit_of(axis, bit).astype(F32) + (0.0 if token is None else token.reshape(()))
        own, came = (v.reshape(before, 1, after * self.rows, -1) for v in (self.out, came))
        low, high = jnp.where(here > 0.5, came, own), jnp.where(here > 0.5, own, came)
        self.out = jnp.concatenate([low, high], axis=1).reshape(-1, own.shape[-1])


def scatter_flow(own, sent, order):
    bits = index_bits()
    width = own.shape[-1]
    dims = [2] * len(bits)
    own, sent = own.reshape(-1, width), sent.reshape(-1, width)
    for n, (axis, bit) in enumerate(order):
        (came,), token = yield [(sent, axis, swap_pairs(axis, bit))]
        dims[bits.index((axis, bit))] = 1
        zero = 0.0 if token is None else token.reshape(())
        if n + 1 == len(order):
            return own + came.astype(F32)
        axis, bit = order[n + 1]
        dim = bits.index((axis, bit))
        here = bit_of(axis, bit)
        own, came = (v.reshape(dims + [-1, width]) for v in (own, came))

        def half(index):
            mine, theirs = (lax.dynamic_slice_in_dim(v, index, 1, dim) for v in (own, came))
            return (mine + theirs.astype(F32) + zero).reshape(-1, width)

        own, sent = half(here), half(1 - here).astype(BF16)


def table_flow(tables, heads_here):
    first = lax.axis_index(TM) == 0
    mine = jnp.where(first, tables[0], tables[1])
    (came,), _ = yield [(jnp.where(first, tables[1], tables[0]), TM, swap_pairs(TM, 0))]
    table = mine + came
    for axis, bit in index_bits():
        if axis != TM:
            (came,), _ = yield [(table, axis, swap_pairs(axis, bit))]
            table = table + came
    return table


WIDE = 768


def column_pick():
    pick = np.zeros((WIN_HW, 256, 128), np.float32)
    for key_col in range(WIN_HW):
        for row in range(SPAN):
            for col in range(WIN_HW):
                entry = row * SPAN + col - key_col + WIN_HW - 1
                pick[key_col, entry, row * WIN_HW + col] = 1
    return pick


def lane_spans(step):
    first, rest = divmod(step * CELLS, 128)
    if rest + CELLS <= 128:
        return [(first, rest, rest + CELLS)]
    return [(first, rest, 128), (first + 1, 0, rest + CELLS - 128)]


def bias_kernel(slab_ref, pick_ref, out_ref, row_ref, wide_ref):
    heads = pl.num_programs(0)

    @pl.when(pl.program_id(0) == 0)
    def _():
        slabs = slab_ref[...]
        for col in range(WIN_HW):
            row_ref[pl.ds(col, slabs.shape[0], stride=8), :] = mm(slabs, pick_ref[col]) * LOG2E

    base = pl.program_id(0) * 128
    lane = lax.broadcasted_iota(jnp.int32, (8, 128), 1)
    for row in range(WIN_HW):
        tiles = [jnp.zeros((8, 128), F32) for _ in range(WIDE // 128)]
        for step in range(STEPS):
            rows = row_ref[pl.ds(pl.multiple_of(base + step * 8, 8), 8), :]
            turn = (step * CELLS - WIN_HW * (WIN_HW - 1 - row)) % 128
            rows = pltpu.roll(rows, turn, 1) if turn else rows
            for tile, low, high in lane_spans(step):
                tiles[tile] = jnp.where((lane >= low) & (lane < high), rows, tiles[tile])
        wide_ref[row * WIN_HW : (row + 1) * WIN_HW, :] = jnp.concatenate(tiles, axis=1)[:WIN_HW]
    wide = wide_ref[:CELLS, :]
    for key_frame in range(WIN_T):
        turned = pltpu.roll(wide, (WIDE - (WIN_T - 1 - key_frame) * CELLS) % WIDE, 1)
        out_ref[0, key_frame * CELLS : (key_frame + 1) * CELLS, :] = turned[:, :TOKENS]


def table_to_bias(tables, rest=None, after=None):
    heads = tables.shape[0]
    slabs = tables.reshape(heads, STEPS, SPAN * SPAN)
    slabs = jnp.pad(slabs, ((0, 0), (0, 16 - STEPS), (0, 256 - SPAN * SPAN)))
    slabs = slabs.reshape(heads * 16, 256)
    held = [] if rest is None else [rest]
    first = 0 if rest is None else heads

    def kernel(slab_ref, pick_ref, *refs):
        bias_kernel(slab_ref, pick_ref, *refs[len(held) :])

    return functools.partial(call, after=after, aliases={2: 0} if held else {})(
        kernel,
        (heads,),
        [whole_block(slabs.shape), whole_block((WIN_HW, 256, 128))]
        + [pl.BlockSpec(memory_space=pl.ANY)] * len(held),
        pl.BlockSpec((1, TOKENS, TOKENS), lambda h: (first + h, 0, 0)),
        jax.ShapeDtypeStruct((2 * heads, TOKENS, TOKENS), F32),
        heads * 500_000_000,
        [pltpu.VMEM((heads * 128, 128), F32), pltpu.VMEM((56, WIDE), F32)],
    )(slabs, jnp.asarray(column_pick(), BF16), *held)


def table_back_kernel(sums_ref, pick_ref, out_ref, row_ref):
    head = pl.program_id(0)
    lane = lax.broadcasted_iota(jnp.int32, (WIN_HW, 128), 1)
    totals = [None] * STEPS
    for row in range(WIN_HW):
        rows = sums_ref[0, row * WIN_HW : (row + 1) * WIN_HW, :]
        start = WIN_HW * (WIN_HW - 1 - row)
        for step in range(STEPS):
            turn = (start - step * CELLS) % 128
            piece = None
            for tile, low, high in lane_spans(step):
                part = rows[:, tile * 128 : (tile + 1) * 128]
                part = jnp.where((lane >= low) & (lane < high), part, 0.0)
                piece = part if piece is None else piece + part
            piece = pltpu.roll(piece, turn, 1) if turn else piece
            totals[step] = piece if totals[step] is None else totals[step] + piece
    blank = jnp.zeros((1, 128), F32)
    for step in range(16):
        rows = jnp.concatenate([totals[step], blank]) if step < STEPS else jnp.zeros((8, 128), F32)
        row_ref[pl.ds(pl.multiple_of(head * 128 + step * 8, 8), 8), :] = rows

    @pl.when(head == pl.num_programs(0) - 1)
    def _():
        total = None
        for col in range(WIN_HW):
            rows = row_ref[pl.ds(col, out_ref.shape[0], stride=8), :]
            high = rows.astype(BF16)
            low = (rows - high.astype(F32)).astype(BF16)
            part = mm(high, pick_ref[col], 1, 1) + mm(low, pick_ref[col], 1, 1)
            total = part if total is None else total + part
        out_ref[...] = total


def sums_to_table(sums, first=0, heads=None, after=None):
    heads = heads or sums.shape[0]
    slabs = functools.partial(call, after=after)(
        table_back_kernel,
        (heads,),
        [
            pl.BlockSpec((1, CELLS, WIDE), lambda h: (first + h, 0, 0)),
            whole_block((WIN_HW, 256, 128)),
        ],
        whole_block((heads * 16, 256)),
        jax.ShapeDtypeStruct((heads * 16, 256), F32),
        heads * 300_000_000,
        [pltpu.VMEM((heads * 128, 128), F32)],
    )(sums, jnp.asarray(column_pick(), BF16))
    return slabs.reshape(heads, 16, 256)[:, :STEPS, : SPAN * SPAN].reshape(heads, -1)


def unit_rows(x):
    centered = x - jnp.mean(x, axis=-1, keepdims=True)
    inverse = lax.rsqrt(jnp.mean(centered * centered, axis=-1, keepdims=True) + 1e-05)
    return centered * inverse, inverse


def norm_back(grad, unit, inverse, gain):
    scaled = grad * gain
    return inverse * (
        scaled
        - jnp.mean(scaled, axis=-1, keepdims=True)
        - unit * jnp.mean(scaled * unit, axis=-1, keepdims=True)
    )


def qkv_kernel(x_ref, vec_ref, wq_ref, wk_ref, wv_ref, out_ref):
    width = x_ref.shape[-1]
    unit, _ = unit_rows(x_ref[0].astype(F32))
    normed = (unit * vec_ref[0:1] + vec_ref[1:2]).astype(BF16)
    for part, ref in enumerate((wq_ref, wk_ref, wv_ref)):
        out = mm(normed, ref[...])
        if part == 0:
            out = out + vec_ref[2:3]
        if part == 2:
            out = out + vec_ref[3:4]
        out_ref[0, :, part * width : (part + 1) * width] = out.astype(BF16)


def run_qkv(x, vec, w_qkv, after=None):
    windows, _, width = x.shape
    weight, at = w_qkv
    return functools.partial(call, after=after)(
        qkv_kernel,
        (windows,),
        [win_block(width), whole_block(vec.shape)]
        + [weight_block(width, width, at + n) for n in range(3)],
        win_block(3 * width),
        jax.ShapeDtypeStruct((windows, TOKENS, 3 * width), BF16),
        2 * windows * TOKENS * width * 3 * width,
    )(x, vec, weight, weight, weight)


GROUP = 4


def head_masks(head_size):
    lane = lax.broadcasted_iota(jnp.int32, (1, GROUP * head_size), 1)
    return [
        jnp.where((lane >= h * head_size) & (lane < (h + 1) * head_size), 1.0, 0.0).astype(BF16)
        for h in range(GROUP)
    ]


def region_labels(flag_ref, late_ref, turned_ref, at_end):
    flags = [flag_ref[1 + n].astype(F32) for n in range(3)]
    flags[0] = flags[0] * at_end
    col = sum(flags[n] * late_ref[:, n : n + 1] for n in range(3))
    return col, sum(flags[n] * turned_ref[n : n + 1, :] for n in range(3))


def late_tokens():
    token = np.arange(TOKENS)
    late = np.zeros((TOKENS, 8), np.float32)
    late[:, 0] = 4 * (token // CELLS >= WIN_T - WIN_T // 2)
    late[:, 1] = 2 * (token // WIN_HW % WIN_HW >= WIN_HW - WIN_HW // 2)
    late[:, 2] = token % WIN_HW >= WIN_HW - WIN_HW // 2
    return late


def attend_kernel(
    shifted, head_size, flag_ref, q_ref, k_ref, v_ref, bias_ref, late_ref, turned_ref, out_ref, log_ref
):
    q, k = q_ref[0], k_ref[0]
    if shifted:
        at_end = jnp.where(pl.program_id(1) == pl.num_programs(1) - 1, 1.0, 0.0)
        col, row = region_labels(flag_ref, late_ref, turned_ref, at_end)
    turned = v_ref[0].astype(F32).T.astype(BF16)
    factor = head_size**-0.5 * LOG2E
    masks = head_masks(head_size)
    outs, logs = [], []
    for h in range(GROUP):
        scores = mm(k * masks[h], q, 1, 1) * factor + bias_ref[h]
        if shifted:
            scores = jnp.where(col == row, scores, masked_score)
        peak = jnp.max(scores, axis=0, keepdims=True)
        raised = jnp.exp2(scores - peak)
        total = jnp.sum(raised, axis=0, keepdims=True)
        mixed = mm(turned[h * head_size : (h + 1) * head_size], raised.astype(BF16))
        outs.append(mixed / total)
        logs.append(peak + jnp.log2(total))
    out_ref[0] = jnp.concatenate(outs, axis=0).T.astype(BF16)
    log_ref[0, 0] = jnp.concatenate(logs + logs, axis=0)


def run_attend(qkv, bias, flags, shifted, after=None):
    windows, _, width3 = qkv.shape
    width = width3 // 3
    wide = GROUP * (width // HEADS)
    groups = HEADS // GROUP
    qkv_specs = [
        pl.BlockSpec((1, TOKENS, wide), lambda g, w, p=part: (w, 0, p * groups + g))
        for part in range(3)
    ]
    return functools.partial(call, after=after)(
        functools.partial(attend_kernel, shifted, width // HEADS),
        (groups, windows),
        [flag_spec()]
        + qkv_specs
        + [
            pl.BlockSpec((GROUP, TOKENS, TOKENS), lambda g, w: (g, 0, 0)),
            whole_block((TOKENS, 8)),
            whole_block((8, TOKENS)),
        ],
        [
            pl.BlockSpec((1, TOKENS, wide), lambda g, w: (w, 0, g)),
            pl.BlockSpec((1, 1, 2 * GROUP, TOKENS), lambda g, w: (w, g, 0, 0)),
        ],
        [
            jax.ShapeDtypeStruct((windows, TOKENS, width), BF16),
            jax.ShapeDtypeStruct((windows, groups, 2 * GROUP, TOKENS), F32),
        ],
        64 * windows * TOKENS * TOKENS * width,
    )(flags, qkv, qkv, qkv, bias, late_tokens(), late_tokens().T)


def attend_back_kernel(
    shifted, head_size, flag_ref, q_ref, k_ref, v_ref, g_ref, o_ref, bias_ref, late_ref, turned_ref,
    log_ref, dq_ref, dk_ref, dv_ref, table_ref, sum_ref,
):
    windows = q_ref.shape[0]
    if shifted:
        labels = [
            region_labels(flag_ref, late_ref, turned_ref, float(w == windows - 1))
            for w in range(windows)
        ]
    scale = head_size**-0.5
    factor = scale * LOG2E
    masks = head_masks(head_size)

    @pl.when(pl.program_id(0) == 0)
    def _():
        sum_ref[...] = jnp.zeros_like(sum_ref)

    turned, weighed = [], []
    for w in range(windows):
        turned.append(k_ref[w].astype(F32).T.astype(BF16))
        weighed.append(g_ref[w].astype(F32).T * o_ref[w].astype(F32).T)
    grad_q = [[] for _ in range(windows)]
    grad_k, grad_v = [None] * windows, [None] * windows
    for h in range(GROUP):
        here = slice(h * head_size, (h + 1) * head_size)
        total = None
        for w in range(windows):
            q, k, v, g = q_ref[w], k_ref[w], v_ref[w], g_ref[w]
            inner = jnp.sum(weighed[w][here], axis=0, keepdims=True)
            scores = mm(k * masks[h], q, 1, 1) * factor + bias_ref[h]
            if shifted:
                scores = jnp.where(labels[w][0] == labels[w][1], scores, masked_score)
            probs = jnp.exp2(scores - log_ref[w, 0, h : h + 1])
            grad_probs = mm(v * masks[h], g, 1, 1)
            grad_scores = (probs * (grad_probs - inner)).astype(BF16)
            part_v = mm(probs.astype(BF16), g * masks[h])
            part_k = mm(grad_scores, q * masks[h])
            grad_v[w] = part_v if grad_v[w] is None else grad_v[w] + part_v
            grad_k[w] = part_k if grad_k[w] is None else grad_k[w] + part_k
            grad_q[w].append(mm(turned[w][here], grad_scores))
            wide = grad_scores.astype(F32)
            total = wide if total is None else total + wide
        sum_ref[:, :TOKENS] = total
        sums = None
        for key_frame in range(WIN_T):
            rows = sum_ref[key_frame * CELLS : (key_frame + 1) * CELLS, :]
            step = (WIN_T - 1 - key_frame) * CELLS
            rows = pltpu.roll(rows, step, 1) if step else rows
            sums = rows if sums is None else sums + rows
        table_ref[h] = sums
    for w in range(windows):
        dq_ref[w] = (jnp.concatenate(grad_q[w], axis=0) * scale).T.astype(BF16)
        dk_ref[w] = (grad_k[w] * scale).astype(BF16)
        dv_ref[w] = grad_v[w].astype(BF16)


def run_attend_back(qkv, grad, attended, bias, flags, log, shifted, first, count, after=None):
    windows, _, width3 = qkv.shape
    width = width3 // 3
    wide = GROUP * (width // HEADS)
    groups = HEADS // GROUP
    qkv_specs = [
        pl.BlockSpec((windows, TOKENS, wide), lambda g, p=part: (0, 0, p * groups + first + g))
        for part in range(3)
    ]
    flat = pl.BlockSpec((windows, TOKENS, wide), lambda g: (0, 0, g))
    flat_shape = jax.ShapeDtypeStruct((windows, TOKENS, count * wide), BF16)
    return functools.partial(call, after=after)(
        functools.partial(attend_back_kernel, shifted, width // HEADS),
        (count,),
        [flag_spec()]
        + qkv_specs
        + [
            pl.BlockSpec((windows, TOKENS, wide), lambda g: (0, 0, first + g)),
            pl.BlockSpec((windows, TOKENS, wide), lambda g: (0, 0, first + g)),
            pl.BlockSpec((GROUP, TOKENS, TOKENS), lambda g: (first + g, 0, 0)),
            whole_block((TOKENS, 8)),
            whole_block((8, TOKENS)),
            pl.BlockSpec((windows, 1, 2 * GROUP, TOKENS), lambda g: (0, first + g, 0, 0)),
        ],
        [flat, flat, flat, pl.BlockSpec((GROUP, CELLS, WIDE), lambda g: (g, 0, 0))],
        [flat_shape] * 3 + [jax.ShapeDtypeStruct((count * GROUP, CELLS, WIDE), F32)],
        160 * windows * TOKENS * TOKENS * count * wide,
        [pltpu.VMEM((TOKENS, WIDE), F32)],
    )(flags, qkv, qkv, qkv, grad, attended, bias, late_tokens(), late_tokens().T, log)


def normal_below(x):
    bell = jnp.exp2(x * x * (-0.5 * LOG2E)) * (1.0 / math.sqrt(2 * math.pi))
    return 0.5 + 0.5 * lax.erf(x * math.sqrt(0.5)), bell


def spread_down(down_ref, w2_ref):
    _, parts, own, width = w2_ref.shape
    for part in range(parts):
        cols = slice(part * width, (part + 1) * width)
        w2_ref[:, part] = down_ref[:, cols].reshape(-1, own, width)


def chunk_rows(w2_ref, first, chunk):
    _, parts, own, width = w2_ref.shape
    step = chunk // (parts * own)
    return w2_ref[first * step : (first + 1) * step].reshape(chunk, width)


def branch_kernel(count, *refs):
    att_refs = refs[:count]
    x_ref, vec_ref, wo_ref, w1_ref, down_ref, mid_ref, hid_ref, slope_ref, out_ref, w2_ref = refs[count:]

    @pl.when(pl.program_id(0) == 0)
    def _():
        spread_down(down_ref, w2_ref)

    chunk = 512
    attended = jnp.concatenate([ref[0] for ref in att_refs], axis=1)
    middle = x_ref[0].astype(F32) + mm(attended, wo_ref[...]) + vec_ref[4:5]
    mid_ref[0] = middle
    unit, _ = unit_rows(middle)
    normed = (unit * vec_ref[5:6] + vec_ref[6:7]).astype(BF16)
    after = middle + vec_ref[7:8]
    for n in range(w1_ref.shape[1] // chunk):
        cols = slice(n * chunk, (n + 1) * chunk)
        pre = mm(normed, w1_ref[:, cols]) + vec_ref[8 + n : 9 + n]
        below, bell = normal_below(pre)
        hidden = (pre * below).astype(BF16)
        hid_ref[0, :, cols] = hidden
        slope_ref[0, :, cols] = (below + pre * bell).astype(BF16)
        after = after + mm(hidden, chunk_rows(w2_ref, n, chunk))
    out_ref[0] = after.astype(out_ref.dtype)


def weight_block(rows, width, column):
    return pl.BlockSpec((rows, width), lambda *ids: (0, column))


def branch_weights(weights, width, wide):
    (wo, wo_at), (w1, w1_at), (down, down_at) = weights
    specs = [
        weight_block(width, width, wo_at),
        weight_block(width, wide, w1_at),
        weight_block(width, wide, down_at),
    ]
    return (wo, w1, down), specs


def run_branch(x, attended, vec, weights, out_dtype, after=None):
    windows, _, width = x.shape
    wide = 4 * width
    arrays, specs = branch_weights(weights, width, wide)
    return functools.partial(call, after=after)(
        functools.partial(branch_kernel, len(attended)),
        (windows,),
        [win_block(part.shape[-1]) for part in attended]
        + [win_block(width), whole_block(vec.shape)]
        + specs,
        [win_block(width), win_block(wide), win_block(wide), win_block(width)],
        [
            jax.ShapeDtypeStruct((windows, TOKENS, width), F32),
            jax.ShapeDtypeStruct((windows, TOKENS, wide), BF16),
            jax.ShapeDtypeStruct((windows, TOKENS, wide), BF16),
            jax.ShapeDtypeStruct((windows, TOKENS, width), out_dtype),
        ],
        2 * windows * TOKENS * width * (width + 2 * wide),
        [pltpu.VMEM((width // 16, wide // width, 16, width), BF16)],
    )(*attended, x, vec, *arrays)


def add_rows(ref, rows, value):
    ref[rows, :] += jnp.sum(value.astype(F32), axis=0, keepdims=True)


def split_out(sums_ref, core, own_ref, sent_ref):
    own_ref[...] = sums_ref[:, core]
    sent_ref[...] = sums_ref[:, 1 - core].astype(BF16)


def branch_back_kernel(count, split, flag_ref, *refs):
    att_refs = refs[:count]
    grad_ref, mid_ref, hid_ref, slope_ref, vec_ref, wo_ref, w1_ref, down_ref = refs[count : count + 8]
    gm_ref, ga_ref, vecs_ref = refs[count + 8 : count + 11]
    outs, (d1_ref, d2_ref, w2_ref) = refs[count + 11 : -3], refs[-3:]
    chunk = 512
    width, wide = w1_ref.shape

    @pl.when(pl.program_id(0) == 0)
    def _():
        spread_down(down_ref, w2_ref)
        d1_ref[...] = jnp.zeros_like(d1_ref)
        d2_ref[...] = jnp.zeros_like(d2_ref)
        vecs_ref[...] = jnp.zeros_like(vecs_ref)

    grad = grad_ref[0].astype(F32)
    branch = grad.astype(BF16)
    unit, inverse = unit_rows(mid_ref[0])
    normed = (unit * vec_ref[5:6] + vec_ref[6:7]).astype(BF16)
    add_rows(vecs_ref, slice(7, 8), branch)
    back = None
    blocks = chunk // d2_ref.shape[2]
    for n in range(wide // chunk):
        cols = slice(n * chunk, (n + 1) * chunk)
        total = mm(hid_ref[0, :, cols], branch, 0, 0)
        at = slice(n * blocks // 2, (n + 1) * blocks // 2)
        d2_ref[at] += total.reshape((-1,) + d2_ref.shape[1:])
        grad_pre = mm(branch, chunk_rows(w2_ref, n, chunk), 1, 1) * slope_ref[0, :, cols].astype(F32)
        grad_pre = grad_pre.astype(BF16)
        add_rows(vecs_ref, slice(8 + n, 9 + n), grad_pre)
        d1_ref[:, :, :, cols] += mm(normed, grad_pre, 0, 0).reshape(d1_ref.shape[:3] + (chunk,))
        part = mm(grad_pre, w1_ref[:, cols], 1, 1)
        back = part if back is None else back + part
    add_rows(vecs_ref, slice(5, 6), back * unit)
    add_rows(vecs_ref, slice(6, 7), back)
    middle_grad = grad + norm_back(back, unit, inverse, vec_ref[5:6])
    gm_ref[0] = middle_grad
    branch = middle_grad.astype(BF16)
    add_rows(vecs_ref, slice(4, 5), branch)
    attended = jnp.concatenate([ref[0] for ref in att_refs], axis=1)
    total = mm(attended, branch, 0, 0)
    d1_ref[:, :, :, wide:] += total.reshape(d1_ref.shape[:3] + (width,))
    ga_ref[0] = mm(branch, wo_ref[...], 1, 1).astype(BF16)

    @pl.when(pl.program_id(0) == pl.num_programs(0) - 1)
    def _():
        if split:
            split_out(d1_ref, flag_ref[0], *outs[:2])
            split_out(d2_ref, flag_ref[0], *outs[2:])
        else:
            (out_ref,) = outs
            out_ref[:, : wide + width] = d1_ref[...].reshape(width, -1).astype(BF16)
            parts = wide // width
            for part in range(parts):
                first = wide + width + part * width
                piece = d2_ref[:, :, part * 16 : (part + 1) * 16, :].reshape(width, width)
                out_ref[:, first : first + width] = piece.astype(BF16)


def run_branch_back(grad, middle, attended, hidden, slope, vec, weights, flags, split, after=None):
    windows, _, width = middle.shape
    wide = 4 * width
    arrays, specs = branch_weights(weights, width, wide)
    flat = win_block(width)
    pairs = width // 32
    if split:
        shapes = []
        for rows, cols in ((16, wide + width), (64, width)):
            shapes.append(jax.ShapeDtypeStruct((pairs, rows, cols), F32))
            shapes.append(jax.ShapeDtypeStruct((pairs, rows, cols), BF16))
    else:
        shapes = [jax.ShapeDtypeStruct((width, 2 * wide + width), BF16)]
    return functools.partial(call, after=after)(
        functools.partial(branch_back_kernel, len(attended), split),
        (windows,),
        [flag_spec()]
        + [win_block(part.shape[-1]) for part in attended]
        + [flat, flat, win_block(wide), win_block(wide), whole_block(vec.shape)]
        + specs,
        [flat, flat, whole_block(vec.shape)] + [whole_block(s.shape) for s in shapes],
        [
            jax.ShapeDtypeStruct((windows, TOKENS, width), F32),
            jax.ShapeDtypeStruct((windows, TOKENS, width), BF16),
            jax.ShapeDtypeStruct(vec.shape, F32),
        ]
        + shapes,
        4 * windows * TOKENS * width * (width + 2 * wide),
        [
            pltpu.VMEM((pairs, 2, 16, wide + width), F32),
            pltpu.VMEM((pairs, 2, 64, width), F32),
            pltpu.VMEM((pairs * 2, wide // width, 16, width), BF16),
        ],
    )(flags, *attended, grad, middle, hidden, slope, vec, *arrays)


def qkv_back_kernel(count, flag_ref, *refs):
    grads, refs = refs[: 3 * count], refs[3 * count :]
    x_ref, gm_ref, vec_ref, wq_ref, wk_ref, wv_ref, rest_ref, mask_ref, pick_ref, spread_ref = refs[:10]
    out_ref, own_ref, sent_ref, dw_ref, vecs_ref = refs[10:]
    width = x_ref.shape[-1]

    @pl.when(pl.program_id(0) == 0)
    def _():
        dw_ref[...] = jnp.zeros_like(dw_ref)
        vecs_ref[...] = rest_ref[...]

    unit, inverse = unit_rows(x_ref[0].astype(F32))
    normed = (unit * vec_ref[0:1] + vec_ref[1:2]).astype(BF16)
    back = None
    for part, ref in enumerate((wq_ref, wk_ref, wv_ref)):
        grad = jnp.concatenate([g[0] for g in grads[part * count : (part + 1) * count]], axis=1)
        total = mm(normed, grad, 0, 0)
        cols = slice(part * width, (part + 1) * width)
        dw_ref[:, :, :, cols] += total.reshape(dw_ref.shape[:3] + (width,))
        here = mm(grad, ref[...], 1, 1)
        back = here if back is None else back + here
        if part == 0:
            add_rows(vecs_ref, slice(2, 3), grad)
        if part == 2:
            add_rows(vecs_ref, slice(3, 4), grad)
    add_rows(vecs_ref, slice(0, 1), back * unit)
    add_rows(vecs_ref, slice(1, 2), back)
    out_ref[0] = (gm_ref[0] + norm_back(back, unit, inverse, vec_ref[0:1])).astype(out_ref.dtype)

    @pl.when(pl.program_id(0) == pl.num_programs(0) - 1)
    def _():
        rows = vecs_ref[...]
        high = rows.astype(BF16)
        low = (rows - high.astype(F32)).astype(BF16)
        total = None
        for piece in (high, low):
            piece = (mm(pick_ref[...], piece, 0, 0) * mask_ref[...].astype(F32)).astype(BF16)
            piece = mm(piece, spread_ref[0], 1, 1)
            total = piece if total is None else total + piece
        dw_ref[:, :, :, 3 * width :] = total.reshape(dw_ref.shape[:3] + (128,))
        split_out(dw_ref, flag_ref[0], own_ref, sent_ref)


def run_qkv_back(grads, x, grad_middle, vec, w_qkv, rest, flags, out_dtype, after=None):
    windows, _, width = x.shape
    flat = win_block(width)
    weight, at = w_qkv
    extra = [jnp.asarray(a, BF16) for a in vector_slots()]
    shape = (width // 32, 16, 3 * width + 128)
    return functools.partial(call, after=after)(
        functools.partial(qkv_back_kernel, len(grads) // 3),
        (windows,),
        [flag_spec()]
        + [win_block(part.shape[-1]) for part in grads]
        + [flat, flat, whole_block(vec.shape)]
        + [weight_block(width, width, at + n) for n in range(3)]
        + [whole_block(rest.shape)]
        + [whole_block(a.shape) for a in extra],
        [flat, whole_block(shape), whole_block(shape)],
        [
            jax.ShapeDtypeStruct((windows, TOKENS, width), out_dtype),
            jax.ShapeDtypeStruct(shape, F32),
            jax.ShapeDtypeStruct(shape, BF16),
        ],
        4 * windows * TOKENS * width * 3 * width,
        [pltpu.VMEM((shape[0], 2) + shape[1:], F32), pltpu.VMEM(rest.shape, F32)],
    )(flags, *grads, x, grad_middle, vec, weight, weight, weight, rest, *extra)


def pack_first_kernel(qkv_ref, *refs):
    vector_refs, (first_ref, rows_ref) = refs[:-2], refs[-2:]
    own, width3 = qkv_ref.shape[1:]
    rows_ref[...] = jnp.zeros_like(rows_ref)
    row = 0
    lane = lax.broadcasted_iota(jnp.int32, (1, 128), 1)
    for ref in vector_refs:
        values = ref[...].astype(F32)
        values = jnp.pad(values, ((0, 0), (0, 128 - values.shape[1])))
        for part in range(ref.shape[1] // own):
            line = jnp.zeros((1, 128), F32)
            for layer in range(LAYERS):
                turn = ((layer - part) * own) % 128
                turned = pltpu.roll(values, turn, 1) if turn else values
                here = (lane >= layer * own) & (lane < (layer + 1) * own)
                line = jnp.where(here, turned[layer : layer + 1], line)
            rows_ref[row : row + 1, :] = line
            row += 1
    first_ref[:, :width3] = qkv_ref[0]
    first_ref[:, width3:] = rows_ref[...].astype(BF16)


def pack_first(qkv, *vectors, after=None):
    own, width3 = qkv.shape[1:]
    return functools.partial(call, after=after)(
        pack_first_kernel,
        (1,),
        [whole_block((1, own, width3))] + [whole_block(v.shape) for v in vectors],
        whole_block((own, width3 + 128)),
        jax.ShapeDtypeStruct((own, width3 + 128), BF16),
        1e6,
        [pltpu.VMEM((16, 128), F32)],
    )(qkv, *vectors)


def pack_branch_kernel(out_ref, fc1_ref, fc2_ref, packed_ref):
    own, width, wide = fc1_ref.shape[1], fc2_ref.shape[2], fc1_ref.shape[2]
    for layer in range(LAYERS):
        first = 2 * wide * layer
        packed_ref[:, first : first + wide] = fc1_ref[layer]
        for part in range(wide // width):
            at = first + wide + part * width
            packed_ref[:, at : at + width] = fc2_ref[layer, part * own : (part + 1) * own, :]
        at = 2 * wide * LAYERS + layer * width
        packed_ref[:, at : at + width] = out_ref[layer]


def gather_branch(weights, after=None):
    own, wide = weights[1].shape[1:]
    width = weights[0].shape[2]
    packed = jax.ShapeDtypeStruct((own, LAYERS * (2 * wide + width)), BF16)
    shard = functools.partial(call, after=after)(
        pack_branch_kernel,
        (1,),
        [whole_block(w.shape) for w in weights],
        whole_block(packed.shape),
        packed,
        1e6,
    )(*weights)
    whole = lax.all_gather(shard, ALL, axis=0, tiled=True)
    outs = 2 * wide * LAYERS // width
    return [((whole, outs + n), (whole, 2 * n), (whole, 2 * n + 1)) for n in range(LAYERS)]


def vector_slots():
    devices, own = 32, 16
    count = devices * own
    mask = np.zeros((devices * 16, count), np.float32)
    pick = np.zeros((16, devices * 16), np.float32)
    spread = np.zeros((LAYERS, 128, count), np.float32)
    for device in range(devices):
        for first, parts in ((0, 1), (1, 1), (2, 2), (4, 1), (5, 1), (6, 1), (7, 1), (8, 4)):
            for part in range(parts):
                row, start = divmod(device * own * parts + part * own, count)
                slot = device * 16 + first + part
                pick[first + row, slot] = 1
                mask[slot, start : start + own] = 1
    for layer in range(LAYERS):
        for lane in range(count):
            spread[layer, layer * own + lane % own, lane] = 1
    return mask, pick, spread


def vectors_kernel(block_ref, mask_ref, pick_ref, spread_ref, out_ref):
    block = block_ref[...]
    for layer in range(LAYERS):
        lines = mm(block, spread_ref[layer]) * mask_ref[...].astype(F32)
        out_ref[layer] = mm(pick_ref[...], lines.astype(BF16))


def vectors_whole(blocks, after=None):
    count, width = blocks.shape
    extra = [jnp.asarray(a, BF16) for a in vector_slots()]
    return functools.partial(call, after=after)(
        vectors_kernel,
        (1,),
        [pl.BlockSpec((count, 128), lambda n: (0, width // 128 - 1))]
        + [whole_block(a.shape) for a in extra],
        whole_block((LAYERS, 16, count)),
        jax.ShapeDtypeStruct((LAYERS, 16, count), F32),
        1e9,
    )(blocks, *extra)


def finish_kernel(
    mix0_ref, mix1_ref, mid_ref, two_ref, later_ref, gain1_ref, bias1_ref, qkv_ref, qvb_ref, out_ref,
    outb_ref, gain2_ref, bias2_ref, fc1_ref, fc1b_ref, fc2_ref, fc2b_ref,
):
    width, wide = out_ref.shape[2], fc1_ref.shape[2]
    own = gain1_ref.shape[1]
    lane = lax.broadcasted_iota(jnp.int32, (1, 128), 1)
    for layer, mix_ref in enumerate((mix0_ref, mix1_ref)):
        qkv_ref[layer] = mix_ref[:, : 3 * width]
        row = 0
        for ref in (gain1_ref, bias1_ref, qvb_ref, outb_ref, gain2_ref, bias2_ref, fc2b_ref, fc1b_ref):
            line = jnp.zeros((1, 128), F32)
            for part in range(ref.shape[1] // own):
                piece = mix_ref[row : row + 1, 3 * width : 3 * width + 128]
                piece = pltpu.roll(piece, part * own, 1) if part else piece
                line = jnp.where((lane >= part * own) & (lane < (part + 1) * own), piece, line)
                row += 1
            ref[layer : layer + 1, :] = line[:, : ref.shape[1]]
    fc1_ref[0] = mid_ref[:, :wide]
    out_ref[0] = mid_ref[:, wide:]
    fc2_ref[0] = two_ref[...]
    fc1_ref[1] = later_ref[:, :wide].astype(F32)
    out_ref[1] = later_ref[:, wide : wide + width].astype(F32)
    for part in range(wide // width):
        first = wide + width + part * width
        piece = later_ref[:, first : first + width].astype(F32)
        fc2_ref[1, part * own : (part + 1) * own, :] = piece


def run_finish(mixes, mid, two, later):
    own, width = 16, two.shape[1]
    wide = mid.shape[1] - width
    shapes = [
        (own,), (own,), (own, 3 * width), (2 * own,), (own, width), (own,),
        (own,), (own,), (own, wide), (4 * own,), (4 * own, width), (own,),
    ]
    operands = [*mixes, mid, two, later]
    return call(
        finish_kernel,
        (1,),
        [whole_block(v.shape) for v in operands],
        [whole_block((LAYERS,) + shape) for shape in shapes],
        [jax.ShapeDtypeStruct((LAYERS,) + shape, F32) for shape in shapes],
        1e6,
    )(*operands)


def place_flags():
    quadrant = lax.axis_index(SPACE)
    last = lax.axis_index(TM) == lax.axis_size(TM) - 1
    flags = [lax.axis_index(CLIP) % 2, last, quadrant // 2, quadrant % 2]
    return jnp.stack([jnp.asarray(f, jnp.int32) for f in flags])


FIRST, TABLES, LATER, ROLL, GRAD, BACK, D_MID, D_TWO, TABLE, D_QKV = range(10)


def local_windows(
    clips_in,
    ln1_gain,
    ln1_bias,
    qkv_weight,
    qv_bias,
    out_weight,
    out_bias,
    ln2_gain,
    ln2_bias,
    fc1_weight,
    fc1_bias,
    fc2_weight,
    fc2_bias,
    pos_table,
    out_grad,
):
    _, frames_here, _, _, width = clips_in.shape
    windows = frames_here // WIN_T
    own = ln1_gain.shape[1]
    heads_here = pos_table.shape[2]
    one, two = stage_orders()
    flat = (windows, TOKENS, width)
    flags = place_flags()
    halo = Halo()
    flow = Flow()

    def stepped(run, *args, names=None, waits=(), **options):
        order = Order(flow.pending() + list(waits))
        out = run(*args, after=order, **options)
        flow.step(order.token, names)
        return out

    def halo_start(name, packed, onward):
        flow.start(name, halo_flow(packed, onward))

    def send_table():
        (came,), _ = yield [(tables, TM, swap_pairs(TM, 0))]
        first = lax.axis_index(TM) == 0
        return jnp.where(first, tables, came), jnp.where(first, came, tables)

    branch = (out_weight, fc1_weight, fc2_weight)
    first = pack_first(
        qkv_weight, ln1_gain, ln1_bias, qv_bias, out_bias, ln2_gain, ln2_bias, fc2_bias, fc1_bias
    )
    flow.start(FIRST, Gather(first, one))
    tables = pos_table.transpose(0, 2, 1)
    flow.start(TABLES, send_table())
    weights0, weights1 = stepped(gather_branch, branch)
    tables = flow.finish(TABLES)
    bias0 = stepped(table_to_bias, tables[0][0])
    bias0 = stepped(table_to_bias, tables[1][0], bias0)
    bias1 = stepped(table_to_bias, tables[0][1])
    stream0, grad_in = clips_in.reshape(flat), out_grad.reshape(flat)
    grad_packed = halo_pack(grad_in, halo, True, after=Order([stream0, bias1]))
    first = flow.finish(FIRST)
    flow.start(LATER, Gather(qkv_weight[1], one))
    vec = stepped(vectors_whole, first, waits=grad_packed)

    qkv0 = stepped(run_qkv, stream0, vec[0], (first, 0))
    att0, log0 = stepped(run_attend, qkv0, bias0, flags, False)
    mid0, hid0, slope0, stream1 = stepped(run_branch, stream0, [att0], vec[0], weights0, F32)
    halo_start(ROLL, halo_pack(stream1, halo, True, center=True), True)
    bias1 = stepped(table_to_bias, tables[1][1], bias1)
    later = flow.finish(LATER)
    rolled1 = halo_unpack(
        stream1, flow.finish(ROLL), halo, True, F32, center=True, after=Order([bias1])
    )
    qkv1 = run_qkv(rolled1, vec[1], (later, 0))
    halo_start(GRAD, grad_packed, True)
    att1, log1 = stepped(run_attend, qkv1, bias1, flags, True)
    mid1, hid1, slope1, rolled_out = stepped(
        run_branch, rolled1, [att1], vec[1], weights1, F32, waits=flow.done[GRAD]
    )
    out_packed = halo_pack(rolled_out, halo, False, joined=True)
    out_parts = halo_gather(out_packed)
    grad = stepped(halo_unpack, grad_in, flow.done[GRAD], halo, True, BF16, names=())

    kept = (
        (stream0, qkv0, att0, log0, mid0, hid0, slope0, bias0, weights0, (first, 0)),
        (rolled1, qkv1, att1, log1, mid1, hid1, slope1, bias1, weights1, (later, 0)),
    )
    tables = [None] * LAYERS
    for layer in reversed(range(LAYERS)):
        stream, qkv, att, log, mid, hid, slope, bias, weights, w_qkv = kept[layer]
        grad_mid, grad_att, rest, *halves = stepped(
            run_branch_back, grad, mid, [att], hid, slope, vec[layer], weights, flags, layer == 0,
            waits=[out_packed if layer else out_parts],
        )
        if layer == 0:
            flow.start(D_MID, scatter_flow(*halves[:2], one))
            flow.start(D_TWO, scatter_flow(*halves[2:], two))
        else:
            mid_share1 = lax.psum_scatter(halves[0], ALL, scatter_dimension=0, tiled=True)
        grads, sums = [], []
        calls = 1 if layer else 2
        groups = HEADS // GROUP // calls
        for n in range(calls):
            *parts, total = stepped(
                run_attend_back, qkv, grad_att, att, bias, flags, log, layer == 1, n * groups, groups,
            )
            grads.append(parts)
            sums.append(total)
        grads = [part for group in zip(*grads) for part in group]
        if layer == 0:
            tables[0] = [
                stepped(sums_to_table, total, names=names) for total, names in zip(sums, ((), None))
            ]
            pairs = [jnp.stack([tables[layer][n] for layer in range(LAYERS)]) for n in range(2)]
            flow.start(TABLE, table_flow(pairs, heads_here))
        grad_stream, *halves = stepped(
            run_qkv_back, grads, stream, grad_mid, vec[layer], w_qkv, rest, flags,
            F32 if layer else BF16,
        )
        if layer:
            halo_start(BACK, halo_pack(grad_stream, halo, False), False)
        flow.start(D_QKV + layer, scatter_flow(*halves, one))
        if layer:
            found = [
                stepped(sums_to_table, sums[0], n * heads_here, heads_here, names=names)
                for n, names in enumerate(((), None))
            ]
            tables[1] = found
            grad = stepped(
                halo_unpack, grad_stream, flow.finish(BACK), halo, False, F32, names=(),
                waits=found,
            )
    in_grad = grad_stream
    clips_out = stepped(
        halo_unpack, rolled_out, out_parts, halo, False, BF16, mean_of=stream1
    )
    while flow.live:
        flow.step(None)
    grads = run_finish(
        [flow.done[D_QKV + layer] for layer in range(LAYERS)],
        flow.done[D_MID],
        flow.done[D_TWO],
        mid_share1,
    )
    return (
        clips_out.reshape(clips_in.shape),
        in_grad.reshape(clips_in.shape),
        *grads,
        flow.done[TABLE].transpose(0, 2, 1),
    )


def windows_are_local(mesh):
    def decide(clips_in, *rest):
        clips, frames_here = clips_in.shape[:2]
        own = rest[0].shape[1]
        return (
            clips == 1
            and frames_here % WIN_T == 0
            and own == 16
            and mesh.shape[TM] == 2
            and mesh.shape[SPACE] == 4
        )

    def program(*args):
        return local_windows(*args) if decide(*args) else per_device(*args)

    return program


def solution(mesh):
    placed = (
        P(CLIP, TM, SPACE, None, None),
        P(None, ALL),
        P(None, ALL),
        P(None, ALL, None),
        P(None, ALL),
        P(None, ALL, None),
        P(None, ALL),
        P(None, ALL),
        P(None, ALL),
        P(None, ALL, None),
        P(None, ALL),
        P(None, ALL, None),
        P(None, ALL),
        P(None, None, TM),
        P(CLIP, TM, SPACE, None, None),
    )
    return jax.shard_map(
        windows_are_local(mesh),
        mesh=mesh,
        in_specs=placed,
        out_specs=(
            P(CLIP, TM, SPACE, None, None),
            P(CLIP, TM, SPACE, None, None),
            P(None, ALL),
            P(None, ALL),
            P(None, ALL, None),
            P(None, ALL),
            P(None, ALL, None),
            P(None, ALL),
            P(None, ALL),
            P(None, ALL),
            P(None, ALL, None),
            P(None, ALL),
            P(None, ALL, None),
            P(None, ALL),
            P(None, None, TM),
        ),
        check_vma=False,
    )
```

```python
import functools
import math

import jax
import jax.numpy as jnp
import numpy as np
from jax import lax
from jax.experimental import pallas as pl
from jax.experimental.pallas import tpu as pltpu
from jax.sharding import PartitionSpec as P

HEADS = 16
WIN_T = 8
WIN_HW = 7
LAYERS = 2


masked_score = -1000000000.0
TM, SPACE, CLIP = "tm", "space", "clip"
ALL = (TM, SPACE, CLIP)


def partner(value, axis, bit):
    mask = 2**bit
    pairs = [(source, source ^ mask) for source in range(lax.axis_size(axis))]
    return lax.ppermute(value, axis, pairs)


def norm_rows(values, gain, offset):
    mean_row = jnp.mean(values, axis=-1, keepdims=True)
    centered = values - mean_row
    spread = jnp.mean(centered * centered, axis=-1, keepdims=True)
    return centered * lax.rsqrt(spread + 1e-05) * gain + offset


def gelu_exact(values):
    return jax.nn.gelu(values, approximate=False)


def project(left, right):
    return jnp.einsum("...i,ij->...j", left, right, preferred_element_type=jnp.float32)


def project_back(left, right):
    return jnp.einsum("...j,ij->...i", left, right, preferred_element_type=jnp.float32)


def outer_sum(left, right):
    flat_left = left.reshape(-1, left.shape[-1])
    flat_right = right.reshape(-1, right.shape[-1])
    return jnp.einsum("ti,tj->ij", flat_left, flat_right, preferred_element_type=jnp.float32)


def column_sum(values):
    return jnp.sum(values.reshape(-1, values.shape[-1]).astype(jnp.float32), axis=0)


def relative_index(win_t, win_hw):
    count = win_t * win_hw * win_hw
    positions = jnp.arange(count, dtype=jnp.int32)
    frame_pos = positions // (win_hw * win_hw)
    row_pos = positions // win_hw % win_hw
    col_pos = positions % win_hw
    span = 2 * win_hw - 1
    frame_off = frame_pos[:, None] - frame_pos[None, :] + win_t - 1
    row_off = row_pos[:, None] - row_pos[None, :] + win_hw - 1
    col_off = col_pos[:, None] - col_pos[None, :] + win_hw - 1
    return frame_off * span * span + row_off * span + col_off


def band_label(coord, extent, window, reach):
    return jnp.where(coord < extent - window, 0, jnp.where(coord < extent - reach, 1, 2)).astype(
        jnp.int32
    )


def region_match(frames):
    quadrant = lax.axis_index(SPACE)
    row_quad = quadrant // 2
    col_quad = quadrant % 2
    local = jnp.arange(WIN_HW, dtype=jnp.int32)
    label_t = band_label(jnp.arange(frames, dtype=jnp.int32), frames, WIN_T, WIN_T // 2)
    label_r = band_label(row_quad * WIN_HW + local, 2 * WIN_HW, WIN_HW, WIN_HW // 2)
    label_c = band_label(col_quad * WIN_HW + local, 2 * WIN_HW, WIN_HW, WIN_HW // 2)
    region = label_t[:, None, None] * 9 + label_r[None, :, None] * 3 + label_c[None, None, :]
    region = region.reshape(frames // WIN_T, WIN_T * WIN_HW * WIN_HW)
    return region[:, :, None] == region[:, None, :]


def space_roll(field, onward):
    side = field.shape[2]
    reach = side // 2
    sent_rows = field[:, :, :reach] if onward else field[:, :, side - reach :]
    came_rows = partner(sent_rows, SPACE, 1)
    if onward:
        rows_done = jnp.concatenate([field, came_rows], axis=2)[:, :, reach : reach + side]
    else:
        rows_done = jnp.concatenate([came_rows, field], axis=2)[:, :, :side]
    sent_cols = rows_done[:, :, :, :reach] if onward else rows_done[:, :, :, side - reach :]
    came_cols = partner(sent_cols, SPACE, 0)
    if onward:
        return jnp.concatenate([rows_done, came_cols], axis=3)[:, :, :, reach : reach + side]
    return jnp.concatenate([came_cols, rows_done], axis=3)[:, :, :, :side]


def gather_layer(shards, layer):
    return tuple(lax.all_gather(w[layer], ALL, axis=0, tiled=True) for w in shards)


def table_bias(table):
    rel = relative_index(WIN_T, WIN_HW)
    return table.astype(jnp.float32)[rel].transpose(2, 0, 1)


def window_scores(queries, keys, bias, same, scale):
    scores = (
        jnp.einsum("wqhd,wkhd->whqk", queries, keys, preferred_element_type=jnp.float32) * scale
        + bias[None]
    )
    if same is not None:
        scores = jnp.where(same[:, None], scores, masked_score)
    return scores


def to_windows(field):
    clips, frames, cells, heads_here, head_size = field.shape
    return field.reshape(clips, frames // WIN_T, WIN_T * cells, heads_here, head_size)


def to_frames(field, frames):
    clips = field.shape[0]
    return field.reshape(clips, frames, WIN_HW * WIN_HW, field.shape[3], field.shape[4])


def layer_forward(stream, params, table, shifted):
    (
        gain_one,
        bias_one,
        mix_weight,
        mix_bias,
        proj_weight,
        proj_bias,
        gain_two,
        bias_two,
        wide_weight,
        wide_bias,
        narrow_weight,
        narrow_bias,
    ) = params
    clips, frames_here, side = (stream.shape[0], stream.shape[1], stream.shape[2])
    width = stream.shape[-1]
    head_size = width // HEADS
    scale = head_size ** (-0.5)
    normed = norm_rows(stream, gain_one.astype(jnp.float32), bias_one.astype(jnp.float32)).astype(
        jnp.bfloat16
    )
    if shifted:
        normed = space_roll(normed, True)
    mixed = project(normed, mix_weight)
    mix_bias32 = mix_bias.astype(jnp.float32)
    head_shape = (clips, frames_here, side * side, HEADS, head_size)
    queries = (mixed[..., :width] + mix_bias32[:width]).astype(jnp.bfloat16).reshape(head_shape)
    keys = mixed[..., width : 2 * width].astype(jnp.bfloat16).reshape(head_shape)
    values = (mixed[..., 2 * width :] + mix_bias32[width:]).astype(jnp.bfloat16).reshape(head_shape)
    queries, keys, values = (
        lax.all_to_all(queries, TM, split_axis=3, concat_axis=1, tiled=True),
        lax.all_to_all(keys, TM, split_axis=3, concat_axis=1, tiled=True),
        lax.all_to_all(values, TM, split_axis=3, concat_axis=1, tiled=True),
    )
    frames = queries.shape[1]
    if shifted:
        queries = jnp.roll(queries, -(WIN_T // 2), axis=1)
        keys = jnp.roll(keys, -(WIN_T // 2), axis=1)
        values = jnp.roll(values, -(WIN_T // 2), axis=1)
    queries, keys, values = (to_windows(queries), to_windows(keys), to_windows(values))
    bias = table_bias(table)
    same = region_match(frames) if shifted else None

    def attend_clip(items):
        clip_queries, clip_keys, clip_values = items
        scores = window_scores(clip_queries, clip_keys, bias, same, scale)
        peak = jnp.max(scores, axis=-1, keepdims=True)
        raised = jnp.exp(scores - peak)
        total = jnp.sum(raised, axis=-1, keepdims=True)
        probs = (raised / total).astype(jnp.bfloat16)
        out_win = jnp.einsum(
            "whqk,wkhd->wqhd", probs, clip_values, preferred_element_type=jnp.float32
        ).astype(jnp.bfloat16)
        return (out_win, peak + jnp.log(total))

    attended_heads, log_total = lax.map(attend_clip, (queries, keys, values))
    attended_heads = to_frames(attended_heads, frames)
    if shifted:
        attended_heads = jnp.roll(attended_heads, WIN_T // 2, axis=1)
    attended = lax.all_to_all(attended_heads, TM, split_axis=1, concat_axis=3, tiled=True)
    attended = attended.reshape(clips, frames_here, side, side, width)
    if shifted:
        attended = space_roll(attended, False)
    middle = stream + project(attended, proj_weight) + proj_bias.astype(jnp.float32)
    normed_two = norm_rows(
        middle, gain_two.astype(jnp.float32), bias_two.astype(jnp.float32)
    ).astype(jnp.bfloat16)
    hidden_pre = project(normed_two, wide_weight) + wide_bias.astype(jnp.float32)
    hidden = gelu_exact(hidden_pre).astype(jnp.bfloat16)
    after = middle + project(hidden, narrow_weight) + narrow_bias.astype(jnp.float32)
    stash = (
        stream,
        normed,
        queries,
        keys,
        values,
        log_total,
        attended,
        middle,
        normed_two,
        hidden_pre,
        hidden,
    )
    return (stash, after)


def layer_backward(grad_after, params, table, stash, shifted):
    (
        gain_one,
        bias_one,
        mix_weight,
        mix_bias,
        proj_weight,
        proj_bias,
        gain_two,
        bias_two,
        wide_weight,
        wide_bias,
        narrow_weight,
        narrow_bias,
    ) = params
    (
        stream,
        normed,
        queries,
        keys,
        values,
        log_total,
        attended,
        middle,
        normed_two,
        hidden_pre,
        hidden,
    ) = stash
    clips, frames_here, side = (stream.shape[0], stream.shape[1], stream.shape[2])
    width = stream.shape[-1]
    head_size = width // HEADS
    scale = head_size ** (-0.5)
    frames = queries.shape[1] * WIN_T
    grad_branch_two = grad_after.astype(jnp.bfloat16)
    narrow_grad = outer_sum(hidden, grad_branch_two)
    narrow_bias_grad = column_sum(grad_branch_two)
    grad_hidden = project_back(grad_branch_two, narrow_weight)
    gelu_pull = jax.vjp(gelu_exact, hidden_pre)[1]
    grad_pre = gelu_pull(grad_hidden)[0].astype(jnp.bfloat16)
    wide_grad = outer_sum(normed_two, grad_pre)
    wide_bias_grad = column_sum(grad_pre)
    grad_normed_two = project_back(grad_pre, wide_weight)
    norm_pull_two = jax.vjp(
        norm_rows, middle, gain_two.astype(jnp.float32), bias_two.astype(jnp.float32)
    )[1]
    grad_mid_part, gain_two_grad, bias_two_grad = norm_pull_two(grad_normed_two)
    grad_middle = grad_after + grad_mid_part
    grad_branch_one = grad_middle.astype(jnp.bfloat16)
    proj_grad = outer_sum(attended, grad_branch_one)
    proj_bias_grad = column_sum(grad_branch_one)
    grad_attended = project_back(grad_branch_one, proj_weight).astype(jnp.bfloat16)
    if shifted:
        grad_attended = space_roll(grad_attended, True)
    grad_attended = grad_attended.reshape(clips, frames_here, side * side, HEADS, head_size)
    grad_attended = lax.all_to_all(grad_attended, TM, split_axis=3, concat_axis=1, tiled=True)
    if shifted:
        grad_attended = jnp.roll(grad_attended, -(WIN_T // 2), axis=1)
    grad_attended = to_windows(grad_attended)
    bias = table_bias(table)
    same = region_match(frames) if shifted else None

    def attend_back(carry, items):
        clip_queries, clip_keys, clip_values, clip_grad, clip_log = items
        scores = window_scores(clip_queries, clip_keys, bias, same, scale)
        probs = jnp.exp(scores - clip_log)
        grad_probs = jnp.einsum(
            "wqhd,wkhd->whqk", clip_grad, clip_values, preferred_element_type=jnp.float32
        )
        inner = jnp.sum(probs * grad_probs, axis=-1, keepdims=True)
        grad_scores = (probs * (grad_probs - inner)).astype(jnp.bfloat16)
        grad_q = (
            jnp.einsum(
                "whqk,wkhd->wqhd", grad_scores, clip_keys, preferred_element_type=jnp.float32
            )
            * scale
        ).astype(jnp.bfloat16)
        grad_k = (
            jnp.einsum(
                "whqk,wqhd->wkhd", grad_scores, clip_queries, preferred_element_type=jnp.float32
            )
            * scale
        ).astype(jnp.bfloat16)
        grad_v = jnp.einsum(
            "whqk,wqhd->wkhd",
            probs.astype(jnp.bfloat16),
            clip_grad,
            preferred_element_type=jnp.float32,
        ).astype(jnp.bfloat16)
        carry = carry + jnp.sum(grad_scores.astype(jnp.float32), axis=0)
        return (carry, (grad_q, grad_k, grad_v))

    window_tokens = queries.shape[2]
    start_bias = jnp.zeros((queries.shape[3], window_tokens, window_tokens), jnp.float32)
    bias_grad, grads_win = lax.scan(
        attend_back, start_bias, (queries, keys, values, grad_attended, log_total)
    )
    grad_q, grad_k, grad_v = (to_frames(g, frames) for g in grads_win)
    if shifted:
        grad_q = jnp.roll(grad_q, WIN_T // 2, axis=1)
        grad_k = jnp.roll(grad_k, WIN_T // 2, axis=1)
        grad_v = jnp.roll(grad_v, WIN_T // 2, axis=1)
    grad_q, grad_k, grad_v = (
        lax.all_to_all(grad_q, TM, split_axis=1, concat_axis=3, tiled=True),
        lax.all_to_all(grad_k, TM, split_axis=1, concat_axis=3, tiled=True),
        lax.all_to_all(grad_v, TM, split_axis=1, concat_axis=3, tiled=True),
    )
    token_shape = (clips, frames_here, side, side, width)
    grad_q, grad_k, grad_v = (
        grad_q.reshape(token_shape),
        grad_k.reshape(token_shape),
        grad_v.reshape(token_shape),
    )
    grad_mix = jnp.concatenate([grad_q, grad_k, grad_v], axis=-1)
    mix_grad = outer_sum(normed, grad_mix)
    mix_bias_grad = jnp.concatenate([column_sum(grad_q), column_sum(grad_v)])
    grad_normed = project_back(grad_mix, mix_weight)
    if shifted:
        grad_normed = space_roll(grad_normed.astype(jnp.bfloat16), False).astype(jnp.float32)
    norm_pull_one = jax.vjp(
        norm_rows, stream, gain_one.astype(jnp.float32), bias_one.astype(jnp.float32)
    )[1]
    grad_stream_part, gain_one_grad, bias_one_grad = norm_pull_one(grad_normed)
    grad_stream = grad_middle + grad_stream_part
    rel = relative_index(WIN_T, WIN_HW).reshape(-1)
    table_grad = (
        jnp.zeros(table.shape, jnp.float32).at[rel].add(bias_grad.reshape(bias_grad.shape[0], -1).T)
    )
    weight_grads = (
        gain_one_grad,
        bias_one_grad,
        mix_grad,
        mix_bias_grad,
        proj_grad,
        proj_bias_grad,
        gain_two_grad,
        bias_two_grad,
        wide_grad,
        wide_bias_grad,
        narrow_grad,
        narrow_bias_grad,
    )
    return (grad_stream, weight_grads, table_grad)


def per_device(
    clips_in,
    ln1_gain,
    ln1_bias,
    qkv_weight,
    qv_bias,
    out_weight,
    out_bias,
    ln2_gain,
    ln2_bias,
    fc1_weight,
    fc1_bias,
    fc2_weight,
    fc2_bias,
    pos_table,
    out_grad,
):
    clips, frames_here, quads, cells, width = clips_in.shape
    grid_shape = (clips, frames_here, WIN_HW, WIN_HW, width)
    shards = (
        ln1_gain,
        ln1_bias,
        qkv_weight,
        qv_bias,
        out_weight,
        out_bias,
        ln2_gain,
        ln2_bias,
        fc1_weight,
        fc1_bias,
        fc2_weight,
        fc2_bias,
    )
    stream = clips_in.astype(jnp.float32).reshape(grid_shape)
    kept_params = []
    kept_stash = []
    for layer in range(LAYERS):
        params = gather_layer(shards, layer)
        stash, stream = layer_forward(stream, params, pos_table[layer], layer % 2 == 1)
        kept_params.append(params)
        kept_stash.append(stash)
    clips_out = stream.astype(jnp.bfloat16).reshape(clips_in.shape)
    grad_stream = out_grad.astype(jnp.float32).reshape(grid_shape)
    layer_shares = [None] * LAYERS
    table_parts = [None] * LAYERS
    for layer in reversed(range(LAYERS)):
        params = gather_layer(shards, layer)
        grad_stream, weight_grads, table_grad = layer_backward(
            grad_stream, params, pos_table[layer], kept_stash[layer], layer % 2 == 1
        )
        layer_shares[layer] = tuple(
            lax.psum_scatter(g, ALL, scatter_dimension=0, tiled=True) for g in weight_grads
        )
        table_parts[layer] = table_grad
    in_grad = grad_stream.astype(jnp.bfloat16).reshape(clips_in.shape)
    table_total = lax.psum(jnp.stack(table_parts), (SPACE, CLIP))
    stacked = tuple(
        (jnp.stack([layer_shares[n][slot] for n in range(LAYERS)]) for slot in range(12))
    )
    return (
        clips_out,
        in_grad,
        stacked[0],
        stacked[1],
        stacked[2],
        stacked[3],
        stacked[4],
        stacked[5],
        stacked[6],
        stacked[7],
        stacked[8],
        stacked[9],
        stacked[10],
        stacked[11],
        table_total,
    )


F32 = jnp.float32
BF16 = jnp.bfloat16
TOKENS = WIN_T * WIN_HW * WIN_HW
CELLS = WIN_HW * WIN_HW
SPAN = 2 * WIN_HW - 1
STEPS = 2 * WIN_T - 1
LOG2E = math.log2(math.e)
VMEM_BYTES = 56 * 1024 * 1024


def mm(left, right, left_dim=1, right_dim=0):
    dims = (((left_dim,), (right_dim,)), ((), ()))
    return lax.dot_general(left, right, dims, preferred_element_type=F32)


class Order:
    def __init__(self, waits=()):
        self.waits = list(waits)
        self.token = None


def call(
    kernel, grid, in_specs, out_specs, out_shape, flops, scratch=(), after=None, aliases=None
):
    waits = after.waits if after else []
    inputs = len(in_specs)
    single = not isinstance(out_shape, list)
    out_specs = [out_specs] if single else list(out_specs)
    out_shape = [out_shape] if single else list(out_shape)
    outputs = len(out_shape)
    if after:
        out_specs.append(pl.BlockSpec(memory_space=pltpu.SMEM))
        out_shape.append(jax.ShapeDtypeStruct((1, 1), F32))

    def body(*refs):
        ins, outs = refs[:inputs], refs[inputs + len(waits) :]
        if after:
            outs[outputs][0, 0] = 0.0
        kernel(*ins, *outs[:outputs], *outs[len(out_shape) :])

    run = pl.pallas_call(
        body,
        grid=grid,
        in_specs=list(in_specs) + [pl.BlockSpec(memory_space=pl.ANY)] * len(waits),
        out_specs=out_specs,
        out_shape=out_shape,
        scratch_shapes=scratch,
        input_output_aliases=aliases or {},
        cost_estimate=pl.CostEstimate(
            flops=int(flops), transcendentals=0, bytes_accessed=8 * 1024 * 1024
        ),
        compiler_params=pltpu.CompilerParams(vmem_limit_bytes=VMEM_BYTES),
    )

    def result(*args):
        found = run(*args, *waits)
        if after:
            after.token = found[outputs]
        return found[0] if single else found[:outputs]

    return result


def whole_block(shape):
    return pl.BlockSpec(shape, lambda *ids: (0,) * len(shape))


def flag_spec():
    return pl.BlockSpec(memory_space=pltpu.SMEM)


def win_block(width, column=0):
    return pl.BlockSpec((1, TOKENS, width), lambda w: (w, 0, column))


HALF = WIN_T // 2 * CELLS
KINDS = range(1, 8)


class Halo:
    def __init__(self):
        token = np.arange(HALF)
        row, col = token // WIN_HW % WIN_HW, token % WIN_HW
        reach = WIN_HW // 2
        target = token - row * WIN_HW - col
        target = target + (row - reach) % WIN_HW * WIN_HW + (col - reach) % WIN_HW
        leaves = (row < reach) * 2 + (col < reach) * 1
        self.stay = np.zeros((HALF, HALF), np.float32)
        stays = leaves == 0
        self.stay[target[stays], token[stays]] = 1
        self.near, self.near_to = self.ways(leaves, target, (1, 2, 3))
        self.far, self.far_to = self.ways(leaves, target, (0, 1, 2, 3))

    @staticmethod
    def ways(leaves, target, kinds):
        send, place = [], []
        for kind in kinds:
            source = np.nonzero(leaves == kind)[0]
            rows = 64 if kind == 0 else 48
            out, back = np.zeros((rows, HALF), np.float32), np.zeros((HALF, rows), np.float32)
            out[np.arange(len(source)), source] = 1
            back[target[source], np.arange(len(source))] = 1
            send.append(out)
            place.append(back)
        return np.concatenate(send, 0), np.concatenate(place, 1)

    def sends(self, onward):
        return (self.near, self.far) if onward else (self.near_to.T, self.far_to.T)

    def places(self, onward):
        if onward:
            return self.stay, self.near_to, self.far_to
        return self.stay.T, self.near.T, self.far.T


def half_at(half):
    return half // 2, slice(half % 2 * HALF, (half % 2 + 1) * HALF)


class Flow:
    def __init__(self):
        self.live = []
        self.done = {}

    def start(self, name, task):
        self.live.append((name, task, task.sends() if isinstance(task, Gather) else next(task)))

    def pending(self):
        return [value for _, _, sends in self.live for value, _, _ in sends]

    def step(self, token, names=None):
        live = []
        for name, task, sends in self.live:
            if names is not None and name not in names:
                live.append((name, task, sends))
                continue
            came = [lax.ppermute(value, axis, pairs) for value, axis, pairs in sends]
            if isinstance(task, Gather):
                task.step(came[0], token if len(task.steps) > 1 else None)
                if task.steps:
                    live.append((name, task, task.sends()))
                else:
                    self.done[name] = task.out
                continue
            try:
                live.append((name, task, task.send((came, token))))
            except StopIteration as end:
                self.done[name] = end.value
        self.live = live

    def finish(self, name):
        while name not in self.done:
            self.step(None, (name,))
        return self.done[name]


def swap_pairs(axis, bit):
    return [(source, source ^ 2**bit) for source in range(lax.axis_size(axis))]


def halo_flow(packed, onward):
    ring, quads = lax.axis_size(TM), lax.axis_size(SPACE)
    sends = []
    for kind, piece in zip(KINDS, packed):
        step = 0 if not kind & 4 else (-1 if onward else 1)
        pairs = []
        for frame_at in range(ring):
            for quad in range(quads):
                to = (frame_at + step) % ring * quads + (quad ^ (kind & 3))
                pairs.append((frame_at * quads + quad, to))
        sends.append((piece, (TM, SPACE), pairs))
    came, _ = yield sends
    return came


def pack_kernel(center, onward, near_ref, far_ref, x_ref, *refs):
    out_refs, flat_ref = refs[:-1], refs[-1]
    halves = 2 * x_ref.shape[0]
    for w in range(x_ref.shape[0]):
        x = x_ref[w].astype(F32)
        if center:
            x = x - jnp.mean(x, axis=-1, keepdims=True)
        flat_ref[w] = x
    for n in range(halves - 1):
        w, rows = half_at(n + 1 if onward else n)
        sent = mm(near_ref[...], flat_ref[w, rows].astype(BF16)).astype(BF16)
        for kind in range(3):
            out_refs[kind][n * 48 : (n + 1) * 48] = sent[kind * 48 : (kind + 1) * 48]
    w, rows = half_at(0 if onward else halves - 1)
    sent = mm(far_ref[...], flat_ref[w, rows].astype(BF16)).astype(BF16)
    for kind in range(4):
        first = 0 if kind == 0 else 16 + 48 * kind
        out_refs[3 + kind][...] = sent[first : first + out_refs[3 + kind].shape[0]]


def part_rows(windows):
    return [48 * (2 * windows - 1)] * 3 + [64, 48, 48, 48]


def halo_pack(x, halo, onward, center=False, joined=False, after=None):
    windows, _, width = x.shape
    near, far = (jnp.asarray(m, BF16) for m in halo.sends(onward))
    rows = part_rows(windows)

    def kernel(near_ref, far_ref, x_ref, *refs):
        if joined:
            refs = [refs[0].at[pl.ds(sum(rows[:n]), rows[n])] for n in range(7)] + [refs[1]]
        pack_kernel(center, onward, near_ref, far_ref, x_ref, *refs)

    shapes = [(sum(rows), width)] if joined else [(n, width) for n in rows]
    out = functools.partial(call, after=after)(
        kernel,
        (1,),
        [whole_block(m.shape) for m in (near, far, x)],
        [whole_block(shape) for shape in shapes],
        [jax.ShapeDtypeStruct(shape, BF16) for shape in shapes],
        2 * 640 * HALF * width,
        [pltpu.VMEM(x.shape, F32)],
    )(near, far, x)
    return out[0] if joined else out


def halo_gather(packed):
    return lax.all_gather(packed, (TM, SPACE), axis=0, tiled=True)


def halo_senders(onward):
    ring, quads = lax.axis_size(TM), lax.axis_size(SPACE)
    senders = []
    for kind in KINDS:
        step = 0 if not kind & 4 else (1 if onward else -1)
        frame_at = (lax.axis_index(TM) + step + ring) % ring
        senders.append(frame_at * quads + lax.axis_index(SPACE) ^ (kind & 3))
    return jnp.stack([jnp.asarray(n, jnp.int32) for n in senders])


def unpack_kernel(center, onward, add_mean, stay_ref, near_ref, far_ref, x_ref, *refs):
    base_ref, refs = (refs[0], refs[1:]) if add_mean else (None, refs)
    came_refs, (out_ref, flat_ref, total_ref) = refs[:7], refs[7:]
    windows = x_ref.shape[0]
    halves = 2 * windows
    for w in range(windows):
        x = x_ref[w].astype(F32)
        if center:
            x = x - jnp.mean(x, axis=-1, keepdims=True)
        flat_ref[w] = x
    for n in range(halves - 1):
        w, rows = half_at(n + 1 if onward else n)
        x = flat_ref[w, rows]
        high = x.astype(BF16)
        total = mm(stay_ref[...], high)
        if x_ref.dtype == F32:
            total = total + mm(stay_ref[...], (x - high.astype(F32)).astype(BF16))
        came = jnp.concatenate([ref[n * 48 : (n + 1) * 48] for ref in came_refs[:3]], axis=0)
        w, rows = half_at(n if onward else n + 1)
        total_ref[w, rows] = total + mm(near_ref[...], came)
    came = jnp.concatenate([ref[...] for ref in came_refs[3:]], axis=0)
    w, rows = half_at(halves - 1 if onward else 0)
    total_ref[w, rows] = mm(far_ref[...], came)
    for w in range(windows):
        total = total_ref[w]
        if add_mean:
            total = total + jnp.mean(base_ref[w], axis=-1, keepdims=True)
        out_ref[w] = total.astype(out_ref.dtype)


def halo_unpack(x, came, halo, onward, dtype, center=False, mean_of=None, after=None):
    places = [jnp.asarray(m, BF16) for m in halo.places(onward)]
    operands = places + [x] + ([] if mean_of is None else [mean_of])
    joined = not isinstance(came, list)
    senders = [halo_senders(onward)] if joined else []
    operands += [came] if joined else came
    rows = part_rows(x.shape[0])

    def kernel(*refs):
        if joined:
            sender_ref, refs = refs[0], refs[1:]
            count = len(operands)
            parts = []
            for n in range(7):
                first = sender_ref[n] * sum(rows) + sum(rows[:n])
                parts.append(refs[count - 1].at[pl.ds(pl.multiple_of(first, 16), rows[n])])
            refs = refs[: count - 1] + tuple(parts) + refs[count:]
        unpack_kernel(center, onward, mean_of is not None, *refs)

    return functools.partial(call, after=after)(
        kernel,
        (1,),
        [flag_spec()] * joined + [whole_block(v.shape) for v in operands],
        whole_block(x.shape),
        jax.ShapeDtypeStruct(x.shape, dtype),
        8 * x.size * HALF,
        [pltpu.VMEM(x.shape, F32), pltpu.VMEM(x.shape, F32)],
    )(*senders, *operands)


def index_bits():
    bits = []
    for axis in ALL:
        count = lax.axis_size(axis).bit_length() - 1
        bits += [(axis, b) for b in reversed(range(count))]
    return bits


def bit_of(axis, bit):
    return (lax.axis_index(axis) // 2**bit) % 2


def stage_orders():
    bits = index_bits()
    inner = [(CLIP, 0)] if lax.axis_size(CLIP) > 1 else []
    tm = [b for b in bits if b[0] == TM]
    clip = [b for b in bits if b[0] == CLIP and b not in inner]
    space = [b for b in reversed(bits) if b[0] == SPACE]
    return inner + tm + clip + space, inner + clip + tm + space


class Gather:
    def __init__(self, shard, order):
        self.bits, self.steps = index_bits(), list(reversed(order))
        self.dims = [1] * len(self.bits)
        self.rows, self.out = shard.shape[0], shard

    def sends(self):
        axis, bit = self.steps[0]
        return [(self.out, axis, swap_pairs(axis, bit))]

    def step(self, came, token):
        axis, bit = self.steps.pop(0)
        dim = self.bits.index((axis, bit))
        before, after = math.prod(self.dims[:dim]), math.prod(self.dims[dim + 1 :])
        self.dims[dim] = 2
        here = bit_of(axis, bit).astype(F32) + (0.0 if token is None else token.reshape(()))
        own, came = (v.reshape(before, 1, after * self.rows, -1) for v in (self.out, came))
        low, high = jnp.where(here > 0.5, came, own), jnp.where(here > 0.5, own, came)
        self.out = jnp.concatenate([low, high], axis=1).reshape(-1, own.shape[-1])


def scatter_flow(own, sent, order):
    bits = index_bits()
    width = own.shape[-1]
    dims = [2] * len(bits)
    own, sent = own.reshape(-1, width), sent.reshape(-1, width)
    for n, (axis, bit) in enumerate(order):
        (came,), token = yield [(sent, axis, swap_pairs(axis, bit))]
        dims[bits.index((axis, bit))] = 1
        zero = 0.0 if token is None else token.reshape(())
        if n + 1 == len(order):
            return own + came.astype(F32)
        axis, bit = order[n + 1]
        dim = bits.index((axis, bit))
        here = bit_of(axis, bit)
        own, came = (v.reshape(dims + [-1, width]) for v in (own, came))

        def half(index):
            mine, theirs = (lax.dynamic_slice_in_dim(v, index, 1, dim) for v in (own, came))
            return (mine + theirs.astype(F32) + zero).reshape(-1, width)

        own, sent = half(here), half(1 - here).astype(BF16)


def table_flow(tables, heads_here):
    first = lax.axis_index(TM) == 0
    mine = jnp.where(first, tables[0], tables[1])
    (came,), _ = yield [(jnp.where(first, tables[1], tables[0]), TM, swap_pairs(TM, 0))]
    table = mine + came
    for axis, bit in index_bits():
        if axis != TM:
            (came,), _ = yield [(table, axis, swap_pairs(axis, bit))]
            table = table + came
    return table


WIDE = 768


def column_pick():
    pick = np.zeros((WIN_HW, 256, 128), np.float32)
    for key_col in range(WIN_HW):
        for row in range(SPAN):
            for col in range(WIN_HW):
                entry = row * SPAN + col - key_col + WIN_HW - 1
                pick[key_col, entry, row * WIN_HW + col] = 1
    return pick


def lane_spans(step):
    first, rest = divmod(step * CELLS, 128)
    if rest + CELLS <= 128:
        return [(first, rest, rest + CELLS)]
    return [(first, rest, 128), (first + 1, 0, rest + CELLS - 128)]


def bias_kernel(slab_ref, pick_ref, out_ref, row_ref, wide_ref):
    heads = pl.num_programs(0)

    @pl.when(pl.program_id(0) == 0)
    def _():
        slabs = slab_ref[...]
        for col in range(WIN_HW):
            row_ref[pl.ds(col, slabs.shape[0], stride=8), :] = mm(slabs, pick_ref[col]) * LOG2E

    base = pl.program_id(0) * 128
    lane = lax.broadcasted_iota(jnp.int32, (8, 128), 1)
    for row in range(WIN_HW):
        tiles = [jnp.zeros((8, 128), F32) for _ in range(WIDE // 128)]
        for step in range(STEPS):
            rows = row_ref[pl.ds(pl.multiple_of(base + step * 8, 8), 8), :]
            turn = (step * CELLS - WIN_HW * (WIN_HW - 1 - row)) % 128
            rows = pltpu.roll(rows, turn, 1) if turn else rows
            for tile, low, high in lane_spans(step):
                tiles[tile] = jnp.where((lane >= low) & (lane < high), rows, tiles[tile])
        wide_ref[row * WIN_HW : (row + 1) * WIN_HW, :] = jnp.concatenate(tiles, axis=1)[:WIN_HW]
    wide = wide_ref[:CELLS, :]
    for key_frame in range(WIN_T):
        turned = pltpu.roll(wide, (WIDE - (WIN_T - 1 - key_frame) * CELLS) % WIDE, 1)
        out_ref[0, key_frame * CELLS : (key_frame + 1) * CELLS, :] = turned[:, :TOKENS]


def table_to_bias(tables, rest=None, after=None):
    heads = tables.shape[0]
    slabs = tables.reshape(heads, STEPS, SPAN * SPAN)
    slabs = jnp.pad(slabs, ((0, 0), (0, 16 - STEPS), (0, 256 - SPAN * SPAN)))
    slabs = slabs.reshape(heads * 16, 256)
    held = [] if rest is None else [rest]
    first = 0 if rest is None else heads

    def kernel(slab_ref, pick_ref, *refs):
        bias_kernel(slab_ref, pick_ref, *refs[len(held) :])

    return functools.partial(call, after=after, aliases={2: 0} if held else {})(
        kernel,
        (heads,),
        [whole_block(slabs.shape), whole_block((WIN_HW, 256, 128))]
        + [pl.BlockSpec(memory_space=pl.ANY)] * len(held),
        pl.BlockSpec((1, TOKENS, TOKENS), lambda h: (first + h, 0, 0)),
        jax.ShapeDtypeStruct((2 * heads, TOKENS, TOKENS), F32),
        heads * 500_000_000,
        [pltpu.VMEM((heads * 128, 128), F32), pltpu.VMEM((56, WIDE), F32)],
    )(slabs, jnp.asarray(column_pick(), BF16), *held)


def table_back_kernel(sums_ref, pick_ref, out_ref, row_ref):
    head = pl.program_id(0)
    lane = lax.broadcasted_iota(jnp.int32, (WIN_HW, 128), 1)
    totals = [None] * STEPS
    for row in range(WIN_HW):
        rows = sums_ref[0, row * WIN_HW : (row + 1) * WIN_HW, :]
        start = WIN_HW * (WIN_HW - 1 - row)
        for step in range(STEPS):
            turn = (start - step * CELLS) % 128
            piece = None
            for tile, low, high in lane_spans(step):
                part = rows[:, tile * 128 : (tile + 1) * 128]
                part = jnp.where((lane >= low) & (lane < high), part, 0.0)
                piece = part if piece is None else piece + part
            piece = pltpu.roll(piece, turn, 1) if turn else piece
            totals[step] = piece if totals[step] is None else totals[step] + piece
    blank = jnp.zeros((1, 128), F32)
    for step in range(16):
        rows = jnp.concatenate([totals[step], blank]) if step < STEPS else jnp.zeros((8, 128), F32)
        row_ref[pl.ds(pl.multiple_of(head * 128 + step * 8, 8), 8), :] = rows

    @pl.when(head == pl.num_programs(0) - 1)
    def _():
        total = None
        for col in range(WIN_HW):
            rows = row_ref[pl.ds(col, out_ref.shape[0], stride=8), :]
            high = rows.astype(BF16)
            low = (rows - high.astype(F32)).astype(BF16)
            part = mm(high, pick_ref[col], 1, 1) + mm(low, pick_ref[col], 1, 1)
            total = part if total is None else total + part
        out_ref[...] = total


def sums_to_table(sums, first=0, heads=None, after=None):
    heads = heads or sums.shape[0]
    slabs = functools.partial(call, after=after)(
        table_back_kernel,
        (heads,),
        [
            pl.BlockSpec((1, CELLS, WIDE), lambda h: (first + h, 0, 0)),
            whole_block((WIN_HW, 256, 128)),
        ],
        whole_block((heads * 16, 256)),
        jax.ShapeDtypeStruct((heads * 16, 256), F32),
        heads * 300_000_000,
        [pltpu.VMEM((heads * 128, 128), F32)],
    )(sums, jnp.asarray(column_pick(), BF16))
    return slabs.reshape(heads, 16, 256)[:, :STEPS, : SPAN * SPAN].reshape(heads, -1)


def unit_rows(x):
    centered = x - jnp.mean(x, axis=-1, keepdims=True)
    inverse = lax.rsqrt(jnp.mean(centered * centered, axis=-1, keepdims=True) + 1e-05)
    return centered * inverse, inverse


def norm_back(grad, unit, inverse, gain):
    scaled = grad * gain
    return inverse * (
        scaled
        - jnp.mean(scaled, axis=-1, keepdims=True)
        - unit * jnp.mean(scaled * unit, axis=-1, keepdims=True)
    )


def qkv_kernel(x_ref, vec_ref, wq_ref, wk_ref, wv_ref, out_ref):
    width = x_ref.shape[-1]
    unit, _ = unit_rows(x_ref[0].astype(F32))
    normed = (unit * vec_ref[0:1] + vec_ref[1:2]).astype(BF16)
    for part, ref in enumerate((wq_ref, wk_ref, wv_ref)):
        out = mm(normed, ref[...])
        if part == 0:
            out = out + vec_ref[2:3]
        if part == 2:
            out = out + vec_ref[3:4]
        out_ref[0, :, part * width : (part + 1) * width] = out.astype(BF16)


def run_qkv(x, vec, w_qkv, after=None):
    windows, _, width = x.shape
    weight, at = w_qkv
    return functools.partial(call, after=after)(
        qkv_kernel,
        (windows,),
        [win_block(width), whole_block(vec.shape)]
        + [weight_block(width, width, at + n) for n in range(3)],
        win_block(3 * width),
        jax.ShapeDtypeStruct((windows, TOKENS, 3 * width), BF16),
        2 * windows * TOKENS * width * 3 * width,
    )(x, vec, weight, weight, weight)


GROUP = 4


def head_masks(head_size):
    lane = lax.broadcasted_iota(jnp.int32, (1, GROUP * head_size), 1)
    return [
        jnp.where((lane >= h * head_size) & (lane < (h + 1) * head_size), 1.0, 0.0).astype(BF16)
        for h in range(GROUP)
    ]


def region_labels(flag_ref, late_ref, turned_ref, at_end):
    flags = [flag_ref[1 + n].astype(F32) for n in range(3)]
    flags[0] = flags[0] * at_end
    col = sum(flags[n] * late_ref[:, n : n + 1] for n in range(3))
    return col, sum(flags[n] * turned_ref[n : n + 1, :] for n in range(3))


def late_tokens():
    token = np.arange(TOKENS)
    late = np.zeros((TOKENS, 8), np.float32)
    late[:, 0] = 4 * (token // CELLS >= WIN_T - WIN_T // 2)
    late[:, 1] = 2 * (token // WIN_HW % WIN_HW >= WIN_HW - WIN_HW // 2)
    late[:, 2] = token % WIN_HW >= WIN_HW - WIN_HW // 2
    return late


def attend_kernel(
    shifted, head_size, flag_ref, q_ref, k_ref, v_ref, bias_ref, late_ref, turned_ref, out_ref, log_ref
):
    q, k = q_ref[0], k_ref[0]
    if shifted:
        at_end = jnp.where(pl.program_id(1) == pl.num_programs(1) - 1, 1.0, 0.0)
        col, row = region_labels(flag_ref, late_ref, turned_ref, at_end)
    turned = v_ref[0].astype(F32).T.astype(BF16)
    factor = head_size**-0.5 * LOG2E
    masks = head_masks(head_size)
    outs, logs = [], []
    for h in range(GROUP):
        scores = mm(k * masks[h], q, 1, 1) * factor + bias_ref[h]
        if shifted:
            scores = jnp.where(col == row, scores, masked_score)
        peak = jnp.max(scores, axis=0, keepdims=True)
        raised = jnp.exp2(scores - peak)
        total = jnp.sum(raised, axis=0, keepdims=True)
        mixed = mm(turned[h * head_size : (h + 1) * head_size], raised.astype(BF16))
        outs.append(mixed / total)
        logs.append(peak + jnp.log2(total))
    out_ref[0] = jnp.concatenate(outs, axis=0).T.astype(BF16)
    log_ref[0, 0] = jnp.concatenate(logs + logs, axis=0)


def run_attend(qkv, bias, flags, shifted, after=None):
    windows, _, width3 = qkv.shape
    width = width3 // 3
    wide = GROUP * (width // HEADS)
    groups = HEADS // GROUP
    qkv_specs = [
        pl.BlockSpec((1, TOKENS, wide), lambda g, w, p=part: (w, 0, p * groups + g))
        for part in range(3)
    ]
    return functools.partial(call, after=after)(
        functools.partial(attend_kernel, shifted, width // HEADS),
        (groups, windows),
        [flag_spec()]
        + qkv_specs
        + [
            pl.BlockSpec((GROUP, TOKENS, TOKENS), lambda g, w: (g, 0, 0)),
            whole_block((TOKENS, 8)),
            whole_block((8, TOKENS)),
        ],
        [
            pl.BlockSpec((1, TOKENS, wide), lambda g, w: (w, 0, g)),
            pl.BlockSpec((1, 1, 2 * GROUP, TOKENS), lambda g, w: (w, g, 0, 0)),
        ],
        [
            jax.ShapeDtypeStruct((windows, TOKENS, width), BF16),
            jax.ShapeDtypeStruct((windows, groups, 2 * GROUP, TOKENS), F32),
        ],
        64 * windows * TOKENS * TOKENS * width,
    )(flags, qkv, qkv, qkv, bias, late_tokens(), late_tokens().T)


def attend_back_kernel(
    shifted, head_size, flag_ref, q_ref, k_ref, v_ref, g_ref, o_ref, bias_ref, late_ref, turned_ref,
    log_ref, dq_ref, dk_ref, dv_ref, table_ref, sum_ref,
):
    windows = q_ref.shape[0]
    if shifted:
        labels = [
            region_labels(flag_ref, late_ref, turned_ref, float(w == windows - 1))
            for w in range(windows)
        ]
    scale = head_size**-0.5
    factor = scale * LOG2E
    masks = head_masks(head_size)

    @pl.when(pl.program_id(0) == 0)
    def _():
        sum_ref[...] = jnp.zeros_like(sum_ref)

    turned, weighed = [], []
    for w in range(windows):
        turned.append(k_ref[w].astype(F32).T.astype(BF16))
        weighed.append(g_ref[w].astype(F32).T * o_ref[w].astype(F32).T)
    grad_q = [[] for _ in range(windows)]
    grad_k, grad_v = [None] * windows, [None] * windows
    for h in range(GROUP):
        here = slice(h * head_size, (h + 1) * head_size)
        total = None
        for w in range(windows):
            q, k, v, g = q_ref[w], k_ref[w], v_ref[w], g_ref[w]
            inner = jnp.sum(weighed[w][here], axis=0, keepdims=True)
            scores = mm(k * masks[h], q, 1, 1) * factor + bias_ref[h]
            if shifted:
                scores = jnp.where(labels[w][0] == labels[w][1], scores, masked_score)
            probs = jnp.exp2(scores - log_ref[w, 0, h : h + 1])
            grad_probs = mm(v * masks[h], g, 1, 1)
            grad_scores = (probs * (grad_probs - inner)).astype(BF16)
            part_v = mm(probs.astype(BF16), g * masks[h])
            part_k = mm(grad_scores, q * masks[h])
            grad_v[w] = part_v if grad_v[w] is None else grad_v[w] + part_v
            grad_k[w] = part_k if grad_k[w] is None else grad_k[w] + part_k
            grad_q[w].append(mm(turned[w][here], grad_scores))
            wide = grad_scores.astype(F32)
            total = wide if total is None else total + wide
        sum_ref[:, :TOKENS] = total
        sums = None
        for key_frame in range(WIN_T):
            rows = sum_ref[key_frame * CELLS : (key_frame + 1) * CELLS, :]
            step = (WIN_T - 1 - key_frame) * CELLS
            rows = pltpu.roll(rows, step, 1) if step else rows
            sums = rows if sums is None else sums + rows
        table_ref[h] = sums
    for w in range(windows):
        dq_ref[w] = (jnp.concatenate(grad_q[w], axis=0) * scale).T.astype(BF16)
        dk_ref[w] = (grad_k[w] * scale).astype(BF16)
        dv_ref[w] = grad_v[w].astype(BF16)


def run_attend_back(qkv, grad, attended, bias, flags, log, shifted, first, count, after=None):
    windows, _, width3 = qkv.shape
    width = width3 // 3
    wide = GROUP * (width // HEADS)
    groups = HEADS // GROUP
    qkv_specs = [
        pl.BlockSpec((windows, TOKENS, wide), lambda g, p=part: (0, 0, p * groups + first + g))
        for part in range(3)
    ]
    flat = pl.BlockSpec((windows, TOKENS, wide), lambda g: (0, 0, g))
    flat_shape = jax.ShapeDtypeStruct((windows, TOKENS, count * wide), BF16)
    return functools.partial(call, after=after)(
        functools.partial(attend_back_kernel, shifted, width // HEADS),
        (count,),
        [flag_spec()]
        + qkv_specs
        + [
            pl.BlockSpec((windows, TOKENS, wide), lambda g: (0, 0, first + g)),
            pl.BlockSpec((windows, TOKENS, wide), lambda g: (0, 0, first + g)),
            pl.BlockSpec((GROUP, TOKENS, TOKENS), lambda g: (first + g, 0, 0)),
            whole_block((TOKENS, 8)),
            whole_block((8, TOKENS)),
            pl.BlockSpec((windows, 1, 2 * GROUP, TOKENS), lambda g: (0, first + g, 0, 0)),
        ],
        [flat, flat, flat, pl.BlockSpec((GROUP, CELLS, WIDE), lambda g: (g, 0, 0))],
        [flat_shape] * 3 + [jax.ShapeDtypeStruct((count * GROUP, CELLS, WIDE), F32)],
        160 * windows * TOKENS * TOKENS * count * wide,
        [pltpu.VMEM((TOKENS, WIDE), F32)],
    )(flags, qkv, qkv, qkv, grad, attended, bias, late_tokens(), late_tokens().T, log)


def normal_below(x):
    bell = jnp.exp2(x * x * (-0.5 * LOG2E)) * (1.0 / math.sqrt(2 * math.pi))
    return 0.5 + 0.5 * lax.erf(x * math.sqrt(0.5)), bell


def spread_down(down_ref, w2_ref):
    _, parts, own, width = w2_ref.shape
    for part in range(parts):
        cols = slice(part * width, (part + 1) * width)
        w2_ref[:, part] = down_ref[:, cols].reshape(-1, own, width)


def chunk_rows(w2_ref, first, chunk):
    _, parts, own, width = w2_ref.shape
    step = chunk // (parts * own)
    return w2_ref[first * step : (first + 1) * step].reshape(chunk, width)


def branch_kernel(count, *refs):
    att_refs = refs[:count]
    x_ref, vec_ref, wo_ref, w1_ref, down_ref, mid_ref, hid_ref, slope_ref, out_ref, w2_ref = refs[count:]

    @pl.when(pl.program_id(0) == 0)
    def _():
        spread_down(down_ref, w2_ref)

    chunk = 512
    attended = jnp.concatenate([ref[0] for ref in att_refs], axis=1)
    middle = x_ref[0].astype(F32) + mm(attended, wo_ref[...]) + vec_ref[4:5]
    mid_ref[0] = middle
    unit, _ = unit_rows(middle)
    normed = (unit * vec_ref[5:6] + vec_ref[6:7]).astype(BF16)
    after = middle + vec_ref[7:8]
    for n in range(w1_ref.shape[1] // chunk):
        cols = slice(n * chunk, (n + 1) * chunk)
        pre = mm(normed, w1_ref[:, cols]) + vec_ref[8 + n : 9 + n]
        below, bell = normal_below(pre)
        hidden = (pre * below).astype(BF16)
        hid_ref[0, :, cols] = hidden
        slope_ref[0, :, cols] = (below + pre * bell).astype(BF16)
        after = after + mm(hidden, chunk_rows(w2_ref, n, chunk))
    out_ref[0] = after.astype(out_ref.dtype)


def weight_block(rows, width, column):
    return pl.BlockSpec((rows, width), lambda *ids: (0, column))


def branch_weights(weights, width, wide):
    (wo, wo_at), (w1, w1_at), (down, down_at) = weights
    specs = [
        weight_block(width, width, wo_at),
        weight_block(width, wide, w1_at),
        weight_block(width, wide, down_at),
    ]
    return (wo, w1, down), specs


def run_branch(x, attended, vec, weights, out_dtype, after=None):
    windows, _, width = x.shape
    wide = 4 * width
    arrays, specs = branch_weights(weights, width, wide)
    return functools.partial(call, after=after)(
        functools.partial(branch_kernel, len(attended)),
        (windows,),
        [win_block(part.shape[-1]) for part in attended]
        + [win_block(width), whole_block(vec.shape)]
        + specs,
        [win_block(width), win_block(wide), win_block(wide), win_block(width)],
        [
            jax.ShapeDtypeStruct((windows, TOKENS, width), F32),
            jax.ShapeDtypeStruct((windows, TOKENS, wide), BF16),
            jax.ShapeDtypeStruct((windows, TOKENS, wide), BF16),
            jax.ShapeDtypeStruct((windows, TOKENS, width), out_dtype),
        ],
        2 * windows * TOKENS * width * (width + 2 * wide),
        [pltpu.VMEM((width // 16, wide // width, 16, width), BF16)],
    )(*attended, x, vec, *arrays)


def add_rows(ref, rows, value):
    ref[rows, :] += jnp.sum(value.astype(F32), axis=0, keepdims=True)


def split_out(sums_ref, core, own_ref, sent_ref):
    own_ref[...] = sums_ref[:, core]
    sent_ref[...] = sums_ref[:, 1 - core].astype(BF16)


def branch_back_kernel(count, split, flag_ref, *refs):
    att_refs = refs[:count]
    grad_ref, mid_ref, hid_ref, slope_ref, vec_ref, wo_ref, w1_ref, down_ref = refs[count : count + 8]
    gm_ref, ga_ref, vecs_ref = refs[count + 8 : count + 11]
    outs, (d1_ref, d2_ref, w2_ref) = refs[count + 11 : -3], refs[-3:]
    chunk = 512
    width, wide = w1_ref.shape

    @pl.when(pl.program_id(0) == 0)
    def _():
        spread_down(down_ref, w2_ref)
        d1_ref[...] = jnp.zeros_like(d1_ref)
        d2_ref[...] = jnp.zeros_like(d2_ref)
        vecs_ref[...] = jnp.zeros_like(vecs_ref)

    grad = grad_ref[0].astype(F32)
    branch = grad.astype(BF16)
    unit, inverse = unit_rows(mid_ref[0])
    normed = (unit * vec_ref[5:6] + vec_ref[6:7]).astype(BF16)
    add_rows(vecs_ref, slice(7, 8), branch)
    back = None
    blocks = chunk // d2_ref.shape[2]
    for n in range(wide // chunk):
        cols = slice(n * chunk, (n + 1) * chunk)
        total = mm(hid_ref[0, :, cols], branch, 0, 0)
        at = slice(n * blocks // 2, (n + 1) * blocks // 2)
        d2_ref[at] += total.reshape((-1,) + d2_ref.shape[1:])
        grad_pre = mm(branch, chunk_rows(w2_ref, n, chunk), 1, 1) * slope_ref[0, :, cols].astype(F32)
        grad_pre = grad_pre.astype(BF16)
        add_rows(vecs_ref, slice(8 + n, 9 + n), grad_pre)
        d1_ref[:, :, :, cols] += mm(normed, grad_pre, 0, 0).reshape(d1_ref.shape[:3] + (chunk,))
        part = mm(grad_pre, w1_ref[:, cols], 1, 1)
        back = part if back is None else back + part
    add_rows(vecs_ref, slice(5, 6), back * unit)
    add_rows(vecs_ref, slice(6, 7), back)
    middle_grad = grad + norm_back(back, unit, inverse, vec_ref[5:6])
    gm_ref[0] = middle_grad
    branch = middle_grad.astype(BF16)
    add_rows(vecs_ref, slice(4, 5), branch)
    attended = jnp.concatenate([ref[0] for ref in att_refs], axis=1)
    total = mm(attended, branch, 0, 0)
    d1_ref[:, :, :, wide:] += total.reshape(d1_ref.shape[:3] + (width,))
    ga_ref[0] = mm(branch, wo_ref[...], 1, 1).astype(BF16)

    @pl.when(pl.program_id(0) == pl.num_programs(0) - 1)
    def _():
        if split:
            split_out(d1_ref, flag_ref[0], *outs[:2])
            split_out(d2_ref, flag_ref[0], *outs[2:])
        else:
            (out_ref,) = outs
            out_ref[:, : wide + width] = d1_ref[...].reshape(width, -1).astype(BF16)
            parts = wide // width
            for part in range(parts):
                first = wide + width + part * width
                piece = d2_ref[:, :, part * 16 : (part + 1) * 16, :].reshape(width, width)
                out_ref[:, first : first + width] = piece.astype(BF16)


def run_branch_back(grad, middle, attended, hidden, slope, vec, weights, flags, split, after=None):
    windows, _, width = middle.shape
    wide = 4 * width
    arrays, specs = branch_weights(weights, width, wide)
    flat = win_block(width)
    pairs = width // 32
    if split:
        shapes = []
        for rows, cols in ((16, wide + width), (64, width)):
            shapes.append(jax.ShapeDtypeStruct((pairs, rows, cols), F32))
            shapes.append(jax.ShapeDtypeStruct((pairs, rows, cols), BF16))
    else:
        shapes = [jax.ShapeDtypeStruct((width, 2 * wide + width), BF16)]
    return functools.partial(call, after=after)(
        functools.partial(branch_back_kernel, len(attended), split),
        (windows,),
        [flag_spec()]
        + [win_block(part.shape[-1]) for part in attended]
        + [flat, flat, win_block(wide), win_block(wide), whole_block(vec.shape)]
        + specs,
        [flat, flat, whole_block(vec.shape)] + [whole_block(s.shape) for s in shapes],
        [
            jax.ShapeDtypeStruct((windows, TOKENS, width), F32),
            jax.ShapeDtypeStruct((windows, TOKENS, width), BF16),
            jax.ShapeDtypeStruct(vec.shape, F32),
        ]
        + shapes,
        4 * windows * TOKENS * width * (width + 2 * wide),
        [
            pltpu.VMEM((pairs, 2, 16, wide + width), F32),
            pltpu.VMEM((pairs, 2, 64, width), F32),
            pltpu.VMEM((pairs * 2, wide // width, 16, width), BF16),
        ],
    )(flags, *attended, grad, middle, hidden, slope, vec, *arrays)


def qkv_back_kernel(count, flag_ref, *refs):
    grads, refs = refs[: 3 * count], refs[3 * count :]
    x_ref, gm_ref, vec_ref, wq_ref, wk_ref, wv_ref, rest_ref, mask_ref, pick_ref, spread_ref = refs[:10]
    out_ref, own_ref, sent_ref, dw_ref, vecs_ref = refs[10:]
    width = x_ref.shape[-1]

    @pl.when(pl.program_id(0) == 0)
    def _():
        dw_ref[...] = jnp.zeros_like(dw_ref)
        vecs_ref[...] = rest_ref[...]

    unit, inverse = unit_rows(x_ref[0].astype(F32))
    normed = (unit * vec_ref[0:1] + vec_ref[1:2]).astype(BF16)
    back = None
    for part, ref in enumerate((wq_ref, wk_ref, wv_ref)):
        grad = jnp.concatenate([g[0] for g in grads[part * count : (part + 1) * count]], axis=1)
        total = mm(normed, grad, 0, 0)
        cols = slice(part * width, (part + 1) * width)
        dw_ref[:, :, :, cols] += total.reshape(dw_ref.shape[:3] + (width,))
        here = mm(grad, ref[...], 1, 1)
        back = here if back is None else back + here
        if part == 0:
            add_rows(vecs_ref, slice(2, 3), grad)
        if part == 2:
            add_rows(vecs_ref, slice(3, 4), grad)
    add_rows(vecs_ref, slice(0, 1), back * unit)
    add_rows(vecs_ref, slice(1, 2), back)
    out_ref[0] = (gm_ref[0] + norm_back(back, unit, inverse, vec_ref[0:1])).astype(out_ref.dtype)

    @pl.when(pl.program_id(0) == pl.num_programs(0) - 1)
    def _():
        rows = vecs_ref[...]
        high = rows.astype(BF16)
        low = (rows - high.astype(F32)).astype(BF16)
        total = None
        for piece in (high, low):
            piece = (mm(pick_ref[...], piece, 0, 0) * mask_ref[...].astype(F32)).astype(BF16)
            piece = mm(piece, spread_ref[0], 1, 1)
            total = piece if total is None else total + piece
        dw_ref[:, :, :, 3 * width :] = total.reshape(dw_ref.shape[:3] + (128,))
        split_out(dw_ref, flag_ref[0], own_ref, sent_ref)


def run_qkv_back(grads, x, grad_middle, vec, w_qkv, rest, flags, out_dtype, after=None):
    windows, _, width = x.shape
    flat = win_block(width)
    weight, at = w_qkv
    extra = [jnp.asarray(a, BF16) for a in vector_slots()]
    shape = (width // 32, 16, 3 * width + 128)
    return functools.partial(call, after=after)(
        functools.partial(qkv_back_kernel, len(grads) // 3),
        (windows,),
        [flag_spec()]
        + [win_block(part.shape[-1]) for part in grads]
        + [flat, flat, whole_block(vec.shape)]
        + [weight_block(width, width, at + n) for n in range(3)]
        + [whole_block(rest.shape)]
        + [whole_block(a.shape) for a in extra],
        [flat, whole_block(shape), whole_block(shape)],
        [
            jax.ShapeDtypeStruct((windows, TOKENS, width), out_dtype),
            jax.ShapeDtypeStruct(shape, F32),
            jax.ShapeDtypeStruct(shape, BF16),
        ],
        4 * windows * TOKENS * width * 3 * width,
        [pltpu.VMEM((shape[0], 2) + shape[1:], F32), pltpu.VMEM(rest.shape, F32)],
    )(flags, *grads, x, grad_middle, vec, weight, weight, weight, rest, *extra)


def pack_first_kernel(qkv_ref, *refs):
    vector_refs, (first_ref, rows_ref) = refs[:-2], refs[-2:]
    own, width3 = qkv_ref.shape[1:]
    rows_ref[...] = jnp.zeros_like(rows_ref)
    row = 0
    lane = lax.broadcasted_iota(jnp.int32, (1, 128), 1)
    for ref in vector_refs:
        values = ref[...].astype(F32)
        values = jnp.pad(values, ((0, 0), (0, 128 - values.shape[1])))
        for part in range(ref.shape[1] // own):
            line = jnp.zeros((1, 128), F32)
            for layer in range(LAYERS):
                turn = ((layer - part) * own) % 128
                turned = pltpu.roll(values, turn, 1) if turn else values
                here = (lane >= layer * own) & (lane < (layer + 1) * own)
                line = jnp.where(here, turned[layer : layer + 1], line)
            rows_ref[row : row + 1, :] = line
            row += 1
    first_ref[:, :width3] = qkv_ref[0]
    first_ref[:, width3:] = rows_ref[...].astype(BF16)


def pack_first(qkv, *vectors, after=None):
    own, width3 = qkv.shape[1:]
    return functools.partial(call, after=after)(
        pack_first_kernel,
        (1,),
        [whole_block((1, own, width3))] + [whole_block(v.shape) for v in vectors],
        whole_block((own, width3 + 128)),
        jax.ShapeDtypeStruct((own, width3 + 128), BF16),
        1e6,
        [pltpu.VMEM((16, 128), F32)],
    )(qkv, *vectors)


def pack_branch_kernel(out_ref, fc1_ref, fc2_ref, packed_ref):
    own, width, wide = fc1_ref.shape[1], fc2_ref.shape[2], fc1_ref.shape[2]
    for layer in range(LAYERS):
        first = 2 * wide * layer
        packed_ref[:, first : first + wide] = fc1_ref[layer]
        for part in range(wide // width):
            at = first + wide + part * width
            packed_ref[:, at : at + width] = fc2_ref[layer, part * own : (part + 1) * own, :]
        at = 2 * wide * LAYERS + layer * width
        packed_ref[:, at : at + width] = out_ref[layer]


def gather_branch(weights, after=None):
    own, wide = weights[1].shape[1:]
    width = weights[0].shape[2]
    packed = jax.ShapeDtypeStruct((own, LAYERS * (2 * wide + width)), BF16)
    shard = functools.partial(call, after=after)(
        pack_branch_kernel,
        (1,),
        [whole_block(w.shape) for w in weights],
        whole_block(packed.shape),
        packed,
        1e6,
    )(*weights)
    whole = lax.all_gather(shard, ALL, axis=0, tiled=True)
    outs = 2 * wide * LAYERS // width
    return [((whole, outs + n), (whole, 2 * n), (whole, 2 * n + 1)) for n in range(LAYERS)]


def vector_slots():
    devices, own = 32, 16
    count = devices * own
    mask = np.zeros((devices * 16, count), np.float32)
    pick = np.zeros((16, devices * 16), np.float32)
    spread = np.zeros((LAYERS, 128, count), np.float32)
    for device in range(devices):
        for first, parts in ((0, 1), (1, 1), (2, 2), (4, 1), (5, 1), (6, 1), (7, 1), (8, 4)):
            for part in range(parts):
                row, start = divmod(device * own * parts + part * own, count)
                slot = device * 16 + first + part
                pick[first + row, slot] = 1
                mask[slot, start : start + own] = 1
    for layer in range(LAYERS):
        for lane in range(count):
            spread[layer, layer * own + lane % own, lane] = 1
    return mask, pick, spread


def vectors_kernel(block_ref, mask_ref, pick_ref, spread_ref, out_ref):
    block = block_ref[...]
    for layer in range(LAYERS):
        lines = mm(block, spread_ref[layer]) * mask_ref[...].astype(F32)
        out_ref[layer] = mm(pick_ref[...], lines.astype(BF16))


def vectors_whole(blocks, after=None):
    count, width = blocks.shape
    extra = [jnp.asarray(a, BF16) for a in vector_slots()]
    return functools.partial(call, after=after)(
        vectors_kernel,
        (1,),
        [pl.BlockSpec((count, 128), lambda n: (0, width // 128 - 1))]
        + [whole_block(a.shape) for a in extra],
        whole_block((LAYERS, 16, count)),
        jax.ShapeDtypeStruct((LAYERS, 16, count), F32),
        1e9,
    )(blocks, *extra)


def finish_kernel(
    mix0_ref, mix1_ref, mid_ref, two_ref, later_ref, gain1_ref, bias1_ref, qkv_ref, qvb_ref, out_ref,
    outb_ref, gain2_ref, bias2_ref, fc1_ref, fc1b_ref, fc2_ref, fc2b_ref,
):
    width, wide = out_ref.shape[2], fc1_ref.shape[2]
    own = gain1_ref.shape[1]
    lane = lax.broadcasted_iota(jnp.int32, (1, 128), 1)
    for layer, mix_ref in enumerate((mix0_ref, mix1_ref)):
        qkv_ref[layer] = mix_ref[:, : 3 * width]
        row = 0
        for ref in (gain1_ref, bias1_ref, qvb_ref, outb_ref, gain2_ref, bias2_ref, fc2b_ref, fc1b_ref):
            line = jnp.zeros((1, 128), F32)
            for part in range(ref.shape[1] // own):
                piece = mix_ref[row : row + 1, 3 * width : 3 * width + 128]
                piece = pltpu.roll(piece, part * own, 1) if part else piece
                line = jnp.where((lane >= part * own) & (lane < (part + 1) * own), piece, line)
                row += 1
            ref[layer : layer + 1, :] = line[:, : ref.shape[1]]
    fc1_ref[0] = mid_ref[:, :wide]
    out_ref[0] = mid_ref[:, wide:]
    fc2_ref[0] = two_ref[...]
    fc1_ref[1] = later_ref[:, :wide].astype(F32)
    out_ref[1] = later_ref[:, wide : wide + width].astype(F32)
    for part in range(wide // width):
        first = wide + width + part * width
        piece = later_ref[:, first : first + width].astype(F32)
        fc2_ref[1, part * own : (part + 1) * own, :] = piece


def run_finish(mixes, mid, two, later):
    own, width = 16, two.shape[1]
    wide = mid.shape[1] - width
    shapes = [
        (own,), (own,), (own, 3 * width), (2 * own,), (own, width), (own,),
        (own,), (own,), (own, wide), (4 * own,), (4 * own, width), (own,),
    ]
    operands = [*mixes, mid, two, later]
    return call(
        finish_kernel,
        (1,),
        [whole_block(v.shape) for v in operands],
        [whole_block((LAYERS,) + shape) for shape in shapes],
        [jax.ShapeDtypeStruct((LAYERS,) + shape, F32) for shape in shapes],
        1e6,
    )(*operands)


def place_flags():
    quadrant = lax.axis_index(SPACE)
    last = lax.axis_index(TM) == lax.axis_size(TM) - 1
    flags = [lax.axis_index(CLIP) % 2, last, quadrant // 2, quadrant % 2]
    return jnp.stack([jnp.asarray(f, jnp.int32) for f in flags])


FIRST, TABLES, LATER, ROLL, GRAD, BACK, D_MID, D_TWO, TABLE, D_QKV = range(10)


def local_windows(
    clips_in,
    ln1_gain,
    ln1_bias,
    qkv_weight,
    qv_bias,
    out_weight,
    out_bias,
    ln2_gain,
    ln2_bias,
    fc1_weight,
    fc1_bias,
    fc2_weight,
    fc2_bias,
    pos_table,
    out_grad,
):
    _, frames_here, _, _, width = clips_in.shape
    windows = frames_here // WIN_T
    own = ln1_gain.shape[1]
    heads_here = pos_table.shape[2]
    one, two = stage_orders()
    flat = (windows, TOKENS, width)
    flags = place_flags()
    halo = Halo()
    flow = Flow()

    def stepped(run, *args, names=None, waits=(), **options):
        order = Order(flow.pending() + list(waits))
        out = run(*args, after=order, **options)
        flow.step(order.token, names)
        return out

    def halo_start(name, packed, onward):
        flow.start(name, halo_flow(packed, onward))

    def send_table():
        (came,), _ = yield [(tables, TM, swap_pairs(TM, 0))]
        first = lax.axis_index(TM) == 0
        return jnp.where(first, tables, came), jnp.where(first, came, tables)

    branch = (out_weight, fc1_weight, fc2_weight)
    first = pack_first(
        qkv_weight, ln1_gain, ln1_bias, qv_bias, out_bias, ln2_gain, ln2_bias, fc2_bias, fc1_bias
    )
    flow.start(FIRST, Gather(first, one))
    tables = pos_table.transpose(0, 2, 1)
    flow.start(TABLES, send_table())
    weights0, weights1 = stepped(gather_branch, branch)
    tables = flow.finish(TABLES)
    bias0 = stepped(table_to_bias, tables[0][0])
    bias0 = stepped(table_to_bias, tables[1][0], bias0)
    bias1 = stepped(table_to_bias, tables[0][1])
    stream0, grad_in = clips_in.reshape(flat), out_grad.reshape(flat)
    grad_packed = halo_pack(grad_in, halo, True, after=Order([stream0, bias1]))
    first = flow.finish(FIRST)
    flow.start(LATER, Gather(qkv_weight[1], one))
    vec = stepped(vectors_whole, first, waits=grad_packed)

    qkv0 = stepped(run_qkv, stream0, vec[0], (first, 0))
    att0, log0 = stepped(run_attend, qkv0, bias0, flags, False)
    mid0, hid0, slope0, stream1 = stepped(run_branch, stream0, [att0], vec[0], weights0, F32)
    halo_start(ROLL, halo_pack(stream1, halo, True, center=True), True)
    bias1 = stepped(table_to_bias, tables[1][1], bias1)
    later = flow.finish(LATER)
    rolled1 = halo_unpack(
        stream1, flow.finish(ROLL), halo, True, F32, center=True, after=Order([bias1])
    )
    qkv1 = run_qkv(rolled1, vec[1], (later, 0))
    halo_start(GRAD, grad_packed, True)
    att1, log1 = stepped(run_attend, qkv1, bias1, flags, True)
    mid1, hid1, slope1, rolled_out = stepped(
        run_branch, rolled1, [att1], vec[1], weights1, F32, waits=flow.done[GRAD]
    )
    out_packed = halo_pack(rolled_out, halo, False, joined=True)
    out_parts = halo_gather(out_packed)
    grad = stepped(halo_unpack, grad_in, flow.done[GRAD], halo, True, BF16, names=())

    kept = (
        (stream0, qkv0, att0, log0, mid0, hid0, slope0, bias0, weights0, (first, 0)),
        (rolled1, qkv1, att1, log1, mid1, hid1, slope1, bias1, weights1, (later, 0)),
    )
    tables = [None] * LAYERS
    for layer in reversed(range(LAYERS)):
        stream, qkv, att, log, mid, hid, slope, bias, weights, w_qkv = kept[layer]
        grad_mid, grad_att, rest, *halves = stepped(
            run_branch_back, grad, mid, [att], hid, slope, vec[layer], weights, flags, layer == 0,
            waits=[out_packed if layer else out_parts],
        )
        if layer == 0:
            flow.start(D_MID, scatter_flow(*halves[:2], one))
            flow.start(D_TWO, scatter_flow(*halves[2:], two))
        else:
            mid_share1 = lax.psum_scatter(halves[0], ALL, scatter_dimension=0, tiled=True)
        grads, sums = [], []
        calls = 1 if layer else 2
        groups = HEADS // GROUP // calls
        for n in range(calls):
            *parts, total = stepped(
                run_attend_back, qkv, grad_att, att, bias, flags, log, layer == 1, n * groups, groups,
            )
            grads.append(parts)
            sums.append(total)
        grads = [part for group in zip(*grads) for part in group]
        if layer == 0:
            tables[0] = [
                stepped(sums_to_table, total, names=names) for total, names in zip(sums, ((), None))
            ]
            pairs = [jnp.stack([tables[layer][n] for layer in range(LAYERS)]) for n in range(2)]
            flow.start(TABLE, table_flow(pairs, heads_here))
        grad_stream, *halves = stepped(
            run_qkv_back, grads, stream, grad_mid, vec[layer], w_qkv, rest, flags,
            F32 if layer else BF16,
        )
        if layer:
            halo_start(BACK, halo_pack(grad_stream, halo, False), False)
        flow.start(D_QKV + layer, scatter_flow(*halves, one))
        if layer:
            found = [
                stepped(sums_to_table, sums[0], n * heads_here, heads_here, names=names)
                for n, names in enumerate(((), ()))
            ]
            tables[1] = found
            grad = stepped(
                halo_unpack, grad_stream, flow.finish(BACK), halo, False, F32, names=(),
                waits=found,
            )
    in_grad = grad_stream
    clips_out = stepped(
        halo_unpack, rolled_out, out_parts, halo, False, BF16, mean_of=stream1
    )
    while flow.live:
        flow.step(None)
    grads = run_finish(
        [flow.done[D_QKV + layer] for layer in range(LAYERS)],
        flow.done[D_MID],
        flow.done[D_TWO],
        mid_share1,
    )
    return (
        clips_out.reshape(clips_in.shape),
        in_grad.reshape(clips_in.shape),
        *grads,
        flow.done[TABLE].transpose(0, 2, 1),
    )


def windows_are_local(mesh):
    def decide(clips_in, *rest):
        clips, frames_here = clips_in.shape[:2]
        own = rest[0].shape[1]
        return (
            clips == 1
            and frames_here % WIN_T == 0
            and own == 16
            and mesh.shape[TM] == 2
            and mesh.shape[SPACE] == 4
        )

    def program(*args):
        return local_windows(*args) if decide(*args) else per_device(*args)

    return program


def solution(mesh):
    placed = (
        P(CLIP, TM, SPACE, None, None),
        P(None, ALL),
        P(None, ALL),
        P(None, ALL, None),
        P(None, ALL),
        P(None, ALL, None),
        P(None, ALL),
        P(None, ALL),
        P(None, ALL),
        P(None, ALL, None),
        P(None, ALL),
        P(None, ALL, None),
        P(None, ALL),
        P(None, None, TM),
        P(CLIP, TM, SPACE, None, None),
    )
    return jax.shard_map(
        windows_are_local(mesh),
        mesh=mesh,
        in_specs=placed,
        out_specs=(
            P(CLIP, TM, SPACE, None, None),
            P(CLIP, TM, SPACE, None, None),
            P(None, ALL),
            P(None, ALL),
            P(None, ALL, None),
            P(None, ALL),
            P(None, ALL, None),
            P(None, ALL),
            P(None, ALL),
            P(None, ALL),
            P(None, ALL, None),
            P(None, ALL),
            P(None, ALL, None),
            P(None, ALL),
            P(None, None, TM),
        ),
        check_vma=False,
    )
```
